32 devices in a mesh: seq: 8 (over z, x), batch: 4 (over y, core).
Axes of the slice: x: 2, y: 2, z: 4, core: 2. Of those that a mesh axis runs over, the one named last changes fastest.
Arguments:
- tokens: bfloat16 [4, 1024, 768], P('batch', 'seq'), may hold values from -6 to 6
- doc_lengths: int32 [4, 4], P('batch'), may hold values from 1 to 960, 1024 in all within a row
- mixer_norm_gain: float32 [768], replicated, may hold values from 0.5 to 1.5
- mixer_in: bfloat16 [768, 2304], replicated, may hold values from -0.21875 to 0.21875
- shift_taps: float32 [64, 768], replicated, may hold values from -0.75 to 0.75
- mode_coef: float32 [64, 768], replicated, may hold values from -0.0625 to 0.0625
- mode_rate: float32 [64, 768], replicated, may hold values from 0.00024414062 to 0.1
- skip_gain: float32 [768], replicated, may hold values from 0.5 to 1.5
- mixer_out: bfloat16 [768, 768], replicated, may hold values from -0.21875 to 0.21875
- gain_second: float32 [768], replicated, may hold values from 0.5 to 1.5
- up_first: bfloat16 [768, 3072], replicated, may hold values from -0.21875 to 0.21875
- down_first: bfloat16 [3072, 768], replicated, may hold values from -0.109375 to 0.109375
- attention_norm_gain: float32 [768], replicated, may hold values from 0.5 to 1.5
- project_in: bfloat16 [768, 2304], replicated, may hold values from -0.21875 to 0.21875
- project_out: bfloat16 [768, 768], replicated, may hold values from -1.25 to 1.25
- gain_fourth: float32 [768], replicated, may hold values from 0.5 to 1.5
- up_second: bfloat16 [768, 3072], replicated, may hold values from -0.21875 to 0.21875
- down_second: bfloat16 [3072, 768], replicated, may hold values from -0.109375 to 0.109375
- cotangent: bfloat16 [4, 1024, 768], P('batch', 'seq'), may hold values from -6 to 6
Outputs:
- block_out: bfloat16 [4, 1024, 768], P('batch', 'seq')
- token_grad: float32 [4, 1024, 768], P('batch', 'seq')
- gain_first_grad: float32 [768], P('seq')
- mixer_in_grad: float32 [768, 2304], P('seq', 'batch')
- shift_taps_grad: float32 [64, 768], P('batch', 'seq')
- mode_coef_grad: float32 [64, 768], P(None, 'seq')
- mode_rate_grad: float32 [64, 768], P(None, 'seq')
- skip_gain_grad: float32 [768], P('seq')
- mixer_out_grad: float32 [768, 768], P('seq', 'batch')
- gain_second_grad: float32 [768], P('seq')
- up_first_grad: float32 [768, 3072], P('seq', 'batch')
- down_first_grad: float32 [3072, 768], P('seq', 'batch')
- gain_third_grad: float32 [768], P('seq')
- project_in_grad: float32 [768, 2304], P('seq', 'batch')
- project_out_grad: float32 [768, 768], P('seq', 'batch')
- gain_fourth_grad: float32 [768], P('seq')
- up_second_grad: float32 [768, 3072], P('seq', 'batch')
- down_second_grad: float32 [3072, 768], P('seq', 'batch')
The draws below stay inside these ranges and needn't reach their ends.
Inputs may be any that keep to these rules, and one draw needn't show every extreme that they name: `doc_lengths`: each row holds the lengths of the 4 documents packed in order into one stream; they sum to 1024, and the longest has exactly 960 tokens.
All inputs are finite; a program needn't handle non-finite values.
Results may differ from the reference program's by a relative error of at most 0.024.
Values may be sent and summed in bfloat16 or wider, within the bound.
A program may use at most 256 MiB of HBM per device.

```python
import math
import jax
import jax.numpy as jnp
import numpy as np
from jax import lax

D = 768
FF = 3072
HEADS = 12
HD = 64
STATE = 64
SHIFT = 64
DOCS = 4
S = 1024
STREAMS = 4
MOST = 960


def shard_levels(key, extent, shards, smallest, largest):
    loudness, own = 1.0, jax.random.fold_in(key, 6)
    for axis_at, blocks in shards:
        draws = jnp.exp(jax.random.uniform(jax.random.fold_in(own, axis_at), (blocks,), jnp.float32, smallest / len(shards), largest / len(shards)))
        loudness = loudness * jnp.repeat(draws, extent[axis_at] // blocks).reshape([-1 if axis == axis_at else 1 for axis in range(len(extent))])
    return loudness


def length_profile(amount, total, reach, slope):
    weights = [(1 << 20) // math.isqrt(grade ** slope) + 1 for grade in range(2, amount + 1)]
    spare, counts = total - reach - (amount - 1), [1] * (amount - 1)
    while spare > 0:
        movable = [i for i in range(amount - 1) if counts[i] < reach]
        whole, remaining = sum([weights[i] for i in movable]), spare
        for i in movable:
            extra = min(reach - counts[i], max(1, remaining * weights[i] // whole), spare)
            counts[i] = counts[i] + extra
            spare = spare - extra
    return np.array([reach] + counts)


def ragged(key, amount, total, most, lean):
    if amount == 2:
        one = jax.random.randint(key, (), max(1, total - most), min(most, total - 1) + 1)
        return jnp.stack([one, total - one])
    sizes = jnp.asarray(length_profile(amount, total, most, lean), jnp.int32)
    couples = (amount - 1) // 2
    giver, sink = sizes[1:1 + 2 * couples:2], sizes[2:2 + 2 * couples:2]
    margin = jnp.minimum(giver - 1, most - sink)
    moved = jax.random.randint(jax.random.fold_in(key, 1), (couples,), 0, 1 << 20) % (margin + 1)
    sizes = sizes.at[1:1 + 2 * couples:2].set(giver - moved).at[2:2 + 2 * couples:2].set(sink + moved)
    return sizes[jax.random.permutation(jax.random.fold_in(key, 2), amount)]


def scatter_about(key, dims, deviation, most, pieces=(), held_as=jnp.bfloat16):
    loudness = shard_levels(key, dims, pieces, -0.22, 0.18) if pieces else 1.0
    values = jax.random.normal(key, dims, jnp.float32) * deviation * loudness
    return jnp.minimum(jnp.maximum(values, -most), most).astype(held_as)


def setup_inputs(seed: int = 0) -> dict:
    streams_of = jax.random.split(jax.random.key(seed), 20)
    return {
        "tokens": scatter_about(streams_of[0], (STREAMS, S, D), 1.0, 6.0, ((0, 4), (1, 8))),
        "doc_lengths": jax.vmap(lambda own: ragged(own, DOCS, S, MOST, 2))(jax.random.split(streams_of[1], STREAMS)).reshape((STREAMS, DOCS)).astype(jnp.int32),
        "mixer_norm_gain": jnp.clip(1.0 + 0.1 * jax.random.normal(streams_of[2], (D,), jnp.float32), 0.5, 1.5),
        "mixer_in": scatter_about(streams_of[3], (D, 3 * D), D ** -0.5, 0.21875),
        "shift_taps": scatter_about(streams_of[4], (SHIFT, D), SHIFT ** -0.5, 0.75, (), jnp.float32),
        "mode_coef": scatter_about(streams_of[5], (STATE, D), (8 * S) ** -0.5, 0.0625, (), jnp.float32),
        "mode_rate": jnp.clip(jnp.exp(jax.random.uniform(streams_of[6], (STATE, D), jnp.float32, math.log(0.00024414062), math.log(0.1))), 0.00024414062, 0.1),
        "skip_gain": jnp.clip(1.0 + 0.1 * jax.random.normal(streams_of[7], (D,), jnp.float32), 0.5, 1.5),
        "mixer_out": scatter_about(streams_of[8], (D, D), D ** -0.5, 0.21875),
        "gain_second": jnp.clip(1.0 + 0.1 * jax.random.normal(streams_of[9], (D,), jnp.float32), 0.5, 1.5),
        "up_first": scatter_about(streams_of[10], (D, FF), D ** -0.5, 0.21875),
        "down_first": scatter_about(streams_of[11], (FF, D), FF ** -0.5, 0.109375),
        "attention_norm_gain": jnp.clip(1.0 + 0.1 * jax.random.normal(streams_of[12], (D,), jnp.float32), 0.5, 1.5),
        "project_in": scatter_about(streams_of[13], (D, 3 * D), D ** -0.5, 0.21875),
        "project_out": scatter_about(streams_of[14], (D, D), (D // 32) ** -0.5, 1.25),
        "gain_fourth": jnp.clip(1.0 + 0.1 * jax.random.normal(streams_of[15], (D,), jnp.float32), 0.5, 1.5),
        "up_second": scatter_about(streams_of[16], (D, FF), D ** -0.5, 0.21875),
        "down_second": scatter_about(streams_of[17], (FF, D), FF ** -0.5, 0.109375),
        "cotangent": scatter_about(streams_of[18], (STREAMS, S, D), 1.0, 6.0, ((0, 4), (1, 8))),
    }


@jax.custom_vjp
def low(v):
    return lax.optimization_barrier(v.astype(jnp.bfloat16)).astype(jnp.float32)

@jax.custom_vjp
def low_back(v):
    return v

def low_keep(v):
    return (low(v), None)

def low_pass(kept, grad):
    return (grad,)

def back_keep(v):
    return (v, None)

def back_low(kept, grad):
    return (low(grad),)
low.defvjp(low_keep, low_pass)
low_back.defvjp(back_keep, back_low)

def product(left, right):
    return jnp.dot(left, right, precision=lax.Precision.HIGHEST, preferred_element_type=jnp.float32)

def layer_norm(value, gain_vector):
    row_mean = lax.optimization_barrier(jnp.mean(value, axis=-1, keepdims=True))
    cent = value - row_mean
    return cent * lax.rsqrt(lax.optimization_barrier(jnp.mean(cent * cent, axis=-1, keepdims=True)) + 1e-05) * gain_vector

def segment_of(where, ends):
    return lax.optimization_barrier(jnp.sum((where[:, None] >= ends[None, :]).astype(jnp.int32), axis=1))

def kernel_of(coef, rate, times):

    def step(total, pair):
        scale, decay = pair
        return (total + scale[None, :] * jnp.exp(-decay[None, :] * times[:, None]), None)
    start = jnp.zeros((times.shape[0], coef.shape[1]), jnp.float32)
    return lax.scan(jax.checkpoint(step), start, (coef, rate))[0]

def long_conv(signal, kernel):
    length = 2 * signal.shape[0]
    spec = jnp.fft.rfft(signal, n=length, axis=0) * jnp.fft.rfft(kernel, n=length, axis=0)
    return jnp.fft.irfft(spec, n=length, axis=0)[:signal.shape[0]]

def shift_conv(keys, taps):
    count = keys.shape[0]
    lags = taps.shape[0]
    padded = jnp.concatenate([jnp.zeros((lags - 1, keys.shape[1]), jnp.float32), keys], axis=0)
    result_value = jnp.zeros_like(keys)
    for lag in range(lags):
        result_value = result_value + taps[lag] * padded[lags - 1 - lag:lags - 1 - lag + count]
    return result_value

def feed_forward(value, gain_vector, w_up, w_down):
    hidden = low(layer_norm(value, gain_vector))
    raised_rows = low_back(product(hidden, w_up))
    active_tokens = low(jax.nn.gelu(raised_rows))
    return value + low_back(product(active_tokens, w_down))

def attention(query, keys, values, ends):
    count = query.shape[0]
    width = query.shape[1]
    block = math.gcd(count, 512)
    scale = HD ** (-0.5)
    query_heads = query.reshape(count, HEADS, HD)
    key_heads = keys.reshape(count, HEADS, HD)
    value_heads = values.reshape(count, HEADS, HD)
    key_pos = jnp.arange(count, dtype=jnp.int32)
    key_seg = segment_of(key_pos, ends)

    def one(start):
        block_q = lax.dynamic_slice_in_dim(query_heads, start, block, 0)
        query_pos = start + jnp.arange(block, dtype=jnp.int32)
        query_seg = segment_of(query_pos, ends)
        scores = low_back(jnp.einsum('qhd,khd->hqk', block_q, key_heads, precision=lax.Precision.HIGHEST) * scale)
        allowed = (key_pos[None, :] <= query_pos[:, None]) & (query_seg[:, None] == key_seg[None, :])
        masked = jnp.where(allowed[None], scores, -1e+30)
        top = lax.optimization_barrier(jnp.max(masked, axis=-1, keepdims=True))
        weights = jnp.exp(masked - top)
        weights = weights / lax.optimization_barrier(jnp.sum(weights, axis=-1, keepdims=True))
        mixed = jnp.einsum('hqk,khd->qhd', weights, value_heads, precision=lax.Precision.HIGHEST)
        return mixed.reshape(block, width)
    starts = jnp.arange(0, count, block, dtype=jnp.int32)
    return lax.map(jax.checkpoint(one), starts).reshape(count, width)

def stream_forward(params, residual_stream, lengths):
    mixer_norm_gain, mixer_in, shift_taps, mode_coef, mode_rate, skip_gain, mixer_out, gain_second, up_first, down_first, attention_norm_gain, project_in, project_out, gain_fourth, up_second, down_second = params
    count = residual_stream.shape[0]
    width = residual_stream.shape[1]
    ends = jnp.cumsum(lengths).astype(jnp.int32)
    normed_rows = low(layer_norm(residual_stream, mixer_norm_gain))
    mixed = low_back(product(normed_rows, mixer_in))
    query, keys, values = (mixed[:, :width], mixed[:, width:2 * width], mixed[:, 2 * width:])
    product_kv = shift_conv(keys, shift_taps) * values
    times = jnp.arange(count, dtype=jnp.int32).astype(jnp.float32)
    kernel = kernel_of(mode_coef, mode_rate, times)
    response = long_conv(product_kv, kernel) + skip_gain * product_kv
    gated = low(query * response)
    stream_b = residual_stream + low_back(product(gated, mixer_out))
    attention_residual_stream = feed_forward(stream_b, gain_second, up_first, down_first)
    attention_normed_rows = low(layer_norm(attention_residual_stream, attention_norm_gain))
    mixed_c = low(low_back(product(attention_normed_rows, project_in)))
    attended = low(low_back(attention(mixed_c[:, :width], mixed_c[:, width:2 * width], mixed_c[:, 2 * width:], ends)))
    stream_d = attention_residual_stream + low_back(product(attended, project_out))
    return feed_forward(stream_d, gain_fourth, up_second, down_second)

def reference(tokens, doc_lengths, mixer_norm_gain, mixer_in, shift_taps, mode_coef, mode_rate, skip_gain, mixer_out, gain_second, up_first, down_first, attention_norm_gain, project_in, project_out, gain_fourth, up_second, down_second, cotangent):
    weights = tuple((weight.astype(jnp.float32) for weight in (mixer_norm_gain, mixer_in, shift_taps, mode_coef, mode_rate, skip_gain, mixer_out, gain_second, up_first, down_first, attention_norm_gain, project_in, project_out, gain_fourth, up_second, down_second)))

    def whole(params, streams):

        def each(pair):
            return stream_forward(params, pair[0], pair[1])
        return lax.map(each, (streams, doc_lengths))
    result_value, pull = jax.vjp(whole, weights, tokens.astype(jnp.float32))
    grads, token_grad = pull(cotangent.astype(jnp.float32))
    return (result_value.astype(jnp.bfloat16), token_grad, grads[0], grads[1], grads[2], grads[3], grads[4], grads[5], grads[6], grads[7], grads[8], grads[9], grads[10], grads[11], grads[12], grads[13], grads[14], grads[15])
```

```python
import functools
import math

import jax
import jax.numpy as jnp
from jax import lax
from jax.experimental import pallas as pl
from jax.experimental.pallas import tpu as pltpu
from jax.sharding import PartitionSpec as P

HEADS = 12


HIGH = lax.Precision.HIGHEST
NEGATIVE = -1e30


def shifted_2(value, axis, steps):
    count = lax.axis_size(axis)
    leading, last = (max(0, -steps), min(count, count - steps))
    return lax.ppermute(value, axis, [(source, source + steps) for source in range(leading, last)])


def shortened(x):

    def short(part):
        return part.astype(jnp.bfloat16) if part.dtype == jnp.float32 else part

    return jax.tree.map(short, x)


def mult(form, left, right):
    return jnp.einsum(form, left, right, precision=HIGH, preferred_element_type=jnp.float32)


def norm_pieces(value):
    row_mean = jnp.mean(value, axis=-1, keepdims=True)
    cent = value - row_mean
    inverse_deviation = lax.rsqrt(jnp.mean(cent * cent, axis=-1, keepdims=True) + 1e-05)
    return (cent * inverse_deviation, inverse_deviation)


def norm_backward(incoming_gradient, centered_normalized, inverse_deviation, gain_vector):
    gain_share = jnp.sum(incoming_gradient * centered_normalized, axis=0)
    scaled_rows = incoming_gradient * gain_vector
    inner_product = jnp.mean(scaled_rows, axis=-1, keepdims=True)
    cross_term = jnp.mean(scaled_rows * centered_normalized, axis=-1, keepdims=True)
    return (
        inverse_deviation * (scaled_rows - inner_product - centered_normalized * cross_term),
        gain_share,
    )


def segment_of(where, ends):
    return jnp.sum((where[:, None] >= ends[None, :]).astype(jnp.int32), axis=1)


def allowed(query_pos, key_pos, ends):
    same = segment_of(query_pos, ends)[:, None] == segment_of(key_pos, ends)[None, :]
    return (key_pos[None, :] <= query_pos[:, None]) & same


def kernel_rows(coef, rate, times):

    def step(total, pair):
        scale, decay = pair
        return (total + scale[:, None] * jnp.exp(-decay[:, None] * times[None, :]), None)

    start = jnp.zeros((coef.shape[1], times.shape[0]), jnp.float32)
    return lax.scan(step, start, (coef, rate))[0]


def kernel_grads(coef, rate, times, incoming_gradient):

    def step(carry, pair):
        scale, decay = pair
        fall = incoming_gradient * jnp.exp(-decay[:, None] * times[None, :])
        return (carry, (jnp.sum(fall, axis=1), -scale * jnp.sum(fall * times[None, :], axis=1)))

    return lax.scan(step, jnp.zeros((), jnp.float32), (coef, rate))[1]


def angle_pair(left, right, period):
    turns = left[:, None] * right[None, :] % period
    angle = turns.astype(jnp.float32) * (2.0 * math.pi / period)
    return (jnp.cos(angle), jnp.sin(angle))


def dft_tables(blocks, rows):
    wide = 2 * blocks
    block_ids = jnp.arange(blocks, dtype=jnp.int32)
    wide_ids = jnp.arange(wide, dtype=jnp.int32)
    row_ids = jnp.arange(rows, dtype=jnp.int32)
    return (
        angle_pair(block_ids, wide_ids, wide),
        angle_pair(wide_ids, row_ids, wide * rows),
        angle_pair(row_ids, row_ids, rows),
    )


def forward_spectrum(signal, tables, blocks, rows):
    (cos_one, sin_one), (cos_two, sin_two), (cos_three, sin_three) = tables
    folded = signal.reshape(signal.shape[0], blocks, rows)
    first_re = mult("cpr,pf->cfr", folded, cos_one)
    first_im = -mult("cpr,pf->cfr", folded, sin_one)
    turned_re = first_re * cos_two + first_im * sin_two
    turned_im = first_im * cos_two - first_re * sin_two
    spec_re = mult("cfr,rk->cfk", turned_re, cos_three) + mult("cfr,rk->cfk", turned_im, sin_three)
    spec_im = mult("cfr,rk->cfk", turned_im, cos_three) - mult("cfr,rk->cfk", turned_re, sin_three)
    return (spec_re, spec_im)


def inverse_signal(spec_re, spec_im, tables, blocks, rows):
    (cos_one, sin_one), (cos_two, sin_two), (cos_three, sin_three) = tables
    inner_re = mult("cfk,rk->cfr", spec_re, cos_three) - mult("cfk,rk->cfr", spec_im, sin_three)
    inner_im = mult("cfk,rk->cfr", spec_im, cos_three) + mult("cfk,rk->cfr", spec_re, sin_three)
    turned_re = inner_re * cos_two - inner_im * sin_two
    turned_im = inner_im * cos_two + inner_re * sin_two
    result_value = mult("cfr,pf->cpr", turned_re, cos_one) - mult("cfr,pf->cpr", turned_im, sin_one)
    return result_value.reshape(spec_re.shape[0], blocks * rows) / (2.0 * blocks * rows)


def attend_block(state, query, query_pos, key_block, value_block, key_pos, ends, scale):
    top, mass, accum = state
    scores = (
        jnp.einsum("qhd,khd->hqk", query, key_block, preferred_element_type=jnp.float32) * scale
    )
    mask = allowed(query_pos, key_pos, ends)[None]
    newtop = jnp.maximum(top, jnp.max(jnp.where(mask, scores, NEGATIVE), axis=-1))
    weights = jnp.where(mask, jnp.exp(scores - newtop[:, :, None]), 0.0)
    factor = jnp.exp(top - newtop)
    mass = mass * factor + jnp.sum(weights, axis=-1)
    accum = accum * factor[:, :, None] + jnp.einsum(
        "hqk,khd->hqd", weights, value_block.astype(jnp.float32), preferred_element_type=jnp.float32
    )
    return (newtop, mass, accum)


def score_grads(
    query, grads, lse_rows, delta_rows, query_pos, key_block, value_block, key_pos, ends, scale
):
    scores = (
        jnp.einsum("qhd,khd->hqk", query, key_block, preferred_element_type=jnp.float32) * scale
    )
    mask = allowed(query_pos, key_pos, ends)[None]
    probs = jnp.where(mask, jnp.exp(scores - lse_rows[:, :, None]), 0.0)
    dots = jnp.einsum("qhd,khd->hqk", grads, value_block, preferred_element_type=jnp.float32)
    return (probs, (probs * (dots - delta_rows[:, :, None])).astype(jnp.bfloat16))


def query_back(
    query, grads, lse_rows, delta_rows, query_pos, key_block, value_block, key_pos, ends, scale
):
    score_grad = score_grads(
        query, grads, lse_rows, delta_rows, query_pos, key_block, value_block, key_pos, ends, scale
    )[1]
    return (
        jnp.einsum("hqk,khd->qhd", score_grad, key_block, preferred_element_type=jnp.float32)
        * scale
    )


def key_back(
    query, grads, lse_rows, delta_rows, query_pos, key_block, value_block, key_pos, ends, scale
):
    probs, score_grad = score_grads(
        query, grads, lse_rows, delta_rows, query_pos, key_block, value_block, key_pos, ends, scale
    )
    key_part = (
        jnp.einsum("hqk,qhd->khd", score_grad, query, preferred_element_type=jnp.float32) * scale
    )
    value_part = jnp.einsum(
        "hqk,qhd->khd", probs, grads.astype(jnp.float32), preferred_element_type=jnp.float32
    )
    return (key_part, value_part)


def scan_keys(carry, keys, values, update):
    count = keys.shape[0]
    width = keys.shape[1]
    head_size = width // HEADS
    step = math.gcd(count, 1024)
    firsts = step * jnp.arange(count // step, dtype=jnp.int32)

    def inner_product(state, item):
        key_block, value_block, first = item
        key_pos = first + jnp.arange(step, dtype=jnp.int32)
        return (update(state, key_block, value_block, key_pos), None)

    items = (
        keys.reshape(count // step, step, HEADS, head_size),
        values.reshape(count // step, step, HEADS, head_size),
        firsts,
    )
    return lax.scan(inner_product, carry, items)[0]


def feed_forward(residual_stream, gain_vector, w_up, w_down):
    centered_normalized, inverse_deviation = norm_pieces(residual_stream)
    normed_rows = (centered_normalized * gain_vector).astype(jnp.bfloat16)
    raised_rows = jnp.dot(normed_rows, w_up, preferred_element_type=jnp.float32)
    active_tokens = jax.nn.gelu(raised_rows).astype(jnp.bfloat16)
    result_value = residual_stream + jnp.dot(
        active_tokens, w_down, preferred_element_type=jnp.float32
    )
    return (
        result_value,
        (centered_normalized, inverse_deviation, normed_rows, raised_rows, active_tokens),
    )


def feed_back(incoming_gradient, saved_residuals, gain_vector, w_up, w_down):
    centered_normalized, inverse_deviation, normed_rows, raised_rows, active_tokens = (
        saved_residuals
    )
    grad_low = incoming_gradient.astype(jnp.bfloat16)
    down_part = jnp.einsum("tf,td->fd", active_tokens, grad_low, preferred_element_type=jnp.float32)
    active_grad = jnp.einsum("td,fd->tf", grad_low, w_down, preferred_element_type=jnp.float32)
    slope = jax.vjp(jax.nn.gelu, raised_rows)[1](active_grad)[0].astype(jnp.bfloat16)
    up_part = jnp.einsum("td,tf->df", normed_rows, slope, preferred_element_type=jnp.float32)
    normed_gradient = jnp.einsum("tf,df->td", slope, w_up, preferred_element_type=jnp.float32)
    input_gradient, gain_share = norm_backward(
        normed_gradient, centered_normalized, inverse_deviation, gain_vector
    )
    return (incoming_gradient + input_gradient, gain_share, up_part, down_part)


def shards(
    tokens,
    doc_lengths,
    mixer_norm_gain,
    mixer_in,
    shift_taps,
    mode_coef,
    mode_rate,
    skip_gain,
    mixer_out,
    gain_second,
    up_first,
    down_first,
    attention_norm_gain,
    project_in,
    project_out,
    gain_fourth,
    up_second,
    down_second,
    cotangent,
):
    rows = tokens.shape[1]
    width = tokens.shape[2]
    blocks = lax.axis_size("seq")
    rank = lax.axis_index("seq")
    total = rows * blocks
    head_size = width // HEADS
    scale = head_size ** (-0.5)
    lags = shift_taps.shape[0]
    channels = width // blocks
    ends = jnp.cumsum(doc_lengths[0])
    here = rank * rows + jnp.arange(rows, dtype=jnp.int32)
    residual_stream = tokens[0].astype(jnp.float32)
    mixer_centered_normalized, mixer_inverse_deviation = norm_pieces(residual_stream)
    mixer_normed_rows = (mixer_centered_normalized * mixer_norm_gain).astype(jnp.bfloat16)
    mixed_a = jnp.dot(mixer_normed_rows, mixer_in, preferred_element_type=jnp.float32)
    query_a = mixed_a[:, :width]
    key_a = mixed_a[:, width : 2 * width]
    value_a = mixed_a[:, 2 * width :]
    rim = shifted_2(key_a[rows - (lags - 1) :].astype(jnp.bfloat16), "seq", 1).astype(jnp.float32)
    key_ext = jnp.concatenate([rim, key_a], axis=0)
    shifted = jnp.zeros_like(key_a)
    for lag in range(lags):
        shifted = shifted + shift_taps[lag] * key_ext[lags - 1 - lag : lags - 1 - lag + rows]
    product_kv = shifted * value_a
    channel_in = lax.all_to_all(
        product_kv.T.reshape(blocks, channels, rows).astype(jnp.bfloat16),
        "seq",
        split_axis=0,
        concat_axis=2,
        tiled=True,
    ).astype(jnp.float32)[0]
    times = jnp.arange(total, dtype=jnp.int32).astype(jnp.float32)
    coef_here = lax.dynamic_slice_in_dim(mode_coef, rank * channels, channels, 1)
    rate_here = lax.dynamic_slice_in_dim(mode_rate, rank * channels, channels, 1)
    kernel_here = kernel_rows(coef_here, rate_here, times)
    tables = dft_tables(blocks, rows)
    sig_re, sig_im = forward_spectrum(channel_in, tables, blocks, rows)
    ker_re, ker_im = forward_spectrum(kernel_here, tables, blocks, rows)
    conv_chan = inverse_signal(
        sig_re * ker_re - sig_im * ker_im, sig_re * ker_im + sig_im * ker_re, tables, blocks, rows
    )
    conv_home = lax.all_to_all(
        conv_chan.reshape(1, channels, total).astype(jnp.bfloat16),
        "seq",
        split_axis=2,
        concat_axis=0,
        tiled=True,
    ).astype(jnp.float32)
    response = conv_home.reshape(width, rows).T + skip_gain * product_kv
    gated = (query_a * response).astype(jnp.bfloat16)
    stream_b = residual_stream + jnp.dot(gated, mixer_out, preferred_element_type=jnp.float32)
    attention_residual_stream, saved_b = feed_forward(stream_b, gain_second, up_first, down_first)
    attention_centered_normalized, attention_inverse_deviation = norm_pieces(
        attention_residual_stream
    )
    attention_normed_rows = (attention_centered_normalized * attention_norm_gain).astype(
        jnp.bfloat16
    )
    mixed_c = jnp.dot(attention_normed_rows, project_in, preferred_element_type=jnp.float32).astype(
        jnp.bfloat16
    )
    query_flat = mixed_c[:, :width]
    key_flat = mixed_c[:, width : 2 * width]
    value_flat = mixed_c[:, 2 * width :]
    query_c = query_flat.reshape(rows, HEADS, head_size)
    key_heads = key_flat.reshape(rows, HEADS, head_size)
    value_heads = value_flat.reshape(rows, HEADS, head_size)

    def forward_update(state, key_block, value_block, key_pos):
        return attend_block(state, query_c, here, key_block, value_block, key_pos, ends, scale)

    begin = (
        jnp.full((HEADS, rows), NEGATIVE, jnp.float32),
        jnp.zeros((HEADS, rows), jnp.float32),
        jnp.zeros((HEADS, rows, head_size), jnp.float32),
    )
    piece = (
        lax.all_gather(key_flat, "seq", axis=0, tiled=True),
        lax.all_gather(value_flat, "seq", axis=0, tiled=True),
    )
    top, mass, accum = scan_keys(begin, piece[0], piece[1], forward_update)
    lse = top + jnp.log(mass)
    att_full = accum / mass[:, :, None]
    attended = att_full.transpose(1, 0, 2).reshape(rows, width).astype(jnp.bfloat16)
    stream_d = attention_residual_stream + jnp.dot(
        attended, project_out, preferred_element_type=jnp.float32
    )
    result_value, saved_d = feed_forward(stream_d, gain_fourth, up_second, down_second)
    block_out = result_value.astype(jnp.bfloat16)[None]
    incoming_gradient = cotangent[0].astype(jnp.float32)
    incoming_gradient, gain_four_part, up_two_part, down_two_part = feed_back(
        incoming_gradient, saved_d, gain_fourth, up_second, down_second
    )
    grad_low = incoming_gradient.astype(jnp.bfloat16)
    out_part_c = jnp.einsum("td,te->de", attended, grad_low, preferred_element_type=jnp.float32)
    att_grad = jnp.einsum(
        "te,de->td", grad_low, project_out, preferred_element_type=jnp.float32
    ).astype(jnp.bfloat16)
    grad_heads = att_grad.reshape(rows, HEADS, head_size)
    delta = jnp.sum(grad_heads.astype(jnp.float32).transpose(1, 0, 2) * att_full, axis=-1)
    zero_heads = jnp.zeros((rows, HEADS, head_size), jnp.float32)

    def query_update(summed, key_block, value_block, key_pos):
        return summed + query_back(
            query_c, grad_heads, lse, delta, here, key_block, value_block, key_pos, ends, scale
        )

    piece = (
        lax.all_gather(key_flat, "seq", axis=0, tiled=True),
        lax.all_gather(value_flat, "seq", axis=0, tiled=True),
    )
    query_grad = scan_keys(zero_heads, piece[0], piece[1], query_update)
    lse_all, delta_all = (
        lax.all_gather(lse, "seq", axis=1, tiled=True),
        lax.all_gather(delta, "seq", axis=1, tiled=True),
    )
    queries = lax.all_gather(query_flat, "seq", axis=0, tiled=True)
    grads = lax.all_gather(att_grad, "seq", axis=0, tiled=True)
    count = queries.shape[0]
    step = math.gcd(count, 1024)
    firsts = step * jnp.arange(count // step, dtype=jnp.int32)

    def inner_product(summed, item):
        query_block, grad_block, first = item
        query_pos = first + jnp.arange(step, dtype=jnp.int32)
        lse_rows = lax.dynamic_slice_in_dim(lse_all, first, step, 1)
        delta_rows = lax.dynamic_slice_in_dim(delta_all, first, step, 1)
        parts = key_back(
            query_block,
            grad_block,
            lse_rows,
            delta_rows,
            query_pos,
            key_heads,
            value_heads,
            here,
            ends,
            scale,
        )
        return ((summed[0] + parts[0], summed[1] + parts[1]), None)

    items = (
        queries.reshape(count // step, step, HEADS, head_size),
        grads.reshape(count // step, step, HEADS, head_size),
        firsts,
    )
    key_grad, value_grad = lax.scan(inner_product, (zero_heads, zero_heads), items)[0]
    key_grad = key_grad.reshape(rows, width)
    value_grad = value_grad.reshape(rows, width)
    mixed_grad_c = jnp.concatenate(
        [query_grad.reshape(rows, width), key_grad, value_grad], axis=1
    ).astype(jnp.bfloat16)
    in_part_c = jnp.einsum(
        "td,te->de", attention_normed_rows, mixed_grad_c, preferred_element_type=jnp.float32
    )
    attention_normed_gradient = jnp.einsum(
        "te,de->td", mixed_grad_c, project_in, preferred_element_type=jnp.float32
    )
    attention_norm_gradient, attention_gain_share = norm_backward(
        attention_normed_gradient,
        attention_centered_normalized,
        attention_inverse_deviation,
        attention_norm_gain,
    )
    incoming_gradient = incoming_gradient + attention_norm_gradient
    incoming_gradient, gain_two_part, up_one_part, down_one_part = feed_back(
        incoming_gradient, saved_b, gain_second, up_first, down_first
    )
    grad_low = incoming_gradient.astype(jnp.bfloat16)
    out_part_a = jnp.einsum("td,te->de", gated, grad_low, preferred_element_type=jnp.float32)
    gated_grad = jnp.einsum("te,de->td", grad_low, mixer_out, preferred_element_type=jnp.float32)
    query_grad_a = gated_grad * response
    response_grad = gated_grad * query_a
    skip_part = jnp.sum(response_grad * product_kv, axis=0)
    chan_grad = lax.all_to_all(
        response_grad.T.reshape(blocks, channels, rows).astype(jnp.bfloat16),
        "seq",
        split_axis=0,
        concat_axis=2,
        tiled=True,
    ).astype(jnp.float32)[0]
    grad_re, grad_im = forward_spectrum(chan_grad, tables, blocks, rows)
    signal_grad = inverse_signal(
        ker_re * grad_re + ker_im * grad_im,
        ker_re * grad_im - ker_im * grad_re,
        tables,
        blocks,
        rows,
    )
    kernel_grad = inverse_signal(
        sig_re * grad_re + sig_im * grad_im,
        sig_re * grad_im - sig_im * grad_re,
        tables,
        blocks,
        rows,
    )
    coef_part, rate_part = kernel_grads(coef_here, rate_here, times, kernel_grad)
    returned = lax.all_to_all(
        signal_grad.reshape(1, channels, total).astype(jnp.bfloat16),
        "seq",
        split_axis=2,
        concat_axis=0,
        tiled=True,
    ).astype(jnp.float32)
    kv_grad = returned.reshape(width, rows).T + skip_gain * response_grad
    shifted_grad = kv_grad * value_a
    value_grad_a = kv_grad * shifted
    later = shifted_2(shortened(shifted_grad[: lags - 1]), "seq", -1)
    grad_ext = jnp.concatenate([shifted_grad, later], axis=0)
    key_grad_a = jnp.zeros_like(key_a)
    tap_rows = []
    for lag in range(lags):
        key_grad_a = key_grad_a + shift_taps[lag] * grad_ext[lag : lag + rows]
        tap_rows.append(
            jnp.sum(shifted_grad * key_ext[lags - 1 - lag : lags - 1 - lag + rows], axis=0)
        )
    taps_part = jnp.stack(tap_rows)
    mixed_grad_a = jnp.concatenate([query_grad_a, key_grad_a, value_grad_a], axis=1).astype(
        jnp.bfloat16
    )
    in_part_a = jnp.einsum(
        "td,te->de", mixer_normed_rows, mixed_grad_a, preferred_element_type=jnp.float32
    )
    mixer_normed_gradient = jnp.einsum(
        "te,de->td", mixed_grad_a, mixer_in, preferred_element_type=jnp.float32
    )
    mixer_norm_gradient, mixer_gain_share = norm_backward(
        mixer_normed_gradient, mixer_centered_normalized, mixer_inverse_deviation, mixer_norm_gain
    )
    token_grad = (incoming_gradient + mixer_norm_gradient)[None]
    parts = (
        lax.psum_scatter(mixer_gain_share, "seq", scatter_dimension=0, tiled=True),
        lax.psum_scatter(in_part_a, "seq", scatter_dimension=0, tiled=True),
        lax.psum_scatter(taps_part, "seq", scatter_dimension=1, tiled=True),
        lax.psum_scatter(skip_part, "seq", scatter_dimension=0, tiled=True),
        lax.psum_scatter(out_part_a, "seq", scatter_dimension=0, tiled=True),
        lax.psum_scatter(gain_two_part, "seq", scatter_dimension=0, tiled=True),
        lax.psum_scatter(up_one_part, "seq", scatter_dimension=0, tiled=True),
        lax.psum_scatter(down_one_part, "seq", scatter_dimension=0, tiled=True),
        lax.psum_scatter(attention_gain_share, "seq", scatter_dimension=0, tiled=True),
        lax.psum_scatter(in_part_c, "seq", scatter_dimension=0, tiled=True),
        lax.psum_scatter(out_part_c, "seq", scatter_dimension=0, tiled=True),
        lax.psum_scatter(gain_four_part, "seq", scatter_dimension=0, tiled=True),
        lax.psum_scatter(up_two_part, "seq", scatter_dimension=0, tiled=True),
        lax.psum_scatter(down_two_part, "seq", scatter_dimension=0, tiled=True),
    )
    matrices = (
        lax.psum_scatter(
            parts[1].astype(jnp.bfloat16), "batch", scatter_dimension=1, tiled=True
        ).astype(jnp.float32),
        lax.psum_scatter(
            parts[2].astype(jnp.bfloat16), "batch", scatter_dimension=0, tiled=True
        ).astype(jnp.float32),
        lax.psum_scatter(
            parts[4].astype(jnp.bfloat16), "batch", scatter_dimension=1, tiled=True
        ).astype(jnp.float32),
        lax.psum_scatter(
            parts[6].astype(jnp.bfloat16), "batch", scatter_dimension=1, tiled=True
        ).astype(jnp.float32),
        lax.psum_scatter(
            parts[7].astype(jnp.bfloat16), "batch", scatter_dimension=1, tiled=True
        ).astype(jnp.float32),
        lax.psum_scatter(
            parts[9].astype(jnp.bfloat16), "batch", scatter_dimension=1, tiled=True
        ).astype(jnp.float32),
        lax.psum_scatter(
            parts[10].astype(jnp.bfloat16), "batch", scatter_dimension=1, tiled=True
        ).astype(jnp.float32),
        lax.psum_scatter(
            parts[12].astype(jnp.bfloat16), "batch", scatter_dimension=1, tiled=True
        ).astype(jnp.float32),
        lax.psum_scatter(
            parts[13].astype(jnp.bfloat16), "batch", scatter_dimension=1, tiled=True
        ).astype(jnp.float32),
    )
    smalls = lax.psum(
        (parts[0], coef_part, rate_part, parts[3], parts[5], parts[8], parts[11]), "batch"
    )
    return (
        block_out,
        token_grad,
        smalls[0],
        matrices[0],
        matrices[1],
        smalls[1],
        smalls[2],
        smalls[3],
        matrices[2],
        smalls[4],
        matrices[3],
        matrices[4],
        smalls[5],
        matrices[5],
        matrices[6],
        smalls[6],
        matrices[7],
        matrices[8],
    )


MESH = pl.DeviceIdType.MESH
BF = jnp.bfloat16
F32 = jnp.float32
LAYER, PAIR = (0, 1)
GIVEN = (4, 3)
OWN = (5, 3)


def flip(value):
    return 1 - value


def weight_sum_kernel(kinds, *refs):
    refs = list(refs)
    given = [[refs.pop(0) for _ in range(GIVEN[kind])] for kind in kinds]
    outs = [refs.pop(0) for _ in kinds]
    own_of = [[refs.pop(0) for _ in range(OWN[kind])] for kind in kinds]
    sums_of = [[refs.pop(0) for _ in range(7)] for kind in kinds]
    send_sem, recv_sem = refs
    s = lax.axis_index("seq")
    b = lax.axis_index("batch")
    z, x = s // 2, lax.rem(s, 2)
    y, c = b // 2, lax.rem(b, 2)
    zh, zl = z // 2, lax.rem(z, 2)
    sibling = (s, 2 * y + flip(c))
    by_x = (2 * z + flip(x), b)
    by_y = (s, 2 * flip(y) + c)
    by_l = (2 * (2 * zh + flip(zl)) + x, b)
    by_h = (2 * (2 * flip(zh) + zl) + x, b)
    barrier = pltpu.get_barrier_semaphore()
    for other in (sibling, by_x, by_y, by_l, by_h):
        pl.semaphore_signal(barrier, inc=1, device_id=other, device_id_type=MESH)
    pl.semaphore_wait(barrier, 5)
    started = []

    def send(source, target, other):
        at = len(started)
        copy = pltpu.make_async_remote_copy(
            src_ref=source,
            dst_ref=target,
            send_sem=send_sem.at[at],
            recv_sem=recv_sem.at[at],
            device_id=other,
            device_id_type=MESH,
        )
        copy.start()
        started.append(copy)
        return copy

    shared = []
    for kind, inputs, own in zip(kinds, given, own_of):
        mine = []
        own[0][:, 0:128] = inputs[0][...].T
        mine.append(send(own[0].at[:, 0:128], own[0].at[:, 128:256], sibling))
        own[1][0:128, :] = inputs[1][c]
        mine.append(send(inputs[1].at[flip(c)], own[1].at[128:256, :], sibling))
        if kind == LAYER:
            own[2][:, 0:128] = inputs[2][c].T
            own[3][...] = inputs[2][flip(c)].T
            mine.append(send(own[3], own[2].at[:, 128:256], sibling))
            own[4][0:128, :] = inputs[3][...]
            mine.append(send(inputs[3], own[4].at[128:256, :], sibling))
        else:
            own[2][:, 0:128] = inputs[2][...].T
            mine.append(send(own[2].at[:, 0:128], own[2].at[:, 128:256], sibling))
        shared.append(mine)

    stages = []
    for kind, own, sums, mine in zip(kinds, own_of, sums_of, shared):
        for copy in mine:
            copy.wait_recv()
        grads, near_a, near_b, next_a, next_b, third, fourth = sums
        half = grads.shape[4] // 2

        def place(product, at, tile):
            for block in range(8):
                grads[block % 2, at, block // 4, (block // 2) % 2, pl.ds(pl.multiple_of(96 * tile, 16), 96), :] = product[
                    96 * block : 96 * block + 96
                ].astype(BF)

        if kind == LAYER:

            @pl.loop(0, 6)
            def _(step):
                at, chunk = step // 3, lax.rem(step, 3)
                lanes = pl.ds(pl.multiple_of(256 * step, 256), 256)
                product = jnp.dot(own[0][...], own[1][:, lanes], preferred_element_type=F32)
                place(product[:, 0:128], at, 2 * chunk)
                place(product[:, 128:256], at, 2 * chunk + 1)

            @pl.loop(0, 8)
            def _(block):
                lanes = pl.ds(pl.multiple_of(384 * block, 384), 384)
                product = jnp.dot(own[2][...], own[4][:, lanes], preferred_element_type=F32)
                for at in range(2):
                    for tile in range(3):
                        grads[
                            lax.rem(block, 2), at, block // 4, lax.rem(block // 2, 2), 576 + 192 * tile : 768 + 192 * tile, :
                        ] = product[192 * at : 192 * at + 192, 128 * tile : 128 * tile + 128].astype(BF)

        else:

            @pl.loop(0, 2)
            def _(at):
                for chunk in range(3):
                    lanes = pl.ds(pl.multiple_of(768 * at + 256 * chunk, 256), 256)
                    right = own[1][:, lanes]
                    if chunk < 2:
                        product = jnp.dot(own[0][...], right, preferred_element_type=F32)
                    else:
                        first = lax.broadcasted_iota(jnp.int32, right.shape, 1) < 64
                        zero = jnp.zeros_like(right)
                        product = jnp.dot(own[0][...], jnp.where(first, right, zero), preferred_element_type=F32)
                        product += jnp.dot(own[2][...], jnp.where(first, zero, right), preferred_element_type=F32)
                    place(product[:, 0:128], at, 2 * chunk)
                    place(product[:, 128:256], at, 2 * chunk + 1)

        stages.append(
            [
                send(grads.at[flip(x), :, :, :, 0:half, :], near_a, by_x),
                send(grads.at[:, flip(y), :, :, half:, :], near_b, by_y),
            ]
        )

    for index, sums in enumerate(sums_of):
        grads, near_a, near_b, next_a, next_b, third, fourth = sums
        half = grads.shape[4] // 2
        for copy in stages[index]:
            copy.wait_recv()

        @pl.loop(0, 8)
        def _(step):
            high, mid, low = step // 4, lax.rem(step // 2, 2), lax.rem(step, 2)
            grads[x, high, mid, low, 0:half, :] += near_a[high, mid, low]
            grads[high, y, mid, low, half:, :] += near_b[high, mid, low]

        stages[index] = [
            send(grads.at[x, flip(y), :, :, 0:half, :], next_a, by_y),
            send(grads.at[flip(x), y, :, :, half:, :], next_b, by_x),
        ]
    for index, sums in enumerate(sums_of):
        grads, near_a, near_b, next_a, next_b, third, fourth = sums
        half = grads.shape[4] // 2
        for copy in stages[index]:
            copy.wait_recv()

        @pl.loop(0, 4)
        def _(step):
            mid, low = step // 2, lax.rem(step, 2)
            grads[x, y, mid, low, 0:half, :] += next_a[mid, low]
            grads[x, y, mid, low, half:, :] += next_b[mid, low]

        stages[index] = [send(grads.at[x, y, :, flip(zl), :, :], third, by_l)]
    for index, sums in enumerate(sums_of):
        grads, near_a, near_b, next_a, next_b, third, fourth = sums
        for copy in stages[index]:
            copy.wait_recv()

        @pl.loop(0, 2)
        def _(mid):
            grads[x, y, mid, zl] += third[mid]

        stages[index] = [send(grads.at[x, y, flip(zh), zl], fourth, by_h)]
    for index, sums in enumerate(sums_of):
        grads, near_a, near_b, next_a, next_b, third, fourth = sums
        for copy in stages[index]:
            copy.wait_recv()
        outs[index][...] = grads[x, y, zh, zl].astype(F32) + fourth[...].astype(F32)
    for copy in started:
        copy.wait_send()


def weight_sums(kinds, groups, identity):
    lengths = [1152 if kind == LAYER else 576 for kind in kinds]
    own, sums = [], []
    for kind, length in zip(kinds, lengths):
        own += [pltpu.VMEM((768, 256), BF), pltpu.VMEM((256, 1536), BF)]
        if kind == LAYER:
            own += [pltpu.VMEM((384, 256), BF), pltpu.VMEM((384, 128), BF), pltpu.VMEM((256, 3072), BF)]
        else:
            own += [pltpu.VMEM((768, 256), BF)]
        half = length // 2
        sums += [
            pltpu.VMEM((2, 2, 2, 2, length, 128), BF),
            pltpu.VMEM((2, 2, 2, half, 128), BF),
            pltpu.VMEM((2, 2, 2, half, 128), BF),
            pltpu.VMEM((2, 2, half, 128), BF),
            pltpu.VMEM((2, 2, half, 128), BF),
            pltpu.VMEM((2, length, 128), BF),
            pltpu.VMEM((length, 128), BF),
        ]
    copies = sum(GIVEN[kind] + 6 for kind in kinds)
    flat = [array for group in groups for array in group]
    vmem = pl.BlockSpec(memory_space=pltpu.VMEM)
    return pl.pallas_call(
        functools.partial(weight_sum_kernel, kinds),
        out_shape=[jax.ShapeDtypeStruct((length, 128), F32) for length in lengths],
        in_specs=[vmem] * len(flat),
        out_specs=[vmem] * len(kinds),
        scratch_shapes=own + sums + [pltpu.SemaphoreType.DMA((copies,)), pltpu.SemaphoreType.DMA((copies,))],
        compiler_params=pltpu.CompilerParams(
            collective_id=identity, has_side_effects=True, vmem_limit_bytes=60 * 2**20
        ),
    )(*flat)


def by_core(array, count):
    width = array.shape[1] // 4
    return array.reshape(128, 2, 2, width).transpose(2, 0, 1, 3).reshape(2, 128, 2 * width)


def pair_columns(wide, narrow):
    parts = jnp.concatenate([wide.reshape(128, 4, 576), narrow.reshape(128, 4, 192)], axis=2)
    return parts.reshape(128, 2, 2, 768).transpose(2, 0, 1, 3).reshape(2, 128, 1536)


def untile_layer(block):
    up = block[:576].reshape(6, 96, 128).transpose(1, 0, 2).reshape(96, 768)
    down = block[576:].reshape(3, 192, 128).transpose(0, 2, 1).reshape(384, 192)
    return up, down


def untile_pair(block):
    both = block.reshape(6, 96, 128).transpose(1, 0, 2).reshape(96, 768)
    return both[:, :576], both[:, 576:]


def mode_kernel(coef_ref, rate_ref, out_ref):
    blocks = out_ref.shape[0] // 8
    width = out_ref.shape[1]
    row = lax.broadcasted_iota(jnp.int32, (8, width), 0).astype(F32)
    out_ref[...] = jnp.zeros_like(out_ref)

    @pl.loop(0, 8)
    def _(group):
        rate = rate_ref[pl.ds(pl.multiple_of(8 * group, 8), 8), :]
        coef = coef_ref[pl.ds(pl.multiple_of(8 * group, 8), 8), :]
        falls = [coef[n : n + 1] * jnp.exp(-rate[n : n + 1] * row) for n in range(8)]
        steps = [jnp.exp(-rate[n : n + 1] * jnp.maximum(row, 8.0)) for n in range(8)]

        def step(at, falls):
            rows = pl.ds(pl.multiple_of(8 * at, 8), 8)
            out_ref[rows, :] += sum(falls[1:], falls[0])
            return tuple(fall * factor for fall, factor in zip(falls, steps))

        lax.fori_loop(0, blocks, step, tuple(falls), unroll=4)


def mode_rows(coef, rate, total):
    vmem = pl.BlockSpec(memory_space=pltpu.VMEM)
    return pl.pallas_call(
        mode_kernel,
        out_shape=jax.ShapeDtypeStruct((total, coef.shape[1]), F32),
        in_specs=[vmem] * 2,
        out_specs=vmem,
    )(coef, rate)


def mode_grad_kernel(coef_ref, rate_ref, grad_ref, coef_out, rate_out):
    blocks = grad_ref.shape[0] // 8
    width = grad_ref.shape[1]
    row = lax.broadcasted_iota(jnp.int32, (8, width), 0).astype(F32)

    @pl.loop(0, 8)
    def _(group):
        at_group = pl.ds(pl.multiple_of(8 * group, 8), 8)
        rate = rate_ref[at_group, :]
        coef = coef_ref[at_group, :]
        steps = [jnp.exp(-rate[n : n + 1] * jnp.maximum(row, 8.0)) for n in range(8)]
        zero = jnp.minimum(row, 0.0)

        def step(at, carry):
            totals, slopes = carry
            rows = pl.ds(pl.multiple_of(8 * (blocks - 1 - at), 8), 8)
            here = grad_ref[rows, :]
            slopes = tuple(slope * factor + total for slope, factor, total in zip(slopes, steps, totals))
            totals = tuple(total * factor + here for total, factor in zip(totals, steps))
            return totals, slopes

        totals, slopes = lax.fori_loop(0, blocks, step, ((zero,) * 8, (zero,) * 8), unroll=2)
        coef_rows, rate_rows = [], []
        for n in range(8):
            fall = jnp.exp(-rate[n : n + 1] * row)
            coef_rows.append(jnp.sum(fall * totals[n], axis=0, keepdims=True))
            rate_rows.append(
                -coef[n : n + 1] * jnp.sum(fall * (8.0 * steps[n] * slopes[n] + row * totals[n]), axis=0, keepdims=True)
            )
        coef_out[at_group, :] = jnp.concatenate(coef_rows, axis=0)
        rate_out[at_group, :] = jnp.concatenate(rate_rows, axis=0)


def mode_grads(coef, rate, grad):
    vmem = pl.BlockSpec(memory_space=pltpu.VMEM)
    shape = jax.ShapeDtypeStruct(coef.shape, F32)
    return pl.pallas_call(
        mode_grad_kernel, out_shape=[shape, shape], in_specs=[vmem] * 3, out_specs=[vmem] * 2
    )(coef, rate, grad)


def feed_back_only(incoming_gradient, saved_residuals, gain_vector, w_up, w_down):
    centered_normalized, inverse_deviation, normed_rows, raised_rows, active_tokens = (
        saved_residuals
    )
    grad_low = incoming_gradient.astype(jnp.bfloat16)
    active_grad = jnp.einsum("td,fd->tf", grad_low, w_down, preferred_element_type=jnp.float32)
    slope = jax.vjp(jax.nn.gelu, raised_rows)[1](active_grad)[0].astype(jnp.bfloat16)
    normed_gradient = jnp.einsum("tf,df->td", slope, w_up, preferred_element_type=jnp.float32)
    input_gradient, gain_share = norm_backward(
        normed_gradient, centered_normalized, inverse_deviation, gain_vector
    )
    return (incoming_gradient + input_gradient, gain_share, slope)


def shards_fast(
    tokens,
    doc_lengths,
    mixer_norm_gain,
    mixer_in,
    shift_taps,
    mode_coef,
    mode_rate,
    skip_gain,
    mixer_out,
    gain_second,
    up_first,
    down_first,
    attention_norm_gain,
    project_in,
    project_out,
    gain_fourth,
    up_second,
    down_second,
    cotangent,
):
    rows = tokens.shape[1]
    width = tokens.shape[2]
    blocks = lax.axis_size("seq")
    rank = lax.axis_index("seq")
    total = rows * blocks
    head_size = width // HEADS
    scale = head_size ** (-0.5)
    lags = shift_taps.shape[0]
    channels = width // blocks
    ends = jnp.cumsum(doc_lengths[0])
    here = rank * rows + jnp.arange(rows, dtype=jnp.int32)
    residual_stream = tokens[0].astype(jnp.float32)
    mixer_centered_normalized, mixer_inverse_deviation = norm_pieces(residual_stream)
    mixer_normed_rows = (mixer_centered_normalized * mixer_norm_gain).astype(jnp.bfloat16)
    mixed_a = jnp.dot(mixer_normed_rows, mixer_in, preferred_element_type=jnp.float32)
    query_a = mixed_a[:, :width]
    key_a = mixed_a[:, width : 2 * width]
    value_a = mixed_a[:, 2 * width :]
    rim = shifted_2(key_a[rows - (lags - 1) :].astype(jnp.bfloat16), "seq", 1).astype(jnp.float32)
    key_ext = jnp.concatenate([rim, key_a], axis=0)
    shifted = jnp.zeros_like(key_a)
    for lag in range(lags):
        shifted = shifted + shift_taps[lag] * key_ext[lags - 1 - lag : lags - 1 - lag + rows]
    product_kv = shifted * value_a
    channel_in = lax.all_to_all(
        product_kv.T.reshape(blocks, channels, rows).astype(jnp.bfloat16),
        "seq",
        split_axis=0,
        concat_axis=2,
        tiled=True,
    ).astype(jnp.float32)[0]
    times = jnp.arange(total, dtype=jnp.int32).astype(jnp.float32)
    coef_here = lax.dynamic_slice_in_dim(mode_coef, rank * channels, channels, 1)
    rate_here = lax.dynamic_slice_in_dim(mode_rate, rank * channels, channels, 1)
    kernel_here = mode_rows(coef_here, rate_here, total).T
    tables = dft_tables(blocks, rows)
    sig_re, sig_im = forward_spectrum(channel_in, tables, blocks, rows)
    ker_re, ker_im = forward_spectrum(kernel_here, tables, blocks, rows)
    conv_chan = inverse_signal(
        sig_re * ker_re - sig_im * ker_im, sig_re * ker_im + sig_im * ker_re, tables, blocks, rows
    )
    conv_home = lax.all_to_all(
        conv_chan.reshape(1, channels, total).astype(jnp.bfloat16),
        "seq",
        split_axis=2,
        concat_axis=0,
        tiled=True,
    ).astype(jnp.float32)
    response = conv_home.reshape(width, rows).T + skip_gain * product_kv
    gated = (query_a * response).astype(jnp.bfloat16)
    stream_b = residual_stream + jnp.dot(gated, mixer_out, preferred_element_type=jnp.float32)
    attention_residual_stream, saved_b = feed_forward(stream_b, gain_second, up_first, down_first)
    attention_centered_normalized, attention_inverse_deviation = norm_pieces(
        attention_residual_stream
    )
    attention_normed_rows = (attention_centered_normalized * attention_norm_gain).astype(
        jnp.bfloat16
    )
    mixed_c = jnp.dot(attention_normed_rows, project_in, preferred_element_type=jnp.float32).astype(
        jnp.bfloat16
    )
    query_flat = mixed_c[:, :width]
    key_flat = mixed_c[:, width : 2 * width]
    value_flat = mixed_c[:, 2 * width :]
    query_c = query_flat.reshape(rows, HEADS, head_size)
    key_heads = key_flat.reshape(rows, HEADS, head_size)
    value_heads = value_flat.reshape(rows, HEADS, head_size)

    def forward_update(state, key_block, value_block, key_pos):
        return attend_block(state, query_c, here, key_block, value_block, key_pos, ends, scale)

    begin = (
        jnp.full((HEADS, rows), NEGATIVE, jnp.float32),
        jnp.zeros((HEADS, rows), jnp.float32),
        jnp.zeros((HEADS, rows, head_size), jnp.float32),
    )
    piece = (
        lax.all_gather(key_flat, "seq", axis=0, tiled=True),
        lax.all_gather(value_flat, "seq", axis=0, tiled=True),
    )
    top, mass, accum = scan_keys(begin, piece[0], piece[1], forward_update)
    lse = top + jnp.log(mass)
    att_full = accum / mass[:, :, None]
    attended = att_full.transpose(1, 0, 2).reshape(rows, width).astype(jnp.bfloat16)
    stream_d = attention_residual_stream + jnp.dot(
        attended, project_out, preferred_element_type=jnp.float32
    )
    result_value, saved_d = feed_forward(stream_d, gain_fourth, up_second, down_second)
    block_out = result_value.astype(jnp.bfloat16)[None]
    incoming_gradient = cotangent[0].astype(jnp.float32)
    incoming_gradient, gain_four_part, slope_d = feed_back_only(
        incoming_gradient, saved_d, gain_fourth, up_second, down_second
    )
    grad_low_c = incoming_gradient.astype(jnp.bfloat16)
    att_grad = jnp.einsum(
        "te,de->td", grad_low_c, project_out, preferred_element_type=jnp.float32
    ).astype(jnp.bfloat16)
    grad_heads = att_grad.reshape(rows, HEADS, head_size)
    delta = jnp.sum(grad_heads.astype(jnp.float32).transpose(1, 0, 2) * att_full, axis=-1)
    zero_heads = jnp.zeros((rows, HEADS, head_size), jnp.float32)

    def query_update(summed, key_block, value_block, key_pos):
        return summed + query_back(
            query_c, grad_heads, lse, delta, here, key_block, value_block, key_pos, ends, scale
        )

    piece = (
        lax.all_gather(key_flat, "seq", axis=0, tiled=True),
        lax.all_gather(value_flat, "seq", axis=0, tiled=True),
    )
    query_grad = scan_keys(zero_heads, piece[0], piece[1], query_update)
    lse_all, delta_all = (
        lax.all_gather(lse, "seq", axis=1, tiled=True),
        lax.all_gather(delta, "seq", axis=1, tiled=True),
    )
    queries = lax.all_gather(query_flat, "seq", axis=0, tiled=True)
    grads = lax.all_gather(att_grad, "seq", axis=0, tiled=True)
    count = queries.shape[0]
    step = math.gcd(count, 1024)
    firsts = step * jnp.arange(count // step, dtype=jnp.int32)

    def inner_product(summed, item):
        query_block, grad_block, first = item
        query_pos = first + jnp.arange(step, dtype=jnp.int32)
        lse_rows = lax.dynamic_slice_in_dim(lse_all, first, step, 1)
        delta_rows = lax.dynamic_slice_in_dim(delta_all, first, step, 1)
        parts = key_back(
            query_block,
            grad_block,
            lse_rows,
            delta_rows,
            query_pos,
            key_heads,
            value_heads,
            here,
            ends,
            scale,
        )
        return ((summed[0] + parts[0], summed[1] + parts[1]), None)

    items = (
        queries.reshape(count // step, step, HEADS, head_size),
        grads.reshape(count // step, step, HEADS, head_size),
        firsts,
    )
    key_grad, value_grad = lax.scan(inner_product, (zero_heads, zero_heads), items)[0]
    key_grad = key_grad.reshape(rows, width)
    value_grad = value_grad.reshape(rows, width)
    mixed_grad_c = jnp.concatenate(
        [query_grad.reshape(rows, width), key_grad, value_grad], axis=1
    ).astype(jnp.bfloat16)
    attention_normed_gradient = jnp.einsum(
        "te,de->td", mixed_grad_c, project_in, preferred_element_type=jnp.float32
    )
    attention_norm_gradient, attention_gain_share = norm_backward(
        attention_normed_gradient,
        attention_centered_normalized,
        attention_inverse_deviation,
        attention_norm_gain,
    )
    incoming_gradient = incoming_gradient + attention_norm_gradient
    grad_in_b = incoming_gradient.astype(jnp.bfloat16)
    incoming_gradient, gain_two_part, slope_b = feed_back_only(
        incoming_gradient, saved_b, gain_second, up_first, down_first
    )
    grad_low = incoming_gradient.astype(jnp.bfloat16)
    gated_grad = jnp.einsum("te,de->td", grad_low, mixer_out, preferred_element_type=jnp.float32)
    query_grad_a = gated_grad * response
    response_grad = gated_grad * query_a
    skip_part = jnp.sum(response_grad * product_kv, axis=0)
    chan_grad = lax.all_to_all(
        response_grad.T.reshape(blocks, channels, rows).astype(jnp.bfloat16),
        "seq",
        split_axis=0,
        concat_axis=2,
        tiled=True,
    ).astype(jnp.float32)[0]
    grad_re, grad_im = forward_spectrum(chan_grad, tables, blocks, rows)
    signal_grad = inverse_signal(
        ker_re * grad_re + ker_im * grad_im,
        ker_re * grad_im - ker_im * grad_re,
        tables,
        blocks,
        rows,
    )
    kernel_grad = inverse_signal(
        sig_re * grad_re + sig_im * grad_im,
        sig_re * grad_im - sig_im * grad_re,
        tables,
        blocks,
        rows,
    )
    coef_part, rate_part = mode_grads(coef_here, rate_here, kernel_grad.T)
    returned = lax.all_to_all(
        signal_grad.reshape(1, channels, total).astype(jnp.bfloat16),
        "seq",
        split_axis=2,
        concat_axis=0,
        tiled=True,
    ).astype(jnp.float32)
    kv_grad = returned.reshape(width, rows).T + skip_gain * response_grad
    shifted_grad = kv_grad * value_a
    value_grad_a = kv_grad * shifted
    later = shifted_2(shortened(shifted_grad[: lags - 1]), "seq", -1)
    grad_ext = jnp.concatenate([shifted_grad, later], axis=0)
    key_grad_a = jnp.zeros_like(key_a)
    tap_rows = []
    for lag in range(lags):
        key_grad_a = key_grad_a + shift_taps[lag] * grad_ext[lag : lag + rows]
        tap_rows.append(
            jnp.sum(shifted_grad * key_ext[lags - 1 - lag : lags - 1 - lag + rows], axis=0)
        )
    taps_part = jnp.stack(tap_rows)
    mixed_grad_a = jnp.concatenate([query_grad_a, key_grad_a, value_grad_a], axis=1).astype(
        jnp.bfloat16
    )
    mixer_normed_gradient = jnp.einsum(
        "te,de->td", mixed_grad_a, mixer_in, preferred_element_type=jnp.float32
    )
    mixer_norm_gradient, mixer_gain_share = norm_backward(
        mixer_normed_gradient, mixer_centered_normalized, mixer_inverse_deviation, mixer_norm_gain
    )
    token_grad = (incoming_gradient + mixer_norm_gradient)[None]
    groups = (
        (saved_d[2], by_core(slope_d, 4), by_core(cotangent[0], 4), saved_d[4]),
        (attention_normed_rows, pair_columns(mixed_grad_c, grad_low_c), attended),
        (saved_b[2], by_core(slope_b, 4), by_core(grad_in_b, 4), saved_b[4]),
        (mixer_normed_rows, pair_columns(mixed_grad_a, grad_low), gated),
    )
    layer_d, pair_c, layer_b, pair_a = weight_sums((LAYER, PAIR, LAYER, PAIR), groups, 0)
    up_two, down_two = untile_layer(layer_d)
    in_c, out_c = untile_pair(pair_c)
    up_one, down_one = untile_layer(layer_b)
    in_a, out_a = untile_pair(pair_a)
    taps = lax.psum_scatter(taps_part, "seq", scatter_dimension=1, tiled=True)
    taps = lax.psum_scatter(taps.astype(jnp.bfloat16), "batch", scatter_dimension=0, tiled=True).astype(jnp.float32)
    shares = jnp.stack([mixer_gain_share, skip_part, gain_two_part, attention_gain_share, gain_four_part])
    shares = lax.psum_scatter(shares, "seq", scatter_dimension=1, tiled=True)
    shares, coef_part, rate_part = lax.psum((shares, coef_part, rate_part), "batch")
    return (
        block_out,
        token_grad,
        shares[0],
        in_a,
        taps,
        coef_part,
        rate_part,
        shares[1],
        out_a,
        shares[2],
        up_one,
        down_one,
        shares[3],
        in_c,
        out_c,
        shares[4],
        up_two,
        down_two,
    )


def solution(mesh):
    in_specs = (
        P("batch", "seq", None),
        P("batch", None),
        P(),
        P(),
        P(),
        P(),
        P(),
        P(),
        P(),
        P(),
        P(),
        P(),
        P(),
        P(),
        P(),
        P(),
        P(),
        P(),
        P("batch", "seq", None),
    )
    out_specs = (
        P("batch", "seq", None),
        P("batch", "seq", None),
        P("seq"),
        P("seq", "batch"),
        P("batch", "seq"),
        P(None, "seq"),
        P(None, "seq"),
        P("seq"),
        P("seq", "batch"),
        P("seq"),
        P("seq", "batch"),
        P("seq", "batch"),
        P("seq"),
        P("seq", "batch"),
        P("seq", "batch"),
        P("seq"),
        P("seq", "batch"),
        P("seq", "batch"),
    )
    fast = mesh.shape["seq"] == 8 and mesh.shape["batch"] == 4
    return jax.shard_map(shards_fast if fast else shards, mesh=mesh, in_specs=in_specs, out_specs=out_specs, check_vma=False)
```

```python
import functools
import math

import jax
import jax.numpy as jnp
import ml_dtypes
import numpy as np
from jax import lax
from jax.experimental import pallas as pl
from jax.experimental.pallas import tpu as pltpu
from jax.sharding import PartitionSpec as P

HEADS = 12


HIGH = lax.Precision.HIGHEST
NEGATIVE = -1e30


def shifted_2(value, axis, steps):
    count = lax.axis_size(axis)
    leading, last = (max(0, -steps), min(count, count - steps))
    return lax.ppermute(value, axis, [(source, source + steps) for source in range(leading, last)])


def shortened(x):

    def short(part):
        return part.astype(jnp.bfloat16) if part.dtype == jnp.float32 else part

    return jax.tree.map(short, x)


def mult(form, left, right):
    return jnp.einsum(form, left, right, precision=HIGH, preferred_element_type=jnp.float32)


def norm_pieces(value):
    row_mean = jnp.mean(value, axis=-1, keepdims=True)
    cent = value - row_mean
    inverse_deviation = lax.rsqrt(jnp.mean(cent * cent, axis=-1, keepdims=True) + 1e-05)
    return (cent * inverse_deviation, inverse_deviation)


def norm_backward(incoming_gradient, centered_normalized, inverse_deviation, gain_vector):
    gain_share = jnp.sum(incoming_gradient * centered_normalized, axis=0)
    scaled_rows = incoming_gradient * gain_vector
    inner_product = jnp.mean(scaled_rows, axis=-1, keepdims=True)
    cross_term = jnp.mean(scaled_rows * centered_normalized, axis=-1, keepdims=True)
    return (
        inverse_deviation * (scaled_rows - inner_product - centered_normalized * cross_term),
        gain_share,
    )


def segment_of(where, ends):
    return jnp.sum((where[:, None] >= ends[None, :]).astype(jnp.int32), axis=1)


def allowed(query_pos, key_pos, ends):
    same = segment_of(query_pos, ends)[:, None] == segment_of(key_pos, ends)[None, :]
    return (key_pos[None, :] <= query_pos[:, None]) & same


def kernel_rows(coef, rate, times):

    def step(total, pair):
        scale, decay = pair
        return (total + scale[:, None] * jnp.exp(-decay[:, None] * times[None, :]), None)

    start = jnp.zeros((coef.shape[1], times.shape[0]), jnp.float32)
    return lax.scan(step, start, (coef, rate))[0]


def kernel_grads(coef, rate, times, incoming_gradient):

    def step(carry, pair):
        scale, decay = pair
        fall = incoming_gradient * jnp.exp(-decay[:, None] * times[None, :])
        return (carry, (jnp.sum(fall, axis=1), -scale * jnp.sum(fall * times[None, :], axis=1)))

    return lax.scan(step, jnp.zeros((), jnp.float32), (coef, rate))[1]


def angle_pair(left, right, period):
    turns = left[:, None] * right[None, :] % period
    angle = turns.astype(jnp.float32) * (2.0 * math.pi / period)
    return (jnp.cos(angle), jnp.sin(angle))


def dft_tables(blocks, rows):
    wide = 2 * blocks
    block_ids = jnp.arange(blocks, dtype=jnp.int32)
    wide_ids = jnp.arange(wide, dtype=jnp.int32)
    row_ids = jnp.arange(rows, dtype=jnp.int32)
    return (
        angle_pair(block_ids, wide_ids, wide),
        angle_pair(wide_ids, row_ids, wide * rows),
        angle_pair(row_ids, row_ids, rows),
    )


def forward_spectrum(signal, tables, blocks, rows):
    (cos_one, sin_one), (cos_two, sin_two), (cos_three, sin_three) = tables
    folded = signal.reshape(signal.shape[0], blocks, rows)
    first_re = mult("cpr,pf->cfr", folded, cos_one)
    first_im = -mult("cpr,pf->cfr", folded, sin_one)
    turned_re = first_re * cos_two + first_im * sin_two
    turned_im = first_im * cos_two - first_re * sin_two
    spec_re = mult("cfr,rk->cfk", turned_re, cos_three) + mult("cfr,rk->cfk", turned_im, sin_three)
    spec_im = mult("cfr,rk->cfk", turned_im, cos_three) - mult("cfr,rk->cfk", turned_re, sin_three)
    return (spec_re, spec_im)


def inverse_signal(spec_re, spec_im, tables, blocks, rows):
    (cos_one, sin_one), (cos_two, sin_two), (cos_three, sin_three) = tables
    inner_re = mult("cfk,rk->cfr", spec_re, cos_three) - mult("cfk,rk->cfr", spec_im, sin_three)
    inner_im = mult("cfk,rk->cfr", spec_im, cos_three) + mult("cfk,rk->cfr", spec_re, sin_three)
    turned_re = inner_re * cos_two - inner_im * sin_two
    turned_im = inner_im * cos_two + inner_re * sin_two
    result_value = mult("cfr,pf->cpr", turned_re, cos_one) - mult("cfr,pf->cpr", turned_im, sin_one)
    return result_value.reshape(spec_re.shape[0], blocks * rows) / (2.0 * blocks * rows)


def attend_block(state, query, query_pos, key_block, value_block, key_pos, ends, scale):
    top, mass, accum = state
    scores = (
        jnp.einsum("qhd,khd->hqk", query, key_block, preferred_element_type=jnp.float32) * scale
    )
    mask = allowed(query_pos, key_pos, ends)[None]
    newtop = jnp.maximum(top, jnp.max(jnp.where(mask, scores, NEGATIVE), axis=-1))
    weights = jnp.where(mask, jnp.exp(scores - newtop[:, :, None]), 0.0)
    factor = jnp.exp(top - newtop)
    mass = mass * factor + jnp.sum(weights, axis=-1)
    accum = accum * factor[:, :, None] + jnp.einsum(
        "hqk,khd->hqd", weights, value_block.astype(jnp.float32), preferred_element_type=jnp.float32
    )
    return (newtop, mass, accum)


def score_grads(
    query, grads, lse_rows, delta_rows, query_pos, key_block, value_block, key_pos, ends, scale
):
    scores = (
        jnp.einsum("qhd,khd->hqk", query, key_block, preferred_element_type=jnp.float32) * scale
    )
    mask = allowed(query_pos, key_pos, ends)[None]
    probs = jnp.where(mask, jnp.exp(scores - lse_rows[:, :, None]), 0.0)
    dots = jnp.einsum("qhd,khd->hqk", grads, value_block, preferred_element_type=jnp.float32)
    return (probs, (probs * (dots - delta_rows[:, :, None])).astype(jnp.bfloat16))


def query_back(
    query, grads, lse_rows, delta_rows, query_pos, key_block, value_block, key_pos, ends, scale
):
    score_grad = score_grads(
        query, grads, lse_rows, delta_rows, query_pos, key_block, value_block, key_pos, ends, scale
    )[1]
    return (
        jnp.einsum("hqk,khd->qhd", score_grad, key_block, preferred_element_type=jnp.float32)
        * scale
    )


def key_back(
    query, grads, lse_rows, delta_rows, query_pos, key_block, value_block, key_pos, ends, scale
):
    probs, score_grad = score_grads(
        query, grads, lse_rows, delta_rows, query_pos, key_block, value_block, key_pos, ends, scale
    )
    key_part = (
        jnp.einsum("hqk,qhd->khd", score_grad, query, preferred_element_type=jnp.float32) * scale
    )
    value_part = jnp.einsum(
        "hqk,qhd->khd", probs, grads.astype(jnp.float32), preferred_element_type=jnp.float32
    )
    return (key_part, value_part)


def scan_keys(carry, keys, values, update):
    count = keys.shape[0]
    width = keys.shape[1]
    head_size = width // HEADS
    step = math.gcd(count, 1024)
    firsts = step * jnp.arange(count // step, dtype=jnp.int32)

    def inner_product(state, item):
        key_block, value_block, first = item
        key_pos = first + jnp.arange(step, dtype=jnp.int32)
        return (update(state, key_block, value_block, key_pos), None)

    items = (
        keys.reshape(count // step, step, HEADS, head_size),
        values.reshape(count // step, step, HEADS, head_size),
        firsts,
    )
    return lax.scan(inner_product, carry, items)[0]


def feed_forward(residual_stream, gain_vector, w_up, w_down):
    centered_normalized, inverse_deviation = norm_pieces(residual_stream)
    normed_rows = (centered_normalized * gain_vector).astype(jnp.bfloat16)
    raised_rows = jnp.dot(normed_rows, w_up, preferred_element_type=jnp.float32)
    active_tokens = jax.nn.gelu(raised_rows).astype(jnp.bfloat16)
    result_value = residual_stream + jnp.dot(
        active_tokens, w_down, preferred_element_type=jnp.float32
    )
    return (
        result_value,
        (centered_normalized, inverse_deviation, normed_rows, raised_rows, active_tokens),
    )


def feed_back(incoming_gradient, saved_residuals, gain_vector, w_up, w_down):
    centered_normalized, inverse_deviation, normed_rows, raised_rows, active_tokens = (
        saved_residuals
    )
    grad_low = incoming_gradient.astype(jnp.bfloat16)
    down_part = jnp.einsum("tf,td->fd", active_tokens, grad_low, preferred_element_type=jnp.float32)
    active_grad = jnp.einsum("td,fd->tf", grad_low, w_down, preferred_element_type=jnp.float32)
    slope = jax.vjp(jax.nn.gelu, raised_rows)[1](active_grad)[0].astype(jnp.bfloat16)
    up_part = jnp.einsum("td,tf->df", normed_rows, slope, preferred_element_type=jnp.float32)
    normed_gradient = jnp.einsum("tf,df->td", slope, w_up, preferred_element_type=jnp.float32)
    input_gradient, gain_share = norm_backward(
        normed_gradient, centered_normalized, inverse_deviation, gain_vector
    )
    return (incoming_gradient + input_gradient, gain_share, up_part, down_part)


def shards(
    tokens,
    doc_lengths,
    mixer_norm_gain,
    mixer_in,
    shift_taps,
    mode_coef,
    mode_rate,
    skip_gain,
    mixer_out,
    gain_second,
    up_first,
    down_first,
    attention_norm_gain,
    project_in,
    project_out,
    gain_fourth,
    up_second,
    down_second,
    cotangent,
):
    rows = tokens.shape[1]
    width = tokens.shape[2]
    blocks = lax.axis_size("seq")
    rank = lax.axis_index("seq")
    total = rows * blocks
    head_size = width // HEADS
    scale = head_size ** (-0.5)
    lags = shift_taps.shape[0]
    channels = width // blocks
    ends = jnp.cumsum(doc_lengths[0])
    here = rank * rows + jnp.arange(rows, dtype=jnp.int32)
    residual_stream = tokens[0].astype(jnp.float32)
    mixer_centered_normalized, mixer_inverse_deviation = norm_pieces(residual_stream)
    mixer_normed_rows = (mixer_centered_normalized * mixer_norm_gain).astype(jnp.bfloat16)
    mixed_a = jnp.dot(mixer_normed_rows, mixer_in, preferred_element_type=jnp.float32)
    query_a = mixed_a[:, :width]
    key_a = mixed_a[:, width : 2 * width]
    value_a = mixed_a[:, 2 * width :]
    rim = shifted_2(key_a[rows - (lags - 1) :].astype(jnp.bfloat16), "seq", 1).astype(jnp.float32)
    key_ext = jnp.concatenate([rim, key_a], axis=0)
    shifted = jnp.zeros_like(key_a)
    for lag in range(lags):
        shifted = shifted + shift_taps[lag] * key_ext[lags - 1 - lag : lags - 1 - lag + rows]
    product_kv = shifted * value_a
    channel_in = lax.all_to_all(
        product_kv.T.reshape(blocks, channels, rows).astype(jnp.bfloat16),
        "seq",
        split_axis=0,
        concat_axis=2,
        tiled=True,
    ).astype(jnp.float32)[0]
    times = jnp.arange(total, dtype=jnp.int32).astype(jnp.float32)
    coef_here = lax.dynamic_slice_in_dim(mode_coef, rank * channels, channels, 1)
    rate_here = lax.dynamic_slice_in_dim(mode_rate, rank * channels, channels, 1)
    kernel_here = kernel_rows(coef_here, rate_here, times)
    tables = dft_tables(blocks, rows)
    sig_re, sig_im = forward_spectrum(channel_in, tables, blocks, rows)
    ker_re, ker_im = forward_spectrum(kernel_here, tables, blocks, rows)
    conv_chan = inverse_signal(
        sig_re * ker_re - sig_im * ker_im, sig_re * ker_im + sig_im * ker_re, tables, blocks, rows
    )
    conv_home = lax.all_to_all(
        conv_chan.reshape(1, channels, total).astype(jnp.bfloat16),
        "seq",
        split_axis=2,
        concat_axis=0,
        tiled=True,
    ).astype(jnp.float32)
    response = conv_home.reshape(width, rows).T + skip_gain * product_kv
    gated = (query_a * response).astype(jnp.bfloat16)
    stream_b = residual_stream + jnp.dot(gated, mixer_out, preferred_element_type=jnp.float32)
    attention_residual_stream, saved_b = feed_forward(stream_b, gain_second, up_first, down_first)
    attention_centered_normalized, attention_inverse_deviation = norm_pieces(
        attention_residual_stream
    )
    attention_normed_rows = (attention_centered_normalized * attention_norm_gain).astype(
        jnp.bfloat16
    )
    mixed_c = jnp.dot(attention_normed_rows, project_in, preferred_element_type=jnp.float32).astype(
        jnp.bfloat16
    )
    query_flat = mixed_c[:, :width]
    key_flat = mixed_c[:, width : 2 * width]
    value_flat = mixed_c[:, 2 * width :]
    query_c = query_flat.reshape(rows, HEADS, head_size)
    key_heads = key_flat.reshape(rows, HEADS, head_size)
    value_heads = value_flat.reshape(rows, HEADS, head_size)

    def forward_update(state, key_block, value_block, key_pos):
        return attend_block(state, query_c, here, key_block, value_block, key_pos, ends, scale)

    begin = (
        jnp.full((HEADS, rows), NEGATIVE, jnp.float32),
        jnp.zeros((HEADS, rows), jnp.float32),
        jnp.zeros((HEADS, rows, head_size), jnp.float32),
    )
    piece = (
        lax.all_gather(key_flat, "seq", axis=0, tiled=True),
        lax.all_gather(value_flat, "seq", axis=0, tiled=True),
    )
    top, mass, accum = scan_keys(begin, piece[0], piece[1], forward_update)
    lse = top + jnp.log(mass)
    att_full = accum / mass[:, :, None]
    attended = att_full.transpose(1, 0, 2).reshape(rows, width).astype(jnp.bfloat16)
    stream_d = attention_residual_stream + jnp.dot(
        attended, project_out, preferred_element_type=jnp.float32
    )
    result_value, saved_d = feed_forward(stream_d, gain_fourth, up_second, down_second)
    block_out = result_value.astype(jnp.bfloat16)[None]
    incoming_gradient = cotangent[0].astype(jnp.float32)
    incoming_gradient, gain_four_part, up_two_part, down_two_part = feed_back(
        incoming_gradient, saved_d, gain_fourth, up_second, down_second
    )
    grad_low = incoming_gradient.astype(jnp.bfloat16)
    out_part_c = jnp.einsum("td,te->de", attended, grad_low, preferred_element_type=jnp.float32)
    att_grad = jnp.einsum(
        "te,de->td", grad_low, project_out, preferred_element_type=jnp.float32
    ).astype(jnp.bfloat16)
    grad_heads = att_grad.reshape(rows, HEADS, head_size)
    delta = jnp.sum(grad_heads.astype(jnp.float32).transpose(1, 0, 2) * att_full, axis=-1)
    zero_heads = jnp.zeros((rows, HEADS, head_size), jnp.float32)

    def query_update(summed, key_block, value_block, key_pos):
        return summed + query_back(
            query_c, grad_heads, lse, delta, here, key_block, value_block, key_pos, ends, scale
        )

    piece = (
        lax.all_gather(key_flat, "seq", axis=0, tiled=True),
        lax.all_gather(value_flat, "seq", axis=0, tiled=True),
    )
    query_grad = scan_keys(zero_heads, piece[0], piece[1], query_update)
    lse_all, delta_all = (
        lax.all_gather(lse, "seq", axis=1, tiled=True),
        lax.all_gather(delta, "seq", axis=1, tiled=True),
    )
    queries = lax.all_gather(query_flat, "seq", axis=0, tiled=True)
    grads = lax.all_gather(att_grad, "seq", axis=0, tiled=True)
    count = queries.shape[0]
    step = math.gcd(count, 1024)
    firsts = step * jnp.arange(count // step, dtype=jnp.int32)

    def inner_product(summed, item):
        query_block, grad_block, first = item
        query_pos = first + jnp.arange(step, dtype=jnp.int32)
        lse_rows = lax.dynamic_slice_in_dim(lse_all, first, step, 1)
        delta_rows = lax.dynamic_slice_in_dim(delta_all, first, step, 1)
        parts = key_back(
            query_block,
            grad_block,
            lse_rows,
            delta_rows,
            query_pos,
            key_heads,
            value_heads,
            here,
            ends,
            scale,
        )
        return ((summed[0] + parts[0], summed[1] + parts[1]), None)

    items = (
        queries.reshape(count // step, step, HEADS, head_size),
        grads.reshape(count // step, step, HEADS, head_size),
        firsts,
    )
    key_grad, value_grad = lax.scan(inner_product, (zero_heads, zero_heads), items)[0]
    key_grad = key_grad.reshape(rows, width)
    value_grad = value_grad.reshape(rows, width)
    mixed_grad_c = jnp.concatenate(
        [query_grad.reshape(rows, width), key_grad, value_grad], axis=1
    ).astype(jnp.bfloat16)
    in_part_c = jnp.einsum(
        "td,te->de", attention_normed_rows, mixed_grad_c, preferred_element_type=jnp.float32
    )
    attention_normed_gradient = jnp.einsum(
        "te,de->td", mixed_grad_c, project_in, preferred_element_type=jnp.float32
    )
    attention_norm_gradient, attention_gain_share = norm_backward(
        attention_normed_gradient,
        attention_centered_normalized,
        attention_inverse_deviation,
        attention_norm_gain,
    )
    incoming_gradient = incoming_gradient + attention_norm_gradient
    incoming_gradient, gain_two_part, up_one_part, down_one_part = feed_back(
        incoming_gradient, saved_b, gain_second, up_first, down_first
    )
    grad_low = incoming_gradient.astype(jnp.bfloat16)
    out_part_a = jnp.einsum("td,te->de", gated, grad_low, preferred_element_type=jnp.float32)
    gated_grad = jnp.einsum("te,de->td", grad_low, mixer_out, preferred_element_type=jnp.float32)
    query_grad_a = gated_grad * response
    response_grad = gated_grad * query_a
    skip_part = jnp.sum(response_grad * product_kv, axis=0)
    chan_grad = lax.all_to_all(
        response_grad.T.reshape(blocks, channels, rows).astype(jnp.bfloat16),
        "seq",
        split_axis=0,
        concat_axis=2,
        tiled=True,
    ).astype(jnp.float32)[0]
    grad_re, grad_im = forward_spectrum(chan_grad, tables, blocks, rows)
    signal_grad = inverse_signal(
        ker_re * grad_re + ker_im * grad_im,
        ker_re * grad_im - ker_im * grad_re,
        tables,
        blocks,
        rows,
    )
    kernel_grad = inverse_signal(
        sig_re * grad_re + sig_im * grad_im,
        sig_re * grad_im - sig_im * grad_re,
        tables,
        blocks,
        rows,
    )
    coef_part, rate_part = kernel_grads(coef_here, rate_here, times, kernel_grad)
    returned = lax.all_to_all(
        signal_grad.reshape(1, channels, total).astype(jnp.bfloat16),
        "seq",
        split_axis=2,
        concat_axis=0,
        tiled=True,
    ).astype(jnp.float32)
    kv_grad = returned.reshape(width, rows).T + skip_gain * response_grad
    shifted_grad = kv_grad * value_a
    value_grad_a = kv_grad * shifted
    later = shifted_2(shortened(shifted_grad[: lags - 1]), "seq", -1)
    grad_ext = jnp.concatenate([shifted_grad, later], axis=0)
    key_grad_a = jnp.zeros_like(key_a)
    tap_rows = []
    for lag in range(lags):
        key_grad_a = key_grad_a + shift_taps[lag] * grad_ext[lag : lag + rows]
        tap_rows.append(
            jnp.sum(shifted_grad * key_ext[lags - 1 - lag : lags - 1 - lag + rows], axis=0)
        )
    taps_part = jnp.stack(tap_rows)
    mixed_grad_a = jnp.concatenate([query_grad_a, key_grad_a, value_grad_a], axis=1).astype(
        jnp.bfloat16
    )
    in_part_a = jnp.einsum(
        "td,te->de", mixer_normed_rows, mixed_grad_a, preferred_element_type=jnp.float32
    )
    mixer_normed_gradient = jnp.einsum(
        "te,de->td", mixed_grad_a, mixer_in, preferred_element_type=jnp.float32
    )
    mixer_norm_gradient, mixer_gain_share = norm_backward(
        mixer_normed_gradient, mixer_centered_normalized, mixer_inverse_deviation, mixer_norm_gain
    )
    token_grad = (incoming_gradient + mixer_norm_gradient)[None]
    parts = (
        lax.psum_scatter(mixer_gain_share, "seq", scatter_dimension=0, tiled=True),
        lax.psum_scatter(in_part_a, "seq", scatter_dimension=0, tiled=True),
        lax.psum_scatter(taps_part, "seq", scatter_dimension=1, tiled=True),
        lax.psum_scatter(skip_part, "seq", scatter_dimension=0, tiled=True),
        lax.psum_scatter(out_part_a, "seq", scatter_dimension=0, tiled=True),
        lax.psum_scatter(gain_two_part, "seq", scatter_dimension=0, tiled=True),
        lax.psum_scatter(up_one_part, "seq", scatter_dimension=0, tiled=True),
        lax.psum_scatter(down_one_part, "seq", scatter_dimension=0, tiled=True),
        lax.psum_scatter(attention_gain_share, "seq", scatter_dimension=0, tiled=True),
        lax.psum_scatter(in_part_c, "seq", scatter_dimension=0, tiled=True),
        lax.psum_scatter(out_part_c, "seq", scatter_dimension=0, tiled=True),
        lax.psum_scatter(gain_four_part, "seq", scatter_dimension=0, tiled=True),
        lax.psum_scatter(up_two_part, "seq", scatter_dimension=0, tiled=True),
        lax.psum_scatter(down_two_part, "seq", scatter_dimension=0, tiled=True),
    )
    matrices = (
        lax.psum_scatter(
            parts[1].astype(jnp.bfloat16), "batch", scatter_dimension=1, tiled=True
        ).astype(jnp.float32),
        lax.psum_scatter(
            parts[2].astype(jnp.bfloat16), "batch", scatter_dimension=0, tiled=True
        ).astype(jnp.float32),
        lax.psum_scatter(
            parts[4].astype(jnp.bfloat16), "batch", scatter_dimension=1, tiled=True
        ).astype(jnp.float32),
        lax.psum_scatter(
            parts[6].astype(jnp.bfloat16), "batch", scatter_dimension=1, tiled=True
        ).astype(jnp.float32),
        lax.psum_scatter(
            parts[7].astype(jnp.bfloat16), "batch", scatter_dimension=1, tiled=True
        ).astype(jnp.float32),
        lax.psum_scatter(
            parts[9].astype(jnp.bfloat16), "batch", scatter_dimension=1, tiled=True
        ).astype(jnp.float32),
        lax.psum_scatter(
            parts[10].astype(jnp.bfloat16), "batch", scatter_dimension=1, tiled=True
        ).astype(jnp.float32),
        lax.psum_scatter(
            parts[12].astype(jnp.bfloat16), "batch", scatter_dimension=1, tiled=True
        ).astype(jnp.float32),
        lax.psum_scatter(
            parts[13].astype(jnp.bfloat16), "batch", scatter_dimension=1, tiled=True
        ).astype(jnp.float32),
    )
    smalls = lax.psum(
        (parts[0], coef_part, rate_part, parts[3], parts[5], parts[8], parts[11]), "batch"
    )
    return (
        block_out,
        token_grad,
        smalls[0],
        matrices[0],
        matrices[1],
        smalls[1],
        smalls[2],
        smalls[3],
        matrices[2],
        smalls[4],
        matrices[3],
        matrices[4],
        smalls[5],
        matrices[5],
        matrices[6],
        smalls[6],
        matrices[7],
        matrices[8],
    )


MESH = pl.DeviceIdType.MESH
BF = jnp.bfloat16
F32 = jnp.float32
ROWS, WIDE, RANKS = (128, 768, 8)
SPAN = ROWS * RANKS
BLOCK = 128
OWNERS = 6
NT = (((1,), (1,)), ((), ()))
TN = (((0,), (0,)), ((), ()))
ROOT = math.sqrt(2.0 / math.pi)
CUBIC = 0.044715


def flip(value):
    return 1 - value


def mm(left, right):
    return jnp.dot(left, right, preferred_element_type=F32)


def mm_nt(left, right):
    return lax.dot_general(left, right, NT, preferred_element_type=F32)


def mm_tn(left, right):
    return lax.dot_general(left, right, TN, preferred_element_type=F32)


def is_owner(rank):
    return jnp.logical_and(rank >= 1, rank <= OWNERS)


def rows_of(rank):
    return pl.ds(pl.multiple_of(ROWS * rank, ROWS), ROWS)


def lanes_of(block):
    return pl.ds(pl.multiple_of(BLOCK * block, BLOCK), BLOCK)


class Spread:
    def __init__(self, net, source, target, outward, only=None):
        self.net, self.source, self.target, self.outward = net, source, target, outward
        self.base = net.take(RANKS - 1)

    def copy(self, step, source, target, rank):
        at = self.base + step - 1
        return pltpu.make_async_remote_copy(
            src_ref=source,
            dst_ref=target,
            send_sem=self.net.send_sem.at[at],
            recv_sem=self.net.recv_sem.at[at],
            device_id=(rank, self.net.b),
            device_id_type=MESH,
        )

    def each_send(self, act, chosen=None):
        me = self.net.s
        for step in range(1, RANKS):
            rank = lax.rem(me + step, RANKS)
            go = is_owner(rank) if self.outward else is_owner(me)
            if chosen is not None:
                go = jnp.logical_and(go, chosen(rank))

            @pl.when(go)
            def _(step=step, rank=rank):
                if self.outward:
                    act(self.copy(step, self.source(rank - 1), self.target(me), rank))
                else:
                    act(self.copy(step, self.source(rank), self.target(me - 1), rank))

    def start(self, chosen=None):
        self.each_send(lambda copy: copy.start(), chosen)

    def own(self):
        me = self.net.s

        @pl.when(is_owner(me))
        def _():
            if self.outward:
                self.target(me)[...] = self.source(me - 1)[...]
            else:
                self.target(me - 1)[...] = self.source(me)[...]

    def wait_recv(self):
        me = self.net.s
        for step in range(1, RANKS):
            rank = lax.rem(me + RANKS - step, RANKS)

            @pl.when(is_owner(me) if self.outward else is_owner(rank))
            def _(step=step, rank=rank):
                landed = self.target(rank if self.outward else rank - 1)
                self.copy(step, landed, landed, rank).wait_recv()

    def wait_send(self):
        self.each_send(lambda copy: copy.wait_send())


class Net:
    def __init__(self, send_sem, recv_sem):
        self.send_sem, self.recv_sem = send_sem, recv_sem
        self.s = lax.axis_index("seq")
        self.b = lax.axis_index("batch")
        self.used = 0
        self.waiting = []

    def take(self, count):
        at = self.used
        self.used += count
        return at

    def spread(self, source, target, outward):
        made = Spread(self, source, target, outward)
        self.waiting.append(made)
        return made

    def greet(self, others=()):
        barrier = pltpu.get_barrier_semaphore()
        for step in range(1, RANKS):
            pl.semaphore_signal(
                barrier, inc=1, device_id=(lax.rem(self.s + step, RANKS), self.b), device_id_type=MESH
            )
        for other in others:
            pl.semaphore_signal(barrier, inc=1, device_id=other, device_id_type=MESH)
        pl.semaphore_wait(barrier, RANKS - 1 + len(others))

    def finish(self):
        for made in self.waiting:
            made.wait_send()


class Beside:
    def __init__(self, net, source, target, steps):
        self.net, self.steps = net, steps
        self.at = net.take(1)
        other = jnp.clip(net.s + steps, 0, RANKS - 1)
        self.copy = pltpu.make_async_remote_copy(
            src_ref=source,
            dst_ref=target,
            send_sem=net.send_sem.at[self.at],
            recv_sem=net.recv_sem.at[self.at],
            device_id=(other, net.b),
            device_id_type=MESH,
        )
        last = RANKS - 1 if steps > 0 else 0
        first = 0 if steps > 0 else RANKS - 1
        self.sends = net.s != last
        self.takes = net.s != first
        net.waiting.append(self)

    def start(self):
        @pl.when(self.sends)
        def _():
            self.copy.start()

    def wait_recv(self):
        @pl.when(self.takes)
        def _():
            self.copy.wait_recv()

    def wait_send(self):
        @pl.when(self.sends)
        def _():
            self.copy.wait_send()


def pieces(value):
    cent = value - jnp.mean(value, axis=-1, keepdims=True)
    inverse = lax.rsqrt(jnp.mean(cent * cent, axis=-1, keepdims=True) + 1e-05)
    return cent * inverse, inverse


def pieces_back(incoming, normal, inverse, gain):
    share = jnp.sum(incoming * normal, axis=0, keepdims=True)
    scaled = incoming * gain
    first = jnp.mean(scaled, axis=-1, keepdims=True)
    second = jnp.mean(scaled * normal, axis=-1, keepdims=True)
    return inverse * (scaled - first - normal * second), share


def gelu_parts(u):
    square = u * u
    bend = jnp.tanh(ROOT * u * (1.0 + CUBIC * square))
    half = 0.5 * (1.0 + bend)
    value = u * half
    slope = half + 0.5 * u * (1.0 - bend * bend) * (ROOT * (1.0 + 3.0 * CUBIC * square))
    return value, slope


def split(value):
    high = value.astype(BF)
    return high, (value - high.astype(F32)).astype(BF)


def transform(r, high, low, re_out, im_out):
    @pl.loop(0, 4)
    def _(at):
        rows = pl.ds(pl.multiple_of(256 * at, 256), 256)
        for main, rest, out, sign in ((r.cos_high, r.cos_low, re_out, 1.0), (r.sin_high, r.sin_low, im_out, -1.0)):
            total = mm(main[rows, :], high) + mm(rest[rows, :], high)
            if low is not None:
                total = total + mm(main[rows, :], low)
            out[rows, :] = sign * total


def inverse(r, re, im, out):
    re_high, re_low = split(re)
    im_high, im_low = split(im)
    r.pack_re[:, 0:128] = re_high
    r.pack_re[:, 128:256] = re_low
    r.pack_im[:, 0:128] = im_high
    r.pack_im[:, 128:256] = im_low

    @pl.loop(0, 4)
    def _(at):
        rows = pl.ds(pl.multiple_of(256 * at, 256), 256)
        both = mm(r.cos_high[rows, :], r.pack_re[...]) - mm(r.sin_high[rows, :], r.pack_im[...])
        rest = mm(r.cos_low[rows, :], r.pack_re[:, 0:128]) - mm(r.sin_low[rows, :], r.pack_im[:, 0:128])
        out[rows, :] = ((both[:, 0:128] + both[:, 128:256] + rest) * (1.0 / SPAN)).astype(out.dtype)


def modes(coef_ref, rate_ref, out_ref):
    blocks, width = out_ref.shape[0] // 8, out_ref.shape[1]
    row = lax.broadcasted_iota(jnp.int32, (8, width), 0).astype(F32)
    out_ref[...] = jnp.zeros_like(out_ref)

    @pl.loop(0, 8)
    def _(group):
        some = pl.ds(pl.multiple_of(8 * group, 8), 8)
        rate, coef = rate_ref[some, :], coef_ref[some, :]
        falls = [coef[n : n + 1] * jnp.exp(-rate[n : n + 1] * row) for n in range(8)]
        steps = [jnp.exp(-rate[n : n + 1] * jnp.maximum(row, 8.0)) for n in range(8)]

        def step(at, falls):
            rows = pl.ds(pl.multiple_of(8 * at, 8), 8)
            out_ref[rows, :] += sum(falls[1:], falls[0])
            return tuple(fall * factor for fall, factor in zip(falls, steps))

        lax.fori_loop(0, blocks, step, tuple(falls), unroll=4)


def modes_back(coef_ref, rate_ref, grad_ref, coef_out, rate_out):
    blocks, width = grad_ref.shape[0] // 8, grad_ref.shape[1]
    row = lax.broadcasted_iota(jnp.int32, (8, width), 0).astype(F32)

    @pl.loop(0, 8)
    def _(group):
        some = pl.ds(pl.multiple_of(8 * group, 8), 8)
        rate, coef = rate_ref[some, :], coef_ref[some, :]
        steps = [jnp.exp(-rate[n : n + 1] * jnp.maximum(row, 8.0)) for n in range(8)]
        zero = jnp.minimum(row, 0.0)

        def step(at, carry):
            totals, slopes = carry
            here = grad_ref[pl.ds(pl.multiple_of(8 * (blocks - 1 - at), 8), 8), :]
            slopes = tuple(slope * factor + total for slope, factor, total in zip(slopes, steps, totals))
            totals = tuple(total * factor + here for total, factor in zip(totals, steps))
            return totals, slopes

        totals, slopes = lax.fori_loop(0, blocks, step, ((zero,) * 8, (zero,) * 8), unroll=2)
        coef_rows, rate_rows = [], []
        for n in range(8):
            fall = jnp.exp(-rate[n : n + 1] * row)
            coef_rows.append(jnp.sum(fall * totals[n], axis=0, keepdims=True))
            late = jnp.sum(fall * (8.0 * steps[n] * slopes[n] + row * totals[n]), axis=0, keepdims=True)
            rate_rows.append(-coef[n : n + 1] * late)
        coef_out[some, :] = jnp.concatenate(coef_rows, axis=0)
        rate_out[some, :] = jnp.concatenate(rate_rows, axis=0)


def shift_forward(keys, taps, value, shifted):
    @pl.loop(0, OWNERS)
    def _(block):
        lanes = lanes_of(block)
        near = keys[:, lanes]
        total = jnp.zeros((ROWS, BLOCK), F32)
        for rest in range(8):
            turned = pltpu.roll(near, rest, 0) if rest else near
            for part in range(8):
                total = total + taps[8 * part + rest : 8 * part + rest + 1, lanes] * turned[64 - 8 * part : 192 - 8 * part]
        shifted[:, lanes] = total


def shift_back(grads, keys, taps, key_grad, taps_grad):
    @pl.loop(0, OWNERS)
    def _(block):
        lanes = lanes_of(block)
        ahead, near = grads[:, lanes], keys[:, lanes]
        here = ahead[0:ROWS]
        total = jnp.zeros((ROWS, BLOCK), F32)
        rows = {}
        for rest in range(8):
            later = pltpu.roll(ahead, 192 - rest, 0) if rest else ahead
            turned = pltpu.roll(near, rest, 0) if rest else near
            for part in range(8):
                lag = 8 * part + rest
                total = total + taps[lag : lag + 1, lanes] * later[8 * part : 8 * part + ROWS]
                taps_grad[lag : lag + 1, lanes] = jnp.sum(here * turned[64 - 8 * part : 192 - 8 * part], axis=0, keepdims=True)
        key_grad[:, lanes] = total


def head_lanes(shape, head):
    return lax.broadcasted_iota(jnp.int32, shape, 1) // 64 == head


def document_start(ends, first, count):
    at = first + lax.broadcasted_iota(jnp.int32, (count, 1), 0)
    begin = jnp.zeros((count, 1), jnp.int32)
    for index in range(3):
        begin = jnp.where(at >= ends[index], ends[index], begin)
    return at, begin


def allowed_pairs(ends, part):
    query_at, begin = document_start(ends, 256 * part, 256)
    key_at = lax.broadcasted_iota(jnp.int32, (256, 256 * (part + 1)), 1)
    return jnp.logical_and(key_at <= query_at, key_at >= begin)


def attention_forward(r, part):
    rows, keys = slice(256 * part, 256 * part + 256), slice(0, 256 * part + 256)
    mask = allowed_pairs(r.ends, part)

    @pl.loop(0, 2)
    def _(head):
        lanes = head_lanes((256, BLOCK), head)
        query = jnp.where(lanes, r.qkv[0, rows, :].astype(F32) * 0.125, 0.0).astype(BF)
        scores = jnp.where(mask, mm_nt(query, r.qkv[1, keys, :]), NEGATIVE)
        top = jnp.max(scores, axis=1, keepdims=True)
        weights = jnp.exp(scores - top)
        mass = jnp.sum(weights, axis=1, keepdims=True)
        mixed = mm(weights.astype(BF), r.qkv[2, keys, :]) / mass
        r.attended_full[rows, :] = jnp.where(lanes, mixed, r.attended_full[rows, :])
        r.lse[rows, :] = jnp.where(lanes, top + jnp.log(mass), r.lse[rows, :])

    r.attended_low[rows, :] = r.attended_full[rows, :].astype(BF)


def attention_back(r, part):
    rows, keys = slice(256 * part, 256 * part + 256), slice(0, 256 * part + 256)
    mask = allowed_pairs(r.ends, part)

    @pl.loop(0, 2)
    def _(head):
        lanes = head_lanes((256, BLOCK), head)
        query = jnp.where(lanes, r.qkv[0, rows, :].astype(F32) * 0.125, 0.0).astype(BF)
        whole = r.att_grad[rows, :].astype(F32)
        grads = jnp.where(lanes, whole, 0.0)
        delta = jnp.sum(grads * r.attended_full[rows, :], axis=1, keepdims=True)
        lse = jnp.sum(jnp.where(lanes, r.lse[rows, :], 0.0), axis=1, keepdims=True) * (1.0 / 64.0)
        grads = grads.astype(BF)
        scores = mm_nt(query, r.qkv[1, keys, :])
        probs = jnp.where(mask, jnp.exp(scores - lse), 0.0)
        score_grad = (probs * (mm_nt(grads, r.qkv[2, keys, :]) - delta)).astype(BF)
        query_grad = mm(score_grad, r.qkv[1, keys, :]) * 0.125
        r.query_grad[rows, :] = jnp.where(lanes, query_grad, r.query_grad[rows, :])
        r.key_grad[keys, :] += mm_tn(score_grad, query)
        r.value_grad[keys, :] += mm_tn(probs.astype(BF), grads)

    r.qkv_grad[0, rows, :] = r.query_grad[rows, :].astype(BF)
    r.qkv_grad[1, rows, :] = r.key_grad[rows, :].astype(BF)
    r.qkv_grad[2, rows, :] = r.value_grad[rows, :].astype(BF)


def load(r, sems, names):
    copies = {}
    for index, name in enumerate(names):
        copies[name] = pltpu.make_async_copy(getattr(r, name + "_hbm"), getattr(r, name), sems.at[index])
        copies[name].start()
    return copies


TABLES = ("cos_high", "sin_high", "cos_low", "sin_low")


def kernel_a(r):
    net = Net(r.send_sem, r.recv_sem)
    wait = load(r, r.load_sem, ("mixer_in",) + TABLES + ("mixer_out", "up_first", "down_first", "project_in"))
    me = net.s
    stream = r.tokens[0].astype(F32)
    normal, _ = pieces(stream)
    r.normed_a[...] = (normal * r.mixer_norm_gain[...]).astype(BF)
    wait["mixer_in"].wait()
    r.key_ext[64:192, :] = mm(r.normed_a[...], r.mixer_in[:, WIDE : 2 * WIDE])
    r.rim_out[...] = r.key_ext[128:192, :].astype(BF)
    net.greet()
    rim = Beside(net, r.rim_out, r.rim_in, 1)
    rim.start()

    @pl.when(me == 0)
    def _():
        r.rim_in[...] = jnp.zeros_like(r.rim_in)

    r.query_a[...] = mm(r.normed_a[...], r.mixer_in[:, 0:WIDE])
    r.value_a[...] = mm(r.normed_a[...], r.mixer_in[:, 2 * WIDE :])
    rim.wait_recv()
    r.key_ext[0:64, :] = r.rim_in[...].astype(F32)
    shift_forward(r.key_ext, r.shift_taps, None, r.shifted)
    r.product_low[...] = (r.shifted[...] * r.value_a[...]).astype(BF)
    go = net.spread(lambda block: r.product_low.at[:, lanes_of(block)], lambda rank: r.signal.at[rows_of(rank), :], True)
    go.start()
    go.own()
    modes(r.coef, r.rate, r.mode_rows)
    high, low = split(r.mode_rows[...])
    for name in TABLES:
        wait[name].wait()
    transform(r, high, low, r.kernel_re, r.kernel_im)
    turned = r.kernel_re[...] * r.phase_cos[...] - r.kernel_im[...] * r.phase_sin[...]
    r.kernel_im[...] = r.kernel_im[...] * r.phase_cos[...] + r.kernel_re[...] * r.phase_sin[...]
    r.kernel_re[...] = turned
    go.wait_recv()
    transform(r, r.signal[...], None, r.signal_re, r.signal_im)
    inverse(
        r,
        r.signal_re[...] * r.kernel_re[...] - r.signal_im[...] * r.kernel_im[...],
        r.signal_re[...] * r.kernel_im[...] + r.signal_im[...] * r.kernel_re[...],
        r.conv,
    )
    back = net.spread(lambda rank: r.conv.at[rows_of(rank), :], lambda block: r.conv_home.at[:, lanes_of(block)], False)
    back.start()
    back.own()
    for name in ("mixer_out", "up_first", "down_first", "project_in"):
        wait[name].wait()
    back.wait_recv()
    r.response[...] = r.conv_home[...].astype(F32) + r.skip_gain[...] * (r.shifted[...] * r.value_a[...])
    r.gated[...] = (r.query_a[...] * r.response[...]).astype(BF)
    stream_b = r.tokens[0].astype(F32) + mm(r.gated[...], r.mixer_out[...])
    r.stream_b[...] = stream_b
    normal, _ = pieces(stream_b)
    r.normed_b[...] = (normal * r.gain_second[...]).astype(BF)
    r.stream_c[...] = stream_b
    for chunk in range(4):
        lanes = slice(WIDE * chunk, WIDE * chunk + WIDE)
        raised = mm(r.normed_b[...], r.up_first[:, lanes])
        r.raised_b[:, lanes] = raised
        active = gelu_parts(raised)[0].astype(BF)
        r.active_b[:, lanes] = active
        r.stream_c[...] += mm(active, r.down_first[lanes, :])
    normal, _ = pieces(r.stream_c[...])
    r.normed_c[...] = (normal * r.attention_norm_gain[...]).astype(BF)
    for index in range(3):
        r.mixed_c[index] = mm(r.normed_c[...], r.project_in[:, WIDE * index : WIDE * index + WIDE]).astype(BF)
    go = net.spread(lambda block: r.mixed_c.at[:, :, lanes_of(block)], lambda rank: r.qkv.at[:, rows_of(rank), :], True)
    go.start()
    go.own()
    go.wait_recv()
    back = net.spread(lambda rank: r.attended_low.at[rows_of(rank), :], lambda block: r.attended.at[:, lanes_of(block)], False)
    for part in (3, 2, 1, 0):
        attention_forward(r, part)
        back.start(lambda rank, part=part: rank // 2 == part)
    back.own()
    back.wait_recv()
    net.finish()


def kernel_b(r):
    net = Net(r.send_sem, r.recv_sem)
    wait = load(r, r.load_sem, ("project_out", "up_second", "down_second"))
    wait["project_out"].wait()
    stream_d = r.stream_c[...] + mm(r.attended[...], r.project_out[...])
    normal, inverse_d = pieces(stream_d)
    r.normed_d[...] = (normal * r.gain_fourth[...]).astype(BF)
    r.total[...] = stream_d
    wait["up_second"].wait()
    wait["down_second"].wait()
    for chunk in range(4):
        lanes = slice(WIDE * chunk, WIDE * chunk + WIDE)
        raised = mm(r.normed_d[...], r.up_second[:, lanes])
        active, slope = gelu_parts(raised)
        active = active.astype(BF)
        r.active_d[:, lanes] = active
        r.total[...] += mm(active, r.down_second[lanes, :])
        slope = (slope * mm_nt(r.cotangent[0], r.down_second[lanes, :])).astype(BF)
        r.slope_d[chunk % 2, :, WIDE * (chunk // 2) : WIDE * (chunk // 2) + WIDE] = slope
        back = mm_nt(slope, r.up_second[:, lanes])
        if chunk == 0:
            r.grad_d[...] = back
        else:
            r.grad_d[...] += back
    r.block_out[0] = r.total[...].astype(BF)
    grad, r.gain_four[...] = pieces_back(r.grad_d[...], normal, inverse_d, r.gain_fourth[...])
    grad = r.cotangent[0].astype(F32) + grad
    r.grad_d[...] = grad
    r.grad_d_low[...] = grad.astype(BF)
    r.att_grad_home[...] = mm_nt(r.grad_d_low[...], r.project_out[...]).astype(BF)
    net.greet()
    go = net.spread(lambda block: r.att_grad_home.at[:, lanes_of(block)], lambda rank: r.att_grad.at[rows_of(rank), :], True)
    go.start()
    go.own()
    r.key_grad[...] = jnp.zeros_like(r.key_grad)
    r.value_grad[...] = jnp.zeros_like(r.value_grad)
    go.wait_recv()
    back = net.spread(
        lambda rank: r.qkv_grad.at[:, rows_of(rank), :], lambda block: r.mixed_grad_c.at[:, :, lanes_of(block)], False
    )
    for part in (3, 2, 1, 0):
        attention_back(r, part)
        back.start(lambda rank, part=part: rank // 2 == part)
    back.own()
    back.wait_recv()
    net.finish()


def kernel_c(r):
    net = Net(r.send_sem, r.recv_sem)
    wait = load(r, r.load_sem, ("project_in", "up_first", "down_first", "mixer_out") + TABLES)
    normal, inverse_c = pieces(r.stream_c[...])
    wait["project_in"].wait()
    grad = mm_nt(r.mixed_grad_c[0], r.project_in[:, 0:WIDE])
    for index in range(1, 3):
        grad = grad + mm_nt(r.mixed_grad_c[index], r.project_in[:, WIDE * index : WIDE * index + WIDE])
    grad, r.gain_three[...] = pieces_back(grad, normal, inverse_c, r.attention_norm_gain[...])
    grad = grad + r.grad_d[...]
    r.grad_c[...] = grad
    r.grad_c_low[...] = grad.astype(BF)
    wait["up_first"].wait()
    wait["down_first"].wait()
    for chunk in range(4):
        lanes = slice(WIDE * chunk, WIDE * chunk + WIDE)
        slope = gelu_parts(r.raised_b[:, lanes])[1]
        slope = (slope * mm_nt(r.grad_c_low[...], r.down_first[lanes, :])).astype(BF)
        r.slope_b[chunk % 2, :, WIDE * (chunk // 2) : WIDE * (chunk // 2) + WIDE] = slope
        back = mm_nt(slope, r.up_first[:, lanes])
        if chunk == 0:
            r.grad_b[...] = back
        else:
            r.grad_b[...] += back
    normal, inverse_b = pieces(r.stream_b[...])
    grad, r.gain_two[...] = pieces_back(r.grad_b[...], normal, inverse_b, r.gain_second[...])
    grad = grad + r.grad_c[...]
    r.grad_b[...] = grad
    r.grad_b_low[...] = grad.astype(BF)
    wait["mixer_out"].wait()
    gated_grad = mm_nt(r.grad_b_low[...], r.mixer_out[...])
    r.query_grad_a[...] = (gated_grad * r.response[...]).astype(BF)
    response_grad = gated_grad * r.query_a[...]
    r.response_grad[...] = response_grad
    r.response_grad_low[...] = response_grad.astype(BF)
    net.greet()
    go = net.spread(
        lambda block: r.response_grad_low.at[:, lanes_of(block)], lambda rank: r.conv_grad.at[rows_of(rank), :], True
    )
    go.start()
    go.own()
    r.skip_part[...] = jnp.sum(response_grad * (r.shifted[...] * r.value_a[...]), axis=0, keepdims=True)
    for name in TABLES:
        wait[name].wait()
    go.wait_recv()
    transform(r, r.conv_grad[...], None, r.grad_re, r.grad_im)
    inverse(
        r,
        r.grad_re[...] * r.kernel_re[...] + r.grad_im[...] * r.kernel_im[...],
        r.grad_im[...] * r.kernel_re[...] - r.grad_re[...] * r.kernel_im[...],
        r.signal_grad,
    )
    back = net.spread(
        lambda rank: r.signal_grad.at[rows_of(rank), :], lambda block: r.signal_grad_home.at[:, lanes_of(block)], False
    )
    back.start()
    back.own()
    re = r.grad_re[...] * r.signal_re[...] + r.grad_im[...] * r.signal_im[...]
    im = r.grad_im[...] * r.signal_re[...] - r.grad_re[...] * r.signal_im[...]
    inverse(
        r,
        re * r.phase_cos[...] + im * r.phase_sin[...],
        im * r.phase_cos[...] - re * r.phase_sin[...],
        r.kernel_grad,
    )
    modes_back(r.coef, r.rate, r.kernel_grad, r.coef_part, r.rate_part)
    back.wait_recv()
    net.finish()


def kernel_d(r):
    net = Net(r.send_sem, r.recv_sem)
    wait = load(r, r.load_sem, ("mixer_in",))
    signal_grad = r.signal_grad_home[...].astype(F32) + r.skip_gain[...] * r.response_grad[...]
    r.grad_ext[0:ROWS, :] = signal_grad * r.value_a[...]
    r.rim_out[...] = r.grad_ext[0:64, :].astype(BF)
    net.greet()
    rim = Beside(net, r.rim_out, r.rim_in, -1)
    rim.start()
    r.mixed_grad_a[0] = r.query_grad_a[...]
    r.mixed_grad_a[2] = (signal_grad * r.shifted[...]).astype(BF)

    @pl.when(net.s == RANKS - 1)
    def _():
        r.rim_in[...] = jnp.zeros_like(r.rim_in)

    rim.wait_recv()
    r.grad_ext[ROWS:192, :] = r.rim_in[...].astype(F32)
    shift_back(r.grad_ext, r.key_ext, r.shift_taps, r.key_grad_a, r.taps_part)
    r.mixed_grad_a[1] = r.key_grad_a[...].astype(BF)
    wait["mixer_in"].wait()
    grad = mm_nt(r.mixed_grad_a[0], r.mixer_in[:, 0:WIDE])
    for index in range(1, 3):
        grad = grad + mm_nt(r.mixed_grad_a[index], r.mixer_in[:, WIDE * index : WIDE * index + WIDE])
    normal, inverse_a = pieces(r.tokens[0].astype(F32))
    grad, r.gain_one[...] = pieces_back(grad, normal, inverse_a, r.mixer_norm_gain[...])
    r.token_grad[0] = r.grad_b[...] + grad
    net.finish()


class Refs:
    pass


def call(body, identity, inputs, hbm, smem, outs, scratch, copies, loads):
    names = list(inputs) + [name + "_hbm" for name in hbm] + list(smem) + list(outs) + list(scratch) + list(hbm)
    names += ["send_sem", "recv_sem", "load_sem"]

    def run(*refs):
        r = Refs()
        for name, ref in zip(names, refs):
            setattr(r, name, ref)
        body(r)

    vmem = pl.BlockSpec(memory_space=pltpu.VMEM)
    results = pl.pallas_call(
        run,
        out_shape=[jax.ShapeDtypeStruct(shape, kind) for shape, kind in outs.values()],
        in_specs=[vmem] * len(inputs)
        + [pl.BlockSpec(memory_space=pl.ANY)] * len(hbm)
        + [pl.BlockSpec(memory_space=pltpu.SMEM)] * len(smem),
        out_specs=[vmem] * len(outs),
        scratch_shapes=[pltpu.VMEM(shape, kind) for shape, kind in scratch.values()]
        + [pltpu.VMEM(array.shape, array.dtype) for array in hbm.values()]
        + [pltpu.SemaphoreType.DMA((copies,)), pltpu.SemaphoreType.DMA((copies,)), pltpu.SemaphoreType.DMA((loads,))],
        compiler_params=pltpu.CompilerParams(
            collective_id=identity, has_side_effects=True, vmem_limit_bytes=60 * 2**20
        ),
    )(*inputs.values(), *hbm.values(), *smem.values())
    return dict(zip(outs, results))


def odd_tables():
    odd = 2 * np.arange(SPAN, dtype=np.int64) + 1
    angle = (np.outer(odd, odd) % (8 * SPAN)) * (math.pi / (4 * SPAN))
    tables = {}
    for name, table in (("cos", np.cos(angle)), ("sin", np.sin(angle))):
        high = table.astype(ml_dtypes.bfloat16)
        tables[name + "_high"] = jnp.asarray(high)
        tables[name + "_low"] = jnp.asarray((table - high.astype(np.float64)).astype(ml_dtypes.bfloat16))
    phase = (odd * (math.pi / (4 * SPAN)))[:, None] * np.ones((1, BLOCK))
    return tables, jnp.asarray(np.cos(phase), F32), jnp.asarray(np.sin(phase), F32)


LAYER, PAIR = (0, 1)
GIVEN = (4, 3)
OWN = (5, 3)


def weight_sum_kernel(kinds, *refs):
    refs = list(refs)
    given = [[refs.pop(0) for _ in range(GIVEN[kind])] for kind in kinds]
    outs = [refs.pop(0) for _ in kinds]
    own_of = [[refs.pop(0) for _ in range(OWN[kind])] for kind in kinds]
    sums_of = [[refs.pop(0) for _ in range(7)] for kind in kinds]
    send_sem, recv_sem = refs
    s = lax.axis_index("seq")
    b = lax.axis_index("batch")
    z, x = s // 2, lax.rem(s, 2)
    y, c = b // 2, lax.rem(b, 2)
    zh, zl = z // 2, lax.rem(z, 2)
    sibling = (s, 2 * y + flip(c))
    by_x = (2 * z + flip(x), b)
    by_y = (s, 2 * flip(y) + c)
    by_l = (2 * (2 * zh + flip(zl)) + x, b)
    by_h = (2 * (2 * flip(zh) + zl) + x, b)
    barrier = pltpu.get_barrier_semaphore()
    for other in (sibling, by_x, by_y, by_l, by_h):
        pl.semaphore_signal(barrier, inc=1, device_id=other, device_id_type=MESH)
    pl.semaphore_wait(barrier, 5)
    started = []

    def send(source, target, other):
        at = len(started)
        copy = pltpu.make_async_remote_copy(
            src_ref=source,
            dst_ref=target,
            send_sem=send_sem.at[at],
            recv_sem=recv_sem.at[at],
            device_id=other,
            device_id_type=MESH,
        )
        copy.start()
        started.append(copy)
        return copy

    shared = []
    for kind, inputs, own in zip(kinds, given, own_of):
        mine = []
        own[0][:, 0:128] = inputs[0][...].T
        mine.append(send(own[0].at[:, 0:128], own[0].at[:, 128:256], sibling))
        own[1][0:128, :] = inputs[1][c]
        mine.append(send(inputs[1].at[flip(c)], own[1].at[128:256, :], sibling))
        if kind == LAYER:
            own[3][...] = inputs[2][...].T
            for at in range(2):
                rows = pl.ds(pl.multiple_of(192 * (2 * at + c), 64), 192)
                own[2][192 * at : 192 * at + 192, 0:128] = own[3][rows, :]
                rows = pl.ds(pl.multiple_of(192 * (2 * at + flip(c)), 64), 192)
                mine.append(send(own[3].at[rows, :], own[2].at[192 * at : 192 * at + 192, 128:256], sibling))
            own[4][0:128, :] = inputs[3][...]
            mine.append(send(inputs[3], own[4].at[128:256, :], sibling))
        else:
            own[2][:, 0:128] = inputs[2][...].T
            mine.append(send(own[2].at[:, 0:128], own[2].at[:, 128:256], sibling))
        shared.append(mine)

    stages = []
    for kind, own, sums, mine in zip(kinds, own_of, sums_of, shared):
        for copy in mine:
            copy.wait_recv()
        grads, near_a, near_b, next_a, next_b, third, fourth = sums
        half = grads.shape[4] // 2

        def place(product, at, tile):
            for block in range(8):
                grads[block % 2, at, block // 4, (block // 2) % 2, pl.ds(pl.multiple_of(96 * tile, 16), 96), :] = product[
                    96 * block : 96 * block + 96
                ].astype(BF)

        if kind == LAYER:

            @pl.loop(0, 6)
            def _(step):
                at, chunk = step // 3, lax.rem(step, 3)
                lanes = pl.ds(pl.multiple_of(256 * step, 256), 256)
                product = jnp.dot(own[0][...], own[1][:, lanes], preferred_element_type=F32)
                place(product[:, 0:128], at, 2 * chunk)
                place(product[:, 128:256], at, 2 * chunk + 1)

            @pl.loop(0, 8)
            def _(block):
                lanes = pl.ds(pl.multiple_of(384 * block, 384), 384)
                product = jnp.dot(own[2][...], own[4][:, lanes], preferred_element_type=F32)
                for at in range(2):
                    for tile in range(3):
                        grads[
                            lax.rem(block, 2), at, block // 4, lax.rem(block // 2, 2), 576 + 192 * tile : 768 + 192 * tile, :
                        ] = product[192 * at : 192 * at + 192, 128 * tile : 128 * tile + 128].astype(BF)

        else:

            @pl.loop(0, 2)
            def _(at):
                for chunk in range(3):
                    lanes = pl.ds(pl.multiple_of(768 * at + 256 * chunk, 256), 256)
                    right = own[1][:, lanes]
                    if chunk < 2:
                        product = jnp.dot(own[0][...], right, preferred_element_type=F32)
                    else:
                        first = lax.broadcasted_iota(jnp.int32, right.shape, 1) < 64
                        zero = jnp.zeros_like(right)
                        product = jnp.dot(own[0][...], jnp.where(first, right, zero), preferred_element_type=F32)
                        product += jnp.dot(own[2][...], jnp.where(first, zero, right), preferred_element_type=F32)
                    place(product[:, 0:128], at, 2 * chunk)
                    place(product[:, 128:256], at, 2 * chunk + 1)

        stages.append(
            [
                send(grads.at[flip(x), :, :, :, 0:half, :], near_a, by_x),
                send(grads.at[:, flip(y), :, :, half:, :], near_b, by_y),
            ]
        )

    for index, sums in enumerate(sums_of):
        grads, near_a, near_b, next_a, next_b, third, fourth = sums
        half = grads.shape[4] // 2
        for copy in stages[index]:
            copy.wait_recv()

        @pl.loop(0, 8)
        def _(step):
            high, mid, low = step // 4, lax.rem(step // 2, 2), lax.rem(step, 2)
            grads[x, high, mid, low, 0:half, :] += near_a[high, mid, low]
            grads[high, y, mid, low, half:, :] += near_b[high, mid, low]

        stages[index] = [
            send(grads.at[x, flip(y), :, :, 0:half, :], next_a, by_y),
            send(grads.at[flip(x), y, :, :, half:, :], next_b, by_x),
        ]
    for index, sums in enumerate(sums_of):
        grads, near_a, near_b, next_a, next_b, third, fourth = sums
        half = grads.shape[4] // 2
        for copy in stages[index]:
            copy.wait_recv()

        @pl.loop(0, 4)
        def _(step):
            mid, low = step // 2, lax.rem(step, 2)
            grads[x, y, mid, low, 0:half, :] += next_a[mid, low]
            grads[x, y, mid, low, half:, :] += next_b[mid, low]

        stages[index] = [send(grads.at[x, y, :, flip(zl), :, :], third, by_l)]
    for index, sums in enumerate(sums_of):
        grads, near_a, near_b, next_a, next_b, third, fourth = sums
        for copy in stages[index]:
            copy.wait_recv()

        @pl.loop(0, 2)
        def _(mid):
            grads[x, y, mid, zl] += third[mid]

        stages[index] = [send(grads.at[x, y, flip(zh), zl], fourth, by_h)]
    for index, sums in enumerate(sums_of):
        grads, near_a, near_b, next_a, next_b, third, fourth = sums
        for copy in stages[index]:
            copy.wait_recv()
        outs[index][...] = grads[x, y, zh, zl].astype(F32) + fourth[...].astype(F32)
    for copy in started:
        copy.wait_send()


def weight_sums(kinds, groups, identity):
    lengths = [1152 if kind == LAYER else 576 for kind in kinds]
    own, sums = [], []
    for kind, length in zip(kinds, lengths):
        own += [pltpu.VMEM((768, 256), BF), pltpu.VMEM((256, 1536), BF)]
        if kind == LAYER:
            own += [pltpu.VMEM((384, 256), BF), pltpu.VMEM((768, 128), BF), pltpu.VMEM((256, 3072), BF)]
        else:
            own += [pltpu.VMEM((768, 256), BF)]
        half = length // 2
        sums += [
            pltpu.VMEM((2, 2, 2, 2, length, 128), BF),
            pltpu.VMEM((2, 2, 2, half, 128), BF),
            pltpu.VMEM((2, 2, 2, half, 128), BF),
            pltpu.VMEM((2, 2, half, 128), BF),
            pltpu.VMEM((2, 2, half, 128), BF),
            pltpu.VMEM((2, length, 128), BF),
            pltpu.VMEM((length, 128), BF),
        ]
    copies = sum(GIVEN[kind] + (7 if kind == LAYER else 6) for kind in kinds)
    flat = [array for group in groups for array in group]
    vmem = pl.BlockSpec(memory_space=pltpu.VMEM)
    return pl.pallas_call(
        functools.partial(weight_sum_kernel, kinds),
        out_shape=[jax.ShapeDtypeStruct((length, 128), F32) for length in lengths],
        in_specs=[vmem] * len(flat),
        out_specs=[vmem] * len(kinds),
        scratch_shapes=own + sums + [pltpu.SemaphoreType.DMA((copies,)), pltpu.SemaphoreType.DMA((copies,))],
        compiler_params=pltpu.CompilerParams(
            collective_id=identity, has_side_effects=True, vmem_limit_bytes=60 * 2**20
        ),
    )(*flat)


def pair_columns(wide, narrow):
    parts = jnp.concatenate([wide.reshape(128, 4, 576), narrow.reshape(128, 4, 192)], axis=2)
    return parts.reshape(128, 2, 2, 768).transpose(2, 0, 1, 3).reshape(2, 128, 1536)


def untile_layer(block):
    up = block[:576].reshape(6, 96, 128).transpose(1, 0, 2).reshape(96, 768)
    down = block[576:].reshape(3, 192, 128).transpose(0, 2, 1).reshape(384, 192)
    return up, down


def untile_pair(block):
    both = block.reshape(6, 96, 128).transpose(1, 0, 2).reshape(96, 768)
    return both[:, :576], both[:, 576:]


def shards_fast(
    tokens,
    doc_lengths,
    mixer_norm_gain,
    mixer_in,
    shift_taps,
    mode_coef,
    mode_rate,
    skip_gain,
    mixer_out,
    gain_second,
    up_first,
    down_first,
    attention_norm_gain,
    project_in,
    project_out,
    gain_fourth,
    up_second,
    down_second,
    cotangent,
):
    rank = lax.axis_index("seq")
    mixer_norm_gain, skip_gain, gain_second, attention_norm_gain, gain_fourth = (
        gain[None] for gain in (mixer_norm_gain, skip_gain, gain_second, attention_norm_gain, gain_fourth)
    )
    ends = jnp.cumsum(doc_lengths[0]).astype(jnp.int32)
    first = BLOCK * jnp.clip(rank - 1, 0, OWNERS - 1)
    coef = lax.dynamic_slice_in_dim(mode_coef, first, BLOCK, 1)
    rate = lax.dynamic_slice_in_dim(mode_rate, first, BLOCK, 1)
    tables, phase_cos, phase_sin = odd_tables()
    home = (ROWS, WIDE)
    span = (SPAN, BLOCK)
    a = call(
        kernel_a,
        1,
        dict(
            tokens=tokens,
            mixer_norm_gain=mixer_norm_gain,
            shift_taps=shift_taps,
            coef=coef,
            rate=rate,
            skip_gain=skip_gain,
            gain_second=gain_second,
            attention_norm_gain=attention_norm_gain,
            phase_cos=phase_cos,
            phase_sin=phase_sin,
        ),
        dict(mixer_in=mixer_in, **tables, mixer_out=mixer_out, up_first=up_first, down_first=down_first, project_in=project_in),
        dict(ends=ends),
        dict(
            normed_a=(home, BF),
            query_a=(home, F32),
            value_a=(home, F32),
            key_ext=((192, WIDE), F32),
            shifted=(home, F32),
            response=(home, F32),
            gated=(home, BF),
            stream_b=(home, F32),
            normed_b=(home, BF),
            raised_b=((ROWS, 4 * WIDE), F32),
            active_b=((ROWS, 4 * WIDE), BF),
            stream_c=(home, F32),
            normed_c=(home, BF),
            attended=(home, BF),
            qkv=((3, *span), BF),
            lse=(span, F32),
            attended_full=(span, F32),
            kernel_re=(span, F32),
            kernel_im=(span, F32),
            signal_re=(span, F32),
            signal_im=(span, F32),
        ),
        dict(
            rim_out=((64, WIDE), BF),
            rim_in=((64, WIDE), BF),
            product_low=(home, BF),
            signal=(span, BF),
            mode_rows=(span, F32),
            conv=(span, BF),
            conv_home=(home, BF),
            pack_re=((SPAN, 256), BF),
            pack_im=((SPAN, 256), BF),
            mixed_c=((3, *home), BF),
            attended_low=(span, BF),
        ),
        29,
        9,
    )
    b = call(
        kernel_b,
        2,
        dict(
            stream_c=a["stream_c"],
            attended=a["attended"],
            gain_fourth=gain_fourth,
            cotangent=cotangent,
            qkv=a["qkv"],
            lse=a["lse"],
            attended_full=a["attended_full"],
        ),
        dict(project_out=project_out, up_second=up_second, down_second=down_second),
        dict(ends=ends),
        dict(
            block_out=((1, *home), BF),
            normed_d=(home, BF),
            active_d=((ROWS, 4 * WIDE), BF),
            slope_d=((2, ROWS, 2 * WIDE), BF),
            grad_d=(home, F32),
            grad_d_low=(home, BF),
            gain_four=((1, WIDE), F32),
            mixed_grad_c=((3, *home), BF),
        ),
        dict(
            total=(home, F32),
            att_grad_home=(home, BF),
            att_grad=(span, BF),
            query_grad=(span, F32),
            key_grad=(span, F32),
            value_grad=(span, F32),
            qkv_grad=((3, *span), BF),
        ),
        14,
        3,
    )
    c = call(
        kernel_c,
        3,
        dict(
            stream_c=a["stream_c"],
            stream_b=a["stream_b"],
            mixed_grad_c=b["mixed_grad_c"],
            attention_norm_gain=attention_norm_gain,
            gain_second=gain_second,
            grad_d=b["grad_d"],
            raised_b=a["raised_b"],
            response=a["response"],
            query_a=a["query_a"],
            shifted=a["shifted"],
            value_a=a["value_a"],
            kernel_re=a["kernel_re"],
            kernel_im=a["kernel_im"],
            signal_re=a["signal_re"],
            signal_im=a["signal_im"],
            phase_cos=phase_cos,
            phase_sin=phase_sin,
            coef=coef,
            rate=rate,
        ),
        dict(project_in=project_in, up_first=up_first, down_first=down_first, mixer_out=mixer_out, **tables),
        dict(),
        dict(
            gain_three=((1, WIDE), F32),
            gain_two=((1, WIDE), F32),
            skip_part=((1, WIDE), F32),
            grad_c_low=(home, BF),
            slope_b=((2, ROWS, 2 * WIDE), BF),
            grad_b=(home, F32),
            grad_b_low=(home, BF),
            query_grad_a=(home, BF),
            response_grad=(home, F32),
            signal_grad_home=(home, BF),
            coef_part=((64, BLOCK), F32),
            rate_part=((64, BLOCK), F32),
        ),
        dict(
            grad_c=(home, F32),
            response_grad_low=(home, BF),
            conv_grad=(span, BF),
            grad_re=(span, F32),
            grad_im=(span, F32),
            signal_grad=(span, BF),
            kernel_grad=(span, F32),
            pack_re=((SPAN, 256), BF),
            pack_im=((SPAN, 256), BF),
        ),
        14,
        8,
    )
    d = call(
        kernel_d,
        4,
        dict(
            tokens=tokens,
            mixer_norm_gain=mixer_norm_gain,
            shift_taps=shift_taps,
            skip_gain=skip_gain,
            signal_grad_home=c["signal_grad_home"],
            response_grad=c["response_grad"],
            value_a=a["value_a"],
            shifted=a["shifted"],
            key_ext=a["key_ext"],
            query_grad_a=c["query_grad_a"],
            grad_b=c["grad_b"],
        ),
        dict(mixer_in=mixer_in),
        dict(),
        dict(
            mixed_grad_a=((3, *home), BF),
            taps_part=((64, WIDE), F32),
            gain_one=((1, WIDE), F32),
            token_grad=((1, *home), F32),
        ),
        dict(
            grad_ext=((192, WIDE), F32),
            rim_out=((64, WIDE), BF),
            rim_in=((64, WIDE), BF),
            key_grad_a=(home, F32),
        ),
        1,
        1,
    )
    mixed_grad_a = d["mixed_grad_a"].transpose(1, 0, 2).reshape(ROWS, 3 * WIDE)
    mixed_grad_c = b["mixed_grad_c"].transpose(1, 0, 2).reshape(ROWS, 3 * WIDE)
    groups = (
        (b["normed_d"], b["slope_d"], cotangent[0], b["active_d"]),
        (a["normed_c"], pair_columns(mixed_grad_c, b["grad_d_low"]), a["attended"]),
        (a["normed_b"], c["slope_b"], c["grad_c_low"], a["active_b"]),
        (a["normed_a"], pair_columns(mixed_grad_a, c["grad_b_low"]), a["gated"]),
    )
    layer_d, pair_c, layer_b, pair_a = weight_sums((LAYER, PAIR, LAYER, PAIR), groups, 0)
    up_two, down_two = untile_layer(layer_d)
    in_c, out_c = untile_pair(pair_c)
    up_one, down_one = untile_layer(layer_b)
    in_a, out_a = untile_pair(pair_a)
    owner = is_owner(rank)
    modes_part = jnp.concatenate([c["coef_part"], c["rate_part"]], axis=0)
    modes_part = lax.dynamic_update_slice_in_dim(
        jnp.zeros((128, WIDE), F32), jnp.where(owner, modes_part, 0.0), first, 1
    )
    small = jnp.concatenate(
        [d["taps_part"], modes_part, d["gain_one"], c["skip_part"], c["gain_two"], c["gain_three"], b["gain_four"]], axis=0
    )
    small = lax.psum_scatter(small, "seq", scatter_dimension=1, tiled=True)
    taps = lax.psum_scatter(small[0:64].astype(BF), "batch", scatter_dimension=0, tiled=True).astype(F32)
    rest = lax.psum(small[64:], "batch")
    return (
        b["block_out"],
        d["token_grad"],
        rest[128],
        in_a,
        taps,
        rest[0:64],
        rest[64:128],
        rest[129],
        out_a,
        rest[130],
        up_one,
        down_one,
        rest[131],
        in_c,
        out_c,
        rest[132],
        up_two,
        down_two,
    )


def solution(mesh):
    in_specs = (
        P("batch", "seq", None),
        P("batch", None),
        P(),
        P(),
        P(),
        P(),
        P(),
        P(),
        P(),
        P(),
        P(),
        P(),
        P(),
        P(),
        P(),
        P(),
        P(),
        P(),
        P("batch", "seq", None),
    )
    out_specs = (
        P("batch", "seq", None),
        P("batch", "seq", None),
        P("seq"),
        P("seq", "batch"),
        P("batch", "seq"),
        P(None, "seq"),
        P(None, "seq"),
        P("seq"),
        P("seq", "batch"),
        P("seq"),
        P("seq", "batch"),
        P("seq", "batch"),
        P("seq"),
        P("seq", "batch"),
        P("seq", "batch"),
        P("seq"),
        P("seq", "batch"),
        P("seq", "batch"),
    )
    fast = mesh.shape["seq"] == RANKS and mesh.shape["batch"] == 4
    return jax.shard_map(shards_fast if fast else shards, mesh=mesh, in_specs=in_specs, out_specs=out_specs, check_vma=False)
```

```python
import math

import jax
import jax.numpy as jnp
import ml_dtypes
import numpy as np
from jax import lax
from jax.experimental import pallas as pl
from jax.experimental.pallas import tpu as pltpu
from jax.sharding import PartitionSpec as P

HEADS = 12


HIGH = lax.Precision.HIGHEST
NEGATIVE = -1e30


def shifted_2(value, axis, steps):
    count = lax.axis_size(axis)
    leading, last = (max(0, -steps), min(count, count - steps))
    return lax.ppermute(value, axis, [(source, source + steps) for source in range(leading, last)])


def shortened(x):

    def short(part):
        return part.astype(jnp.bfloat16) if part.dtype == jnp.float32 else part

    return jax.tree.map(short, x)


def mult(form, left, right):
    return jnp.einsum(form, left, right, precision=HIGH, preferred_element_type=jnp.float32)


def norm_pieces(value):
    row_mean = jnp.mean(value, axis=-1, keepdims=True)
    cent = value - row_mean
    inverse_deviation = lax.rsqrt(jnp.mean(cent * cent, axis=-1, keepdims=True) + 1e-05)
    return (cent * inverse_deviation, inverse_deviation)


def norm_backward(incoming_gradient, centered_normalized, inverse_deviation, gain_vector):
    gain_share = jnp.sum(incoming_gradient * centered_normalized, axis=0)
    scaled_rows = incoming_gradient * gain_vector
    inner_product = jnp.mean(scaled_rows, axis=-1, keepdims=True)
    cross_term = jnp.mean(scaled_rows * centered_normalized, axis=-1, keepdims=True)
    return (
        inverse_deviation * (scaled_rows - inner_product - centered_normalized * cross_term),
        gain_share,
    )


def segment_of(where, ends):
    return jnp.sum((where[:, None] >= ends[None, :]).astype(jnp.int32), axis=1)


def allowed(query_pos, key_pos, ends):
    same = segment_of(query_pos, ends)[:, None] == segment_of(key_pos, ends)[None, :]
    return (key_pos[None, :] <= query_pos[:, None]) & same


def kernel_rows(coef, rate, times):

    def step(total, pair):
        scale, decay = pair
        return (total + scale[:, None] * jnp.exp(-decay[:, None] * times[None, :]), None)

    start = jnp.zeros((coef.shape[1], times.shape[0]), jnp.float32)
    return lax.scan(step, start, (coef, rate))[0]


def kernel_grads(coef, rate, times, incoming_gradient):

    def step(carry, pair):
        scale, decay = pair
        fall = incoming_gradient * jnp.exp(-decay[:, None] * times[None, :])
        return (carry, (jnp.sum(fall, axis=1), -scale * jnp.sum(fall * times[None, :], axis=1)))

    return lax.scan(step, jnp.zeros((), jnp.float32), (coef, rate))[1]


def angle_pair(left, right, period):
    turns = left[:, None] * right[None, :] % period
    angle = turns.astype(jnp.float32) * (2.0 * math.pi / period)
    return (jnp.cos(angle), jnp.sin(angle))


def dft_tables(blocks, rows):
    wide = 2 * blocks
    block_ids = jnp.arange(blocks, dtype=jnp.int32)
    wide_ids = jnp.arange(wide, dtype=jnp.int32)
    row_ids = jnp.arange(rows, dtype=jnp.int32)
    return (
        angle_pair(block_ids, wide_ids, wide),
        angle_pair(wide_ids, row_ids, wide * rows),
        angle_pair(row_ids, row_ids, rows),
    )


def forward_spectrum(signal, tables, blocks, rows):
    (cos_one, sin_one), (cos_two, sin_two), (cos_three, sin_three) = tables
    folded = signal.reshape(signal.shape[0], blocks, rows)
    first_re = mult("cpr,pf->cfr", folded, cos_one)
    first_im = -mult("cpr,pf->cfr", folded, sin_one)
    turned_re = first_re * cos_two + first_im * sin_two
    turned_im = first_im * cos_two - first_re * sin_two
    spec_re = mult("cfr,rk->cfk", turned_re, cos_three) + mult("cfr,rk->cfk", turned_im, sin_three)
    spec_im = mult("cfr,rk->cfk", turned_im, cos_three) - mult("cfr,rk->cfk", turned_re, sin_three)
    return (spec_re, spec_im)


def inverse_signal(spec_re, spec_im, tables, blocks, rows):
    (cos_one, sin_one), (cos_two, sin_two), (cos_three, sin_three) = tables
    inner_re = mult("cfk,rk->cfr", spec_re, cos_three) - mult("cfk,rk->cfr", spec_im, sin_three)
    inner_im = mult("cfk,rk->cfr", spec_im, cos_three) + mult("cfk,rk->cfr", spec_re, sin_three)
    turned_re = inner_re * cos_two - inner_im * sin_two
    turned_im = inner_im * cos_two + inner_re * sin_two
    result_value = mult("cfr,pf->cpr", turned_re, cos_one) - mult("cfr,pf->cpr", turned_im, sin_one)
    return result_value.reshape(spec_re.shape[0], blocks * rows) / (2.0 * blocks * rows)


def attend_block(state, query, query_pos, key_block, value_block, key_pos, ends, scale):
    top, mass, accum = state
    scores = (
        jnp.einsum("qhd,khd->hqk", query, key_block, preferred_element_type=jnp.float32) * scale
    )
    mask = allowed(query_pos, key_pos, ends)[None]
    newtop = jnp.maximum(top, jnp.max(jnp.where(mask, scores, NEGATIVE), axis=-1))
    weights = jnp.where(mask, jnp.exp(scores - newtop[:, :, None]), 0.0)
    factor = jnp.exp(top - newtop)
    mass = mass * factor + jnp.sum(weights, axis=-1)
    accum = accum * factor[:, :, None] + jnp.einsum(
        "hqk,khd->hqd", weights, value_block.astype(jnp.float32), preferred_element_type=jnp.float32
    )
    return (newtop, mass, accum)


def score_grads(
    query, grads, lse_rows, delta_rows, query_pos, key_block, value_block, key_pos, ends, scale
):
    scores = (
        jnp.einsum("qhd,khd->hqk", query, key_block, preferred_element_type=jnp.float32) * scale
    )
    mask = allowed(query_pos, key_pos, ends)[None]
    probs = jnp.where(mask, jnp.exp(scores - lse_rows[:, :, None]), 0.0)
    dots = jnp.einsum("qhd,khd->hqk", grads, value_block, preferred_element_type=jnp.float32)
    return (probs, (probs * (dots - delta_rows[:, :, None])).astype(jnp.bfloat16))


def query_back(
    query, grads, lse_rows, delta_rows, query_pos, key_block, value_block, key_pos, ends, scale
):
    score_grad = score_grads(
        query, grads, lse_rows, delta_rows, query_pos, key_block, value_block, key_pos, ends, scale
    )[1]
    return (
        jnp.einsum("hqk,khd->qhd", score_grad, key_block, preferred_element_type=jnp.float32)
        * scale
    )


def key_back(
    query, grads, lse_rows, delta_rows, query_pos, key_block, value_block, key_pos, ends, scale
):
    probs, score_grad = score_grads(
        query, grads, lse_rows, delta_rows, query_pos, key_block, value_block, key_pos, ends, scale
    )
    key_part = (
        jnp.einsum("hqk,qhd->khd", score_grad, query, preferred_element_type=jnp.float32) * scale
    )
    value_part = jnp.einsum(
        "hqk,qhd->khd", probs, grads.astype(jnp.float32), preferred_element_type=jnp.float32
    )
    return (key_part, value_part)


def scan_keys(carry, keys, values, update):
    count = keys.shape[0]
    width = keys.shape[1]
    head_size = width // HEADS
    step = math.gcd(count, 1024)
    firsts = step * jnp.arange(count // step, dtype=jnp.int32)

    def inner_product(state, item):
        key_block, value_block, first = item
        key_pos = first + jnp.arange(step, dtype=jnp.int32)
        return (update(state, key_block, value_block, key_pos), None)

    items = (
        keys.reshape(count // step, step, HEADS, head_size),
        values.reshape(count // step, step, HEADS, head_size),
        firsts,
    )
    return lax.scan(inner_product, carry, items)[0]


def feed_forward(residual_stream, gain_vector, w_up, w_down):
    centered_normalized, inverse_deviation = norm_pieces(residual_stream)
    normed_rows = (centered_normalized * gain_vector).astype(jnp.bfloat16)
    raised_rows = jnp.dot(normed_rows, w_up, preferred_element_type=jnp.float32)
    active_tokens = jax.nn.gelu(raised_rows).astype(jnp.bfloat16)
    result_value = residual_stream + jnp.dot(
        active_tokens, w_down, preferred_element_type=jnp.float32
    )
    return (
        result_value,
        (centered_normalized, inverse_deviation, normed_rows, raised_rows, active_tokens),
    )


def feed_back(incoming_gradient, saved_residuals, gain_vector, w_up, w_down):
    centered_normalized, inverse_deviation, normed_rows, raised_rows, active_tokens = (
        saved_residuals
    )
    grad_low = incoming_gradient.astype(jnp.bfloat16)
    down_part = jnp.einsum("tf,td->fd", active_tokens, grad_low, preferred_element_type=jnp.float32)
    active_grad = jnp.einsum("td,fd->tf", grad_low, w_down, preferred_element_type=jnp.float32)
    slope = jax.vjp(jax.nn.gelu, raised_rows)[1](active_grad)[0].astype(jnp.bfloat16)
    up_part = jnp.einsum("td,tf->df", normed_rows, slope, preferred_element_type=jnp.float32)
    normed_gradient = jnp.einsum("tf,df->td", slope, w_up, preferred_element_type=jnp.float32)
    input_gradient, gain_share = norm_backward(
        normed_gradient, centered_normalized, inverse_deviation, gain_vector
    )
    return (incoming_gradient + input_gradient, gain_share, up_part, down_part)


def shards(
    tokens,
    doc_lengths,
    mixer_norm_gain,
    mixer_in,
    shift_taps,
    mode_coef,
    mode_rate,
    skip_gain,
    mixer_out,
    gain_second,
    up_first,
    down_first,
    attention_norm_gain,
    project_in,
    project_out,
    gain_fourth,
    up_second,
    down_second,
    cotangent,
):
    rows = tokens.shape[1]
    width = tokens.shape[2]
    blocks = lax.axis_size("seq")
    rank = lax.axis_index("seq")
    total = rows * blocks
    head_size = width // HEADS
    scale = head_size ** (-0.5)
    lags = shift_taps.shape[0]
    channels = width // blocks
    ends = jnp.cumsum(doc_lengths[0])
    here = rank * rows + jnp.arange(rows, dtype=jnp.int32)
    residual_stream = tokens[0].astype(jnp.float32)
    mixer_centered_normalized, mixer_inverse_deviation = norm_pieces(residual_stream)
    mixer_normed_rows = (mixer_centered_normalized * mixer_norm_gain).astype(jnp.bfloat16)
    mixed_a = jnp.dot(mixer_normed_rows, mixer_in, preferred_element_type=jnp.float32)
    query_a = mixed_a[:, :width]
    key_a = mixed_a[:, width : 2 * width]
    value_a = mixed_a[:, 2 * width :]
    rim = shifted_2(key_a[rows - (lags - 1) :].astype(jnp.bfloat16), "seq", 1).astype(jnp.float32)
    key_ext = jnp.concatenate([rim, key_a], axis=0)
    shifted = jnp.zeros_like(key_a)
    for lag in range(lags):
        shifted = shifted + shift_taps[lag] * key_ext[lags - 1 - lag : lags - 1 - lag + rows]
    product_kv = shifted * value_a
    channel_in = lax.all_to_all(
        product_kv.T.reshape(blocks, channels, rows).astype(jnp.bfloat16),
        "seq",
        split_axis=0,
        concat_axis=2,
        tiled=True,
    ).astype(jnp.float32)[0]
    times = jnp.arange(total, dtype=jnp.int32).astype(jnp.float32)
    coef_here = lax.dynamic_slice_in_dim(mode_coef, rank * channels, channels, 1)
    rate_here = lax.dynamic_slice_in_dim(mode_rate, rank * channels, channels, 1)
    kernel_here = kernel_rows(coef_here, rate_here, times)
    tables = dft_tables(blocks, rows)
    sig_re, sig_im = forward_spectrum(channel_in, tables, blocks, rows)
    ker_re, ker_im = forward_spectrum(kernel_here, tables, blocks, rows)
    conv_chan = inverse_signal(
        sig_re * ker_re - sig_im * ker_im, sig_re * ker_im + sig_im * ker_re, tables, blocks, rows
    )
    conv_home = lax.all_to_all(
        conv_chan.reshape(1, channels, total).astype(jnp.bfloat16),
        "seq",
        split_axis=2,
        concat_axis=0,
        tiled=True,
    ).astype(jnp.float32)
    response = conv_home.reshape(width, rows).T + skip_gain * product_kv
    gated = (query_a * response).astype(jnp.bfloat16)
    stream_b = residual_stream + jnp.dot(gated, mixer_out, preferred_element_type=jnp.float32)
    attention_residual_stream, saved_b = feed_forward(stream_b, gain_second, up_first, down_first)
    attention_centered_normalized, attention_inverse_deviation = norm_pieces(
        attention_residual_stream
    )
    attention_normed_rows = (attention_centered_normalized * attention_norm_gain).astype(
        jnp.bfloat16
    )
    mixed_c = jnp.dot(attention_normed_rows, project_in, preferred_element_type=jnp.float32).astype(
        jnp.bfloat16
    )
    query_flat = mixed_c[:, :width]
    key_flat = mixed_c[:, width : 2 * width]
    value_flat = mixed_c[:, 2 * width :]
    query_c = query_flat.reshape(rows, HEADS, head_size)
    key_heads = key_flat.reshape(rows, HEADS, head_size)
    value_heads = value_flat.reshape(rows, HEADS, head_size)

    def forward_update(state, key_block, value_block, key_pos):
        return attend_block(state, query_c, here, key_block, value_block, key_pos, ends, scale)

    begin = (
        jnp.full((HEADS, rows), NEGATIVE, jnp.float32),
        jnp.zeros((HEADS, rows), jnp.float32),
        jnp.zeros((HEADS, rows, head_size), jnp.float32),
    )
    piece = (
        lax.all_gather(key_flat, "seq", axis=0, tiled=True),
        lax.all_gather(value_flat, "seq", axis=0, tiled=True),
    )
    top, mass, accum = scan_keys(begin, piece[0], piece[1], forward_update)
    lse = top + jnp.log(mass)
    att_full = accum / mass[:, :, None]
    attended = att_full.transpose(1, 0, 2).reshape(rows, width).astype(jnp.bfloat16)
    stream_d = attention_residual_stream + jnp.dot(
        attended, project_out, preferred_element_type=jnp.float32
    )
    result_value, saved_d = feed_forward(stream_d, gain_fourth, up_second, down_second)
    block_out = result_value.astype(jnp.bfloat16)[None]
    incoming_gradient = cotangent[0].astype(jnp.float32)
    incoming_gradient, gain_four_part, up_two_part, down_two_part = feed_back(
        incoming_gradient, saved_d, gain_fourth, up_second, down_second
    )
    grad_low = incoming_gradient.astype(jnp.bfloat16)
    out_part_c = jnp.einsum("td,te->de", attended, grad_low, preferred_element_type=jnp.float32)
    att_grad = jnp.einsum(
        "te,de->td", grad_low, project_out, preferred_element_type=jnp.float32
    ).astype(jnp.bfloat16)
    grad_heads = att_grad.reshape(rows, HEADS, head_size)
    delta = jnp.sum(grad_heads.astype(jnp.float32).transpose(1, 0, 2) * att_full, axis=-1)
    zero_heads = jnp.zeros((rows, HEADS, head_size), jnp.float32)

    def query_update(summed, key_block, value_block, key_pos):
        return summed + query_back(
            query_c, grad_heads, lse, delta, here, key_block, value_block, key_pos, ends, scale
        )

    piece = (
        lax.all_gather(key_flat, "seq", axis=0, tiled=True),
        lax.all_gather(value_flat, "seq", axis=0, tiled=True),
    )
    query_grad = scan_keys(zero_heads, piece[0], piece[1], query_update)
    lse_all, delta_all = (
        lax.all_gather(lse, "seq", axis=1, tiled=True),
        lax.all_gather(delta, "seq", axis=1, tiled=True),
    )
    queries = lax.all_gather(query_flat, "seq", axis=0, tiled=True)
    grads = lax.all_gather(att_grad, "seq", axis=0, tiled=True)
    count = queries.shape[0]
    step = math.gcd(count, 1024)
    firsts = step * jnp.arange(count // step, dtype=jnp.int32)

    def inner_product(summed, item):
        query_block, grad_block, first = item
        query_pos = first + jnp.arange(step, dtype=jnp.int32)
        lse_rows = lax.dynamic_slice_in_dim(lse_all, first, step, 1)
        delta_rows = lax.dynamic_slice_in_dim(delta_all, first, step, 1)
        parts = key_back(
            query_block,
            grad_block,
            lse_rows,
            delta_rows,
            query_pos,
            key_heads,
            value_heads,
            here,
            ends,
            scale,
        )
        return ((summed[0] + parts[0], summed[1] + parts[1]), None)

    items = (
        queries.reshape(count // step, step, HEADS, head_size),
        grads.reshape(count // step, step, HEADS, head_size),
        firsts,
    )
    key_grad, value_grad = lax.scan(inner_product, (zero_heads, zero_heads), items)[0]
    key_grad = key_grad.reshape(rows, width)
    value_grad = value_grad.reshape(rows, width)
    mixed_grad_c = jnp.concatenate(
        [query_grad.reshape(rows, width), key_grad, value_grad], axis=1
    ).astype(jnp.bfloat16)
    in_part_c = jnp.einsum(
        "td,te->de", attention_normed_rows, mixed_grad_c, preferred_element_type=jnp.float32
    )
    attention_normed_gradient = jnp.einsum(
        "te,de->td", mixed_grad_c, project_in, preferred_element_type=jnp.float32
    )
    attention_norm_gradient, attention_gain_share = norm_backward(
        attention_normed_gradient,
        attention_centered_normalized,
        attention_inverse_deviation,
        attention_norm_gain,
    )
    incoming_gradient = incoming_gradient + attention_norm_gradient
    incoming_gradient, gain_two_part, up_one_part, down_one_part = feed_back(
        incoming_gradient, saved_b, gain_second, up_first, down_first
    )
    grad_low = incoming_gradient.astype(jnp.bfloat16)
    out_part_a = jnp.einsum("td,te->de", gated, grad_low, preferred_element_type=jnp.float32)
    gated_grad = jnp.einsum("te,de->td", grad_low, mixer_out, preferred_element_type=jnp.float32)
    query_grad_a = gated_grad * response
    response_grad = gated_grad * query_a
    skip_part = jnp.sum(response_grad * product_kv, axis=0)
    chan_grad = lax.all_to_all(
        response_grad.T.reshape(blocks, channels, rows).astype(jnp.bfloat16),
        "seq",
        split_axis=0,
        concat_axis=2,
        tiled=True,
    ).astype(jnp.float32)[0]
    grad_re, grad_im = forward_spectrum(chan_grad, tables, blocks, rows)
    signal_grad = inverse_signal(
        ker_re * grad_re + ker_im * grad_im,
        ker_re * grad_im - ker_im * grad_re,
        tables,
        blocks,
        rows,
    )
    kernel_grad = inverse_signal(
        sig_re * grad_re + sig_im * grad_im,
        sig_re * grad_im - sig_im * grad_re,
        tables,
        blocks,
        rows,
    )
    coef_part, rate_part = kernel_grads(coef_here, rate_here, times, kernel_grad)
    returned = lax.all_to_all(
        signal_grad.reshape(1, channels, total).astype(jnp.bfloat16),
        "seq",
        split_axis=2,
        concat_axis=0,
        tiled=True,
    ).astype(jnp.float32)
    kv_grad = returned.reshape(width, rows).T + skip_gain * response_grad
    shifted_grad = kv_grad * value_a
    value_grad_a = kv_grad * shifted
    later = shifted_2(shortened(shifted_grad[: lags - 1]), "seq", -1)
    grad_ext = jnp.concatenate([shifted_grad, later], axis=0)
    key_grad_a = jnp.zeros_like(key_a)
    tap_rows = []
    for lag in range(lags):
        key_grad_a = key_grad_a + shift_taps[lag] * grad_ext[lag : lag + rows]
        tap_rows.append(
            jnp.sum(shifted_grad * key_ext[lags - 1 - lag : lags - 1 - lag + rows], axis=0)
        )
    taps_part = jnp.stack(tap_rows)
    mixed_grad_a = jnp.concatenate([query_grad_a, key_grad_a, value_grad_a], axis=1).astype(
        jnp.bfloat16
    )
    in_part_a = jnp.einsum(
        "td,te->de", mixer_normed_rows, mixed_grad_a, preferred_element_type=jnp.float32
    )
    mixer_normed_gradient = jnp.einsum(
        "te,de->td", mixed_grad_a, mixer_in, preferred_element_type=jnp.float32
    )
    mixer_norm_gradient, mixer_gain_share = norm_backward(
        mixer_normed_gradient, mixer_centered_normalized, mixer_inverse_deviation, mixer_norm_gain
    )
    token_grad = (incoming_gradient + mixer_norm_gradient)[None]
    parts = (
        lax.psum_scatter(mixer_gain_share, "seq", scatter_dimension=0, tiled=True),
        lax.psum_scatter(in_part_a, "seq", scatter_dimension=0, tiled=True),
        lax.psum_scatter(taps_part, "seq", scatter_dimension=1, tiled=True),
        lax.psum_scatter(skip_part, "seq", scatter_dimension=0, tiled=True),
        lax.psum_scatter(out_part_a, "seq", scatter_dimension=0, tiled=True),
        lax.psum_scatter(gain_two_part, "seq", scatter_dimension=0, tiled=True),
        lax.psum_scatter(up_one_part, "seq", scatter_dimension=0, tiled=True),
        lax.psum_scatter(down_one_part, "seq", scatter_dimension=0, tiled=True),
        lax.psum_scatter(attention_gain_share, "seq", scatter_dimension=0, tiled=True),
        lax.psum_scatter(in_part_c, "seq", scatter_dimension=0, tiled=True),
        lax.psum_scatter(out_part_c, "seq", scatter_dimension=0, tiled=True),
        lax.psum_scatter(gain_four_part, "seq", scatter_dimension=0, tiled=True),
        lax.psum_scatter(up_two_part, "seq", scatter_dimension=0, tiled=True),
        lax.psum_scatter(down_two_part, "seq", scatter_dimension=0, tiled=True),
    )
    matrices = (
        lax.psum_scatter(
            parts[1].astype(jnp.bfloat16), "batch", scatter_dimension=1, tiled=True
        ).astype(jnp.float32),
        lax.psum_scatter(
            parts[2].astype(jnp.bfloat16), "batch", scatter_dimension=0, tiled=True
        ).astype(jnp.float32),
        lax.psum_scatter(
            parts[4].astype(jnp.bfloat16), "batch", scatter_dimension=1, tiled=True
        ).astype(jnp.float32),
        lax.psum_scatter(
            parts[6].astype(jnp.bfloat16), "batch", scatter_dimension=1, tiled=True
        ).astype(jnp.float32),
        lax.psum_scatter(
            parts[7].astype(jnp.bfloat16), "batch", scatter_dimension=1, tiled=True
        ).astype(jnp.float32),
        lax.psum_scatter(
            parts[9].astype(jnp.bfloat16), "batch", scatter_dimension=1, tiled=True
        ).astype(jnp.float32),
        lax.psum_scatter(
            parts[10].astype(jnp.bfloat16), "batch", scatter_dimension=1, tiled=True
        ).astype(jnp.float32),
        lax.psum_scatter(
            parts[12].astype(jnp.bfloat16), "batch", scatter_dimension=1, tiled=True
        ).astype(jnp.float32),
        lax.psum_scatter(
            parts[13].astype(jnp.bfloat16), "batch", scatter_dimension=1, tiled=True
        ).astype(jnp.float32),
    )
    smalls = lax.psum(
        (parts[0], coef_part, rate_part, parts[3], parts[5], parts[8], parts[11]), "batch"
    )
    return (
        block_out,
        token_grad,
        smalls[0],
        matrices[0],
        matrices[1],
        smalls[1],
        smalls[2],
        smalls[3],
        matrices[2],
        smalls[4],
        matrices[3],
        matrices[4],
        smalls[5],
        matrices[5],
        matrices[6],
        smalls[6],
        matrices[7],
        matrices[8],
    )


MESH = pl.DeviceIdType.MESH
BF = jnp.bfloat16
F32 = jnp.float32
ROWS, WIDE, RANKS = (128, 768, 8)
SPAN = ROWS * RANKS
BLOCK = 128
OWNERS = 6
NT = (((1,), (1,)), ((), ()))
TN = (((0,), (0,)), ((), ()))
ROOT = math.sqrt(2.0 / math.pi)
CUBIC = 0.044715


def flip(value):
    return 1 - value


def mm(left, right):
    return jnp.dot(left, right, preferred_element_type=F32)


def mm_nt(left, right):
    return lax.dot_general(left, right, NT, preferred_element_type=F32)


def mm_tn(left, right):
    return lax.dot_general(left, right, TN, preferred_element_type=F32)


def is_owner(rank):
    return jnp.logical_and(rank >= 1, rank <= OWNERS)


def rows_of(rank):
    return pl.ds(pl.multiple_of(ROWS * rank, ROWS), ROWS)


def lanes_of(block):
    return pl.ds(pl.multiple_of(BLOCK * block, BLOCK), BLOCK)


class Spread:
    def __init__(self, net, source, target, outward, only=None):
        self.net, self.source, self.target, self.outward = net, source, target, outward
        self.base = net.take(RANKS - 1)

    def copy(self, step, source, target, rank):
        at = self.base + step - 1
        return pltpu.make_async_remote_copy(
            src_ref=source,
            dst_ref=target,
            send_sem=self.net.send_sem.at[at],
            recv_sem=self.net.recv_sem.at[at],
            device_id=(rank, self.net.b),
            device_id_type=MESH,
        )

    def each_send(self, act, chosen=None):
        me = self.net.s
        for step in range(1, RANKS):
            rank = lax.rem(me + step, RANKS)
            go = is_owner(rank) if self.outward else is_owner(me)
            if chosen is not None:
                go = jnp.logical_and(go, chosen(rank))

            @pl.when(go)
            def _(step=step, rank=rank):
                if self.outward:
                    act(self.copy(step, self.source(rank - 1), self.target(me), rank))
                else:
                    act(self.copy(step, self.source(rank), self.target(me - 1), rank))

    def start(self, chosen=None):
        self.each_send(lambda copy: copy.start(), chosen)

    def own(self):
        me = self.net.s

        @pl.when(is_owner(me))
        def _():
            if self.outward:
                self.target(me)[...] = self.source(me - 1)[...]
            else:
                self.target(me - 1)[...] = self.source(me)[...]

    def wait_recv(self):
        me = self.net.s
        for step in range(1, RANKS):
            rank = lax.rem(me + RANKS - step, RANKS)

            @pl.when(is_owner(me) if self.outward else is_owner(rank))
            def _(step=step, rank=rank):
                landed = self.target(rank if self.outward else rank - 1)
                self.copy(step, landed, landed, rank).wait_recv()

    def wait_send(self):
        self.each_send(lambda copy: copy.wait_send())


class Net:
    def __init__(self, send_sem, recv_sem):
        self.send_sem, self.recv_sem = send_sem, recv_sem
        self.s = lax.axis_index("seq")
        self.b = lax.axis_index("batch")
        self.y, self.c = self.b // 2, lax.rem(self.b, 2)
        z, self.x = self.s // 2, lax.rem(self.s, 2)
        self.high, self.low = z // 2, lax.rem(z, 2)
        self.sibling = (self.s, 2 * self.y + flip(self.c))
        self.by_y = (self.s, 2 * flip(self.y) + self.c)
        self.by_both = (self.s, 2 * flip(self.y) + flip(self.c))
        self.by_x = (2 * z + flip(self.x), self.b)
        self.by_low = (2 * (2 * self.high + flip(self.low)) + self.x, self.b)
        self.by_high = (2 * (2 * flip(self.high) + self.low) + self.x, self.b)
        self.used = 0
        self.waiting = []

    def take(self, count):
        at = self.used
        self.used += count
        return at

    def spread(self, source, target, outward):
        made = Spread(self, source, target, outward)
        self.waiting.append(made)
        return made

    def send(self, source, target, other):
        at = self.take(1)
        copy = pltpu.make_async_remote_copy(
            src_ref=source,
            dst_ref=target,
            send_sem=self.send_sem.at[at],
            recv_sem=self.recv_sem.at[at],
            device_id=other,
            device_id_type=MESH,
        )
        copy.start()
        self.waiting.append(copy)
        return copy

    def hello(self):
        barrier = pltpu.get_barrier_semaphore()
        for step in range(1, RANKS):
            pl.semaphore_signal(
                barrier, inc=1, device_id=(lax.rem(self.s + step, RANKS), self.b), device_id_type=MESH
            )
        for other in (self.sibling, self.by_y, self.by_both):
            pl.semaphore_signal(barrier, inc=1, device_id=other, device_id_type=MESH)

    def ready(self):
        pl.semaphore_wait(pltpu.get_barrier_semaphore(), RANKS + 2)

    def turn_of(self, step, y, c):
        return (2 * y + flip(c), 2 * flip(y) + c, 2 * flip(y) + flip(c), 2 * y + c)[step]

    def order(self):
        owners = (self.sibling, self.by_y, self.by_both, None)
        return [(self.turn_of(step, self.y, self.c), owners[step]) for step in range(4)]

    def drop(self, copy):
        self.waiting = [made for made in self.waiting if made is not copy]

    def finish(self):
        for made in self.waiting:
            made.wait_send()


class Beside:
    def __init__(self, net, source, target, steps):
        self.net, self.steps = net, steps
        self.at = net.take(1)
        other = jnp.clip(net.s + steps, 0, RANKS - 1)
        self.copy = pltpu.make_async_remote_copy(
            src_ref=source,
            dst_ref=target,
            send_sem=net.send_sem.at[self.at],
            recv_sem=net.recv_sem.at[self.at],
            device_id=(other, net.b),
            device_id_type=MESH,
        )
        last = RANKS - 1 if steps > 0 else 0
        first = 0 if steps > 0 else RANKS - 1
        self.sends = net.s != last
        self.takes = net.s != first
        net.waiting.append(self)

    def start(self):
        @pl.when(self.sends)
        def _():
            self.copy.start()

    def wait_recv(self):
        @pl.when(self.takes)
        def _():
            self.copy.wait_recv()

    def wait_send(self):
        @pl.when(self.sends)
        def _():
            self.copy.wait_send()


def pieces(value):
    cent = value - jnp.mean(value, axis=-1, keepdims=True)
    inverse = lax.rsqrt(jnp.mean(cent * cent, axis=-1, keepdims=True) + 1e-05)
    return cent * inverse, inverse


def pieces_back(incoming, normal, inverse, gain):
    share = jnp.sum(incoming * normal, axis=0, keepdims=True)
    scaled = incoming * gain
    first = jnp.mean(scaled, axis=-1, keepdims=True)
    second = jnp.mean(scaled * normal, axis=-1, keepdims=True)
    return inverse * (scaled - first - normal * second), share


def gelu_parts(u):
    square = u * u
    bend = jnp.tanh(ROOT * u * (1.0 + CUBIC * square))
    half = 0.5 * (1.0 + bend)
    value = u * half
    slope = half + 0.5 * u * (1.0 - bend * bend) * (ROOT * (1.0 + 3.0 * CUBIC * square))
    return value, slope


def split(value):
    high = value.astype(BF)
    return high, (value - high.astype(F32)).astype(BF)


def transform(r, signal, re_out, im_out):
    @pl.loop(0, 4)
    def _(at):
        rows = pl.ds(pl.multiple_of(256 * at, 256), 256)
        re_out[rows, :] = mm(r.cos_table[rows, :], signal)
        im_out[rows, :] = -mm(r.sin_table[rows, :], signal)


def transform_two(r, signal, re_out, im_out):
    high, low = split(signal)
    r.pack_re[:, 0:128] = high
    r.pack_re[:, 128:256] = low

    @pl.loop(0, 4)
    def _(at):
        rows = pl.ds(pl.multiple_of(256 * at, 256), 256)
        re, im = mm(r.cos_table[rows, :], r.pack_re[...]), mm(r.sin_table[rows, :], r.pack_re[...])
        re_out[rows, :] = re[:, 0:128] + re[:, 128:256]
        im_out[rows, :] = -(im[:, 0:128] + im[:, 128:256])


def inverse(r, re, im, out):
    re_high, re_low = split(re)
    im_high, im_low = split(im)
    r.pack_re[:, 0:128] = re_high
    r.pack_re[:, 128:256] = re_low
    r.pack_im[:, 0:128] = im_high
    r.pack_im[:, 128:256] = im_low

    @pl.loop(0, 4)
    def _(at):
        rows = pl.ds(pl.multiple_of(256 * at, 256), 256)
        both = mm(r.cos_table[rows, :], r.pack_re[...]) - mm(r.sin_table[rows, :], r.pack_im[...])
        out[rows, :] = ((both[:, 0:128] + both[:, 128:256]) * (1.0 / SPAN)).astype(out.dtype)


def modes(coef_ref, rate_ref, out_ref):
    blocks, width = out_ref.shape[0] // 8, out_ref.shape[1]
    row = lax.broadcasted_iota(jnp.int32, (8, width), 0).astype(F32)
    out_ref[...] = jnp.zeros_like(out_ref)

    @pl.loop(0, 8)
    def _(group):
        some = pl.ds(pl.multiple_of(8 * group, 8), 8)
        rate, coef = rate_ref[some, :], coef_ref[some, :]
        falls = [coef[n : n + 1] * jnp.exp(-rate[n : n + 1] * row) for n in range(8)]
        steps = [jnp.exp(-rate[n : n + 1] * jnp.maximum(row, 8.0)) for n in range(8)]

        def step(at, falls):
            rows = pl.ds(pl.multiple_of(8 * at, 8), 8)
            out_ref[rows, :] += sum(falls[1:], falls[0])
            return tuple(fall * factor for fall, factor in zip(falls, steps))

        lax.fori_loop(0, blocks, step, tuple(falls), unroll=4)


def modes_back(coef_ref, rate_ref, grad_ref, coef_out, rate_out):
    blocks, width = grad_ref.shape[0] // 8, grad_ref.shape[1]
    row = lax.broadcasted_iota(jnp.int32, (8, width), 0).astype(F32)

    @pl.loop(0, 8)
    def _(group):
        some = pl.ds(pl.multiple_of(8 * group, 8), 8)
        rate, coef = rate_ref[some, :], coef_ref[some, :]
        steps = [jnp.exp(-rate[n : n + 1] * jnp.maximum(row, 8.0)) for n in range(8)]
        zero = jnp.minimum(row, 0.0)

        def step(at, carry):
            totals, slopes = carry
            here = grad_ref[pl.ds(pl.multiple_of(8 * (blocks - 1 - at), 8), 8), :]
            slopes = tuple(slope * factor + total for slope, factor, total in zip(slopes, steps, totals))
            totals = tuple(total * factor + here for total, factor in zip(totals, steps))
            return totals, slopes

        totals, slopes = lax.fori_loop(0, blocks, step, ((zero,) * 8, (zero,) * 8), unroll=2)
        coef_rows, rate_rows = [], []
        for n in range(8):
            fall = jnp.exp(-rate[n : n + 1] * row)
            coef_rows.append(jnp.sum(fall * totals[n], axis=0, keepdims=True))
            late = jnp.sum(fall * (8.0 * steps[n] * slopes[n] + row * totals[n]), axis=0, keepdims=True)
            rate_rows.append(-coef[n : n + 1] * late)
        coef_out[some, :] = jnp.concatenate(coef_rows, axis=0)
        rate_out[some, :] = jnp.concatenate(rate_rows, axis=0)


def shift_forward(keys, taps, value, shifted):
    @pl.loop(0, OWNERS)
    def _(block):
        lanes = lanes_of(block)
        near = keys[:, lanes]
        total = jnp.zeros((ROWS, BLOCK), F32)
        for rest in range(8):
            turned = pltpu.roll(near, rest, 0) if rest else near
            for part in range(8):
                total = total + taps[8 * part + rest : 8 * part + rest + 1, lanes] * turned[64 - 8 * part : 192 - 8 * part]
        shifted[:, lanes] = total


def shift_back(grads, keys, taps, key_grad, taps_grad):
    @pl.loop(0, OWNERS)
    def _(block):
        lanes = lanes_of(block)
        ahead, near = grads[:, lanes], keys[:, lanes]
        here = ahead[0:ROWS]
        total = jnp.zeros((ROWS, BLOCK), F32)
        rows = {}
        for rest in range(8):
            later = pltpu.roll(ahead, 192 - rest, 0) if rest else ahead
            turned = pltpu.roll(near, rest, 0) if rest else near
            for part in range(8):
                lag = 8 * part + rest
                total = total + taps[lag : lag + 1, lanes] * later[8 * part : 8 * part + ROWS]
                taps_grad[lag : lag + 1, lanes] = jnp.sum(here * turned[64 - 8 * part : 192 - 8 * part], axis=0, keepdims=True)
        key_grad[:, lanes] = total


def head_lanes(shape, head):
    return lax.broadcasted_iota(jnp.int32, shape, 1) // 64 == head


def document_start(ends, first, count):
    at = first + lax.broadcasted_iota(jnp.int32, (count, 1), 0)
    begin = jnp.zeros((count, 1), jnp.int32)
    for index in range(3):
        begin = jnp.where(at >= ends[index], ends[index], begin)
    return at, begin


def allowed_pairs(ends, part):
    query_at, begin = document_start(ends, 256 * part, 256)
    key_at = lax.broadcasted_iota(jnp.int32, (256, 256 * (part + 1)), 1)
    return jnp.logical_and(key_at <= query_at, key_at >= begin)


def attention_forward(r, part):
    rows, keys = slice(256 * part, 256 * part + 256), slice(0, 256 * part + 256)
    mask = allowed_pairs(r.ends, part)

    @pl.loop(0, 2)
    def _(head):
        lanes = head_lanes((256, BLOCK), head)
        query = jnp.where(lanes, r.qkv[0, rows, :].astype(F32) * 0.125, 0.0).astype(BF)
        scores = jnp.where(mask, mm_nt(query, r.qkv[1, keys, :]), NEGATIVE)
        top = jnp.max(scores, axis=1, keepdims=True)
        weights = jnp.exp(scores - top)
        mass = jnp.sum(weights, axis=1, keepdims=True)
        mixed = mm(weights.astype(BF), r.qkv[2, keys, :]) / mass
        r.attended_full[rows, :] = jnp.where(lanes, mixed, r.attended_full[rows, :])
        r.lse[rows, :] = jnp.where(lanes, top + jnp.log(mass), r.lse[rows, :])

    r.attended_low[rows, :] = r.attended_full[rows, :].astype(BF)


def attention_back(r, part):
    rows, keys = slice(256 * part, 256 * part + 256), slice(0, 256 * part + 256)
    mask = allowed_pairs(r.ends, part)

    @pl.loop(0, 2)
    def _(head):
        lanes = head_lanes((256, BLOCK), head)
        query = jnp.where(lanes, r.qkv[0, rows, :].astype(F32) * 0.125, 0.0).astype(BF)
        whole = r.att_grad[rows, :].astype(F32)
        grads = jnp.where(lanes, whole, 0.0)
        delta = jnp.sum(grads * r.attended_full[rows, :], axis=1, keepdims=True)
        lse = jnp.sum(jnp.where(lanes, r.lse[rows, :], 0.0), axis=1, keepdims=True) * (1.0 / 64.0)
        grads = grads.astype(BF)
        scores = mm_nt(query, r.qkv[1, keys, :])
        probs = jnp.where(mask, jnp.exp(scores - lse), 0.0)
        score_grad = (probs * (mm_nt(grads, r.qkv[2, keys, :]) - delta)).astype(BF)
        query_grad = mm(score_grad, r.qkv[1, keys, :]) * 0.125
        r.query_grad[rows, :] = jnp.where(lanes, query_grad, r.query_grad[rows, :])
        r.key_grad[keys, :] += mm_tn(score_grad, query)
        r.value_grad[keys, :] += mm_tn(probs.astype(BF), grads)

    r.qkv_grad[0, rows, :] = r.query_grad[rows, :].astype(BF)
    r.qkv_grad[1, rows, :] = r.key_grad[rows, :].astype(BF)
    r.qkv_grad[2, rows, :] = r.value_grad[rows, :].astype(BF)


class Gather:
    def __init__(self, net, source, target):
        self.net, self.target = net, target
        here = target(net.y, net.c)
        self.first = net.send(source, here, net.sibling)
        self.across = net.send(source, here, net.by_y)

    def forward(self):
        self.across.wait_recv()
        landed = self.target(flip(self.net.y), self.net.c)
        self.second = self.net.send(landed, landed, self.net.sibling)

    def wait(self):
        self.first.wait_recv()
        self.second.wait_recv()

    def free(self):
        for copy in (self.first, self.across, self.second):
            copy.wait_send()
            self.net.drop(copy)


class Locals:
    def __init__(self, sems):
        self.sems, self.used, self.waiting = sems, 0, []

    def start(self, source, target):
        copy = pltpu.make_async_copy(source, target, self.sems.at[self.used])
        self.used += 1
        copy.start()
        return copy

    def put(self, source, target):
        self.waiting.append(self.start(source, target))

    def finish(self):
        for copy in self.waiting:
            copy.wait()


LAYER, PAIR = (0, 1)
LENGTH = (1152, 576)


class Sum:
    def __init__(self, r, net, name, kind):
        self.net, self.kind = net, kind
        for part in ("right", "grads", "near_a", "near_b", "next_a", "next_b", "own", "third"):
            setattr(self, part, getattr(r, name + "_" + part))
        if kind == LAYER:
            self.across = getattr(r, name + "_across")
        self.half = LENGTH[kind] // 2
        self.shared = []

    def give(self, kept, step, columns, other):
        own = self.right.at[rows_of(self.net.b), :]
        if other is None:
            own[...] = columns
        else:
            kept[step] = columns
            self.shared.append(self.net.send(kept.at[step], own, other))

    def share_pairs(self, pairs):
        own = self.right.at[rows_of(self.net.b), :]
        for index, other in self.net.order():
            if other is None:
                own[...] = pairs[index]
            else:
                self.shared.append(self.net.send(pairs.at[index], own, other))

    def free(self, copies):
        for copy in copies:
            copy.wait_send()
            self.net.drop(copy)

    def free_rows(self):
        self.free(self.shared[:3])

    def free_columns(self):
        self.free(self.shared[-3:])

    def share_rows(self, turned):
        net = self.net
        own = pl.ds(pl.multiple_of(192 * net.b, 64), 192)
        self.across[:, lanes_of(net.b)] = turned[own, :]
        for index, other in self.net.order()[:3]:
            rows = pl.ds(pl.multiple_of(192 * index, 64), 192)
            self.shared.append(net.send(turned.at[rows, :], self.across.at[:, lanes_of(net.b)], other))

    def wait_shared(self):
        for copy in self.shared:
            copy.wait_recv()

    def place(self, product, tile):
        for block in range(8):
            at = pl.ds(pl.multiple_of(96 * tile, 16), 96)
            self.grads[block % 2, (block // 2) % 2, block // 4, at, :] = product[96 * block : 96 * block + 96].astype(BF)

    def product(self, left, second):
        self.wait_shared()
        if self.kind == LAYER:

            @pl.loop(0, 3)
            def _(chunk):
                lanes = pl.ds(pl.multiple_of(256 * chunk, 256), 256)
                product = mm(left[...], self.right[:, lanes])
                self.place(product[:, 0:128], 2 * chunk)
                self.place(product[:, 128:256], 2 * chunk + 1)

            @pl.loop(0, 8)
            def _(block):
                lanes = pl.ds(pl.multiple_of(384 * block, 384), 384)
                product = mm(self.across[...], second[:, lanes])
                for tile in range(3):
                    self.grads[
                        lax.rem(block, 2), lax.rem(block // 2, 2), block // 4, 576 + 192 * tile : 768 + 192 * tile, :
                    ] = product[:, 128 * tile : 128 * tile + 128].astype(BF)

        else:

            @pl.loop(0, 2)
            def _(chunk):
                lanes = pl.ds(pl.multiple_of(256 * chunk, 256), 256)
                product = mm(left[...], self.right[:, lanes])
                self.place(product[:, 0:128], 2 * chunk)
                self.place(product[:, 128:256], 2 * chunk + 1)

            right = self.right[:, 512:768]
            first = lax.broadcasted_iota(jnp.int32, right.shape, 1) < 64
            zero = jnp.zeros_like(right)
            product = mm(left[...], jnp.where(first, right, zero)) + mm(second[...], jnp.where(first, zero, right))
            self.place(product[:, 0:128], 4)
            self.place(product[:, 128:256], 5)

        net, half = self.net, self.half
        self.moving = [
            net.send(self.grads.at[flip(net.x), :, :, 0:half, :], self.near_a, net.by_x),
            net.send(self.grads.at[:, flip(net.low), :, half:, :], self.near_b, net.by_low),
        ]

    def arrive(self):
        for copy in self.moving:
            copy.wait_recv()

    def second(self):
        net, half, grads = self.net, self.half, self.grads
        self.arrive()

        @pl.loop(0, 4)
        def _(step):
            one, two = step // 2, lax.rem(step, 2)
            grads[net.x, one, two, 0:half, :] += self.near_a[one, two]
            grads[one, net.low, two, half:, :] += self.near_b[one, two]

        self.moving = [
            net.send(grads.at[net.x, flip(net.low), :, 0:half, :], self.next_a, net.by_low),
            net.send(grads.at[flip(net.x), net.low, :, half:, :], self.next_b, net.by_x),
        ]

    def last(self):
        net, half, grads = self.net, self.half, self.grads
        self.arrive()

        @pl.loop(0, 2)
        def _(step):
            grads[net.x, net.low, step, 0:half, :] += self.next_a[step]
            grads[net.x, net.low, step, half:, :] += self.next_b[step]

        self.moving = [net.send(grads.at[net.x, net.low, flip(net.high)], self.third, net.by_high)]

    def end(self, near):
        net = self.net
        near.put(self.grads.at[net.x, net.low, net.high], self.own)
        self.arrive()


def sum_scratch(name, kind):
    length = LENGTH[kind]
    half = length // 2
    made = {
        name + "_right": ((512, WIDE), BF),
        name + "_grads": ((2, 2, 2, length, 128), BF),
        name + "_near_a": ((2, 2, half, 128), BF),
        name + "_near_b": ((2, 2, half, 128), BF),
        name + "_next_a": ((2, half, 128), BF),
        name + "_next_b": ((2, half, 128), BF),
    }
    if kind == LAYER:
        made[name + "_across"] = ((192, 512), BF)
    return made


def pair_columns(wide, narrow, out):
    first = lax.broadcasted_iota(jnp.int32, (ROWS, BLOCK), 1) < 64

    def tile(at):
        at = at % (3 * WIDE)
        return wide[at // WIDE, :, at % WIDE : at % WIDE + BLOCK].astype(F32)

    def turned(at):
        return jnp.where(first, pltpu.roll(tile(at - BLOCK), 64, 1), pltpu.roll(tile(at), 64, 1))

    def thin(at):
        return narrow[:, at : at + BLOCK].astype(F32)

    def thin_turned(at):
        upper = pltpu.roll(thin(at), 64, 1)
        return jnp.where(first, pltpu.roll(thin(at - BLOCK), 64, 1), upper) if at else upper

    for block in range(4):
        start = 576 * block
        if block % 2 == 0:
            for part in range(4):
                out[block, :, BLOCK * part : BLOCK * part + BLOCK] = tile(start + BLOCK * part).astype(BF)
            lower, upper, rest = tile(start + 512), thin_turned(192 * block), thin_turned(192 * block + BLOCK)
        else:
            for part in range(4):
                out[block, :, BLOCK * part : BLOCK * part + BLOCK] = turned(start + 64 + BLOCK * part).astype(BF)
            lower, upper, rest = turned(start + 576), thin(192 * block - 64), thin(192 * block + 64)
        out[block, :, 512:640] = jnp.where(first, lower, upper).astype(BF)
        out[block, :, 640:768] = rest.astype(BF)


def turn(blocks, out):
    for block in range(4):
        out[:, BLOCK * block : BLOCK * block + BLOCK] = blocks[BLOCK * block : BLOCK * block + BLOCK, :].T


TABLES = ("cos_table", "sin_table")
KEPT = (
    "qkv",
    "lse",
    "attended_full",
    "bend_b",
    "stream_b",
    "response",
    "query_a",
    "shifted",
    "value_a",
    "key_ext",
    "kernel_re",
    "kernel_im",
    "signal_re",
    "signal_im",
)
LEFTS = ("normed_a", "gated", "normed_b", "active_b", "normed_c")


def kernel_a(r):
    net = Net(r.send_sem, r.recv_sem)
    near = Locals(r.local_sem)
    net.hello()
    wait = {}
    for name in ("mixer_in",) + TABLES + ("mixer_out", "up_first", "down_first", "project_in"):
        wait[name] = near.start(getattr(r, name + "_hbm"), getattr(r, name))
    r.ends[0] = r.doc_lengths[0, 0]
    r.ends[1] = r.ends[0] + r.doc_lengths[0, 1]
    r.ends[2] = r.ends[1] + r.doc_lengths[0, 2]

    def keep(*names):
        for name in names:
            near.put(getattr(r, name), getattr(r, name + "_kept"))

    gathers = []

    def gather(name):
        all_of = getattr(r, name + "_all")
        mine = getattr(r, name)
        near.put(mine, all_of.at[rows_of(net.b), :])
        gathers.append(Gather(net, mine, lambda y, c: all_of.at[rows_of(2 * y + c), :]))

    me = net.s
    stream = r.tokens[0].astype(F32)
    normal, _ = pieces(stream)
    r.normed_a[...] = (normal * r.mixer_norm_gain[...][None]).astype(BF)
    wait["mixer_in"].wait()
    r.key_ext[64:192, :] = mm(r.normed_a[...], r.mixer_in[:, WIDE : 2 * WIDE])
    r.rim_out[...] = r.key_ext[128:192, :].astype(BF)
    net.ready()
    rim = Beside(net, r.rim_out, r.rim_in, 1)
    rim.start()
    gather("normed_a")

    @pl.when(me == 0)
    def _():
        r.rim_in[...] = jnp.zeros_like(r.rim_in)

    r.query_a[...] = mm(r.normed_a[...], r.mixer_in[:, 0:WIDE])
    r.value_a[...] = mm(r.normed_a[...], r.mixer_in[:, 2 * WIDE :])
    keep("query_a", "value_a")
    rim.wait_recv()
    r.key_ext[0:64, :] = r.rim_in[...].astype(F32)
    shift_forward(r.key_ext, r.shift_taps, None, r.shifted)
    r.product_low[...] = (r.shifted[...] * r.value_a[...]).astype(BF)
    go = net.spread(lambda block: r.product_low.at[:, lanes_of(block)], lambda rank: r.signal.at[rows_of(rank), :], True)
    go.start()
    go.own()
    keep("key_ext", "shifted")
    block = lanes_of(jnp.clip(me - 1, 0, OWNERS - 1))
    r.coef[...] = r.mode_coef[:, block]
    r.rate[...] = r.mode_rate[:, block]
    modes(r.coef, r.rate, r.mode_rows)
    for name in TABLES:
        wait[name].wait()
    transform_two(r, r.mode_rows[...], r.kernel_re, r.kernel_im)
    turned = r.kernel_re[...] * r.phase_cos[...] - r.kernel_im[...] * r.phase_sin[...]
    r.kernel_im[...] = r.kernel_im[...] * r.phase_cos[...] + r.kernel_re[...] * r.phase_sin[...]
    r.kernel_re[...] = turned
    keep("kernel_re", "kernel_im")
    go.wait_recv()
    transform(r, r.signal[...], r.signal_re, r.signal_im)
    inverse(
        r,
        r.signal_re[...] * r.kernel_re[...] - r.signal_im[...] * r.kernel_im[...],
        r.signal_re[...] * r.kernel_im[...] + r.signal_im[...] * r.kernel_re[...],
        r.conv,
    )
    back = net.spread(lambda rank: r.conv.at[rows_of(rank), :], lambda block: r.conv_home.at[:, lanes_of(block)], False)
    back.start()
    back.own()
    turned = r.signal_re[...] * r.phase_cos[...] - r.signal_im[...] * r.phase_sin[...]
    r.signal_im[...] = -(r.signal_im[...] * r.phase_cos[...] + r.signal_re[...] * r.phase_sin[...])
    r.signal_re[...] = turned
    keep("signal_re", "signal_im")
    for name in ("mixer_out", "up_first", "down_first", "project_in"):
        wait[name].wait()
    back.wait_recv()
    r.response[...] = r.conv_home[...].astype(F32) + r.skip_gain[...][None] * (r.shifted[...] * r.value_a[...])
    r.gated[...] = (r.query_a[...] * r.response[...]).astype(BF)
    gather("gated")
    stream_b = r.tokens[0].astype(F32) + mm(r.gated[...], r.mixer_out[...])
    r.stream_b[...] = stream_b
    normal, _ = pieces(stream_b)
    r.normed_b[...] = (normal * r.gain_second[...][None]).astype(BF)
    gather("normed_b")
    r.stream_c[...] = stream_b
    for chunk in range(4):
        lanes = slice(WIDE * chunk, WIDE * chunk + WIDE)
        active, bend = gelu_parts(mm(r.normed_b[...], r.up_first[:, lanes]))
        r.bend_b[:, lanes] = bend.astype(BF)
        active = active.astype(BF)
        r.active_b[:, lanes] = active
        r.stream_c[...] += mm(active, r.down_first[lanes, :])
    normal, _ = pieces(r.stream_c[...])
    r.normed_c[...] = (normal * r.attention_norm_gain[...][None]).astype(BF)
    for index in range(3):
        r.mixed_c[index] = mm(r.normed_c[...], r.project_in[:, WIDE * index : WIDE * index + WIDE]).astype(BF)
    go = net.spread(lambda block: r.mixed_c.at[:, :, lanes_of(block)], lambda rank: r.qkv.at[:, rows_of(rank), :], True)
    go.start()
    go.own()
    keep("response", "stream_b", "bend_b")
    gather("active_b")
    gather("normed_c")
    for made in gathers[:3]:
        made.forward()
    go.wait_recv()
    keep("qkv")
    back = net.spread(lambda rank: r.attended_low.at[rows_of(rank), :], lambda block: r.attended.at[:, lanes_of(block)], False)
    for part in (3, 2, 1, 0):
        attention_forward(r, part)
        back.start(lambda rank, part=part: rank // 2 == part)
    back.own()
    keep("lse", "attended_full")
    for made in gathers[3:]:
        made.forward()
    back.wait_recv()
    for made in gathers:
        made.wait()
    net.finish()
    near.finish()


def kernel_b(r):
    net = Net(r.send_sem, r.recv_sem)
    near = Locals(r.local_sem)
    net.hello()
    wait = {}

    def fetch(name, into=None):
        wait[name] = near.start(getattr(r, name + "_hbm"), getattr(r, into or name))

    for name, into in (("project_out", "out_weight"), ("up_second", "up"), ("down_second", "down")):
        fetch(name, into)
    for name in KEPT[:10]:
        fetch(name)
    fetch("project_in", "in_weight")
    fetch("normed_c_all", "pair_one")
    for name in TABLES:
        fetch(name)
    r.ends[0] = r.doc_lengths[0, 0]
    r.ends[1] = r.ends[0] + r.doc_lengths[0, 1]
    r.ends[2] = r.ends[1] + r.doc_lengths[0, 2]
    sum_d, sum_c = Sum(r, net, "sum_d", LAYER), Sum(r, net, "sum_c", PAIR)
    sum_b, sum_a = Sum(r, net, "sum_b", LAYER), Sum(r, net, "sum_a", PAIR)
    own_rows = rows_of(net.b)

    gain_d = r.gain_fourth[...][None]
    wait["project_out"].wait()
    stream_d = r.stream_c[...] + mm(r.attended[...], r.out_weight[...])
    normal, inverse_d = pieces(stream_d)
    normed_d = (normal * gain_d).astype(BF)
    r.layer_left[own_rows, :] = normed_d
    r.total[...] = stream_d
    r.turned[...] = r.cotangent[0].T
    r.pair_two[own_rows, :] = r.attended[...]
    net.ready()
    gather_att = Gather(net, r.pair_two.at[own_rows, :], lambda y, c: r.pair_two.at[rows_of(2 * y + c), :])
    gather_d = Gather(net, r.layer_left.at[own_rows, :], lambda y, c: r.layer_left.at[rows_of(2 * y + c), :])
    sum_d.share_rows(r.turned)
    wait["up_second"].wait()
    wait["down_second"].wait()
    gathers = []
    for step, (index, other) in enumerate(net.order()):
        lanes = pl.ds(pl.multiple_of(WIDE * index, WIDE), WIDE)
        raised = mm(r.layer_left[own_rows, :], r.up[:, lanes])
        active, slope = gelu_parts(raised)
        active = active.astype(BF)
        r.layer_second[own_rows, lanes] = active

        def spot(y, c, step=step):
            at = pl.ds(pl.multiple_of(WIDE * net.turn_of(step, y, c), WIDE), WIDE)
            return r.layer_second.at[rows_of(2 * y + c), at]

        gathers.append(Gather(net, spot(net.y, net.c), spot))
        r.total[...] += mm(active, r.down[lanes, :])
        slope = (slope * mm_nt(r.cotangent[0], r.down[lanes, :])).astype(BF)
        sum_d.give(r.slopes, step, slope, other)
        back = mm_nt(slope, r.up[:, lanes])
        if step == 0:
            r.grad_d[...] = back
        else:
            r.grad_d[...] += back
    grad, gain_four = pieces_back(r.grad_d[...], normal, inverse_d, gain_d)
    grad = r.cotangent[0].astype(F32) + grad
    r.grad_d[...] = grad
    r.grad_d_low[...] = grad.astype(BF)
    r.att_grad_home[...] = mm_nt(r.grad_d_low[...], r.out_weight[...]).astype(BF)
    go = net.spread(lambda block: r.att_grad_home.at[:, lanes_of(block)], lambda rank: r.att_grad.at[rows_of(rank), :], True)
    go.start()
    go.own()
    fetch("up_first", "up")
    fetch("down_first", "down")
    fetch("mixer_out", "out_weight")
    r.block_out[0] = r.total[...].astype(BF)

    r.key_grad[...] = jnp.zeros_like(r.key_grad)
    r.value_grad[...] = jnp.zeros_like(r.value_grad)
    gather_att.forward()
    gather_d.forward()
    gathers[0].forward()
    gathers[1].forward()
    for name in ("qkv", "lse", "attended_full"):
        wait[name].wait()
    go.wait_recv()
    back = net.spread(
        lambda rank: r.qkv_grad.at[:, rows_of(rank), :], lambda block: r.mixed_grad_c.at[:, :, lanes_of(block)], False
    )
    for part in (3, 2, 1, 0):
        attention_back(r, part)
        back.start(lambda rank, part=part: rank // 2 == part)
    back.own()
    for name, into in (
        ("kernel_re", "lse"),
        ("kernel_im", "attended_full"),
        ("signal_re", "query_grad"),
        ("signal_im", "key_grad"),
    ):
        fetch(name, into)
    gathers[2].forward()
    gathers[3].forward()
    gather_d.wait()
    turn(r.layer_left, r.turned_one)
    for made in gathers:
        made.wait()
    sum_d.product(r.turned_one, r.layer_second)
    for made in [gather_d] + gathers:
        made.free()
    fetch("normed_b_all", "layer_left")
    fetch("active_b_all", "layer_second")

    normal, inverse_c = pieces(r.stream_c[...])
    wait["project_in"].wait()
    back.wait_recv()
    grad = mm_nt(r.mixed_grad_c[0], r.in_weight[:, 0:WIDE])
    for index in range(1, 3):
        grad = grad + mm_nt(r.mixed_grad_c[index], r.in_weight[:, WIDE * index : WIDE * index + WIDE])
    fetch("mixer_in", "in_weight")
    grad, gain_three = pieces_back(grad, normal, inverse_c, r.attention_norm_gain[...][None])
    grad = grad + r.grad_d[...]
    r.total[...] = grad
    r.grad_c_low[...] = grad.astype(BF)
    sum_d.free_rows()
    r.turned[...] = r.grad_c_low[...].T
    sum_b.share_rows(r.turned)
    sum_d.free_columns()
    wait["up_first"].wait()
    wait["down_first"].wait()
    wait["bend_b"].wait()
    for step, (index, other) in enumerate(net.order()):
        lanes = pl.ds(pl.multiple_of(WIDE * index, WIDE), WIDE)
        slope = (r.bend_b[:, lanes].astype(F32) * mm_nt(r.grad_c_low[...], r.down[lanes, :])).astype(BF)
        sum_b.give(r.slopes, step, slope, other)
        part = mm_nt(slope, r.up[:, lanes])
        if step == 0:
            r.grad_b[...] = part
        else:
            r.grad_b[...] += part
    for name in ("stream_b", "response", "query_a", "shifted", "value_a", "key_ext", "mixer_out"):
        wait[name].wait()
    normal, inverse_b = pieces(r.stream_b[...])
    grad, gain_two = pieces_back(r.grad_b[...], normal, inverse_b, r.gain_second[...][None])
    grad = grad + r.total[...]
    r.grad_b[...] = grad
    r.grad_b_low[...] = grad.astype(BF)
    gated_grad = mm_nt(r.grad_b_low[...], r.out_weight[...])
    r.mixed_grad_a[0] = (gated_grad * r.response[...]).astype(BF)
    response_grad = gated_grad * r.query_a[...]
    r.response_grad[...] = response_grad
    r.response_grad_low[...] = response_grad.astype(BF)
    go = net.spread(
        lambda block: r.response_grad_low.at[:, lanes_of(block)], lambda rank: r.conv_grad.at[rows_of(rank), :], True
    )
    go.start()
    go.own()
    skip_part = jnp.sum(response_grad * (r.shifted[...] * r.value_a[...]), axis=0, keepdims=True)
    pair_columns(r.mixed_grad_c, r.grad_d_low, r.pairs)
    sum_c.share_pairs(r.pairs)
    wait["normed_c_all"].wait()
    turn(r.pair_one, r.turned_one)
    gather_att.wait()
    turn(r.pair_two, r.turned_two)
    gather_att.free()
    fetch("normed_a_all", "pair_one")
    fetch("gated_all", "pair_two")

    for name in TABLES + ("kernel_re", "kernel_im", "signal_re", "signal_im"):
        wait[name].wait()
    kernel_re, kernel_im, signal_re, signal_im = r.lse, r.attended_full, r.query_grad, r.key_grad
    go.wait_recv()
    transform(r, r.conv_grad[...], r.grad_re, r.grad_im)
    inverse(
        r,
        r.grad_re[...] * kernel_re[...] + r.grad_im[...] * kernel_im[...],
        r.grad_im[...] * kernel_re[...] - r.grad_re[...] * kernel_im[...],
        r.signal_grad,
    )
    back = net.spread(
        lambda rank: r.signal_grad.at[rows_of(rank), :], lambda block: r.signal_grad_home.at[:, lanes_of(block)], False
    )
    back.start()
    back.own()
    sum_d.second()
    sum_c.product(r.turned_one, r.turned_two)
    back.wait_recv()

    signal_grad = r.signal_grad_home[...].astype(F32) + r.skip_gain[...][None] * r.response_grad[...]
    r.grad_ext[0:ROWS, :] = signal_grad * r.value_a[...]
    r.rim_out[...] = r.grad_ext[0:64, :].astype(BF)
    rim = Beside(net, r.rim_out, r.rim_in, -1)
    rim.start()
    r.mixed_grad_a[2] = (signal_grad * r.shifted[...]).astype(BF)

    @pl.when(net.s == RANKS - 1)
    def _():
        r.rim_in[...] = jnp.zeros_like(r.rim_in)

    wait["normed_b_all"].wait()
    turn(r.layer_left, r.turned_one)
    wait["active_b_all"].wait()
    sum_b.product(r.turned_one, r.layer_second)
    rim.wait_recv()
    r.grad_ext[ROWS:192, :] = r.rim_in[...].astype(F32)
    shift_back(r.grad_ext, r.key_ext, r.shift_taps, r.total, r.taps)
    r.mixed_grad_a[1] = r.total[...].astype(BF)
    sum_c.free_columns()
    pair_columns(r.mixed_grad_a, r.grad_b_low, r.pairs)
    sum_a.share_pairs(r.pairs)
    wait["mixer_in"].wait()
    grad = mm_nt(r.mixed_grad_a[0], r.in_weight[:, 0:WIDE])
    for index in range(1, 3):
        grad = grad + mm_nt(r.mixed_grad_a[index], r.in_weight[:, WIDE * index : WIDE * index + WIDE])
    normal, inverse_a = pieces(r.tokens[0].astype(F32))
    grad, gain_one = pieces_back(grad, normal, inverse_a, r.mixer_norm_gain[...][None])
    r.token_grad[0] = r.grad_b[...] + grad

    gains = jnp.concatenate([gain_one, skip_part, gain_two, gain_three, gain_four, jnp.zeros((3, WIDE), F32)], axis=0)
    for block in range(4):
        r.small[block // 2, block % 2, 0:16, :] = r.taps[16 * block : 16 * block + 16, :]
        r.small[block // 2, block % 2, 16:24, :] = gains
    swap = net.send(r.small.at[:, flip(net.c)], r.small_c, net.sibling)
    wait["normed_a_all"].wait()
    turn(r.pair_one, r.turned_one)
    wait["gated_all"].wait()
    turn(r.pair_two, r.turned_two)
    sum_a.product(r.turned_one, r.turned_two)
    swap.wait_recv()
    r.small[:, net.c] += r.small_c[...]
    swap = net.send(r.small.at[flip(net.y), net.c], r.small_swap.at[0], net.by_y)
    sum_d.last()
    sum_c.second()
    swap.wait_recv()
    r.small_sum[0] = r.small[net.y, net.c] + r.small_swap[0]
    swap = net.send(r.small_sum.at[0], r.small_swap.at[1], net.by_x)

    re = r.grad_re[...] * signal_re[...] - r.grad_im[...] * signal_im[...]
    im = r.grad_re[...] * signal_im[...] + r.grad_im[...] * signal_re[...]
    inverse(r, re, im, r.value_grad)
    block = lanes_of(jnp.clip(net.s - 1, 0, OWNERS - 1))
    r.coef[...] = r.mode_coef[:, block]
    r.rate[...] = r.mode_rate[:, block]
    modes_back(r.coef, r.rate, r.value_grad, r.mode_part.at[0, 0:64], r.mode_part.at[0, 64:128])
    mode = net.send(r.mode_part.at[0], r.mode_swap.at[0], net.sibling)
    sum_b.second()
    mode.wait_recv()
    r.mode_part[1] = r.mode_part[0] + r.mode_swap[0]
    mode = net.send(r.mode_part.at[1], r.mode_swap.at[1], net.by_y)
    swap.wait_recv()
    r.small_sum[1] = r.small_sum[0] + r.small_swap[1]
    swap = net.send(r.small_sum.at[1], r.small_swap.at[2], net.by_low)
    sum_d.end(near)
    sum_c.last()
    sum_a.second()
    mode.wait_recv()
    r.mode_part[2] = r.mode_part[1] + r.mode_swap[1]
    back = net.spread(lambda rank: r.mode_part.at[2], lambda block: r.mode_home.at[:, lanes_of(block)], False)
    back.start()
    back.own()
    swap.wait_recv()
    r.small_sum[2] = r.small_sum[1] + r.small_swap[2]
    swap = net.send(r.small_sum.at[2], r.small_swap.at[3], net.by_high)
    sum_b.last()
    sum_a.last()
    sum_c.end(near)
    turn_back = lax.rem(WIDE - 96 * net.s, WIDE)
    back.wait_recv()
    r.mode_out[...] = pltpu.roll(r.mode_home[...], turn_back, 1)[:, 0:128]
    swap.wait_recv()
    r.small_out[...] = pltpu.roll(r.small_sum[2] + r.small_swap[3], turn_back, 1)[:, 0:128]
    sum_b.end(near)
    sum_a.end(near)
    net.finish()
    near.finish()


def kernel_z(*refs):
    block_in, token_in, mode, small = refs[:4]
    sums = refs[4:12]
    (
        block_out,
        token_grad,
        gain_one,
        mixer_in,
        taps,
        coef,
        rate,
        skip,
        mixer_out,
        gain_two,
        up_first,
        down_first,
        gain_three,
        project_in,
        project_out,
        gain_four,
        up_second,
        down_second,
    ) = refs[12:]
    block_out[...] = block_in[...]
    token_grad[...] = token_in[...]
    taps[...] = small[0:16, 0:96]
    for at, out in enumerate((gain_one, skip, gain_two, gain_three, gain_four)):
        out[...] = small[16 + at, 0:96]
    coef[...] = mode[0:64, 0:96]
    rate[...] = mode[64:128, 0:96]

    def block(index, first, count):
        rows = slice(first, first + count)
        return sums[2 * index][rows, :].astype(F32) + sums[2 * index + 1][rows, :].astype(F32)

    for index, up, down in ((0, up_second, down_second), (2, up_first, down_first)):
        for tile in range(6):
            up[:, 128 * tile : 128 * tile + 128] = block(index, 96 * tile, 96)
        for tile in range(3):
            down[128 * tile : 128 * tile + 128, :] = block(index, 576 + 192 * tile, 192).T
    for index, wide, narrow in ((1, project_in, project_out), (3, mixer_in, mixer_out)):
        for tile in range(4):
            wide[:, 128 * tile : 128 * tile + 128] = block(index, 96 * tile, 96)
        mixed = block(index, 384, 96)
        wide[:, 512:576] = mixed[:, 0:64]
        narrow[:, 0:64] = mixed[:, 64:128]
        narrow[:, 64:192] = block(index, 480, 96)


class Refs:
    pass


def call(body, identity, inputs, hbm, smem, outs, hbm_outs, scratch, semaphores):
    names = list(inputs) + [name + "_hbm" for name in hbm] + list(smem) + list(outs) + list(hbm_outs) + list(scratch)
    names += ["ends", "send_sem", "recv_sem", "local_sem"]

    def run(*refs):
        r = Refs()
        for name, ref in zip(names, refs):
            setattr(r, name, ref)
        body(r)

    vmem = pl.BlockSpec(memory_space=pltpu.VMEM)
    results = pl.pallas_call(
        run,
        out_shape=[jax.ShapeDtypeStruct(shape, kind) for shape, kind in (*outs.values(), *hbm_outs.values())],
        in_specs=[vmem] * len(inputs)
        + [pl.BlockSpec(memory_space=pl.ANY)] * len(hbm)
        + [pl.BlockSpec(memory_space=pltpu.SMEM)] * len(smem),
        out_specs=[vmem] * len(outs) + [pl.BlockSpec(memory_space=pl.ANY)] * len(hbm_outs),
        scratch_shapes=[pltpu.VMEM(shape, kind) for shape, kind in scratch.values()]
        + [pltpu.SMEM((3,), jnp.int32)]
        + [pltpu.SemaphoreType.DMA((semaphores[0],)), pltpu.SemaphoreType.DMA((semaphores[0],))]
        + [pltpu.SemaphoreType.DMA((semaphores[1],))],
        compiler_params=pltpu.CompilerParams(
            collective_id=identity, has_side_effects=True, vmem_limit_bytes=VMEM_BYTES
        ),
    )(*inputs.values(), *hbm.values(), *smem.values())
    return dict(zip((*outs, *hbm_outs), results))


VMEM_BYTES = 66_900_000


def odd_tables():
    odd = 2 * np.arange(SPAN, dtype=np.int64) + 1
    angle = (np.outer(odd, odd) % (8 * SPAN)) * (math.pi / (4 * SPAN))
    phase = (odd * (math.pi / (4 * SPAN)))[:, None] * np.ones((1, BLOCK))
    tables = {
        "cos_table": jnp.asarray(np.cos(angle).astype(ml_dtypes.bfloat16)),
        "sin_table": jnp.asarray(np.sin(angle).astype(ml_dtypes.bfloat16)),
    }
    return tables, jnp.asarray(np.cos(phase), F32), jnp.asarray(np.sin(phase), F32)


def shards_fast(
    tokens,
    doc_lengths,
    mixer_norm_gain,
    mixer_in,
    shift_taps,
    mode_coef,
    mode_rate,
    skip_gain,
    mixer_out,
    gain_second,
    up_first,
    down_first,
    attention_norm_gain,
    project_in,
    project_out,
    gain_fourth,
    up_second,
    down_second,
    cotangent,
):
    tables, phase_cos, phase_sin = odd_tables()
    home, thrice, tall = (ROWS, WIDE), (3, ROWS, WIDE), (ROWS, 4 * WIDE)
    span = (SPAN, BLOCK)
    kept = dict(
        query_a=(home, F32),
        value_a=(home, F32),
        key_ext=((192, WIDE), F32),
        shifted=(home, F32),
        response=(home, F32),
        stream_b=(home, F32),
        bend_b=(tall, BF),
        qkv=((3, *span), BF),
        lse=(span, F32),
        attended_full=(span, F32),
        kernel_re=(span, F32),
        kernel_im=(span, F32),
        signal_re=(span, F32),
        signal_im=(span, F32),
    )
    lefts = dict(normed_a=(home, BF), gated=(home, BF), normed_b=(home, BF), active_b=(tall, BF), normed_c=(home, BF))
    modes_scratch = dict(coef=((64, BLOCK), F32), rate=((64, BLOCK), F32))
    packs = dict(pack_re=((SPAN, 256), BF), pack_im=((SPAN, 256), BF))
    rims = dict(rim_out=((64, WIDE), BF), rim_in=((64, WIDE), BF))
    table_scratch = dict(cos_table=((SPAN, SPAN), BF), sin_table=((SPAN, SPAN), BF))
    a = call(
        kernel_a,
        0,
        dict(
            tokens=tokens,
            mixer_norm_gain=mixer_norm_gain,
            shift_taps=shift_taps,
            mode_coef=mode_coef,
            mode_rate=mode_rate,
            skip_gain=skip_gain,
            gain_second=gain_second,
            attention_norm_gain=attention_norm_gain,
            phase_cos=phase_cos,
            phase_sin=phase_sin,
        ),
        dict(mixer_in=mixer_in, **tables, mixer_out=mixer_out, up_first=up_first, down_first=down_first, project_in=project_in),
        dict(doc_lengths=doc_lengths),
        dict(stream_c=(home, F32), attended=(home, BF)),
        dict(
            **{name + "_kept": made for name, made in kept.items()},
            **{name + "_all": ((4 * shape[0], shape[1]), kind) for name, (shape, kind) in lefts.items()},
        ),
        dict(
            **kept,
            **lefts,
            **modes_scratch,
            **packs,
            **rims,
            **table_scratch,
            product_low=(home, BF),
            signal=(span, BF),
            mode_rows=(span, F32),
            conv=(span, BF),
            conv_home=(home, BF),
            mixed_c=(thrice, BF),
            attended_low=(span, BF),
            mixer_in=((WIDE, 3 * WIDE), BF),
            mixer_out=((WIDE, WIDE), BF),
            up_first=((WIDE, 4 * WIDE), BF),
            down_first=((4 * WIDE, WIDE), BF),
            project_in=((WIDE, 3 * WIDE), BF),
        ),
        (48, 32),
    )
    kinds = dict(sum_d=LAYER, sum_c=PAIR, sum_b=LAYER, sum_a=PAIR)
    sum_outs, sums = {}, {}
    for name, kind in kinds.items():
        sum_outs[name + "_own"] = ((LENGTH[kind], 128), BF)
        sum_outs[name + "_third"] = ((LENGTH[kind], 128), BF)
        sums.update(sum_scratch(name, kind))
    b = call(
        kernel_b,
        1,
        dict(
            tokens=tokens,
            cotangent=cotangent,
            stream_c=a["stream_c"],
            attended=a["attended"],
            mixer_norm_gain=mixer_norm_gain,
            shift_taps=shift_taps,
            mode_coef=mode_coef,
            mode_rate=mode_rate,
            skip_gain=skip_gain,
            gain_second=gain_second,
            attention_norm_gain=attention_norm_gain,
            gain_fourth=gain_fourth,
        ),
        dict(
            project_out=project_out,
            up_second=up_second,
            down_second=down_second,
            **{name: a[name + "_kept"] for name in kept},
            **{name + "_all": a[name + "_all"] for name in lefts},
            **tables,
            project_in=project_in,
            up_first=up_first,
            down_first=down_first,
            mixer_out=mixer_out,
            mixer_in=mixer_in,
        ),
        dict(doc_lengths=doc_lengths),
        dict(
            block_out=((1, *home), BF),
            token_grad=((1, *home), F32),
            mode_out=((128, 128), F32),
            small_out=((24, 128), F32),
        ),
        sum_outs,
        dict(
            **{name: made for name, made in kept.items() if not name.startswith(("kernel", "signal"))},
            **modes_scratch,
            **packs,
            **rims,
            **table_scratch,
            **sums,
            up=((WIDE, 4 * WIDE), BF),
            down=((4 * WIDE, WIDE), BF),
            in_weight=((WIDE, 3 * WIDE), BF),
            out_weight=((WIDE, WIDE), BF),
            layer_left=((512, WIDE), BF),
            layer_second=((512, 4 * WIDE), BF),
            pair_one=((512, WIDE), BF),
            pair_two=((512, WIDE), BF),
            turned_one=((WIDE, 512), BF),
            turned_two=((WIDE, 512), BF),
            turned=((WIDE, ROWS), BF),
            slopes=(thrice, BF),
            pairs=((4, *home), BF),
            total=(home, F32),
            grad_d=(home, F32),
            grad_d_low=(home, BF),
            att_grad_home=(home, BF),
            att_grad=(span, BF),
            query_grad=(span, F32),
            key_grad=(span, F32),
            value_grad=(span, F32),
            qkv_grad=((3, *span), BF),
            mixed_grad_c=(thrice, BF),
            grad_c_low=(home, BF),
            grad_b=(home, F32),
            grad_b_low=(home, BF),
            mixed_grad_a=(thrice, BF),
            response_grad=(home, F32),
            response_grad_low=(home, BF),
            conv_grad=(span, BF),
            grad_re=(span, F32),
            grad_im=(span, F32),
            signal_grad=(span, BF),
            signal_grad_home=(home, BF),
            grad_ext=((192, WIDE), F32),
            taps=((64, WIDE), F32),
            small=((2, 2, 24, WIDE), F32),
            small_c=((2, 24, WIDE), F32),
            small_swap=((4, 24, WIDE), F32),
            small_sum=((3, 24, WIDE), F32),
            mode_part=((3, 128, 128), F32),
            mode_swap=((2, 128, 128), F32),
            mode_home=((128, WIDE), F32),
        ),
        (160, 64),
    )
    vmem = pl.BlockSpec(memory_space=pltpu.VMEM)
    given = [b[name] for name in ("block_out", "token_grad", "mode_out", "small_out")]
    for name in kinds:
        given += [b[name + "_own"], b[name + "_third"]]
    gain = ((96,), F32)
    wide, narrow, up, down, mode = ((96, 576), F32), ((96, 192), F32), ((96, 768), F32), ((384, 192), F32), ((64, 96), F32)
    shapes = (
        ((1, *home), BF),
        ((1, *home), F32),
        gain,
        wide,
        ((16, 96), F32),
        mode,
        mode,
        gain,
        narrow,
        gain,
        up,
        down,
        gain,
        wide,
        narrow,
        gain,
        up,
        down,
    )
    return tuple(
        pl.pallas_call(
            kernel_z,
            out_shape=[jax.ShapeDtypeStruct(shape, kind) for shape, kind in shapes],
            in_specs=[vmem] * len(given),
            out_specs=[vmem] * len(shapes),
        )(*given)
    )


def solution(mesh):
    in_specs = (
        P("batch", "seq", None),
        P("batch", None),
        P(),
        P(),
        P(),
        P(),
        P(),
        P(),
        P(),
        P(),
        P(),
        P(),
        P(),
        P(),
        P(),
        P(),
        P(),
        P(),
        P("batch", "seq", None),
    )
    out_specs = (
        P("batch", "seq", None),
        P("batch", "seq", None),
        P("seq"),
        P("seq", "batch"),
        P("batch", "seq"),
        P(None, "seq"),
        P(None, "seq"),
        P("seq"),
        P("seq", "batch"),
        P("seq"),
        P("seq", "batch"),
        P("seq", "batch"),
        P("seq"),
        P("seq", "batch"),
        P("seq", "batch"),
        P("seq"),
        P("seq", "batch"),
        P("seq", "batch"),
    )
    fast = mesh.shape["seq"] == RANKS and mesh.shape["batch"] == 4
    return jax.shard_map(shards_fast if fast else shards, mesh=mesh, in_specs=in_specs, out_specs=out_specs, check_vma=False)
```

```python
import math

import jax
import jax.numpy as jnp
import ml_dtypes
import numpy as np
from jax import lax
from jax.experimental import pallas as pl
from jax.experimental.pallas import tpu as pltpu
from jax.sharding import PartitionSpec as P

HEADS = 12


HIGH = lax.Precision.HIGHEST
NEGATIVE = -1e30


def shifted_2(value, axis, steps):
    count = lax.axis_size(axis)
    leading, last = (max(0, -steps), min(count, count - steps))
    return lax.ppermute(value, axis, [(source, source + steps) for source in range(leading, last)])


def shortened(x):

    def short(part):
        return part.astype(jnp.bfloat16) if part.dtype == jnp.float32 else part

    return jax.tree.map(short, x)


def mult(form, left, right):
    return jnp.einsum(form, left, right, precision=HIGH, preferred_element_type=jnp.float32)


def norm_pieces(value):
    row_mean = jnp.mean(value, axis=-1, keepdims=True)
    cent = value - row_mean
    inverse_deviation = lax.rsqrt(jnp.mean(cent * cent, axis=-1, keepdims=True) + 1e-05)
    return (cent * inverse_deviation, inverse_deviation)


def norm_backward(incoming_gradient, centered_normalized, inverse_deviation, gain_vector):
    gain_share = jnp.sum(incoming_gradient * centered_normalized, axis=0)
    scaled_rows = incoming_gradient * gain_vector
    inner_product = jnp.mean(scaled_rows, axis=-1, keepdims=True)
    cross_term = jnp.mean(scaled_rows * centered_normalized, axis=-1, keepdims=True)
    return (
        inverse_deviation * (scaled_rows - inner_product - centered_normalized * cross_term),
        gain_share,
    )


def segment_of(where, ends):
    return jnp.sum((where[:, None] >= ends[None, :]).astype(jnp.int32), axis=1)


def allowed(query_pos, key_pos, ends):
    same = segment_of(query_pos, ends)[:, None] == segment_of(key_pos, ends)[None, :]
    return (key_pos[None, :] <= query_pos[:, None]) & same


def kernel_rows(coef, rate, times):

    def step(total, pair):
        scale, decay = pair
        return (total + scale[:, None] * jnp.exp(-decay[:, None] * times[None, :]), None)

    start = jnp.zeros((coef.shape[1], times.shape[0]), jnp.float32)
    return lax.scan(step, start, (coef, rate))[0]


def kernel_grads(coef, rate, times, incoming_gradient):

    def step(carry, pair):
        scale, decay = pair
        fall = incoming_gradient * jnp.exp(-decay[:, None] * times[None, :])
        return (carry, (jnp.sum(fall, axis=1), -scale * jnp.sum(fall * times[None, :], axis=1)))

    return lax.scan(step, jnp.zeros((), jnp.float32), (coef, rate))[1]


def angle_pair(left, right, period):
    turns = left[:, None] * right[None, :] % period
    angle = turns.astype(jnp.float32) * (2.0 * math.pi / period)
    return (jnp.cos(angle), jnp.sin(angle))


def dft_tables(blocks, rows):
    wide = 2 * blocks
    block_ids = jnp.arange(blocks, dtype=jnp.int32)
    wide_ids = jnp.arange(wide, dtype=jnp.int32)
    row_ids = jnp.arange(rows, dtype=jnp.int32)
    return (
        angle_pair(block_ids, wide_ids, wide),
        angle_pair(wide_ids, row_ids, wide * rows),
        angle_pair(row_ids, row_ids, rows),
    )


def forward_spectrum(signal, tables, blocks, rows):
    (cos_one, sin_one), (cos_two, sin_two), (cos_three, sin_three) = tables
    folded = signal.reshape(signal.shape[0], blocks, rows)
    first_re = mult("cpr,pf->cfr", folded, cos_one)
    first_im = -mult("cpr,pf->cfr", folded, sin_one)
    turned_re = first_re * cos_two + first_im * sin_two
    turned_im = first_im * cos_two - first_re * sin_two
    spec_re = mult("cfr,rk->cfk", turned_re, cos_three) + mult("cfr,rk->cfk", turned_im, sin_three)
    spec_im = mult("cfr,rk->cfk", turned_im, cos_three) - mult("cfr,rk->cfk", turned_re, sin_three)
    return (spec_re, spec_im)


def inverse_signal(spec_re, spec_im, tables, blocks, rows):
    (cos_one, sin_one), (cos_two, sin_two), (cos_three, sin_three) = tables
    inner_re = mult("cfk,rk->cfr", spec_re, cos_three) - mult("cfk,rk->cfr", spec_im, sin_three)
    inner_im = mult("cfk,rk->cfr", spec_im, cos_three) + mult("cfk,rk->cfr", spec_re, sin_three)
    turned_re = inner_re * cos_two - inner_im * sin_two
    turned_im = inner_im * cos_two + inner_re * sin_two
    result_value = mult("cfr,pf->cpr", turned_re, cos_one) - mult("cfr,pf->cpr", turned_im, sin_one)
    return result_value.reshape(spec_re.shape[0], blocks * rows) / (2.0 * blocks * rows)


def attend_block(state, query, query_pos, key_block, value_block, key_pos, ends, scale):
    top, mass, accum = state
    scores = (
        jnp.einsum("qhd,khd->hqk", query, key_block, preferred_element_type=jnp.float32) * scale
    )
    mask = allowed(query_pos, key_pos, ends)[None]
    newtop = jnp.maximum(top, jnp.max(jnp.where(mask, scores, NEGATIVE), axis=-1))
    weights = jnp.where(mask, jnp.exp(scores - newtop[:, :, None]), 0.0)
    factor = jnp.exp(top - newtop)
    mass = mass * factor + jnp.sum(weights, axis=-1)
    accum = accum * factor[:, :, None] + jnp.einsum(
        "hqk,khd->hqd", weights, value_block.astype(jnp.float32), preferred_element_type=jnp.float32
    )
    return (newtop, mass, accum)


def score_grads(
    query, grads, lse_rows, delta_rows, query_pos, key_block, value_block, key_pos, ends, scale
):
    scores = (
        jnp.einsum("qhd,khd->hqk", query, key_block, preferred_element_type=jnp.float32) * scale
    )
    mask = allowed(query_pos, key_pos, ends)[None]
    probs = jnp.where(mask, jnp.exp(scores - lse_rows[:, :, None]), 0.0)
    dots = jnp.einsum("qhd,khd->hqk", grads, value_block, preferred_element_type=jnp.float32)
    return (probs, (probs * (dots - delta_rows[:, :, None])).astype(jnp.bfloat16))


def query_back(
    query, grads, lse_rows, delta_rows, query_pos, key_block, value_block, key_pos, ends, scale
):
    score_grad = score_grads(
        query, grads, lse_rows, delta_rows, query_pos, key_block, value_block, key_pos, ends, scale
    )[1]
    return (
        jnp.einsum("hqk,khd->qhd", score_grad, key_block, preferred_element_type=jnp.float32)
        * scale
    )


def key_back(
    query, grads, lse_rows, delta_rows, query_pos, key_block, value_block, key_pos, ends, scale
):
    probs, score_grad = score_grads(
        query, grads, lse_rows, delta_rows, query_pos, key_block, value_block, key_pos, ends, scale
    )
    key_part = (
        jnp.einsum("hqk,qhd->khd", score_grad, query, preferred_element_type=jnp.float32) * scale
    )
    value_part = jnp.einsum(
        "hqk,qhd->khd", probs, grads.astype(jnp.float32), preferred_element_type=jnp.float32
    )
    return (key_part, value_part)


def scan_keys(carry, keys, values, update):
    count = keys.shape[0]
    width = keys.shape[1]
    head_size = width // HEADS
    step = math.gcd(count, 1024)
    firsts = step * jnp.arange(count // step, dtype=jnp.int32)

    def inner_product(state, item):
        key_block, value_block, first = item
        key_pos = first + jnp.arange(step, dtype=jnp.int32)
        return (update(state, key_block, value_block, key_pos), None)

    items = (
        keys.reshape(count // step, step, HEADS, head_size),
        values.reshape(count // step, step, HEADS, head_size),
        firsts,
    )
    return lax.scan(inner_product, carry, items)[0]


def feed_forward(residual_stream, gain_vector, w_up, w_down):
    centered_normalized, inverse_deviation = norm_pieces(residual_stream)
    normed_rows = (centered_normalized * gain_vector).astype(jnp.bfloat16)
    raised_rows = jnp.dot(normed_rows, w_up, preferred_element_type=jnp.float32)
    active_tokens = jax.nn.gelu(raised_rows).astype(jnp.bfloat16)
    result_value = residual_stream + jnp.dot(
        active_tokens, w_down, preferred_element_type=jnp.float32
    )
    return (
        result_value,
        (centered_normalized, inverse_deviation, normed_rows, raised_rows, active_tokens),
    )


def feed_back(incoming_gradient, saved_residuals, gain_vector, w_up, w_down):
    centered_normalized, inverse_deviation, normed_rows, raised_rows, active_tokens = (
        saved_residuals
    )
    grad_low = incoming_gradient.astype(jnp.bfloat16)
    down_part = jnp.einsum("tf,td->fd", active_tokens, grad_low, preferred_element_type=jnp.float32)
    active_grad = jnp.einsum("td,fd->tf", grad_low, w_down, preferred_element_type=jnp.float32)
    slope = jax.vjp(jax.nn.gelu, raised_rows)[1](active_grad)[0].astype(jnp.bfloat16)
    up_part = jnp.einsum("td,tf->df", normed_rows, slope, preferred_element_type=jnp.float32)
    normed_gradient = jnp.einsum("tf,df->td", slope, w_up, preferred_element_type=jnp.float32)
    input_gradient, gain_share = norm_backward(
        normed_gradient, centered_normalized, inverse_deviation, gain_vector
    )
    return (incoming_gradient + input_gradient, gain_share, up_part, down_part)


def shards(
    tokens,
    doc_lengths,
    mixer_norm_gain,
    mixer_in,
    shift_taps,
    mode_coef,
    mode_rate,
    skip_gain,
    mixer_out,
    gain_second,
    up_first,
    down_first,
    attention_norm_gain,
    project_in,
    project_out,
    gain_fourth,
    up_second,
    down_second,
    cotangent,
):
    rows = tokens.shape[1]
    width = tokens.shape[2]
    blocks = lax.axis_size("seq")
    rank = lax.axis_index("seq")
    total = rows * blocks
    head_size = width // HEADS
    scale = head_size ** (-0.5)
    lags = shift_taps.shape[0]
    channels = width // blocks
    ends = jnp.cumsum(doc_lengths[0])
    here = rank * rows + jnp.arange(rows, dtype=jnp.int32)
    residual_stream = tokens[0].astype(jnp.float32)
    mixer_centered_normalized, mixer_inverse_deviation = norm_pieces(residual_stream)
    mixer_normed_rows = (mixer_centered_normalized * mixer_norm_gain).astype(jnp.bfloat16)
    mixed_a = jnp.dot(mixer_normed_rows, mixer_in, preferred_element_type=jnp.float32)
    query_a = mixed_a[:, :width]
    key_a = mixed_a[:, width : 2 * width]
    value_a = mixed_a[:, 2 * width :]
    rim = shifted_2(key_a[rows - (lags - 1) :].astype(jnp.bfloat16), "seq", 1).astype(jnp.float32)
    key_ext = jnp.concatenate([rim, key_a], axis=0)
    shifted = jnp.zeros_like(key_a)
    for lag in range(lags):
        shifted = shifted + shift_taps[lag] * key_ext[lags - 1 - lag : lags - 1 - lag + rows]
    product_kv = shifted * value_a
    channel_in = lax.all_to_all(
        product_kv.T.reshape(blocks, channels, rows).astype(jnp.bfloat16),
        "seq",
        split_axis=0,
        concat_axis=2,
        tiled=True,
    ).astype(jnp.float32)[0]
    times = jnp.arange(total, dtype=jnp.int32).astype(jnp.float32)
    coef_here = lax.dynamic_slice_in_dim(mode_coef, rank * channels, channels, 1)
    rate_here = lax.dynamic_slice_in_dim(mode_rate, rank * channels, channels, 1)
    kernel_here = kernel_rows(coef_here, rate_here, times)
    tables = dft_tables(blocks, rows)
    sig_re, sig_im = forward_spectrum(channel_in, tables, blocks, rows)
    ker_re, ker_im = forward_spectrum(kernel_here, tables, blocks, rows)
    conv_chan = inverse_signal(
        sig_re * ker_re - sig_im * ker_im, sig_re * ker_im + sig_im * ker_re, tables, blocks, rows
    )
    conv_home = lax.all_to_all(
        conv_chan.reshape(1, channels, total).astype(jnp.bfloat16),
        "seq",
        split_axis=2,
        concat_axis=0,
        tiled=True,
    ).astype(jnp.float32)
    response = conv_home.reshape(width, rows).T + skip_gain * product_kv
    gated = (query_a * response).astype(jnp.bfloat16)
    stream_b = residual_stream + jnp.dot(gated, mixer_out, preferred_element_type=jnp.float32)
    attention_residual_stream, saved_b = feed_forward(stream_b, gain_second, up_first, down_first)
    attention_centered_normalized, attention_inverse_deviation = norm_pieces(
        attention_residual_stream
    )
    attention_normed_rows = (attention_centered_normalized * attention_norm_gain).astype(
        jnp.bfloat16
    )
    mixed_c = jnp.dot(attention_normed_rows, project_in, preferred_element_type=jnp.float32).astype(
        jnp.bfloat16
    )
    query_flat = mixed_c[:, :width]
    key_flat = mixed_c[:, width : 2 * width]
    value_flat = mixed_c[:, 2 * width :]
    query_c = query_flat.reshape(rows, HEADS, head_size)
    key_heads = key_flat.reshape(rows, HEADS, head_size)
    value_heads = value_flat.reshape(rows, HEADS, head_size)

    def forward_update(state, key_block, value_block, key_pos):
        return attend_block(state, query_c, here, key_block, value_block, key_pos, ends, scale)

    begin = (
        jnp.full((HEADS, rows), NEGATIVE, jnp.float32),
        jnp.zeros((HEADS, rows), jnp.float32),
        jnp.zeros((HEADS, rows, head_size), jnp.float32),
    )
    piece = (
        lax.all_gather(key_flat, "seq", axis=0, tiled=True),
        lax.all_gather(value_flat, "seq", axis=0, tiled=True),
    )
    top, mass, accum = scan_keys(begin, piece[0], piece[1], forward_update)
    lse = top + jnp.log(mass)
    att_full = accum / mass[:, :, None]
    attended = att_full.transpose(1, 0, 2).reshape(rows, width).astype(jnp.bfloat16)
    stream_d = attention_residual_stream + jnp.dot(
        attended, project_out, preferred_element_type=jnp.float32
    )
    result_value, saved_d = feed_forward(stream_d, gain_fourth, up_second, down_second)
    block_out = result_value.astype(jnp.bfloat16)[None]
    incoming_gradient = cotangent[0].astype(jnp.float32)
    incoming_gradient, gain_four_part, up_two_part, down_two_part = feed_back(
        incoming_gradient, saved_d, gain_fourth, up_second, down_second
    )
    grad_low = incoming_gradient.astype(jnp.bfloat16)
    out_part_c = jnp.einsum("td,te->de", attended, grad_low, preferred_element_type=jnp.float32)
    att_grad = jnp.einsum(
        "te,de->td", grad_low, project_out, preferred_element_type=jnp.float32
    ).astype(jnp.bfloat16)
    grad_heads = att_grad.reshape(rows, HEADS, head_size)
    delta = jnp.sum(grad_heads.astype(jnp.float32).transpose(1, 0, 2) * att_full, axis=-1)
    zero_heads = jnp.zeros((rows, HEADS, head_size), jnp.float32)

    def query_update(summed, key_block, value_block, key_pos):
        return summed + query_back(
            query_c, grad_heads, lse, delta, here, key_block, value_block, key_pos, ends, scale
        )

    piece = (
        lax.all_gather(key_flat, "seq", axis=0, tiled=True),
        lax.all_gather(value_flat, "seq", axis=0, tiled=True),
    )
    query_grad = scan_keys(zero_heads, piece[0], piece[1], query_update)
    lse_all, delta_all = (
        lax.all_gather(lse, "seq", axis=1, tiled=True),
        lax.all_gather(delta, "seq", axis=1, tiled=True),
    )
    queries = lax.all_gather(query_flat, "seq", axis=0, tiled=True)
    grads = lax.all_gather(att_grad, "seq", axis=0, tiled=True)
    count = queries.shape[0]
    step = math.gcd(count, 1024)
    firsts = step * jnp.arange(count // step, dtype=jnp.int32)

    def inner_product(summed, item):
        query_block, grad_block, first = item
        query_pos = first + jnp.arange(step, dtype=jnp.int32)
        lse_rows = lax.dynamic_slice_in_dim(lse_all, first, step, 1)
        delta_rows = lax.dynamic_slice_in_dim(delta_all, first, step, 1)
        parts = key_back(
            query_block,
            grad_block,
            lse_rows,
            delta_rows,
            query_pos,
            key_heads,
            value_heads,
            here,
            ends,
            scale,
        )
        return ((summed[0] + parts[0], summed[1] + parts[1]), None)

    items = (
        queries.reshape(count // step, step, HEADS, head_size),
        grads.reshape(count // step, step, HEADS, head_size),
        firsts,
    )
    key_grad, value_grad = lax.scan(inner_product, (zero_heads, zero_heads), items)[0]
    key_grad = key_grad.reshape(rows, width)
    value_grad = value_grad.reshape(rows, width)
    mixed_grad_c = jnp.concatenate(
        [query_grad.reshape(rows, width), key_grad, value_grad], axis=1
    ).astype(jnp.bfloat16)
    in_part_c = jnp.einsum(
        "td,te->de", attention_normed_rows, mixed_grad_c, preferred_element_type=jnp.float32
    )
    attention_normed_gradient = jnp.einsum(
        "te,de->td", mixed_grad_c, project_in, preferred_element_type=jnp.float32
    )
    attention_norm_gradient, attention_gain_share = norm_backward(
        attention_normed_gradient,
        attention_centered_normalized,
        attention_inverse_deviation,
        attention_norm_gain,
    )
    incoming_gradient = incoming_gradient + attention_norm_gradient
    incoming_gradient, gain_two_part, up_one_part, down_one_part = feed_back(
        incoming_gradient, saved_b, gain_second, up_first, down_first
    )
    grad_low = incoming_gradient.astype(jnp.bfloat16)
    out_part_a = jnp.einsum("td,te->de", gated, grad_low, preferred_element_type=jnp.float32)
    gated_grad = jnp.einsum("te,de->td", grad_low, mixer_out, preferred_element_type=jnp.float32)
    query_grad_a = gated_grad * response
    response_grad = gated_grad * query_a
    skip_part = jnp.sum(response_grad * product_kv, axis=0)
    chan_grad = lax.all_to_all(
        response_grad.T.reshape(blocks, channels, rows).astype(jnp.bfloat16),
        "seq",
        split_axis=0,
        concat_axis=2,
        tiled=True,
    ).astype(jnp.float32)[0]
    grad_re, grad_im = forward_spectrum(chan_grad, tables, blocks, rows)
    signal_grad = inverse_signal(
        ker_re * grad_re + ker_im * grad_im,
        ker_re * grad_im - ker_im * grad_re,
        tables,
        blocks,
        rows,
    )
    kernel_grad = inverse_signal(
        sig_re * grad_re + sig_im * grad_im,
        sig_re * grad_im - sig_im * grad_re,
        tables,
        blocks,
        rows,
    )
    coef_part, rate_part = kernel_grads(coef_here, rate_here, times, kernel_grad)
    returned = lax.all_to_all(
        signal_grad.reshape(1, channels, total).astype(jnp.bfloat16),
        "seq",
        split_axis=2,
        concat_axis=0,
        tiled=True,
    ).astype(jnp.float32)
    kv_grad = returned.reshape(width, rows).T + skip_gain * response_grad
    shifted_grad = kv_grad * value_a
    value_grad_a = kv_grad * shifted
    later = shifted_2(shortened(shifted_grad[: lags - 1]), "seq", -1)
    grad_ext = jnp.concatenate([shifted_grad, later], axis=0)
    key_grad_a = jnp.zeros_like(key_a)
    tap_rows = []
    for lag in range(lags):
        key_grad_a = key_grad_a + shift_taps[lag] * grad_ext[lag : lag + rows]
        tap_rows.append(
            jnp.sum(shifted_grad * key_ext[lags - 1 - lag : lags - 1 - lag + rows], axis=0)
        )
    taps_part = jnp.stack(tap_rows)
    mixed_grad_a = jnp.concatenate([query_grad_a, key_grad_a, value_grad_a], axis=1).astype(
        jnp.bfloat16
    )
    in_part_a = jnp.einsum(
        "td,te->de", mixer_normed_rows, mixed_grad_a, preferred_element_type=jnp.float32
    )
    mixer_normed_gradient = jnp.einsum(
        "te,de->td", mixed_grad_a, mixer_in, preferred_element_type=jnp.float32
    )
    mixer_norm_gradient, mixer_gain_share = norm_backward(
        mixer_normed_gradient, mixer_centered_normalized, mixer_inverse_deviation, mixer_norm_gain
    )
    token_grad = (incoming_gradient + mixer_norm_gradient)[None]
    parts = (
        lax.psum_scatter(mixer_gain_share, "seq", scatter_dimension=0, tiled=True),
        lax.psum_scatter(in_part_a, "seq", scatter_dimension=0, tiled=True),
        lax.psum_scatter(taps_part, "seq", scatter_dimension=1, tiled=True),
        lax.psum_scatter(skip_part, "seq", scatter_dimension=0, tiled=True),
        lax.psum_scatter(out_part_a, "seq", scatter_dimension=0, tiled=True),
        lax.psum_scatter(gain_two_part, "seq", scatter_dimension=0, tiled=True),
        lax.psum_scatter(up_one_part, "seq", scatter_dimension=0, tiled=True),
        lax.psum_scatter(down_one_part, "seq", scatter_dimension=0, tiled=True),
        lax.psum_scatter(attention_gain_share, "seq", scatter_dimension=0, tiled=True),
        lax.psum_scatter(in_part_c, "seq", scatter_dimension=0, tiled=True),
        lax.psum_scatter(out_part_c, "seq", scatter_dimension=0, tiled=True),
        lax.psum_scatter(gain_four_part, "seq", scatter_dimension=0, tiled=True),
        lax.psum_scatter(up_two_part, "seq", scatter_dimension=0, tiled=True),
        lax.psum_scatter(down_two_part, "seq", scatter_dimension=0, tiled=True),
    )
    matrices = (
        lax.psum_scatter(
            parts[1].astype(jnp.bfloat16), "batch", scatter_dimension=1, tiled=True
        ).astype(jnp.float32),
        lax.psum_scatter(
            parts[2].astype(jnp.bfloat16), "batch", scatter_dimension=0, tiled=True
        ).astype(jnp.float32),
        lax.psum_scatter(
            parts[4].astype(jnp.bfloat16), "batch", scatter_dimension=1, tiled=True
        ).astype(jnp.float32),
        lax.psum_scatter(
            parts[6].astype(jnp.bfloat16), "batch", scatter_dimension=1, tiled=True
        ).astype(jnp.float32),
        lax.psum_scatter(
            parts[7].astype(jnp.bfloat16), "batch", scatter_dimension=1, tiled=True
        ).astype(jnp.float32),
        lax.psum_scatter(
            parts[9].astype(jnp.bfloat16), "batch", scatter_dimension=1, tiled=True
        ).astype(jnp.float32),
        lax.psum_scatter(
            parts[10].astype(jnp.bfloat16), "batch", scatter_dimension=1, tiled=True
        ).astype(jnp.float32),
        lax.psum_scatter(
            parts[12].astype(jnp.bfloat16), "batch", scatter_dimension=1, tiled=True
        ).astype(jnp.float32),
        lax.psum_scatter(
            parts[13].astype(jnp.bfloat16), "batch", scatter_dimension=1, tiled=True
        ).astype(jnp.float32),
    )
    smalls = lax.psum(
        (parts[0], coef_part, rate_part, parts[3], parts[5], parts[8], parts[11]), "batch"
    )
    return (
        block_out,
        token_grad,
        smalls[0],
        matrices[0],
        matrices[1],
        smalls[1],
        smalls[2],
        smalls[3],
        matrices[2],
        smalls[4],
        matrices[3],
        matrices[4],
        smalls[5],
        matrices[5],
        matrices[6],
        smalls[6],
        matrices[7],
        matrices[8],
    )


MESH = pl.DeviceIdType.MESH
BF = jnp.bfloat16
F32 = jnp.float32
ROWS, WIDE, RANKS = (128, 768, 8)
SPAN = ROWS * RANKS
BLOCK = 128
OWNERS = 6
NT = (((1,), (1,)), ((), ()))
TN = (((0,), (0,)), ((), ()))
ROOT = math.sqrt(2.0 / math.pi)
CUBIC = 0.044715


def flip(value):
    return 1 - value


def mm(left, right):
    return jnp.dot(left, right, preferred_element_type=F32)


def mm_nt(left, right):
    return lax.dot_general(left, right, NT, preferred_element_type=F32)


def mm_tn(left, right):
    return lax.dot_general(left, right, TN, preferred_element_type=F32)


def is_owner(rank):
    return jnp.logical_and(rank >= 1, rank <= OWNERS)


def rows_of(rank):
    return pl.ds(pl.multiple_of(ROWS * rank, ROWS), ROWS)


def lanes_of(block):
    return pl.ds(pl.multiple_of(BLOCK * block, BLOCK), BLOCK)


PARTNERS = ((1, 1, 1), (1, 1, 0), (1, 0, 1), (1, 0, 0), (0, 1, 1), (0, 1, 0), (0, 0, 1))


class Spread:
    def __init__(self, net, source, target, outward, only=None):
        self.net, self.source, self.target, self.outward = net, source, target, outward
        self.base = net.take(RANKS - 1)

    def copy(self, step, source, target, rank):
        at = self.base + step - 1
        return pltpu.make_async_remote_copy(
            src_ref=source,
            dst_ref=target,
            send_sem=self.net.send_sem.at[at],
            recv_sem=self.net.recv_sem.at[at],
            device_id=(rank, self.net.b),
            device_id_type=MESH,
        )

    def each_send(self, act, chosen=None):
        me = self.net.s
        for step in range(1, RANKS):
            rank = self.net.partner(step)
            go = is_owner(rank) if self.outward else is_owner(me)
            if chosen is not None:
                go = jnp.logical_and(go, chosen(rank))

            @pl.when(go)
            def _(step=step, rank=rank):
                if self.outward:
                    act(self.copy(step, self.source(rank - 1), self.target(me), rank))
                else:
                    act(self.copy(step, self.source(rank), self.target(me - 1), rank))

    def start(self, chosen=None):
        self.each_send(lambda copy: copy.start(), chosen)

    def own(self):
        me = self.net.s

        @pl.when(is_owner(me))
        def _():
            if self.outward:
                self.target(me)[...] = self.source(me - 1)[...]
            else:
                self.target(me - 1)[...] = self.source(me)[...]

    def wait_recv(self):
        me = self.net.s
        for step in range(1, RANKS):
            rank = self.net.partner(step)

            @pl.when(is_owner(me) if self.outward else is_owner(rank))
            def _(step=step, rank=rank):
                landed = self.target(rank if self.outward else rank - 1)
                self.copy(step, landed, landed, rank).wait_recv()

    def wait_send(self):
        self.each_send(lambda copy: copy.wait_send())


class Net:
    def __init__(self, send_sem, recv_sem):
        self.send_sem, self.recv_sem = send_sem, recv_sem
        self.s = lax.axis_index("seq")
        self.b = lax.axis_index("batch")
        self.y, self.c = self.b // 2, lax.rem(self.b, 2)
        z, self.x = self.s // 2, lax.rem(self.s, 2)
        self.high, self.low = z // 2, lax.rem(z, 2)
        self.sibling = (self.s, 2 * self.y + flip(self.c))
        self.by_y = (self.s, 2 * flip(self.y) + self.c)
        self.by_both = (self.s, 2 * flip(self.y) + flip(self.c))
        self.by_x = (2 * z + flip(self.x), self.b)
        self.by_low = (2 * (2 * self.high + flip(self.low)) + self.x, self.b)
        self.by_high = (2 * (2 * flip(self.high) + self.low) + self.x, self.b)
        self.used = 0
        self.waiting = []

    def partner(self, step):
        far, near, side = PARTNERS[step - 1]
        high = flip(self.high) if far else self.high
        low = flip(self.low) if near else self.low
        return 4 * high + 2 * low + (flip(self.x) if side else self.x)

    def take(self, count):
        at = self.used
        self.used += count
        return at

    def spread(self, source, target, outward):
        made = Spread(self, source, target, outward)
        self.waiting.append(made)
        return made

    def send(self, source, target, other):
        at = self.take(1)
        copy = pltpu.make_async_remote_copy(
            src_ref=source,
            dst_ref=target,
            send_sem=self.send_sem.at[at],
            recv_sem=self.recv_sem.at[at],
            device_id=other,
            device_id_type=MESH,
        )
        copy.start()
        self.waiting.append(copy)
        return copy

    def hello(self):
        barrier = pltpu.get_barrier_semaphore()
        for step in range(1, RANKS):
            pl.semaphore_signal(
                barrier, inc=1, device_id=(lax.rem(self.s + step, RANKS), self.b), device_id_type=MESH
            )
        for other in (self.sibling, self.by_y, self.by_both):
            pl.semaphore_signal(barrier, inc=1, device_id=other, device_id_type=MESH)

    def ready(self):
        pl.semaphore_wait(pltpu.get_barrier_semaphore(), RANKS + 2)

    def turn_of(self, step, y, c):
        return (2 * y + flip(c), 2 * flip(y) + c, 2 * flip(y) + flip(c), 2 * y + c)[step]

    def order(self):
        owners = (self.sibling, self.by_y, self.by_both, None)
        return [(self.turn_of(step, self.y, self.c), owners[step]) for step in range(4)]

    def drop(self, copy):
        self.waiting = [made for made in self.waiting if made is not copy]

    def finish(self):
        for made in self.waiting:
            made.wait_send()


class Beside:
    def __init__(self, net, source, target, steps):
        self.net, self.steps = net, steps
        self.at = net.take(1)
        other = jnp.clip(net.s + steps, 0, RANKS - 1)
        self.copy = pltpu.make_async_remote_copy(
            src_ref=source,
            dst_ref=target,
            send_sem=net.send_sem.at[self.at],
            recv_sem=net.recv_sem.at[self.at],
            device_id=(other, net.b),
            device_id_type=MESH,
        )
        last = RANKS - 1 if steps > 0 else 0
        first = 0 if steps > 0 else RANKS - 1
        self.sends = net.s != last
        self.takes = net.s != first
        net.waiting.append(self)

    def start(self):
        @pl.when(self.sends)
        def _():
            self.copy.start()

    def wait_recv(self):
        @pl.when(self.takes)
        def _():
            self.copy.wait_recv()

    def wait_send(self):
        @pl.when(self.sends)
        def _():
            self.copy.wait_send()


def pieces(value):
    cent = value - jnp.mean(value, axis=-1, keepdims=True)
    inverse = lax.rsqrt(jnp.mean(cent * cent, axis=-1, keepdims=True) + 1e-05)
    return cent * inverse, inverse


def pieces_back(incoming, normal, inverse, gain):
    share = jnp.sum(incoming * normal, axis=0, keepdims=True)
    scaled = incoming * gain
    first = jnp.mean(scaled, axis=-1, keepdims=True)
    second = jnp.mean(scaled * normal, axis=-1, keepdims=True)
    return inverse * (scaled - first - normal * second), share


def gelu_parts(u):
    square = u * u
    bend = jnp.tanh(ROOT * u * (1.0 + CUBIC * square))
    half = 0.5 * (1.0 + bend)
    value = u * half
    slope = half + 0.5 * u * (1.0 - bend * bend) * (ROOT * (1.0 + 3.0 * CUBIC * square))
    return value, slope


def split(value):
    high = value.astype(BF)
    return high, (value - high.astype(F32)).astype(BF)


def transform(r, signal, re_out, im_out):
    @pl.loop(0, 4)
    def _(at):
        rows = pl.ds(pl.multiple_of(256 * at, 256), 256)
        re_out[rows, :] = mm(r.cos_table[rows, :], signal)
        im_out[rows, :] = -mm(r.sin_table[rows, :], signal)


def transform_two(r, signal, re_out, im_out):
    high, low = split(signal)
    r.pack_re[:, 0:128] = high
    r.pack_re[:, 128:256] = low

    @pl.loop(0, 4)
    def _(at):
        rows = pl.ds(pl.multiple_of(256 * at, 256), 256)
        re, im = mm(r.cos_table[rows, :], r.pack_re[...]), mm(r.sin_table[rows, :], r.pack_re[...])
        re_out[rows, :] = re[:, 0:128] + re[:, 128:256]
        im_out[rows, :] = -(im[:, 0:128] + im[:, 128:256])


def inverse(r, re, im, out):
    re_high, re_low = split(re)
    im_high, im_low = split(im)
    r.pack_re[:, 0:128] = re_high
    r.pack_re[:, 128:256] = re_low
    r.pack_im[:, 0:128] = im_high
    r.pack_im[:, 128:256] = im_low

    @pl.loop(0, 4)
    def _(at):
        rows = pl.ds(pl.multiple_of(256 * at, 256), 256)
        both = mm(r.cos_table[rows, :], r.pack_re[...]) - mm(r.sin_table[rows, :], r.pack_im[...])
        out[rows, :] = ((both[:, 0:128] + both[:, 128:256]) * (1.0 / SPAN)).astype(out.dtype)


def modes(coef_ref, rate_ref, out_ref):
    blocks, width = out_ref.shape[0] // 8, out_ref.shape[1]
    row = lax.broadcasted_iota(jnp.int32, (8, width), 0).astype(F32)
    out_ref[...] = jnp.zeros_like(out_ref)

    @pl.loop(0, 8)
    def _(group):
        some = pl.ds(pl.multiple_of(8 * group, 8), 8)
        rate, coef = rate_ref[some, :], coef_ref[some, :]
        falls = [coef[n : n + 1] * jnp.exp(-rate[n : n + 1] * row) for n in range(8)]
        steps = [jnp.exp(-rate[n : n + 1] * jnp.maximum(row, 8.0)) for n in range(8)]

        def step(at, falls):
            rows = pl.ds(pl.multiple_of(8 * at, 8), 8)
            out_ref[rows, :] += sum(falls[1:], falls[0])
            return tuple(fall * factor for fall, factor in zip(falls, steps))

        lax.fori_loop(0, blocks, step, tuple(falls), unroll=4)


def modes_back(coef_ref, rate_ref, grad_ref, coef_out, rate_out):
    blocks, width = grad_ref.shape[0] // 8, grad_ref.shape[1]
    row = lax.broadcasted_iota(jnp.int32, (8, width), 0).astype(F32)

    @pl.loop(0, 8)
    def _(group):
        some = pl.ds(pl.multiple_of(8 * group, 8), 8)
        rate, coef = rate_ref[some, :], coef_ref[some, :]
        steps = [jnp.exp(-rate[n : n + 1] * jnp.maximum(row, 8.0)) for n in range(8)]
        zero = jnp.minimum(row, 0.0)

        def step(at, carry):
            totals, slopes = carry
            here = grad_ref[pl.ds(pl.multiple_of(8 * (blocks - 1 - at), 8), 8), :]
            slopes = tuple(slope * factor + total for slope, factor, total in zip(slopes, steps, totals))
            totals = tuple(total * factor + here for total, factor in zip(totals, steps))
            return totals, slopes

        totals, slopes = lax.fori_loop(0, blocks, step, ((zero,) * 8, (zero,) * 8), unroll=2)
        coef_rows, rate_rows = [], []
        for n in range(8):
            fall = jnp.exp(-rate[n : n + 1] * row)
            coef_rows.append(jnp.sum(fall * totals[n], axis=0, keepdims=True))
            late = jnp.sum(fall * (8.0 * steps[n] * slopes[n] + row * totals[n]), axis=0, keepdims=True)
            rate_rows.append(-coef[n : n + 1] * late)
        coef_out[some, :] = jnp.concatenate(coef_rows, axis=0)
        rate_out[some, :] = jnp.concatenate(rate_rows, axis=0)


def shift_forward(keys, taps, value, shifted):
    @pl.loop(0, OWNERS)
    def _(block):
        lanes = lanes_of(block)
        near = keys[:, lanes]
        total = jnp.zeros((ROWS, BLOCK), F32)
        for rest in range(8):
            turned = pltpu.roll(near, rest, 0) if rest else near
            for part in range(8):
                total = total + taps[8 * part + rest : 8 * part + rest + 1, lanes] * turned[64 - 8 * part : 192 - 8 * part]
        shifted[:, lanes] = total


def shift_back(grads, keys, taps, key_grad, taps_grad):
    @pl.loop(0, OWNERS)
    def _(block):
        lanes = lanes_of(block)
        ahead, near = grads[:, lanes], keys[:, lanes]
        here = ahead[0:ROWS]
        total = jnp.zeros((ROWS, BLOCK), F32)
        rows = {}
        for rest in range(8):
            later = pltpu.roll(ahead, 192 - rest, 0) if rest else ahead
            turned = pltpu.roll(near, rest, 0) if rest else near
            for part in range(8):
                lag = 8 * part + rest
                total = total + taps[lag : lag + 1, lanes] * later[8 * part : 8 * part + ROWS]
                taps_grad[lag : lag + 1, lanes] = jnp.sum(here * turned[64 - 8 * part : 192 - 8 * part], axis=0, keepdims=True)
        key_grad[:, lanes] = total


def head_lanes(shape, head):
    return lax.broadcasted_iota(jnp.int32, shape, 1) // 64 == head


def document_start(ends, first, count):
    at = first + lax.broadcasted_iota(jnp.int32, (count, 1), 0)
    begin = jnp.zeros((count, 1), jnp.int32)
    for index in range(3):
        begin = jnp.where(at >= ends[index], ends[index], begin)
    return at, begin


def allowed_pairs(ends, part):
    query_at, begin = document_start(ends, 256 * part, 256)
    key_at = lax.broadcasted_iota(jnp.int32, (256, 256 * (part + 1)), 1)
    return jnp.logical_and(key_at <= query_at, key_at >= begin)


def attention_forward(r, part):
    rows, keys = slice(256 * part, 256 * part + 256), slice(0, 256 * part + 256)
    mask = allowed_pairs(r.ends, part)

    @pl.loop(0, 2)
    def _(head):
        lanes = head_lanes((256, BLOCK), head)
        query = jnp.where(lanes, r.qkv[0, rows, :].astype(F32) * 0.125, 0.0).astype(BF)
        scores = jnp.where(mask, mm_nt(query, r.qkv[1, keys, :]), NEGATIVE)
        top = jnp.max(scores, axis=1, keepdims=True)
        weights = jnp.exp(scores - top)
        mass = jnp.sum(weights, axis=1, keepdims=True)
        mixed = mm(weights.astype(BF), r.qkv[2, keys, :]) / mass
        r.attended_full[rows, :] = jnp.where(lanes, mixed, r.attended_full[rows, :])
        r.lse[rows, :] = jnp.where(lanes, top + jnp.log(mass), r.lse[rows, :])

    r.attended_low[rows, :] = r.attended_full[rows, :].astype(BF)


def attention_back(r, part):
    rows, keys = slice(256 * part, 256 * part + 256), slice(0, 256 * part + 256)
    mask = allowed_pairs(r.ends, part)

    @pl.loop(0, 2)
    def _(head):
        lanes = head_lanes((256, BLOCK), head)
        query = jnp.where(lanes, r.qkv[0, rows, :].astype(F32) * 0.125, 0.0).astype(BF)
        whole = r.att_grad[rows, :].astype(F32)
        grads = jnp.where(lanes, whole, 0.0)
        delta = jnp.sum(grads * r.attended_full[rows, :], axis=1, keepdims=True)
        lse = jnp.sum(jnp.where(lanes, r.lse[rows, :], 0.0), axis=1, keepdims=True) * (1.0 / 64.0)
        grads = grads.astype(BF)
        scores = mm_nt(query, r.qkv[1, keys, :])
        probs = jnp.where(mask, jnp.exp(scores - lse), 0.0)
        score_grad = (probs * (mm_nt(grads, r.qkv[2, keys, :]) - delta)).astype(BF)
        query_grad = mm(score_grad, r.qkv[1, keys, :]) * 0.125
        r.query_grad[rows, :] = jnp.where(lanes, query_grad, r.query_grad[rows, :])
        r.key_grad[keys, :] += mm_tn(score_grad, query)
        r.value_grad[keys, :] += mm_tn(probs.astype(BF), grads)

    r.qkv_grad[0, rows, :] = r.query_grad[rows, :].astype(BF)
    r.qkv_grad[1, rows, :] = r.key_grad[rows, :].astype(BF)
    r.qkv_grad[2, rows, :] = r.value_grad[rows, :].astype(BF)


class Gather:
    def __init__(self, net, source, target):
        self.net, self.target = net, target
        here = target(net.y, net.c)
        self.first = net.send(source, here, net.sibling)
        self.across = net.send(source, here, net.by_y)

    def forward(self):
        self.across.wait_recv()
        landed = self.target(flip(self.net.y), self.net.c)
        self.second = self.net.send(landed, landed, self.net.sibling)

    def wait(self):
        self.first.wait_recv()
        self.second.wait_recv()

    def free(self):
        for copy in (self.first, self.across, self.second):
            copy.wait_send()
            self.net.drop(copy)


class Locals:
    def __init__(self, sems):
        self.sems, self.used, self.waiting = sems, 0, []

    def start(self, source, target):
        copy = pltpu.make_async_copy(source, target, self.sems.at[self.used])
        self.used += 1
        copy.start()
        return copy

    def put(self, source, target):
        self.waiting.append(self.start(source, target))

    def finish(self):
        for copy in self.waiting:
            copy.wait()


LAYER, PAIR = (0, 1)
QUARTERS = 2
LENGTH = (1152, 576)


class Sum:
    def __init__(self, r, net, name, kind):
        self.net, self.kind = net, kind
        for part in ("right", "grads", "near_a", "near_b", "next_a", "next_b", "own", "third"):
            setattr(self, part, getattr(r, name + "_" + part))
        if kind == LAYER:
            self.across = getattr(r, name + "_across")
        self.half = QUARTERS * LENGTH[kind] // 4
        self.shared = []

    def give(self, kept, step, columns, other):
        own = self.right.at[rows_of(self.net.b), :]
        if other is None:
            own[...] = columns
        else:
            kept[step] = columns
            self.shared.append(self.net.send(kept.at[step], own, other))

    def share_pairs(self, pairs):
        own = self.right.at[rows_of(self.net.b), :]
        for index, other in self.net.order():
            if other is None:
                own[...] = pairs[index]
            else:
                self.shared.append(self.net.send(pairs.at[index], own, other))

    def free(self, copies):
        for copy in copies:
            copy.wait_send()
            self.net.drop(copy)

    def free_rows(self):
        self.free(self.shared[:3])

    def free_columns(self):
        self.free(self.shared[-3:])

    def share_rows(self, turned):
        net = self.net
        own = pl.ds(pl.multiple_of(192 * net.b, 64), 192)
        self.across[:, lanes_of(net.b)] = turned[own, :]
        for index, other in self.net.order()[:3]:
            rows = pl.ds(pl.multiple_of(192 * index, 64), 192)
            self.shared.append(net.send(turned.at[rows, :], self.across.at[:, lanes_of(net.b)], other))

    def wait_shared(self):
        for copy in self.shared:
            copy.wait_recv()

    def place(self, product, tile):
        for block in range(8):
            at = pl.ds(pl.multiple_of(96 * tile, 16), 96)
            self.grads[block % 2, (block // 2) % 2, block // 4, at, :] = product[96 * block : 96 * block + 96].astype(BF)

    def product(self, left, second):
        self.wait_shared()
        if self.kind == LAYER:

            @pl.loop(0, 3)
            def _(chunk):
                lanes = pl.ds(pl.multiple_of(256 * chunk, 256), 256)
                product = mm(left[...], self.right[:, lanes])
                self.place(product[:, 0:128], 2 * chunk)
                self.place(product[:, 128:256], 2 * chunk + 1)

            @pl.loop(0, 8)
            def _(block):
                lanes = pl.ds(pl.multiple_of(384 * block, 384), 384)
                product = mm(self.across[...], second[:, lanes])
                for tile in range(3):
                    self.grads[
                        lax.rem(block, 2), lax.rem(block // 2, 2), block // 4, 576 + 192 * tile : 768 + 192 * tile, :
                    ] = product[:, 128 * tile : 128 * tile + 128].astype(BF)

        else:

            @pl.loop(0, 2)
            def _(chunk):
                lanes = pl.ds(pl.multiple_of(256 * chunk, 256), 256)
                product = mm(left[...], self.right[:, lanes])
                self.place(product[:, 0:128], 2 * chunk)
                self.place(product[:, 128:256], 2 * chunk + 1)

            right = self.right[:, 512:768]
            first = lax.broadcasted_iota(jnp.int32, right.shape, 1) < 64
            zero = jnp.zeros_like(right)
            product = mm(left[...], jnp.where(first, right, zero)) + mm(second[...], jnp.where(first, zero, right))
            self.place(product[:, 0:128], 4)
            self.place(product[:, 128:256], 5)

        net, half = self.net, self.half
        self.moving = [
            net.send(self.grads.at[flip(net.x), :, :, 0:half, :], self.near_a, net.by_x),
            net.send(self.grads.at[:, flip(net.low), :, half:, :], self.near_b, net.by_low),
        ]

    def arrive(self):
        for copy in self.moving:
            copy.wait_recv()

    def second(self):
        net, half, grads = self.net, self.half, self.grads
        self.arrive()

        @pl.loop(0, 4)
        def _(step):
            one, two = step // 2, lax.rem(step, 2)
            grads[net.x, one, two, 0:half, :] += self.near_a[one, two]
            grads[one, net.low, two, half:, :] += self.near_b[one, two]

        self.moving = [
            net.send(grads.at[net.x, flip(net.low), :, 0:half, :], self.next_a, net.by_low),
            net.send(grads.at[flip(net.x), net.low, :, half:, :], self.next_b, net.by_x),
        ]

    def last(self):
        net, half, grads = self.net, self.half, self.grads
        self.arrive()

        @pl.loop(0, 2)
        def _(step):
            grads[net.x, net.low, step, 0:half, :] += self.next_a[step]
            grads[net.x, net.low, step, half:, :] += self.next_b[step]

        self.moving = [net.send(grads.at[net.x, net.low, flip(net.high)], self.third, net.by_high)]

    def end(self, near):
        net = self.net
        near.put(self.grads.at[net.x, net.low, net.high], self.own)
        self.arrive()


def sum_scratch(name, kind):
    length = LENGTH[kind]
    half = QUARTERS * length // 4
    made = {
        name + "_right": ((512, WIDE), BF),
        name + "_grads": ((2, 2, 2, length, 128), BF),
        name + "_near_a": ((2, 2, half, 128), BF),
        name + "_near_b": ((2, 2, length - half, 128), BF),
        name + "_next_a": ((2, half, 128), BF),
        name + "_next_b": ((2, length - half, 128), BF),
    }
    if kind == LAYER:
        made[name + "_across"] = ((192, 512), BF)
    return made


def pair_columns(wide, narrow, out):
    first = lax.broadcasted_iota(jnp.int32, (ROWS, BLOCK), 1) < 64

    def tile(at):
        at = at % (3 * WIDE)
        return wide[at // WIDE, :, at % WIDE : at % WIDE + BLOCK].astype(F32)

    def turned(at):
        return jnp.where(first, pltpu.roll(tile(at - BLOCK), 64, 1), pltpu.roll(tile(at), 64, 1))

    def thin(at):
        return narrow[:, at : at + BLOCK].astype(F32)

    def thin_turned(at):
        upper = pltpu.roll(thin(at), 64, 1)
        return jnp.where(first, pltpu.roll(thin(at - BLOCK), 64, 1), upper) if at else upper

    for block in range(4):
        start = 576 * block
        if block % 2 == 0:
            for part in range(4):
                out[block, :, BLOCK * part : BLOCK * part + BLOCK] = tile(start + BLOCK * part).astype(BF)
            lower, upper, rest = tile(start + 512), thin_turned(192 * block), thin_turned(192 * block + BLOCK)
        else:
            for part in range(4):
                out[block, :, BLOCK * part : BLOCK * part + BLOCK] = turned(start + 64 + BLOCK * part).astype(BF)
            lower, upper, rest = turned(start + 576), thin(192 * block - 64), thin(192 * block + 64)
        out[block, :, 512:640] = jnp.where(first, lower, upper).astype(BF)
        out[block, :, 640:768] = rest.astype(BF)


def turn(blocks, out):
    for block in range(4):
        out[:, BLOCK * block : BLOCK * block + BLOCK] = blocks[BLOCK * block : BLOCK * block + BLOCK, :].T


TABLES = ("cos_table", "sin_table")
KEPT = (
    "value_next",
    "qkv",
    "lse",
    "attended_full",
    "bend_b",
    "stream_b",
    "response",
    "query_a",
    "shifted",
    "value_a",
    "key_ext",
    "kernel_re",
    "kernel_im",
    "signal_re",
    "signal_im",
)
LEFTS = ("normed_a", "gated", "normed_b", "active_b", "normed_c")


def kernel_a(r):
    net = Net(r.send_sem, r.recv_sem)
    near = Locals(r.local_sem)
    net.hello()
    wait = {}

    def fetch(*names):
        for name in names:
            wait[name] = near.start(getattr(r, name + "_hbm"), getattr(r, name))

    thirds = []
    for index in (2, 0, 1):
        lanes = slice(WIDE * index, WIDE * index + WIDE)
        thirds.append(near.start(r.mixer_in_hbm.at[:, lanes], r.mixer_in.at[:, lanes]))
    r.ends[0] = r.doc_lengths[0, 0]
    r.ends[1] = r.ends[0] + r.doc_lengths[0, 1]
    r.ends[2] = r.ends[1] + r.doc_lengths[0, 2]

    def keep(*names):
        for name in names:
            near.put(getattr(r, name), getattr(r, name + "_kept"))

    gathers = []

    def gather(name):
        all_of = getattr(r, name + "_all")
        mine = getattr(r, name)
        near.put(mine, all_of.at[rows_of(net.b), :])
        gathers.append(Gather(net, mine, lambda y, c: all_of.at[rows_of(2 * y + c), :]))

    me = net.s
    gain_a = r.mixer_norm_gain[...][None]
    net.ready()
    rim = Beside(net, r.tokens.at[0, 64:128, :], r.rim_in, 1)
    rim.start()

    @pl.when(me == 0)
    def _():
        r.rim_in[...] = jnp.zeros_like(r.rim_in)

    normal, _ = pieces(r.tokens[0].astype(F32))
    r.normed_a[...] = (normal * gain_a).astype(BF)
    gather("normed_a")
    thirds[0].wait()
    r.value_a[...] = mm(r.normed_a[...], r.mixer_in[:, 2 * WIDE :])
    r.value_low[...] = r.value_a[0:64, :].astype(BF)
    later = Beside(net, r.value_low, r.value_next, -1)
    later.start()

    @pl.when(me == RANKS - 1)
    def _():
        r.value_next[...] = jnp.zeros_like(r.value_next)

    thirds[1].wait()
    r.query_a[...] = mm(r.normed_a[...], r.mixer_in[:, 0:WIDE])
    keep("query_a", "value_a")
    thirds[2].wait()
    fetch("shift_taps", "mode_coef", "mode_rate", *TABLES, "phase_cos", "phase_sin", "mixer_out")
    fetch("up_first", "down_first", "project_in")
    r.key_ext[64:192, :] = mm(r.normed_a[...], r.mixer_in[:, WIDE : 2 * WIDE])
    rim.wait_recv()
    normal, _ = pieces(r.rim_in[...].astype(F32))
    r.key_ext[0:64, :] = mm((normal * gain_a).astype(BF), r.mixer_in[:, WIDE : 2 * WIDE])
    for name in ("shift_taps", "mode_coef", "mode_rate"):
        wait[name].wait()
    shift_forward(r.key_ext, r.shift_taps, None, r.shifted)
    r.product_low[...] = (r.shifted[...] * r.value_a[...]).astype(BF)
    go = net.spread(lambda block: r.product_low.at[:, lanes_of(block)], lambda rank: r.signal.at[rows_of(rank), :], True)
    go.start()
    go.own()
    keep("key_ext", "shifted")
    block = lanes_of(jnp.clip(me - 1, 0, OWNERS - 1))
    r.coef[...] = r.mode_coef[:, block]
    r.rate[...] = r.mode_rate[:, block]
    modes(r.coef, r.rate, r.mode_rows)
    for name in TABLES + ("phase_cos", "phase_sin"):
        wait[name].wait()
    transform_two(r, r.mode_rows[...], r.kernel_re, r.kernel_im)
    turned = r.kernel_re[...] * r.phase_cos[...] - r.kernel_im[...] * r.phase_sin[...]
    r.kernel_im[...] = r.kernel_im[...] * r.phase_cos[...] + r.kernel_re[...] * r.phase_sin[...]
    r.kernel_re[...] = turned
    keep("kernel_re", "kernel_im")
    go.wait_recv()
    transform(r, r.signal[...], r.signal_re, r.signal_im)
    inverse(
        r,
        r.signal_re[...] * r.kernel_re[...] - r.signal_im[...] * r.kernel_im[...],
        r.signal_re[...] * r.kernel_im[...] + r.signal_im[...] * r.kernel_re[...],
        r.conv,
    )
    back = net.spread(lambda rank: r.conv.at[rows_of(rank), :], lambda block: r.conv_home.at[:, lanes_of(block)], False)
    back.start()
    back.own()
    for name in ("mixer_out", "up_first", "down_first", "project_in"):
        wait[name].wait()
    back.wait_recv()
    r.response[...] = r.conv_home[...].astype(F32) + r.skip_gain[...][None] * (r.shifted[...] * r.value_a[...])
    r.gated[...] = (r.query_a[...] * r.response[...]).astype(BF)
    gather("gated")
    stream_b = r.tokens[0].astype(F32) + mm(r.gated[...], r.mixer_out[...])
    r.stream_b[...] = stream_b
    normal, _ = pieces(stream_b)
    r.normed_b[...] = (normal * r.gain_second[...][None]).astype(BF)
    gather("normed_b")
    r.stream_c[...] = stream_b
    for chunk in range(4):
        lanes = slice(WIDE * chunk, WIDE * chunk + WIDE)
        active, bend = gelu_parts(mm(r.normed_b[...], r.up_first[:, lanes]))
        r.bend_b[:, lanes] = bend.astype(BF)
        active = active.astype(BF)
        r.active_b[:, lanes] = active
        r.stream_c[...] += mm(active, r.down_first[lanes, :])
    normal, _ = pieces(r.stream_c[...])
    r.normed_c[...] = (normal * r.attention_norm_gain[...][None]).astype(BF)
    for index in range(3):
        r.mixed_c[index] = mm(r.normed_c[...], r.project_in[:, WIDE * index : WIDE * index + WIDE]).astype(BF)
    go = net.spread(lambda block: r.mixed_c.at[:, :, lanes_of(block)], lambda rank: r.qkv.at[:, rows_of(rank), :], True)
    go.start()
    go.own()
    keep("response", "stream_b", "bend_b")
    gather("active_b")
    gather("normed_c")
    for made in gathers[:3]:
        made.forward()
    turned = r.signal_re[...] * r.phase_cos[...] - r.signal_im[...] * r.phase_sin[...]
    r.signal_im[...] = -(r.signal_im[...] * r.phase_cos[...] + r.signal_re[...] * r.phase_sin[...])
    r.signal_re[...] = turned
    keep("signal_re", "signal_im")
    later.wait_recv()
    keep("value_next")
    go.wait_recv()
    keep("qkv")
    back = net.spread(lambda rank: r.attended_low.at[rows_of(rank), :], lambda block: r.attended.at[:, lanes_of(block)], False)
    for part in (3, 2, 1, 0):
        attention_forward(r, part)
        back.start(lambda rank, part=part: rank // 2 == part)
    back.own()
    keep("lse", "attended_full")
    for made in gathers[3:]:
        made.forward()
    back.wait_recv()
    for made in gathers:
        made.wait()
    net.finish()
    near.finish()


def kernel_b(r):
    net = Net(r.send_sem, r.recv_sem)
    near = Locals(r.local_sem)
    net.hello()
    wait = {}

    def fetch(name, into=None):
        wait[name] = near.start(getattr(r, name + "_hbm"), getattr(r, into or name))

    fetch("project_out", "out_weight")
    chunks = []
    for step, (index, other) in enumerate(net.order()):
        lanes = pl.ds(pl.multiple_of(WIDE * index, WIDE), WIDE)
        chunks.append(
            (
                near.start(r.up_second_hbm.at[:, lanes], r.up.at[:, lanes]),
                near.start(r.down_second_hbm.at[lanes, :], r.down.at[lanes, :]),
            )
        )
    r.ends[0] = r.doc_lengths[0, 0]
    r.ends[1] = r.ends[0] + r.doc_lengths[0, 1]
    r.ends[2] = r.ends[1] + r.doc_lengths[0, 2]
    sum_d, sum_c = Sum(r, net, "sum_d", LAYER), Sum(r, net, "sum_c", PAIR)
    sum_b, sum_a = Sum(r, net, "sum_b", LAYER), Sum(r, net, "sum_a", PAIR)
    own_rows = rows_of(net.b)

    gain_d = r.gain_fourth[...][None]
    wait["project_out"].wait()
    stream_d = r.stream_c[...] + mm(r.attended[...], r.out_weight[...])
    normal, inverse_d = pieces(stream_d)
    normed_d = (normal * gain_d).astype(BF)
    r.layer_left[own_rows, :] = normed_d
    r.total[...] = stream_d
    r.turned[...] = r.cotangent[0].T
    r.pair_two[own_rows, :] = r.attended[...]
    net.ready()
    gather_d = Gather(net, r.layer_left.at[own_rows, :], lambda y, c: r.layer_left.at[rows_of(2 * y + c), :])
    sum_d.share_rows(r.turned)
    gathers = []
    for step, (index, other) in enumerate(net.order()):
        lanes = pl.ds(pl.multiple_of(WIDE * index, WIDE), WIDE)
        for copy in chunks[step]:
            copy.wait()
        if step == 3:
            for name in KEPT[:11]:
                fetch(name)
            fetch("project_in", "in_weight")
            fetch("normed_c_all", "pair_one")
            for name in ("shift_taps", "mode_coef", "mode_rate") + TABLES:
                fetch(name)
        raised = mm(r.layer_left[own_rows, :], r.up[:, lanes])
        active, slope = gelu_parts(raised)
        active = active.astype(BF)
        r.layer_second[own_rows, lanes] = active

        def spot(y, c, step=step):
            at = pl.ds(pl.multiple_of(WIDE * net.turn_of(step, y, c), WIDE), WIDE)
            return r.layer_second.at[rows_of(2 * y + c), at]

        gathers.append(Gather(net, spot(net.y, net.c), spot))
        r.total[...] += mm(active, r.down[lanes, :])
        slope = (slope * mm_nt(r.cotangent[0], r.down[lanes, :])).astype(BF)
        sum_d.give(r.slopes, step, slope, other)
        back = mm_nt(slope, r.up[:, lanes])
        if step == 0:
            r.grad_d[...] = back
        else:
            r.grad_d[...] += back
    grad, gain_four = pieces_back(r.grad_d[...], normal, inverse_d, gain_d)
    grad = r.cotangent[0].astype(F32) + grad
    r.grad_d[...] = grad
    r.grad_d_low[...] = grad.astype(BF)
    r.att_grad_home[...] = mm_nt(r.grad_d_low[...], r.out_weight[...]).astype(BF)
    go = net.spread(lambda block: r.att_grad_home.at[:, lanes_of(block)], lambda rank: r.att_grad.at[rows_of(rank), :], True)
    go.start()
    go.own()
    gather_att = Gather(net, r.pair_two.at[own_rows, :], lambda y, c: r.pair_two.at[rows_of(2 * y + c), :])
    fetch("up_first", "up")
    fetch("down_first", "down")
    fetch("mixer_out", "out_weight")
    r.block_out[0] = r.total[...].astype(BF)

    r.key_grad[...] = jnp.zeros_like(r.key_grad)
    r.value_grad[...] = jnp.zeros_like(r.value_grad)
    for name in ("qkv", "lse", "attended_full"):
        wait[name].wait()
    go.wait_recv()
    back = net.spread(
        lambda rank: r.qkv_grad.at[:, rows_of(rank), :], lambda block: r.mixed_grad_c.at[:, :, lanes_of(block)], False
    )
    for part in (3, 2, 1, 0):
        attention_back(r, part)
        back.start(lambda rank, part=part: rank // 2 == part)
    back.own()
    for name, into in (
        ("kernel_re", "lse"),
        ("kernel_im", "attended_full"),
        ("signal_re", "query_grad"),
        ("signal_im", "key_grad"),
    ):
        fetch(name, into)
    for made in [gather_d] + gathers:
        made.forward()
    gather_d.wait()
    turn(r.layer_left, r.turned_one)
    for made in gathers:
        made.wait()
    sum_d.product(r.turned_one, r.layer_second)
    for made in [gather_d] + gathers:
        made.free()
    fetch("normed_b_all", "layer_left")
    fetch("active_b_all", "layer_second")

    normal, inverse_c = pieces(r.stream_c[...])
    wait["project_in"].wait()
    back.wait_recv()
    grad = mm_nt(r.mixed_grad_c[0], r.in_weight[:, 0:WIDE])
    for index in range(1, 3):
        grad = grad + mm_nt(r.mixed_grad_c[index], r.in_weight[:, WIDE * index : WIDE * index + WIDE])
    fetch("mixer_in", "in_weight")
    pair_columns(r.mixed_grad_c, r.grad_d_low, r.pairs)
    sum_c.share_pairs(r.pairs)
    grad, gain_three = pieces_back(grad, normal, inverse_c, r.attention_norm_gain[...][None])
    grad = grad + r.grad_d[...]
    r.total[...] = grad
    r.grad_c_low[...] = grad.astype(BF)
    sum_d.free_rows()
    r.turned[...] = r.grad_c_low[...].T
    sum_b.share_rows(r.turned)
    sum_d.free_columns()
    wait["up_first"].wait()
    wait["down_first"].wait()
    wait["bend_b"].wait()
    for step, (index, other) in enumerate(net.order()):
        lanes = pl.ds(pl.multiple_of(WIDE * index, WIDE), WIDE)
        slope = (r.bend_b[:, lanes].astype(F32) * mm_nt(r.grad_c_low[...], r.down[lanes, :])).astype(BF)
        sum_b.give(r.slopes, step, slope, other)
        part = mm_nt(slope, r.up[:, lanes])
        if step == 0:
            r.grad_b[...] = part
        else:
            r.grad_b[...] += part
    for name in ("stream_b", "response", "query_a", "shifted", "value_a", "key_ext", "mixer_out"):
        wait[name].wait()
    normal, inverse_b = pieces(r.stream_b[...])
    grad, gain_two = pieces_back(r.grad_b[...], normal, inverse_b, r.gain_second[...][None])
    grad = grad + r.total[...]
    r.grad_b[...] = grad
    r.grad_b_low[...] = grad.astype(BF)
    gated_grad = mm_nt(r.grad_b_low[...], r.out_weight[...])
    r.mixed_grad_a[0] = (gated_grad * r.response[...]).astype(BF)
    response_grad = gated_grad * r.query_a[...]
    r.response_grad[...] = response_grad
    r.response_grad_low[...] = response_grad.astype(BF)
    go = net.spread(
        lambda block: r.response_grad_low.at[:, lanes_of(block)], lambda rank: r.conv_grad.at[rows_of(rank), :], True
    )
    go.start()
    go.own()
    after = Beside(net, r.response_grad_low.at[0:64, :], r.response_next, -1)
    after.start()

    @pl.when(net.s == RANKS - 1)
    def _():
        r.response_next[...] = jnp.zeros_like(r.response_next)

    skip_part = jnp.sum(response_grad * (r.shifted[...] * r.value_a[...]), axis=0, keepdims=True)
    sum_d.second()
    gather_att.forward()
    wait["normed_c_all"].wait()
    turn(r.pair_one, r.turned_one)
    gather_att.wait()
    turn(r.pair_two, r.turned_two)
    gather_att.free()
    fetch("normed_a_all", "pair_one")
    fetch("gated_all", "pair_two")
    sum_c.product(r.turned_one, r.turned_two)
    wait["normed_b_all"].wait()
    turn(r.layer_left, r.turned_one)

    for name in TABLES + ("kernel_re", "kernel_im", "signal_re", "signal_im"):
        wait[name].wait()
    kernel_re, kernel_im, signal_re, signal_im = r.lse, r.attended_full, r.query_grad, r.key_grad
    go.wait_recv()
    r.signal_grad[SPAN:, :] = jnp.zeros((64, BLOCK), BF)
    transform(r, r.conv_grad[...], r.grad_re, r.grad_im)
    inverse(
        r,
        r.grad_re[...] * kernel_re[...] + r.grad_im[...] * kernel_im[...],
        r.grad_im[...] * kernel_re[...] - r.grad_re[...] * kernel_im[...],
        r.signal_grad,
    )
    back = net.spread(
        lambda rank: r.signal_grad.at[pl.ds(pl.multiple_of(ROWS * rank, ROWS), 192), :],
        lambda block: r.signal_grad_home.at[:, lanes_of(block)],
        False,
    )
    back.start()
    back.own()
    wait["active_b_all"].wait()
    sum_b.product(r.turned_one, r.layer_second)
    sum_d.last()
    sum_c.second()
    after.wait_recv()
    for name in ("shift_taps", "mode_coef", "mode_rate", "value_next"):
        wait[name].wait()
    back.wait_recv()

    skip = r.skip_gain[...][None]
    signal_grad = r.signal_grad_home[0:ROWS, :].astype(F32) + skip * r.response_grad[...]
    r.grad_ext[0:ROWS, :] = signal_grad * r.value_a[...]
    r.mixed_grad_a[2] = (signal_grad * r.shifted[...]).astype(BF)
    signal_grad = r.signal_grad_home[ROWS:192, :].astype(F32) + skip * r.response_next[...].astype(F32)
    r.grad_ext[ROWS:192, :] = signal_grad * r.value_next[...].astype(F32)
    shift_back(r.grad_ext, r.key_ext, r.shift_taps, r.total, r.taps)
    r.mixed_grad_a[1] = r.total[...].astype(BF)
    sum_c.free_columns()
    pair_columns(r.mixed_grad_a, r.grad_b_low, r.pairs)
    sum_a.share_pairs(r.pairs)
    wait["mixer_in"].wait()
    grad = mm_nt(r.mixed_grad_a[0], r.in_weight[:, 0:WIDE])
    for index in range(1, 3):
        grad = grad + mm_nt(r.mixed_grad_a[index], r.in_weight[:, WIDE * index : WIDE * index + WIDE])
    normal, inverse_a = pieces(r.tokens[0].astype(F32))
    grad, gain_one = pieces_back(grad, normal, inverse_a, r.mixer_norm_gain[...][None])
    r.token_grad[0] = r.grad_b[...] + grad

    gains = jnp.concatenate([gain_one, skip_part, gain_two, gain_three, gain_four, jnp.zeros((3, WIDE), F32)], axis=0)
    for block in range(4):
        r.small[block // 2, block % 2, 0:16, :] = r.taps[16 * block : 16 * block + 16, :]
        r.small[block // 2, block % 2, 16:24, :] = gains
    swap = net.send(r.small.at[:, flip(net.c)], r.small_c, net.sibling)
    re = r.grad_re[...] * signal_re[...] - r.grad_im[...] * signal_im[...]
    im = r.grad_re[...] * signal_im[...] + r.grad_im[...] * signal_re[...]
    inverse(r, re, im, r.value_grad)
    block = lanes_of(jnp.clip(net.s - 1, 0, OWNERS - 1))
    r.coef[...] = r.mode_coef[:, block]
    r.rate[...] = r.mode_rate[:, block]
    wait["normed_a_all"].wait()
    turn(r.pair_one, r.turned_one)
    wait["gated_all"].wait()
    turn(r.pair_two, r.turned_two)
    sum_b.second()
    swap.wait_recv()
    r.small[:, net.c] += r.small_c[...]
    swap = net.send(r.small.at[flip(net.y), net.c], r.small_swap.at[0], net.by_y)
    sum_c.last()
    sum_a.product(r.turned_one, r.turned_two)
    modes_back(r.coef, r.rate, r.value_grad, r.mode_part.at[0, 0:64], r.mode_part.at[0, 64:128])
    mode = net.send(r.mode_part.at[0], r.mode_swap.at[0], net.sibling)
    swap.wait_recv()
    r.small_sum[0] = r.small[net.y, net.c] + r.small_swap[0]
    swap = net.send(r.small_sum.at[0], r.small_swap.at[1], net.by_x)
    sum_b.last()
    mode.wait_recv()
    r.mode_part[1] = r.mode_part[0] + r.mode_swap[0]
    mode = net.send(r.mode_part.at[1], r.mode_swap.at[1], net.by_y)
    sum_a.second()
    mode.wait_recv()
    r.mode_part[2] = r.mode_part[1] + r.mode_swap[1]
    back = net.spread(lambda rank: r.mode_part.at[2], lambda block: r.mode_home.at[:, lanes_of(block)], False)
    back.start()
    back.own()
    swap.wait_recv()
    r.small_sum[1] = r.small_sum[0] + r.small_swap[1]
    swap = net.send(r.small_sum.at[1], r.small_swap.at[2], net.by_low)
    sum_a.last()
    swap.wait_recv()
    r.small_sum[2] = r.small_sum[1] + r.small_swap[2]
    swap = net.send(r.small_sum.at[2], r.small_swap.at[3], net.by_high)
    sum_d.end(near)
    sum_c.end(near)
    turn_back = lax.rem(WIDE - 96 * net.s, WIDE)
    back.wait_recv()
    r.mode_out[...] = pltpu.roll(r.mode_home[...], turn_back, 1)[:, 0:128]
    swap.wait_recv()
    r.small_out[...] = pltpu.roll(r.small_sum[2] + r.small_swap[3], turn_back, 1)[:, 0:128]
    sum_b.end(near)
    sum_a.end(near)
    net.finish()
    near.finish()


def kernel_z(*refs):
    block_in, token_in, mode, small = refs[:4]
    sums = refs[4:12]
    (
        block_out,
        token_grad,
        gain_one,
        mixer_in,
        taps,
        coef,
        rate,
        skip,
        mixer_out,
        gain_two,
        up_first,
        down_first,
        gain_three,
        project_in,
        project_out,
        gain_four,
        up_second,
        down_second,
    ) = refs[12:]
    block_out[...] = block_in[...]
    token_grad[...] = token_in[...]
    taps[...] = small[0:16, 0:96]
    for at, out in enumerate((gain_one, skip, gain_two, gain_three, gain_four)):
        out[...] = small[16 + at, 0:96]
    coef[...] = mode[0:64, 0:96]
    rate[...] = mode[64:128, 0:96]

    def block(index, first, count):
        rows = slice(first, first + count)
        return sums[2 * index][rows, :].astype(F32) + sums[2 * index + 1][rows, :].astype(F32)

    for index, up, down in ((0, up_second, down_second), (2, up_first, down_first)):
        for tile in range(6):
            up[:, 128 * tile : 128 * tile + 128] = block(index, 96 * tile, 96)
        for tile in range(3):
            down[:, 128 * tile : 128 * tile + 128] = block(index, 576 + 192 * tile, 192)
    for index, wide, narrow in ((1, project_in, project_out), (3, mixer_in, mixer_out)):
        for tile in range(4):
            wide[:, 128 * tile : 128 * tile + 128] = block(index, 96 * tile, 96)
        mixed = block(index, 384, 96)
        wide[:, 512:576] = mixed[:, 0:64]
        narrow[:, 0:64] = mixed[:, 64:128]
        narrow[:, 64:192] = block(index, 480, 96)


class Refs:
    pass


def call(body, identity, inputs, hbm, smem, outs, hbm_outs, scratch, semaphores):
    names = list(inputs) + [name + "_hbm" for name in hbm] + list(smem) + list(outs) + list(hbm_outs) + list(scratch)
    names += ["ends", "send_sem", "recv_sem", "local_sem"]

    def run(*refs):
        r = Refs()
        for name, ref in zip(names, refs):
            setattr(r, name, ref)
        body(r)

    vmem = pl.BlockSpec(memory_space=pltpu.VMEM)
    results = pl.pallas_call(
        run,
        out_shape=[jax.ShapeDtypeStruct(shape, kind) for shape, kind in (*outs.values(), *hbm_outs.values())],
        in_specs=[vmem] * len(inputs)
        + [pl.BlockSpec(memory_space=pl.ANY)] * len(hbm)
        + [pl.BlockSpec(memory_space=pltpu.SMEM)] * len(smem),
        out_specs=[vmem] * len(outs) + [pl.BlockSpec(memory_space=pl.ANY)] * len(hbm_outs),
        scratch_shapes=[pltpu.VMEM(shape, kind) for shape, kind in scratch.values()]
        + [pltpu.SMEM((3,), jnp.int32)]
        + [pltpu.SemaphoreType.DMA((semaphores[0],)), pltpu.SemaphoreType.DMA((semaphores[0],))]
        + [pltpu.SemaphoreType.DMA((semaphores[1],))],
        compiler_params=pltpu.CompilerParams(
            collective_id=identity, has_side_effects=True, vmem_limit_bytes=VMEM_BYTES
        ),
    )(*inputs.values(), *hbm.values(), *smem.values())
    return dict(zip((*outs, *hbm_outs), results))


VMEM_BYTES = 66_900_000


def odd_tables():
    odd = 2 * np.arange(SPAN, dtype=np.int64) + 1
    angle = (np.outer(odd, odd) % (8 * SPAN)) * (math.pi / (4 * SPAN))
    phase = (odd * (math.pi / (4 * SPAN)))[:, None] * np.ones((1, BLOCK))
    tables = {
        "cos_table": jnp.asarray(np.cos(angle).astype(ml_dtypes.bfloat16)),
        "sin_table": jnp.asarray(np.sin(angle).astype(ml_dtypes.bfloat16)),
    }
    return tables, jnp.asarray(np.cos(phase), F32), jnp.asarray(np.sin(phase), F32)


def shards_fast(
    tokens,
    doc_lengths,
    mixer_norm_gain,
    mixer_in,
    shift_taps,
    mode_coef,
    mode_rate,
    skip_gain,
    mixer_out,
    gain_second,
    up_first,
    down_first,
    attention_norm_gain,
    project_in,
    project_out,
    gain_fourth,
    up_second,
    down_second,
    cotangent,
):
    tables, phase_cos, phase_sin = odd_tables()
    home, thrice, tall = (ROWS, WIDE), (3, ROWS, WIDE), (ROWS, 4 * WIDE)
    span = (SPAN, BLOCK)
    kept = dict(
        value_next=((64, WIDE), BF),
        query_a=(home, F32),
        value_a=(home, F32),
        key_ext=((192, WIDE), F32),
        shifted=(home, F32),
        response=(home, F32),
        stream_b=(home, F32),
        bend_b=(tall, BF),
        qkv=((3, *span), BF),
        lse=(span, F32),
        attended_full=(span, F32),
        kernel_re=(span, F32),
        kernel_im=(span, F32),
        signal_re=(span, F32),
        signal_im=(span, F32),
    )
    lefts = dict(normed_a=(home, BF), gated=(home, BF), normed_b=(home, BF), active_b=(tall, BF), normed_c=(home, BF))
    modes_scratch = dict(
        coef=((64, BLOCK), F32),
        rate=((64, BLOCK), F32),
        shift_taps=((64, WIDE), F32),
        mode_coef=((64, WIDE), F32),
        mode_rate=((64, WIDE), F32),
    )
    packs = dict(pack_re=((SPAN, 256), BF), pack_im=((SPAN, 256), BF))
    table_scratch = dict(cos_table=((SPAN, SPAN), BF), sin_table=((SPAN, SPAN), BF))
    a = call(
        kernel_a,
        0,
        dict(
            tokens=tokens,
            mixer_norm_gain=mixer_norm_gain,
            skip_gain=skip_gain,
            gain_second=gain_second,
            attention_norm_gain=attention_norm_gain,
        ),
        dict(
            mixer_in=mixer_in,
            shift_taps=shift_taps,
            mode_coef=mode_coef,
            mode_rate=mode_rate,
            **tables,
            phase_cos=phase_cos,
            phase_sin=phase_sin,
            mixer_out=mixer_out,
            up_first=up_first,
            down_first=down_first,
            project_in=project_in,
        ),
        dict(doc_lengths=doc_lengths),
        dict(stream_c=(home, F32), attended=(home, BF)),
        dict(
            **{name + "_kept": made for name, made in kept.items()},
            **{name + "_all": ((4 * shape[0], shape[1]), kind) for name, (shape, kind) in lefts.items()},
        ),
        dict(
            **kept,
            **lefts,
            **modes_scratch,
            **packs,
            rim_in=((64, WIDE), BF),
            **table_scratch,
            phase_cos=(span, F32),
            phase_sin=(span, F32),
            value_low=((64, WIDE), BF),
            product_low=(home, BF),
            signal=(span, BF),
            mode_rows=(span, F32),
            conv=(span, BF),
            conv_home=(home, BF),
            mixed_c=(thrice, BF),
            attended_low=(span, BF),
            mixer_in=((WIDE, 3 * WIDE), BF),
            mixer_out=((WIDE, WIDE), BF),
            up_first=((WIDE, 4 * WIDE), BF),
            down_first=((4 * WIDE, WIDE), BF),
            project_in=((WIDE, 3 * WIDE), BF),
        ),
        (48, 40),
    )
    kinds = dict(sum_d=LAYER, sum_c=PAIR, sum_b=LAYER, sum_a=PAIR)
    sum_outs, sums = {}, {}
    for name, kind in kinds.items():
        sum_outs[name + "_own"] = ((LENGTH[kind], 128), BF)
        sum_outs[name + "_third"] = ((LENGTH[kind], 128), BF)
        sums.update(sum_scratch(name, kind))
    b = call(
        kernel_b,
        1,
        dict(
            tokens=tokens,
            cotangent=cotangent,
            stream_c=a["stream_c"],
            attended=a["attended"],
            mixer_norm_gain=mixer_norm_gain,
            skip_gain=skip_gain,
            gain_second=gain_second,
            attention_norm_gain=attention_norm_gain,
            gain_fourth=gain_fourth,
        ),
        dict(
            project_out=project_out,
            up_second=up_second,
            down_second=down_second,
            **{name: a[name + "_kept"] for name in kept},
            **{name + "_all": a[name + "_all"] for name in lefts},
            **tables,
            shift_taps=shift_taps,
            mode_coef=mode_coef,
            mode_rate=mode_rate,
            project_in=project_in,
            up_first=up_first,
            down_first=down_first,
            mixer_out=mixer_out,
            mixer_in=mixer_in,
        ),
        dict(doc_lengths=doc_lengths),
        dict(
            block_out=((1, *home), BF),
            token_grad=((1, *home), F32),
            mode_out=((128, 128), F32),
            small_out=((24, 128), F32),
        ),
        sum_outs,
        dict(
            **{name: made for name, made in kept.items() if not name.startswith(("kernel", "signal"))},
            **modes_scratch,
            **packs,
            **table_scratch,
            **sums,
            up=((WIDE, 4 * WIDE), BF),
            down=((4 * WIDE, WIDE), BF),
            in_weight=((WIDE, 3 * WIDE), BF),
            out_weight=((WIDE, WIDE), BF),
            layer_left=((512, WIDE), BF),
            layer_second=((512, 4 * WIDE), BF),
            pair_one=((512, WIDE), BF),
            pair_two=((512, WIDE), BF),
            turned_one=((WIDE, 512), BF),
            turned_two=((WIDE, 512), BF),
            turned=((WIDE, ROWS), BF),
            slopes=(thrice, BF),
            pairs=((4, *home), BF),
            total=(home, F32),
            grad_d=(home, F32),
            grad_d_low=(home, BF),
            att_grad_home=(home, BF),
            att_grad=(span, BF),
            query_grad=(span, F32),
            key_grad=(span, F32),
            value_grad=(span, F32),
            qkv_grad=((3, *span), BF),
            mixed_grad_c=(thrice, BF),
            grad_c_low=(home, BF),
            grad_b=(home, F32),
            grad_b_low=(home, BF),
            mixed_grad_a=(thrice, BF),
            response_grad=(home, F32),
            response_grad_low=(home, BF),
            conv_grad=(span, BF),
            grad_re=(span, F32),
            grad_im=(span, F32),
            signal_grad=((SPAN + 64, BLOCK), BF),
            signal_grad_home=((192, WIDE), BF),
            response_next=((64, WIDE), BF),
            grad_ext=((192, WIDE), F32),
            taps=((64, WIDE), F32),
            small=((2, 2, 24, WIDE), F32),
            small_c=((2, 24, WIDE), F32),
            small_swap=((4, 24, WIDE), F32),
            small_sum=((3, 24, WIDE), F32),
            mode_part=((3, 128, 128), F32),
            mode_swap=((2, 128, 128), F32),
            mode_home=((128, WIDE), F32),
        ),
        (160, 64),
    )
    vmem = pl.BlockSpec(memory_space=pltpu.VMEM)
    given = [b[name] for name in ("block_out", "token_grad", "mode_out", "small_out")]
    for name in kinds:
        given += [b[name + "_own"], b[name + "_third"]]
    gain = ((96,), F32)
    wide, narrow, up, down, mode = ((96, 576), F32), ((96, 192), F32), ((96, 768), F32), ((192, 384), F32), ((64, 96), F32)
    shapes = (
        ((1, *home), BF),
        ((1, *home), F32),
        gain,
        wide,
        ((16, 96), F32),
        mode,
        mode,
        gain,
        narrow,
        gain,
        up,
        down,
        gain,
        wide,
        narrow,
        gain,
        up,
        down,
    )
    results = pl.pallas_call(
        kernel_z,
        out_shape=[jax.ShapeDtypeStruct(shape, kind) for shape, kind in shapes],
        in_specs=[vmem] * len(given),
        out_specs=[vmem] * len(shapes),
    )(*given)
    return tuple(result.T if result.shape == (192, 384) else result for result in results)


def solution(mesh):
    in_specs = (
        P("batch", "seq", None),
        P("batch", None),
        P(),
        P(),
        P(),
        P(),
        P(),
        P(),
        P(),
        P(),
        P(),
        P(),
        P(),
        P(),
        P(),
        P(),
        P(),
        P(),
        P("batch", "seq", None),
    )
    out_specs = (
        P("batch", "seq", None),
        P("batch", "seq", None),
        P("seq"),
        P("seq", "batch"),
        P("batch", "seq"),
        P(None, "seq"),
        P(None, "seq"),
        P("seq"),
        P("seq", "batch"),
        P("seq"),
        P("seq", "batch"),
        P("seq", "batch"),
        P("seq"),
        P("seq", "batch"),
        P("seq", "batch"),
        P("seq"),
        P("seq", "batch"),
        P("seq", "batch"),
    )
    fast = mesh.shape["seq"] == RANKS and mesh.shape["batch"] == 4
    return jax.shard_map(shards_fast if fast else shards, mesh=mesh, in_specs=in_specs, out_specs=out_specs, check_vma=False)
```

```python
import math

import jax
import jax.numpy as jnp
import ml_dtypes
import numpy as np
from jax import lax
from jax.experimental import pallas as pl
from jax.experimental.pallas import tpu as pltpu
from jax.sharding import PartitionSpec as P

HEADS = 12


HIGH = lax.Precision.HIGHEST
NEGATIVE = -1e30


def shifted_2(value, axis, steps):
    count = lax.axis_size(axis)
    leading, last = (max(0, -steps), min(count, count - steps))
    return lax.ppermute(value, axis, [(source, source + steps) for source in range(leading, last)])


def shortened(x):

    def short(part):
        return part.astype(jnp.bfloat16) if part.dtype == jnp.float32 else part

    return jax.tree.map(short, x)


def mult(form, left, right):
    return jnp.einsum(form, left, right, precision=HIGH, preferred_element_type=jnp.float32)


def norm_pieces(value):
    row_mean = jnp.mean(value, axis=-1, keepdims=True)
    cent = value - row_mean
    inverse_deviation = lax.rsqrt(jnp.mean(cent * cent, axis=-1, keepdims=True) + 1e-05)
    return (cent * inverse_deviation, inverse_deviation)


def norm_backward(incoming_gradient, centered_normalized, inverse_deviation, gain_vector):
    gain_share = jnp.sum(incoming_gradient * centered_normalized, axis=0)
    scaled_rows = incoming_gradient * gain_vector
    inner_product = jnp.mean(scaled_rows, axis=-1, keepdims=True)
    cross_term = jnp.mean(scaled_rows * centered_normalized, axis=-1, keepdims=True)
    return (
        inverse_deviation * (scaled_rows - inner_product - centered_normalized * cross_term),
        gain_share,
    )


def segment_of(where, ends):
    return jnp.sum((where[:, None] >= ends[None, :]).astype(jnp.int32), axis=1)


def allowed(query_pos, key_pos, ends):
    same = segment_of(query_pos, ends)[:, None] == segment_of(key_pos, ends)[None, :]
    return (key_pos[None, :] <= query_pos[:, None]) & same


def kernel_rows(coef, rate, times):

    def step(total, pair):
        scale, decay = pair
        return (total + scale[:, None] * jnp.exp(-decay[:, None] * times[None, :]), None)

    start = jnp.zeros((coef.shape[1], times.shape[0]), jnp.float32)
    return lax.scan(step, start, (coef, rate))[0]


def kernel_grads(coef, rate, times, incoming_gradient):

    def step(carry, pair):
        scale, decay = pair
        fall = incoming_gradient * jnp.exp(-decay[:, None] * times[None, :])
        return (carry, (jnp.sum(fall, axis=1), -scale * jnp.sum(fall * times[None, :], axis=1)))

    return lax.scan(step, jnp.zeros((), jnp.float32), (coef, rate))[1]


def angle_pair(left, right, period):
    turns = left[:, None] * right[None, :] % period
    angle = turns.astype(jnp.float32) * (2.0 * math.pi / period)
    return (jnp.cos(angle), jnp.sin(angle))


def dft_tables(blocks, rows):
    wide = 2 * blocks
    block_ids = jnp.arange(blocks, dtype=jnp.int32)
    wide_ids = jnp.arange(wide, dtype=jnp.int32)
    row_ids = jnp.arange(rows, dtype=jnp.int32)
    return (
        angle_pair(block_ids, wide_ids, wide),
        angle_pair(wide_ids, row_ids, wide * rows),
        angle_pair(row_ids, row_ids, rows),
    )


def forward_spectrum(signal, tables, blocks, rows):
    (cos_one, sin_one), (cos_two, sin_two), (cos_three, sin_three) = tables
    folded = signal.reshape(signal.shape[0], blocks, rows)
    first_re = mult("cpr,pf->cfr", folded, cos_one)
    first_im = -mult("cpr,pf->cfr", folded, sin_one)
    turned_re = first_re * cos_two + first_im * sin_two
    turned_im = first_im * cos_two - first_re * sin_two
    spec_re = mult("cfr,rk->cfk", turned_re, cos_three) + mult("cfr,rk->cfk", turned_im, sin_three)
    spec_im = mult("cfr,rk->cfk", turned_im, cos_three) - mult("cfr,rk->cfk", turned_re, sin_three)
    return (spec_re, spec_im)


def inverse_signal(spec_re, spec_im, tables, blocks, rows):
    (cos_one, sin_one), (cos_two, sin_two), (cos_three, sin_three) = tables
    inner_re = mult("cfk,rk->cfr", spec_re, cos_three) - mult("cfk,rk->cfr", spec_im, sin_three)
    inner_im = mult("cfk,rk->cfr", spec_im, cos_three) + mult("cfk,rk->cfr", spec_re, sin_three)
    turned_re = inner_re * cos_two - inner_im * sin_two
    turned_im = inner_im * cos_two + inner_re * sin_two
    result_value = mult("cfr,pf->cpr", turned_re, cos_one) - mult("cfr,pf->cpr", turned_im, sin_one)
    return result_value.reshape(spec_re.shape[0], blocks * rows) / (2.0 * blocks * rows)


def attend_block(state, query, query_pos, key_block, value_block, key_pos, ends, scale):
    top, mass, accum = state
    scores = (
        jnp.einsum("qhd,khd->hqk", query, key_block, preferred_element_type=jnp.float32) * scale
    )
    mask = allowed(query_pos, key_pos, ends)[None]
    newtop = jnp.maximum(top, jnp.max(jnp.where(mask, scores, NEGATIVE), axis=-1))
    weights = jnp.where(mask, jnp.exp(scores - newtop[:, :, None]), 0.0)
    factor = jnp.exp(top - newtop)
    mass = mass * factor + jnp.sum(weights, axis=-1)
    accum = accum * factor[:, :, None] + jnp.einsum(
        "hqk,khd->hqd", weights, value_block.astype(jnp.float32), preferred_element_type=jnp.float32
    )
    return (newtop, mass, accum)


def score_grads(
    query, grads, lse_rows, delta_rows, query_pos, key_block, value_block, key_pos, ends, scale
):
    scores = (
        jnp.einsum("qhd,khd->hqk", query, key_block, preferred_element_type=jnp.float32) * scale
    )
    mask = allowed(query_pos, key_pos, ends)[None]
    probs = jnp.where(mask, jnp.exp(scores - lse_rows[:, :, None]), 0.0)
    dots = jnp.einsum("qhd,khd->hqk", grads, value_block, preferred_element_type=jnp.float32)
    return (probs, (probs * (dots - delta_rows[:, :, None])).astype(jnp.bfloat16))


def query_back(
    query, grads, lse_rows, delta_rows, query_pos, key_block, value_block, key_pos, ends, scale
):
    score_grad = score_grads(
        query, grads, lse_rows, delta_rows, query_pos, key_block, value_block, key_pos, ends, scale
    )[1]
    return (
        jnp.einsum("hqk,khd->qhd", score_grad, key_block, preferred_element_type=jnp.float32)
        * scale
    )


def key_back(
    query, grads, lse_rows, delta_rows, query_pos, key_block, value_block, key_pos, ends, scale
):
    probs, score_grad = score_grads(
        query, grads, lse_rows, delta_rows, query_pos, key_block, value_block, key_pos, ends, scale
    )
    key_part = (
        jnp.einsum("hqk,qhd->khd", score_grad, query, preferred_element_type=jnp.float32) * scale
    )
    value_part = jnp.einsum(
        "hqk,qhd->khd", probs, grads.astype(jnp.float32), preferred_element_type=jnp.float32
    )
    return (key_part, value_part)


def scan_keys(carry, keys, values, update):
    count = keys.shape[0]
    width = keys.shape[1]
    head_size = width // HEADS
    step = math.gcd(count, 1024)
    firsts = step * jnp.arange(count // step, dtype=jnp.int32)

    def inner_product(state, item):
        key_block, value_block, first = item
        key_pos = first + jnp.arange(step, dtype=jnp.int32)
        return (update(state, key_block, value_block, key_pos), None)

    items = (
        keys.reshape(count // step, step, HEADS, head_size),
        values.reshape(count // step, step, HEADS, head_size),
        firsts,
    )
    return lax.scan(inner_product, carry, items)[0]


def feed_forward(residual_stream, gain_vector, w_up, w_down):
    centered_normalized, inverse_deviation = norm_pieces(residual_stream)
    normed_rows = (centered_normalized * gain_vector).astype(jnp.bfloat16)
    raised_rows = jnp.dot(normed_rows, w_up, preferred_element_type=jnp.float32)
    active_tokens = jax.nn.gelu(raised_rows).astype(jnp.bfloat16)
    result_value = residual_stream + jnp.dot(
        active_tokens, w_down, preferred_element_type=jnp.float32
    )
    return (
        result_value,
        (centered_normalized, inverse_deviation, normed_rows, raised_rows, active_tokens),
    )


def feed_back(incoming_gradient, saved_residuals, gain_vector, w_up, w_down):
    centered_normalized, inverse_deviation, normed_rows, raised_rows, active_tokens = (
        saved_residuals
    )
    grad_low = incoming_gradient.astype(jnp.bfloat16)
    down_part = jnp.einsum("tf,td->fd", active_tokens, grad_low, preferred_element_type=jnp.float32)
    active_grad = jnp.einsum("td,fd->tf", grad_low, w_down, preferred_element_type=jnp.float32)
    slope = jax.vjp(jax.nn.gelu, raised_rows)[1](active_grad)[0].astype(jnp.bfloat16)
    up_part = jnp.einsum("td,tf->df", normed_rows, slope, preferred_element_type=jnp.float32)
    normed_gradient = jnp.einsum("tf,df->td", slope, w_up, preferred_element_type=jnp.float32)
    input_gradient, gain_share = norm_backward(
        normed_gradient, centered_normalized, inverse_deviation, gain_vector
    )
    return (incoming_gradient + input_gradient, gain_share, up_part, down_part)


def shards(
    tokens,
    doc_lengths,
    mixer_norm_gain,
    mixer_in,
    shift_taps,
    mode_coef,
    mode_rate,
    skip_gain,
    mixer_out,
    gain_second,
    up_first,
    down_first,
    attention_norm_gain,
    project_in,
    project_out,
    gain_fourth,
    up_second,
    down_second,
    cotangent,
):
    rows = tokens.shape[1]
    width = tokens.shape[2]
    blocks = lax.axis_size("seq")
    rank = lax.axis_index("seq")
    total = rows * blocks
    head_size = width // HEADS
    scale = head_size ** (-0.5)
    lags = shift_taps.shape[0]
    channels = width // blocks
    ends = jnp.cumsum(doc_lengths[0])
    here = rank * rows + jnp.arange(rows, dtype=jnp.int32)
    residual_stream = tokens[0].astype(jnp.float32)
    mixer_centered_normalized, mixer_inverse_deviation = norm_pieces(residual_stream)
    mixer_normed_rows = (mixer_centered_normalized * mixer_norm_gain).astype(jnp.bfloat16)
    mixed_a = jnp.dot(mixer_normed_rows, mixer_in, preferred_element_type=jnp.float32)
    query_a = mixed_a[:, :width]
    key_a = mixed_a[:, width : 2 * width]
    value_a = mixed_a[:, 2 * width :]
    rim = shifted_2(key_a[rows - (lags - 1) :].astype(jnp.bfloat16), "seq", 1).astype(jnp.float32)
    key_ext = jnp.concatenate([rim, key_a], axis=0)
    shifted = jnp.zeros_like(key_a)
    for lag in range(lags):
        shifted = shifted + shift_taps[lag] * key_ext[lags - 1 - lag : lags - 1 - lag + rows]
    product_kv = shifted * value_a
    channel_in = lax.all_to_all(
        product_kv.T.reshape(blocks, channels, rows).astype(jnp.bfloat16),
        "seq",
        split_axis=0,
        concat_axis=2,
        tiled=True,
    ).astype(jnp.float32)[0]
    times = jnp.arange(total, dtype=jnp.int32).astype(jnp.float32)
    coef_here = lax.dynamic_slice_in_dim(mode_coef, rank * channels, channels, 1)
    rate_here = lax.dynamic_slice_in_dim(mode_rate, rank * channels, channels, 1)
    kernel_here = kernel_rows(coef_here, rate_here, times)
    tables = dft_tables(blocks, rows)
    sig_re, sig_im = forward_spectrum(channel_in, tables, blocks, rows)
    ker_re, ker_im = forward_spectrum(kernel_here, tables, blocks, rows)
    conv_chan = inverse_signal(
        sig_re * ker_re - sig_im * ker_im, sig_re * ker_im + sig_im * ker_re, tables, blocks, rows
    )
    conv_home = lax.all_to_all(
        conv_chan.reshape(1, channels, total).astype(jnp.bfloat16),
        "seq",
        split_axis=2,
        concat_axis=0,
        tiled=True,
    ).astype(jnp.float32)
    response = conv_home.reshape(width, rows).T + skip_gain * product_kv
    gated = (query_a * response).astype(jnp.bfloat16)
    stream_b = residual_stream + jnp.dot(gated, mixer_out, preferred_element_type=jnp.float32)
    attention_residual_stream, saved_b = feed_forward(stream_b, gain_second, up_first, down_first)
    attention_centered_normalized, attention_inverse_deviation = norm_pieces(
        attention_residual_stream
    )
    attention_normed_rows = (attention_centered_normalized * attention_norm_gain).astype(
        jnp.bfloat16
    )
    mixed_c = jnp.dot(attention_normed_rows, project_in, preferred_element_type=jnp.float32).astype(
        jnp.bfloat16
    )
    query_flat = mixed_c[:, :width]
    key_flat = mixed_c[:, width : 2 * width]
    value_flat = mixed_c[:, 2 * width :]
    query_c = query_flat.reshape(rows, HEADS, head_size)
    key_heads = key_flat.reshape(rows, HEADS, head_size)
    value_heads = value_flat.reshape(rows, HEADS, head_size)

    def forward_update(state, key_block, value_block, key_pos):
        return attend_block(state, query_c, here, key_block, value_block, key_pos, ends, scale)

    begin = (
        jnp.full((HEADS, rows), NEGATIVE, jnp.float32),
        jnp.zeros((HEADS, rows), jnp.float32),
        jnp.zeros((HEADS, rows, head_size), jnp.float32),
    )
    piece = (
        lax.all_gather(key_flat, "seq", axis=0, tiled=True),
        lax.all_gather(value_flat, "seq", axis=0, tiled=True),
    )
    top, mass, accum = scan_keys(begin, piece[0], piece[1], forward_update)
    lse = top + jnp.log(mass)
    att_full = accum / mass[:, :, None]
    attended = att_full.transpose(1, 0, 2).reshape(rows, width).astype(jnp.bfloat16)
    stream_d = attention_residual_stream + jnp.dot(
        attended, project_out, preferred_element_type=jnp.float32
    )
    result_value, saved_d = feed_forward(stream_d, gain_fourth, up_second, down_second)
    block_out = result_value.astype(jnp.bfloat16)[None]
    incoming_gradient = cotangent[0].astype(jnp.float32)
    incoming_gradient, gain_four_part, up_two_part, down_two_part = feed_back(
        incoming_gradient, saved_d, gain_fourth, up_second, down_second
    )
    grad_low = incoming_gradient.astype(jnp.bfloat16)
    out_part_c = jnp.einsum("td,te->de", attended, grad_low, preferred_element_type=jnp.float32)
    att_grad = jnp.einsum(
        "te,de->td", grad_low, project_out, preferred_element_type=jnp.float32
    ).astype(jnp.bfloat16)
    grad_heads = att_grad.reshape(rows, HEADS, head_size)
    delta = jnp.sum(grad_heads.astype(jnp.float32).transpose(1, 0, 2) * att_full, axis=-1)
    zero_heads = jnp.zeros((rows, HEADS, head_size), jnp.float32)

    def query_update(summed, key_block, value_block, key_pos):
        return summed + query_back(
            query_c, grad_heads, lse, delta, here, key_block, value_block, key_pos, ends, scale
        )

    piece = (
        lax.all_gather(key_flat, "seq", axis=0, tiled=True),
        lax.all_gather(value_flat, "seq", axis=0, tiled=True),
    )
    query_grad = scan_keys(zero_heads, piece[0], piece[1], query_update)
    lse_all, delta_all = (
        lax.all_gather(lse, "seq", axis=1, tiled=True),
        lax.all_gather(delta, "seq", axis=1, tiled=True),
    )
    queries = lax.all_gather(query_flat, "seq", axis=0, tiled=True)
    grads = lax.all_gather(att_grad, "seq", axis=0, tiled=True)
    count = queries.shape[0]
    step = math.gcd(count, 1024)
    firsts = step * jnp.arange(count // step, dtype=jnp.int32)

    def inner_product(summed, item):
        query_block, grad_block, first = item
        query_pos = first + jnp.arange(step, dtype=jnp.int32)
        lse_rows = lax.dynamic_slice_in_dim(lse_all, first, step, 1)
        delta_rows = lax.dynamic_slice_in_dim(delta_all, first, step, 1)
        parts = key_back(
            query_block,
            grad_block,
            lse_rows,
            delta_rows,
            query_pos,
            key_heads,
            value_heads,
            here,
            ends,
            scale,
        )
        return ((summed[0] + parts[0], summed[1] + parts[1]), None)

    items = (
        queries.reshape(count // step, step, HEADS, head_size),
        grads.reshape(count // step, step, HEADS, head_size),
        firsts,
    )
    key_grad, value_grad = lax.scan(inner_product, (zero_heads, zero_heads), items)[0]
    key_grad = key_grad.reshape(rows, width)
    value_grad = value_grad.reshape(rows, width)
    mixed_grad_c = jnp.concatenate(
        [query_grad.reshape(rows, width), key_grad, value_grad], axis=1
    ).astype(jnp.bfloat16)
    in_part_c = jnp.einsum(
        "td,te->de", attention_normed_rows, mixed_grad_c, preferred_element_type=jnp.float32
    )
    attention_normed_gradient = jnp.einsum(
        "te,de->td", mixed_grad_c, project_in, preferred_element_type=jnp.float32
    )
    attention_norm_gradient, attention_gain_share = norm_backward(
        attention_normed_gradient,
        attention_centered_normalized,
        attention_inverse_deviation,
        attention_norm_gain,
    )
    incoming_gradient = incoming_gradient + attention_norm_gradient
    incoming_gradient, gain_two_part, up_one_part, down_one_part = feed_back(
        incoming_gradient, saved_b, gain_second, up_first, down_first
    )
    grad_low = incoming_gradient.astype(jnp.bfloat16)
    out_part_a = jnp.einsum("td,te->de", gated, grad_low, preferred_element_type=jnp.float32)
    gated_grad = jnp.einsum("te,de->td", grad_low, mixer_out, preferred_element_type=jnp.float32)
    query_grad_a = gated_grad * response
    response_grad = gated_grad * query_a
    skip_part = jnp.sum(response_grad * product_kv, axis=0)
    chan_grad = lax.all_to_all(
        response_grad.T.reshape(blocks, channels, rows).astype(jnp.bfloat16),
        "seq",
        split_axis=0,
        concat_axis=2,
        tiled=True,
    ).astype(jnp.float32)[0]
    grad_re, grad_im = forward_spectrum(chan_grad, tables, blocks, rows)
    signal_grad = inverse_signal(
        ker_re * grad_re + ker_im * grad_im,
        ker_re * grad_im - ker_im * grad_re,
        tables,
        blocks,
        rows,
    )
    kernel_grad = inverse_signal(
        sig_re * grad_re + sig_im * grad_im,
        sig_re * grad_im - sig_im * grad_re,
        tables,
        blocks,
        rows,
    )
    coef_part, rate_part = kernel_grads(coef_here, rate_here, times, kernel_grad)
    returned = lax.all_to_all(
        signal_grad.reshape(1, channels, total).astype(jnp.bfloat16),
        "seq",
        split_axis=2,
        concat_axis=0,
        tiled=True,
    ).astype(jnp.float32)
    kv_grad = returned.reshape(width, rows).T + skip_gain * response_grad
    shifted_grad = kv_grad * value_a
    value_grad_a = kv_grad * shifted
    later = shifted_2(shortened(shifted_grad[: lags - 1]), "seq", -1)
    grad_ext = jnp.concatenate([shifted_grad, later], axis=0)
    key_grad_a = jnp.zeros_like(key_a)
    tap_rows = []
    for lag in range(lags):
        key_grad_a = key_grad_a + shift_taps[lag] * grad_ext[lag : lag + rows]
        tap_rows.append(
            jnp.sum(shifted_grad * key_ext[lags - 1 - lag : lags - 1 - lag + rows], axis=0)
        )
    taps_part = jnp.stack(tap_rows)
    mixed_grad_a = jnp.concatenate([query_grad_a, key_grad_a, value_grad_a], axis=1).astype(
        jnp.bfloat16
    )
    in_part_a = jnp.einsum(
        "td,te->de", mixer_normed_rows, mixed_grad_a, preferred_element_type=jnp.float32
    )
    mixer_normed_gradient = jnp.einsum(
        "te,de->td", mixed_grad_a, mixer_in, preferred_element_type=jnp.float32
    )
    mixer_norm_gradient, mixer_gain_share = norm_backward(
        mixer_normed_gradient, mixer_centered_normalized, mixer_inverse_deviation, mixer_norm_gain
    )
    token_grad = (incoming_gradient + mixer_norm_gradient)[None]
    parts = (
        lax.psum_scatter(mixer_gain_share, "seq", scatter_dimension=0, tiled=True),
        lax.psum_scatter(in_part_a, "seq", scatter_dimension=0, tiled=True),
        lax.psum_scatter(taps_part, "seq", scatter_dimension=1, tiled=True),
        lax.psum_scatter(skip_part, "seq", scatter_dimension=0, tiled=True),
        lax.psum_scatter(out_part_a, "seq", scatter_dimension=0, tiled=True),
        lax.psum_scatter(gain_two_part, "seq", scatter_dimension=0, tiled=True),
        lax.psum_scatter(up_one_part, "seq", scatter_dimension=0, tiled=True),
        lax.psum_scatter(down_one_part, "seq", scatter_dimension=0, tiled=True),
        lax.psum_scatter(attention_gain_share, "seq", scatter_dimension=0, tiled=True),
        lax.psum_scatter(in_part_c, "seq", scatter_dimension=0, tiled=True),
        lax.psum_scatter(out_part_c, "seq", scatter_dimension=0, tiled=True),
        lax.psum_scatter(gain_four_part, "seq", scatter_dimension=0, tiled=True),
        lax.psum_scatter(up_two_part, "seq", scatter_dimension=0, tiled=True),
        lax.psum_scatter(down_two_part, "seq", scatter_dimension=0, tiled=True),
    )
    matrices = (
        lax.psum_scatter(
            parts[1].astype(jnp.bfloat16), "batch", scatter_dimension=1, tiled=True
        ).astype(jnp.float32),
        lax.psum_scatter(
            parts[2].astype(jnp.bfloat16), "batch", scatter_dimension=0, tiled=True
        ).astype(jnp.float32),
        lax.psum_scatter(
            parts[4].astype(jnp.bfloat16), "batch", scatter_dimension=1, tiled=True
        ).astype(jnp.float32),
        lax.psum_scatter(
            parts[6].astype(jnp.bfloat16), "batch", scatter_dimension=1, tiled=True
        ).astype(jnp.float32),
        lax.psum_scatter(
            parts[7].astype(jnp.bfloat16), "batch", scatter_dimension=1, tiled=True
        ).astype(jnp.float32),
        lax.psum_scatter(
            parts[9].astype(jnp.bfloat16), "batch", scatter_dimension=1, tiled=True
        ).astype(jnp.float32),
        lax.psum_scatter(
            parts[10].astype(jnp.bfloat16), "batch", scatter_dimension=1, tiled=True
        ).astype(jnp.float32),
        lax.psum_scatter(
            parts[12].astype(jnp.bfloat16), "batch", scatter_dimension=1, tiled=True
        ).astype(jnp.float32),
        lax.psum_scatter(
            parts[13].astype(jnp.bfloat16), "batch", scatter_dimension=1, tiled=True
        ).astype(jnp.float32),
    )
    smalls = lax.psum(
        (parts[0], coef_part, rate_part, parts[3], parts[5], parts[8], parts[11]), "batch"
    )
    return (
        block_out,
        token_grad,
        smalls[0],
        matrices[0],
        matrices[1],
        smalls[1],
        smalls[2],
        smalls[3],
        matrices[2],
        smalls[4],
        matrices[3],
        matrices[4],
        smalls[5],
        matrices[5],
        matrices[6],
        smalls[6],
        matrices[7],
        matrices[8],
    )


MESH = pl.DeviceIdType.MESH
BF = jnp.bfloat16
F32 = jnp.float32
ROWS, WIDE, RANKS = (128, 768, 8)
SPAN = ROWS * RANKS
BLOCK = 128
OWNERS = 6
NT = (((1,), (1,)), ((), ()))
TN = (((0,), (0,)), ((), ()))
ROOT = math.sqrt(2.0 / math.pi)
CUBIC = 0.044715


def flip(value):
    return 1 - value


def mm(left, right):
    return jnp.dot(left, right, preferred_element_type=F32)


def mm_nt(left, right):
    return lax.dot_general(left, right, NT, preferred_element_type=F32)


def mm_tn(left, right):
    return lax.dot_general(left, right, TN, preferred_element_type=F32)


def is_owner(rank):
    return jnp.logical_and(rank >= 1, rank <= OWNERS)


def rows_of(rank):
    return pl.ds(pl.multiple_of(ROWS * rank, ROWS), ROWS)


def lanes_of(block):
    return pl.ds(pl.multiple_of(BLOCK * block, BLOCK), BLOCK)


PARTNERS = ((1, 1, 1), (1, 1, 0), (1, 0, 1), (1, 0, 0), (0, 1, 1), (0, 1, 0), (0, 0, 1))


class Spread:
    def __init__(self, net, source, target, outward, only=None):
        self.net, self.source, self.target, self.outward = net, source, target, outward
        self.base = net.take(RANKS - 1)

    def copy(self, step, source, target, rank):
        at = self.base + step - 1
        return pltpu.make_async_remote_copy(
            src_ref=source,
            dst_ref=target,
            send_sem=self.net.send_sem.at[at],
            recv_sem=self.net.recv_sem.at[at],
            device_id=(rank, self.net.b),
            device_id_type=MESH,
        )

    def each_send(self, act, chosen=None):
        me = self.net.s
        for step in range(1, RANKS):
            rank = self.net.partner(step)
            go = is_owner(rank) if self.outward else is_owner(me)
            if chosen is not None:
                go = jnp.logical_and(go, chosen(rank))

            @pl.when(go)
            def _(step=step, rank=rank):
                if self.outward:
                    act(self.copy(step, self.source(rank - 1), self.target(me), rank))
                else:
                    act(self.copy(step, self.source(rank), self.target(me - 1), rank))

    def start(self, chosen=None):
        self.each_send(lambda copy: copy.start(), chosen)

    def own(self):
        me = self.net.s

        @pl.when(is_owner(me))
        def _():
            if self.outward:
                self.target(me)[...] = self.source(me - 1)[...]
            else:
                self.target(me - 1)[...] = self.source(me)[...]

    def wait_recv(self, steps=range(1, RANKS)):
        me = self.net.s
        for step in steps:
            rank = self.net.partner(step)

            @pl.when(is_owner(me) if self.outward else is_owner(rank))
            def _(step=step, rank=rank):
                landed = self.target(rank if self.outward else rank - 1)
                self.copy(step, landed, landed, rank).wait_recv()

    def wait_send(self):
        self.each_send(lambda copy: copy.wait_send())


class Net:
    def __init__(self, send_sem, recv_sem):
        self.send_sem, self.recv_sem = send_sem, recv_sem
        self.s = lax.axis_index("seq")
        self.b = lax.axis_index("batch")
        self.y, self.c = self.b // 2, lax.rem(self.b, 2)
        z, self.x = self.s // 2, lax.rem(self.s, 2)
        self.high, self.low = z // 2, lax.rem(z, 2)
        self.sibling = (self.s, 2 * self.y + flip(self.c))
        self.by_y = (self.s, 2 * flip(self.y) + self.c)
        self.by_both = (self.s, 2 * flip(self.y) + flip(self.c))
        self.by_x = (2 * z + flip(self.x), self.b)
        self.by_low = (2 * (2 * self.high + flip(self.low)) + self.x, self.b)
        self.by_high = (2 * (2 * flip(self.high) + self.low) + self.x, self.b)
        self.used = 0
        self.waiting = []

    def partner(self, step):
        far, near, side = PARTNERS[step - 1]
        high = flip(self.high) if far else self.high
        low = flip(self.low) if near else self.low
        return 4 * high + 2 * low + (flip(self.x) if side else self.x)

    def take(self, count):
        at = self.used
        self.used += count
        return at

    def spread(self, source, target, outward):
        made = Spread(self, source, target, outward)
        self.waiting.append(made)
        return made

    def send(self, source, target, other):
        at = self.take(1)
        copy = pltpu.make_async_remote_copy(
            src_ref=source,
            dst_ref=target,
            send_sem=self.send_sem.at[at],
            recv_sem=self.recv_sem.at[at],
            device_id=other,
            device_id_type=MESH,
        )
        copy.start()
        self.waiting.append(copy)
        return copy

    def hello(self):
        barrier = pltpu.get_barrier_semaphore()
        for step in range(1, RANKS):
            pl.semaphore_signal(
                barrier, inc=1, device_id=(lax.rem(self.s + step, RANKS), self.b), device_id_type=MESH
            )
        for other in (self.sibling, self.by_y, self.by_both):
            pl.semaphore_signal(barrier, inc=1, device_id=other, device_id_type=MESH)

    def ready(self):
        pl.semaphore_wait(pltpu.get_barrier_semaphore(), RANKS + 2)

    def turn_of(self, step, y, c):
        return (2 * y + flip(c), 2 * flip(y) + c, 2 * flip(y) + flip(c), 2 * y + c)[step]

    def order(self):
        owners = (self.sibling, self.by_y, self.by_both, None)
        return [(self.turn_of(step, self.y, self.c), owners[step]) for step in range(4)]

    def drop(self, copy):
        self.waiting = [made for made in self.waiting if made is not copy]

    def finish(self):
        for made in self.waiting:
            made.wait_send()


class Beside:
    def __init__(self, net, source, target, steps):
        self.net, self.steps = net, steps
        self.at = net.take(1)
        other = jnp.clip(net.s + steps, 0, RANKS - 1)
        self.copy = pltpu.make_async_remote_copy(
            src_ref=source,
            dst_ref=target,
            send_sem=net.send_sem.at[self.at],
            recv_sem=net.recv_sem.at[self.at],
            device_id=(other, net.b),
            device_id_type=MESH,
        )
        last = RANKS - 1 if steps > 0 else 0
        first = 0 if steps > 0 else RANKS - 1
        self.sends = net.s != last
        self.takes = net.s != first
        net.waiting.append(self)

    def start(self):
        @pl.when(self.sends)
        def _():
            self.copy.start()

    def wait_recv(self):
        @pl.when(self.takes)
        def _():
            self.copy.wait_recv()

    def wait_send(self):
        @pl.when(self.sends)
        def _():
            self.copy.wait_send()


def pieces(value):
    cent = value - jnp.mean(value, axis=-1, keepdims=True)
    inverse = lax.rsqrt(jnp.mean(cent * cent, axis=-1, keepdims=True) + 1e-05)
    return cent * inverse, inverse


def pieces_back(incoming, normal, inverse, gain):
    share = jnp.sum(incoming * normal, axis=0, keepdims=True)
    scaled = incoming * gain
    first = jnp.mean(scaled, axis=-1, keepdims=True)
    second = jnp.mean(scaled * normal, axis=-1, keepdims=True)
    return inverse * (scaled - first - normal * second), share


def gelu_parts(u):
    square = u * u
    bend = jnp.tanh(ROOT * u * (1.0 + CUBIC * square))
    half = 0.5 * (1.0 + bend)
    value = u * half
    slope = half + 0.5 * u * (1.0 - bend * bend) * (ROOT * (1.0 + 3.0 * CUBIC * square))
    return value, slope


def split(value):
    high = value.astype(BF)
    return high, (value - high.astype(F32)).astype(BF)


def transform(r, net, go, signal, re_out, im_out):
    for index, steps in enumerate(((7,), (5, 6), (3, 4), (1, 2))):
        go.wait_recv(steps)
        high = flip(net.high) if index >= 2 else net.high
        low = flip(net.low) if index % 2 else net.low
        some = pl.ds(pl.multiple_of(512 * high + 256 * low, 256), 256)
        re, im = mm(r.cos_table[:, some], signal[some, :]), mm(r.sin_table[:, some], signal[some, :])
        if index == 0:
            re_out[...] = re
            im_out[...] = -im
        else:
            re_out[...] += re
            im_out[...] -= im


def transform_two(r, signal, re_out, im_out):
    high, low = split(signal)
    r.pack_re[:, 0:128] = high
    r.pack_re[:, 128:256] = low

    @pl.loop(0, 4)
    def _(at):
        rows = pl.ds(pl.multiple_of(256 * at, 256), 256)
        re, im = mm(r.cos_table[rows, :], r.pack_re[...]), mm(r.sin_table[rows, :], r.pack_re[...])
        re_out[rows, :] = re[:, 0:128] + re[:, 128:256]
        im_out[rows, :] = -(im[:, 0:128] + im[:, 128:256])


def inverse(r, re, im, out, back=None):
    re_high, re_low = split(re)
    im_high, im_low = split(im)
    r.pack_re[:, 0:128] = re_high
    r.pack_re[:, 128:256] = re_low
    r.pack_im[:, 0:128] = im_high
    r.pack_im[:, 128:256] = im_low
    for at in (3, 2, 1, 0):
        rows = slice(256 * at, 256 * at + 256)
        both = mm(r.cos_table[rows, :], r.pack_re[...]) - mm(r.sin_table[rows, :], r.pack_im[...])
        out[rows, :] = ((both[:, 0:128] + both[:, 128:256]) * (1.0 / SPAN)).astype(out.dtype)
        if back is not None:
            back.start(lambda rank, at=at: rank // 2 == at)


def modes(coef_ref, rate_ref, out_ref):
    blocks, width = out_ref.shape[0] // 8, out_ref.shape[1]
    row = lax.broadcasted_iota(jnp.int32, (8, width), 0).astype(F32)
    out_ref[...] = jnp.zeros_like(out_ref)

    @pl.loop(0, 8)
    def _(group):
        some = pl.ds(pl.multiple_of(8 * group, 8), 8)
        rate, coef = rate_ref[some, :], coef_ref[some, :]
        falls = [coef[n : n + 1] * jnp.exp(-rate[n : n + 1] * row) for n in range(8)]
        steps = [jnp.exp(-rate[n : n + 1] * jnp.maximum(row, 8.0)) for n in range(8)]

        def step(at, falls):
            rows = pl.ds(pl.multiple_of(8 * at, 8), 8)
            out_ref[rows, :] += sum(falls[1:], falls[0])
            return tuple(fall * factor for fall, factor in zip(falls, steps))

        lax.fori_loop(0, blocks, step, tuple(falls), unroll=4)


def modes_back(coef_ref, rate_ref, grad_ref, coef_out, rate_out):
    blocks, width = grad_ref.shape[0] // 8, grad_ref.shape[1]
    row = lax.broadcasted_iota(jnp.int32, (8, width), 0).astype(F32)

    @pl.loop(0, 8)
    def _(group):
        some = pl.ds(pl.multiple_of(8 * group, 8), 8)
        rate, coef = rate_ref[some, :], coef_ref[some, :]
        steps = [jnp.exp(-rate[n : n + 1] * jnp.maximum(row, 8.0)) for n in range(8)]
        zero = jnp.minimum(row, 0.0)

        def step(at, carry):
            totals, slopes = carry
            here = grad_ref[pl.ds(pl.multiple_of(8 * (blocks - 1 - at), 8), 8), :]
            slopes = tuple(slope * factor + total for slope, factor, total in zip(slopes, steps, totals))
            totals = tuple(total * factor + here for total, factor in zip(totals, steps))
            return totals, slopes

        totals, slopes = lax.fori_loop(0, blocks, step, ((zero,) * 8, (zero,) * 8), unroll=2)
        coef_rows, rate_rows = [], []
        for n in range(8):
            fall = jnp.exp(-rate[n : n + 1] * row)
            coef_rows.append(jnp.sum(fall * totals[n], axis=0, keepdims=True))
            late = jnp.sum(fall * (8.0 * steps[n] * slopes[n] + row * totals[n]), axis=0, keepdims=True)
            rate_rows.append(-coef[n : n + 1] * late)
        coef_out[some, :] = jnp.concatenate(coef_rows, axis=0)
        rate_out[some, :] = jnp.concatenate(rate_rows, axis=0)


def shift_forward(keys, taps, value, shifted):
    @pl.loop(0, OWNERS)
    def _(block):
        lanes = lanes_of(block)
        near = keys[:, lanes]
        total = jnp.zeros((ROWS, BLOCK), F32)
        for rest in range(8):
            turned = pltpu.roll(near, rest, 0) if rest else near
            for part in range(8):
                total = total + taps[8 * part + rest : 8 * part + rest + 1, lanes] * turned[64 - 8 * part : 192 - 8 * part]
        shifted[:, lanes] = total


def shift_back(grads, keys, taps, key_grad, taps_grad):
    @pl.loop(0, OWNERS)
    def _(block):
        lanes = lanes_of(block)
        ahead, near = grads[:, lanes], keys[:, lanes]
        here = ahead[0:ROWS]
        total = jnp.zeros((ROWS, BLOCK), F32)
        rows = {}
        for rest in range(8):
            later = pltpu.roll(ahead, 192 - rest, 0) if rest else ahead
            turned = pltpu.roll(near, rest, 0) if rest else near
            for part in range(8):
                lag = 8 * part + rest
                total = total + taps[lag : lag + 1, lanes] * later[8 * part : 8 * part + ROWS]
                taps_grad[lag : lag + 1, lanes] = jnp.sum(here * turned[64 - 8 * part : 192 - 8 * part], axis=0, keepdims=True)
        key_grad[:, lanes] = total


def head_lanes(shape, head):
    return lax.broadcasted_iota(jnp.int32, shape, 1) // 64 == head


def document_start(ends, first, count):
    at = first + lax.broadcasted_iota(jnp.int32, (count, 1), 0)
    begin = jnp.zeros((count, 1), jnp.int32)
    for index in range(3):
        begin = jnp.where(at >= ends[index], ends[index], begin)
    return at, begin


def allowed_pairs(ends, part):
    query_at, begin = document_start(ends, 256 * part, 256)
    key_at = lax.broadcasted_iota(jnp.int32, (256, 256 * (part + 1)), 1)
    return jnp.logical_and(key_at <= query_at, key_at >= begin)


def attention_forward(r, part):
    rows, keys = slice(256 * part, 256 * part + 256), slice(0, 256 * part + 256)
    mask = allowed_pairs(r.ends, part)

    @pl.loop(0, 2)
    def _(head):
        lanes = head_lanes((256, BLOCK), head)
        query = jnp.where(lanes, r.qkv[0, rows, :].astype(F32) * 0.125, 0.0).astype(BF)
        scores = jnp.where(mask, mm_nt(query, r.qkv[1, keys, :]), NEGATIVE)
        top = jnp.max(scores, axis=1, keepdims=True)
        weights = jnp.exp(scores - top)
        mass = jnp.sum(weights, axis=1, keepdims=True)
        mixed = mm(weights.astype(BF), r.qkv[2, keys, :]) / mass
        r.attended_full[rows, :] = jnp.where(lanes, mixed, r.attended_full[rows, :])
        r.lse[rows, :] = jnp.where(lanes, top + jnp.log(mass), r.lse[rows, :])

    r.attended_low[rows, :] = r.attended_full[rows, :].astype(BF)


def attention_back(r, part):
    rows, keys = slice(256 * part, 256 * part + 256), slice(0, 256 * part + 256)
    mask = allowed_pairs(r.ends, part)

    @pl.loop(0, 2)
    def _(head):
        lanes = head_lanes((256, BLOCK), head)
        query = jnp.where(lanes, r.qkv[0, rows, :].astype(F32) * 0.125, 0.0).astype(BF)
        whole = r.att_grad[rows, :].astype(F32)
        grads = jnp.where(lanes, whole, 0.0)
        delta = jnp.sum(grads * r.attended_full[rows, :], axis=1, keepdims=True)
        lse = jnp.sum(jnp.where(lanes, r.lse[rows, :], 0.0), axis=1, keepdims=True) * (1.0 / 64.0)
        grads = grads.astype(BF)
        scores = mm_nt(query, r.qkv[1, keys, :])
        probs = jnp.where(mask, jnp.exp(scores - lse), 0.0)
        score_grad = (probs * (mm_nt(grads, r.qkv[2, keys, :]) - delta)).astype(BF)
        query_grad = mm(score_grad, r.qkv[1, keys, :]) * 0.125
        r.query_grad[rows, :] = jnp.where(lanes, query_grad, r.query_grad[rows, :])
        r.key_grad[keys, :] += mm_tn(score_grad, query)
        r.value_grad[keys, :] += mm_tn(probs.astype(BF), grads)

    r.qkv_grad[0, rows, :] = r.query_grad[rows, :].astype(BF)
    r.qkv_grad[1, rows, :] = r.key_grad[rows, :].astype(BF)
    r.qkv_grad[2, rows, :] = r.value_grad[rows, :].astype(BF)


class Gather:
    def __init__(self, net, source, target):
        self.net, self.target = net, target
        here = target(net.y, net.c)
        self.first = net.send(source, here, net.sibling)
        self.across = net.send(source, here, net.by_y)

    def forward(self):
        self.across.wait_recv()
        landed = self.target(flip(self.net.y), self.net.c)
        self.second = self.net.send(landed, landed, self.net.sibling)

    def wait(self):
        self.first.wait_recv()
        self.second.wait_recv()

    def free(self):
        for copy in (self.first, self.across, self.second):
            copy.wait_send()
            self.net.drop(copy)


class Locals:
    def __init__(self, sems):
        self.sems, self.used, self.waiting = sems, 0, []

    def start(self, source, target):
        copy = pltpu.make_async_copy(source, target, self.sems.at[self.used])
        self.used += 1
        copy.start()
        return copy

    def put(self, source, target):
        self.waiting.append(self.start(source, target))

    def finish(self):
        for copy in self.waiting:
            copy.wait()


UP, DOWN, PAIR = (0, 1, 2)
LENGTH = 576
FIRST = 352


class Sum:
    def __init__(self, r, net, name, kind):
        self.net, self.kind, self.half = net, kind, FIRST
        for part in ("grads", "near_a", "near_b", "next_a", "next_b", "own", "third"):
            setattr(self, part, getattr(r, name + "_" + part))
        if kind == DOWN:
            self.across = getattr(r, name + "_across")
        else:
            self.right = getattr(r, name + "_right")
        self.shared = []

    def give(self, kept, step, columns, other):
        own = self.right.at[rows_of(self.net.b), :]
        if other is None:
            own[...] = columns
        else:
            kept[step] = columns
            self.shared.append(self.net.send(kept.at[step], own, other))

    def share_pairs(self, pairs):
        own = self.right.at[rows_of(self.net.b), :]
        for index, other in self.net.order():
            if other is None:
                own[...] = pairs[index]
            else:
                self.shared.append(self.net.send(pairs.at[index], own, other))

    def free(self, copies):
        for copy in copies:
            copy.wait_send()
            self.net.drop(copy)

    def free_shared(self):
        self.free(self.shared)

    def share_rows(self, turned):
        net = self.net
        own = pl.ds(pl.multiple_of(192 * net.b, 64), 192)
        self.across[:, lanes_of(net.b)] = turned[own, :]
        for index, other in self.net.order()[:3]:
            rows = pl.ds(pl.multiple_of(192 * index, 64), 192)
            self.shared.append(net.send(turned.at[rows, :], self.across.at[:, lanes_of(net.b)], other))

    def wait_shared(self):
        for copy in self.shared:
            copy.wait_recv()

    def place(self, product, tile):
        for block in range(8):
            at = pl.ds(pl.multiple_of(96 * tile, 16), 96)
            self.grads[block % 2, (block // 2) % 2, block // 4, at, :] = product[96 * block : 96 * block + 96].astype(BF)

    def product(self, left, second):
        self.wait_shared()
        if self.kind == DOWN:

            @pl.loop(0, 8)
            def _(block):
                lanes = pl.ds(pl.multiple_of(384 * block, 384), 384)
                product = mm(self.across[...], second[:, lanes])
                for tile in range(3):
                    self.grads[
                        lax.rem(block, 2), lax.rem(block // 2, 2), block // 4, 192 * tile : 192 * tile + 192, :
                    ] = product[:, 128 * tile : 128 * tile + 128].astype(BF)

        else:

            @pl.loop(0, 3 if self.kind == UP else 2)
            def _(chunk):
                lanes = pl.ds(pl.multiple_of(256 * chunk, 256), 256)
                product = mm(left[...], self.right[:, lanes])
                self.place(product[:, 0:128], 2 * chunk)
                self.place(product[:, 128:256], 2 * chunk + 1)

        if self.kind == PAIR:
            right = self.right[:, 512:768]
            first = lax.broadcasted_iota(jnp.int32, right.shape, 1) < 64
            zero = jnp.zeros_like(right)
            product = mm(left[...], jnp.where(first, right, zero)) + mm(second[...], jnp.where(first, zero, right))
            self.place(product[:, 0:128], 4)
            self.place(product[:, 128:256], 5)

        net, half = self.net, self.half
        self.moving = [
            net.send(self.grads.at[flip(net.x), :, :, 0:half, :], self.near_a, net.by_x),
            net.send(self.grads.at[:, flip(net.low), :, half:, :], self.near_b, net.by_low),
        ]

    def arrive(self):
        for copy in self.moving:
            copy.wait_recv()

    def second(self):
        net, half, grads = self.net, self.half, self.grads
        self.arrive()

        @pl.loop(0, 4)
        def _(step):
            one, two = step // 2, lax.rem(step, 2)
            grads[net.x, one, two, 0:half, :] += self.near_a[one, two]
            grads[one, net.low, two, half:, :] += self.near_b[one, two]

        self.moving = [
            net.send(grads.at[net.x, flip(net.low), :, 0:half, :], self.next_a, net.by_low),
            net.send(grads.at[flip(net.x), net.low, :, half:, :], self.next_b, net.by_x),
        ]

    def last(self):
        net, half, grads = self.net, self.half, self.grads
        self.arrive()

        @pl.loop(0, 2)
        def _(step):
            grads[net.x, net.low, step, 0:half, :] += self.next_a[step]
            grads[net.x, net.low, step, half:, :] += self.next_b[step]

        self.moving = [net.send(grads.at[net.x, net.low, flip(net.high)], self.third, net.by_high)]

    def end(self, near):
        net = self.net
        near.put(self.grads.at[net.x, net.low, net.high], self.own)
        self.arrive()


def sum_scratch(name, kind):
    made = {
        name + "_grads": ((2, 2, 2, LENGTH, 128), BF),
        name + "_near_a": ((2, 2, FIRST, 128), BF),
        name + "_near_b": ((2, 2, LENGTH - FIRST, 128), BF),
        name + "_next_a": ((2, FIRST, 128), BF),
        name + "_next_b": ((2, LENGTH - FIRST, 128), BF),
    }
    if kind == DOWN:
        made[name + "_across"] = ((192, 512), BF)
    else:
        made[name + "_right"] = ((512, WIDE), BF)
    return made


def pair_columns(wide, narrow, out):
    first = lax.broadcasted_iota(jnp.int32, (ROWS, BLOCK), 1) < 64

    def tile(at):
        at = at % (3 * WIDE)
        return wide[at // WIDE, :, at % WIDE : at % WIDE + BLOCK].astype(F32)

    def turned(at):
        return jnp.where(first, pltpu.roll(tile(at - BLOCK), 64, 1), pltpu.roll(tile(at), 64, 1))

    def thin(at):
        return narrow[:, at : at + BLOCK].astype(F32)

    def thin_turned(at):
        upper = pltpu.roll(thin(at), 64, 1)
        return jnp.where(first, pltpu.roll(thin(at - BLOCK), 64, 1), upper) if at else upper

    for block in range(4):
        start = 576 * block
        if block % 2 == 0:
            for part in range(4):
                out[block, :, BLOCK * part : BLOCK * part + BLOCK] = tile(start + BLOCK * part).astype(BF)
            lower, upper, rest = tile(start + 512), thin_turned(192 * block), thin_turned(192 * block + BLOCK)
        else:
            for part in range(4):
                out[block, :, BLOCK * part : BLOCK * part + BLOCK] = turned(start + 64 + BLOCK * part).astype(BF)
            lower, upper, rest = turned(start + 576), thin(192 * block - 64), thin(192 * block + 64)
        out[block, :, 512:640] = jnp.where(first, lower, upper).astype(BF)
        out[block, :, 640:768] = rest.astype(BF)


def turn(blocks, out):
    for block in range(4):
        out[:, BLOCK * block : BLOCK * block + BLOCK] = blocks[BLOCK * block : BLOCK * block + BLOCK, :].T


TABLES = ("cos_table", "sin_table")
KEPT = (
    "value_next",
    "qkv",
    "lse",
    "attended_full",
    "bend_b",
    "stream_b",
    "response",
    "query_a",
    "shifted",
    "value_a",
    "key_ext",
    "kernel_re",
    "kernel_im",
    "signal_re",
    "signal_im",
)
LEFTS = ("normed_a", "gated", "normed_b", "active_b", "normed_c")


def kernel_a(r):
    net = Net(r.send_sem, r.recv_sem)
    near = Locals(r.local_sem)
    net.hello()
    wait = {}

    def fetch(*names):
        for name in names:
            wait[name] = near.start(getattr(r, name + "_hbm"), getattr(r, name))

    thirds = []
    for index in (2, 0, 1):
        lanes = slice(WIDE * index, WIDE * index + WIDE)
        thirds.append(near.start(r.mixer_in_hbm.at[:, lanes], r.mixer_in.at[:, lanes]))
    r.ends[0] = r.doc_lengths[0, 0]
    r.ends[1] = r.ends[0] + r.doc_lengths[0, 1]
    r.ends[2] = r.ends[1] + r.doc_lengths[0, 2]

    def keep(*names):
        for name in names:
            near.put(getattr(r, name), getattr(r, name + "_kept"))

    gathers = []

    def gather(name):
        all_of = getattr(r, name + "_all")
        mine = getattr(r, name)
        near.put(mine, all_of.at[rows_of(net.b), :])
        gathers.append(Gather(net, mine, lambda y, c: all_of.at[rows_of(2 * y + c), :]))

    me = net.s
    gain_a = r.mixer_norm_gain[...][None]
    net.ready()
    rim = Beside(net, r.tokens.at[0, 64:128, :], r.rim_in, 1)
    rim.start()

    @pl.when(me == 0)
    def _():
        r.rim_in[...] = jnp.zeros_like(r.rim_in)

    normal, _ = pieces(r.tokens[0].astype(F32))
    r.normed_a[...] = (normal * gain_a).astype(BF)
    gather("normed_a")
    thirds[0].wait()
    r.value_a[...] = mm(r.normed_a[...], r.mixer_in[:, 2 * WIDE :])
    r.value_low[...] = r.value_a[0:64, :].astype(BF)
    later = Beside(net, r.value_low, r.value_next, -1)
    later.start()

    @pl.when(me == RANKS - 1)
    def _():
        r.value_next[...] = jnp.zeros_like(r.value_next)

    thirds[1].wait()
    r.query_a[...] = mm(r.normed_a[...], r.mixer_in[:, 0:WIDE])
    keep("query_a", "value_a")
    thirds[2].wait()
    fetch("shift_taps", "mode_coef", "mode_rate", *TABLES, "phase_cos", "phase_sin", "mixer_out")
    fetch("up_first", "down_first", "project_in")
    r.key_ext[64:192, :] = mm(r.normed_a[...], r.mixer_in[:, WIDE : 2 * WIDE])
    rim.wait_recv()
    normal, _ = pieces(r.rim_in[...].astype(F32))
    r.key_ext[0:64, :] = mm((normal * gain_a).astype(BF), r.mixer_in[:, WIDE : 2 * WIDE])
    for name in ("shift_taps", "mode_coef", "mode_rate"):
        wait[name].wait()
    shift_forward(r.key_ext, r.shift_taps, None, r.shifted)
    r.product_low[...] = (r.shifted[...] * r.value_a[...]).astype(BF)
    go = net.spread(lambda block: r.product_low.at[:, lanes_of(block)], lambda rank: r.signal.at[rows_of(rank), :], True)
    go.start()
    go.own()
    keep("key_ext", "shifted")
    block = lanes_of(jnp.clip(me - 1, 0, OWNERS - 1))
    r.coef[...] = r.mode_coef[:, block]
    r.rate[...] = r.mode_rate[:, block]
    modes(r.coef, r.rate, r.mode_rows)
    for name in TABLES + ("phase_cos", "phase_sin"):
        wait[name].wait()
    transform_two(r, r.mode_rows[...], r.kernel_re, r.kernel_im)
    turned = r.kernel_re[...] * r.phase_cos[...] - r.kernel_im[...] * r.phase_sin[...]
    r.kernel_im[...] = r.kernel_im[...] * r.phase_cos[...] + r.kernel_re[...] * r.phase_sin[...]
    r.kernel_re[...] = turned
    keep("kernel_re", "kernel_im")
    transform(r, net, go, r.signal, r.signal_re, r.signal_im)
    back = net.spread(lambda rank: r.conv.at[rows_of(rank), :], lambda block: r.conv_home.at[:, lanes_of(block)], False)
    inverse(
        r,
        r.signal_re[...] * r.kernel_re[...] - r.signal_im[...] * r.kernel_im[...],
        r.signal_re[...] * r.kernel_im[...] + r.signal_im[...] * r.kernel_re[...],
        r.conv,
        back,
    )
    back.own()
    for name in ("mixer_out", "up_first", "down_first", "project_in"):
        wait[name].wait()
    back.wait_recv()
    r.response[...] = r.conv_home[...].astype(F32) + r.skip_gain[...][None] * (r.shifted[...] * r.value_a[...])
    r.gated[...] = (r.query_a[...] * r.response[...]).astype(BF)
    gather("gated")
    stream_b = r.tokens[0].astype(F32) + mm(r.gated[...], r.mixer_out[...])
    r.stream_b[...] = stream_b
    normal, _ = pieces(stream_b)
    r.normed_b[...] = (normal * r.gain_second[...][None]).astype(BF)
    gather("normed_b")
    r.stream_c[...] = stream_b
    for chunk in range(4):
        lanes = slice(WIDE * chunk, WIDE * chunk + WIDE)
        active, bend = gelu_parts(mm(r.normed_b[...], r.up_first[:, lanes]))
        r.bend_b[:, lanes] = bend.astype(BF)
        active = active.astype(BF)
        r.active_b[:, lanes] = active
        r.stream_c[...] += mm(active, r.down_first[lanes, :])
    normal, _ = pieces(r.stream_c[...])
    r.normed_c[...] = (normal * r.attention_norm_gain[...][None]).astype(BF)
    for index in range(3):
        r.mixed_c[index] = mm(r.normed_c[...], r.project_in[:, WIDE * index : WIDE * index + WIDE]).astype(BF)
    go = net.spread(lambda block: r.mixed_c.at[:, :, lanes_of(block)], lambda rank: r.qkv.at[:, rows_of(rank), :], True)
    go.start()
    go.own()
    keep("response", "stream_b", "bend_b")
    gather("active_b")
    gather("normed_c")
    for made in gathers[:3]:
        made.forward()
    turned = r.signal_re[...] * r.phase_cos[...] - r.signal_im[...] * r.phase_sin[...]
    r.signal_im[...] = -(r.signal_im[...] * r.phase_cos[...] + r.signal_re[...] * r.phase_sin[...])
    r.signal_re[...] = turned
    keep("signal_re", "signal_im")
    later.wait_recv()
    keep("value_next")
    go.wait_recv()
    keep("qkv")
    back = net.spread(lambda rank: r.attended_low.at[rows_of(rank), :], lambda block: r.attended.at[:, lanes_of(block)], False)
    for part in (3, 2, 1, 0):
        attention_forward(r, part)
        back.start(lambda rank, part=part: rank // 2 == part)
    back.own()
    keep("lse", "attended_full")
    for made in gathers[3:]:
        made.forward()
    back.wait_recv()
    for made in gathers:
        made.wait()
    net.finish()
    near.finish()


def kernel_b(r):
    net = Net(r.send_sem, r.recv_sem)
    near = Locals(r.local_sem)
    net.hello()
    wait = {}

    def fetch(name, into=None):
        wait[name] = near.start(getattr(r, name + "_hbm"), getattr(r, into or name))

    for name, into in (("project_out", "out_weight"), ("attended", "attended"), ("stream_c", "stream_c"), ("cotangent", "cotangent")):
        fetch(name, into)
    chunks = []
    for step, (index, other) in enumerate(net.order()):
        lanes = pl.ds(pl.multiple_of(WIDE * index, WIDE), WIDE)
        chunks.append(
            (
                near.start(r.up_second_hbm.at[:, lanes], r.up.at[:, lanes]),
                near.start(r.down_second_hbm.at[lanes, :], r.down.at[lanes, :]),
            )
        )
    r.ends[0] = r.doc_lengths[0, 0]
    r.ends[1] = r.ends[0] + r.doc_lengths[0, 1]
    r.ends[2] = r.ends[1] + r.doc_lengths[0, 2]
    up_d, down_d, pair_c = Sum(r, net, "up_d", UP), Sum(r, net, "down_d", DOWN), Sum(r, net, "pair_c", PAIR)
    up_b, down_b, pair_a = Sum(r, net, "up_b", UP), Sum(r, net, "down_b", DOWN), Sum(r, net, "pair_a", PAIR)
    own_rows = rows_of(net.b)

    gain_d = r.gain_fourth[...][None]
    for name in ("project_out", "attended", "stream_c", "cotangent"):
        wait[name].wait()
    stream_d = r.stream_c[...] + mm(r.attended[...], r.out_weight[...])
    normal, inverse_d = pieces(stream_d)
    normed_d = (normal * gain_d).astype(BF)
    r.layer_left[own_rows, :] = normed_d
    r.total[...] = stream_d
    r.turned[...] = r.cotangent[0].T
    r.pair_two[own_rows, :] = r.attended[...]
    net.ready()
    gather_d = Gather(net, r.layer_left.at[own_rows, :], lambda y, c: r.layer_left.at[rows_of(2 * y + c), :])
    down_d.share_rows(r.turned)
    spots = []
    for step, (index, other) in enumerate(net.order()):
        lanes = pl.ds(pl.multiple_of(WIDE * index, WIDE), WIDE)
        for copy in chunks[step]:
            copy.wait()
        if step == 3:
            for name in KEPT[:11]:
                fetch(name)
            fetch("project_in", "in_weight")
            fetch("normed_c_all", "pair_one")
            fetch("tokens")
            for name in ("shift_taps", "mode_coef", "mode_rate") + TABLES:
                fetch(name)
        raised = mm(r.layer_left[own_rows, :], r.up[:, lanes])
        active, slope = gelu_parts(raised)
        active = active.astype(BF)
        r.layer_second[own_rows, lanes] = active

        def spot(y, c, step=step):
            at = pl.ds(pl.multiple_of(WIDE * net.turn_of(step, y, c), WIDE), WIDE)
            return r.layer_second.at[rows_of(2 * y + c), at]

        spots.append(spot)
        slope = (slope * mm_nt(r.cotangent[0], r.down[lanes, :])).astype(BF)
        up_d.give(r.slopes, step, slope, other)
        back = mm_nt(slope, r.up[:, lanes])
        if step == 0:
            r.grad_d[...] = back
        else:
            r.grad_d[...] += back
    gathers = [Gather(net, spot(net.y, net.c), spot) for spot in spots]
    grad, gain_four = pieces_back(r.grad_d[...], normal, inverse_d, gain_d)
    grad = r.cotangent[0].astype(F32) + grad
    r.grad_d[...] = grad
    r.grad_d_low[...] = grad.astype(BF)
    r.att_grad_home[...] = mm_nt(r.grad_d_low[...], r.out_weight[...]).astype(BF)
    go = net.spread(lambda block: r.att_grad_home.at[:, lanes_of(block)], lambda rank: r.att_grad.at[rows_of(rank), :], True)
    go.start()
    go.own()
    gather_att = Gather(net, r.pair_two.at[own_rows, :], lambda y, c: r.pair_two.at[rows_of(2 * y + c), :])
    fetch("up_first", "up")
    fetch("mixer_out", "out_weight")

    r.key_grad[...] = jnp.zeros_like(r.key_grad)
    r.value_grad[...] = jnp.zeros_like(r.value_grad)
    gather_d.forward()
    for name in ("qkv", "lse", "attended_full"):
        wait[name].wait()
    gather_d.wait()
    turn(r.layer_left, r.turned_one)
    gather_d.free()
    fetch("normed_b_all", "layer_left")
    up_d.product(r.turned_one, None)
    go.wait_recv()
    back = net.spread(
        lambda rank: r.qkv_grad.at[:, rows_of(rank), :], lambda block: r.mixed_grad_c.at[:, :, lanes_of(block)], False
    )
    for part in (3, 2, 1, 0):
        attention_back(r, part)
        back.start(lambda rank, part=part: rank // 2 == part)
    back.own()
    for name, into in (
        ("kernel_re", "lse"),
        ("kernel_im", "attended_full"),
        ("signal_re", "query_grad"),
        ("signal_im", "key_grad"),
    ):
        fetch(name, into)
    up_d.second()
    r.block_out[0] = (r.total[...] + mm(r.layer_second[own_rows, :], r.down[...])).astype(BF)
    fetch("down_first", "down")
    for made in gathers:
        made.forward()
    for made in gathers:
        made.wait()
    down_d.product(None, r.layer_second)
    for made in gathers:
        made.free()
    fetch("active_b_all", "layer_second")
    up_d.last()

    normal, inverse_c = pieces(r.stream_c[...])
    wait["project_in"].wait()
    back.wait_recv()
    grad = mm_nt(r.mixed_grad_c[0], r.in_weight[:, 0:WIDE])
    for index in range(1, 3):
        grad = grad + mm_nt(r.mixed_grad_c[index], r.in_weight[:, WIDE * index : WIDE * index + WIDE])
    fetch("mixer_in", "in_weight")
    pair_columns(r.mixed_grad_c, r.grad_d_low, r.pairs)
    pair_c.share_pairs(r.pairs)
    grad, gain_three = pieces_back(grad, normal, inverse_c, r.attention_norm_gain[...][None])
    grad = grad + r.grad_d[...]
    r.total[...] = grad
    r.grad_c_low[...] = grad.astype(BF)
    down_d.free_shared()
    r.turned[...] = r.grad_c_low[...].T
    down_b.share_rows(r.turned)
    up_d.free_shared()
    wait["up_first"].wait()
    wait["down_first"].wait()
    wait["bend_b"].wait()
    for step, (index, other) in enumerate(net.order()):
        lanes = pl.ds(pl.multiple_of(WIDE * index, WIDE), WIDE)
        slope = (r.bend_b[:, lanes].astype(F32) * mm_nt(r.grad_c_low[...], r.down[lanes, :])).astype(BF)
        up_b.give(r.slopes, step, slope, other)
        part = mm_nt(slope, r.up[:, lanes])
        if step == 0:
            r.grad_b[...] = part
        else:
            r.grad_b[...] += part
    for name in ("stream_b", "response", "query_a", "shifted", "value_a", "key_ext", "mixer_out"):
        wait[name].wait()
    normal, inverse_b = pieces(r.stream_b[...])
    grad, gain_two = pieces_back(r.grad_b[...], normal, inverse_b, r.gain_second[...][None])
    grad = grad + r.total[...]
    r.grad_b[...] = grad
    r.grad_b_low[...] = grad.astype(BF)
    gated_grad = mm_nt(r.grad_b_low[...], r.out_weight[...])
    r.mixed_grad_a[0] = (gated_grad * r.response[...]).astype(BF)
    response_grad = gated_grad * r.query_a[...]
    r.response_grad[...] = response_grad
    r.response_grad_low[...] = response_grad.astype(BF)
    go = net.spread(
        lambda block: r.response_grad_low.at[:, lanes_of(block)], lambda rank: r.conv_grad.at[rows_of(rank), :], True
    )
    go.start()
    go.own()
    after = Beside(net, r.response_grad_low.at[0:64, :], r.response_next, -1)
    after.start()

    @pl.when(net.s == RANKS - 1)
    def _():
        r.response_next[...] = jnp.zeros_like(r.response_next)

    skip_part = jnp.sum(response_grad * (r.shifted[...] * r.value_a[...]), axis=0, keepdims=True)
    down_d.second()
    gather_att.forward()
    wait["normed_c_all"].wait()
    turn(r.pair_one, r.turned_one)
    gather_att.wait()
    turn(r.pair_two, r.turned_two)
    gather_att.free()
    fetch("normed_a_all", "pair_one")
    fetch("gated_all", "pair_two")
    pair_c.product(r.turned_one, r.turned_two)
    wait["active_b_all"].wait()
    down_b.product(None, r.layer_second)
    wait["normed_b_all"].wait()
    turn(r.layer_left, r.turned_one)
    up_d.end(near)

    for name in TABLES + ("kernel_re", "kernel_im", "signal_re", "signal_im"):
        wait[name].wait()
    kernel_re, kernel_im, signal_re, signal_im = r.lse, r.attended_full, r.query_grad, r.key_grad
    r.signal_grad[SPAN:, :] = jnp.zeros((64, BLOCK), BF)
    transform(r, net, go, r.conv_grad, r.grad_re, r.grad_im)
    back = net.spread(
        lambda rank: r.signal_grad.at[pl.ds(pl.multiple_of(ROWS * rank, ROWS), 192), :],
        lambda block: r.signal_grad_home.at[:, lanes_of(block)],
        False,
    )
    inverse(
        r,
        r.grad_re[...] * kernel_re[...] + r.grad_im[...] * kernel_im[...],
        r.grad_im[...] * kernel_re[...] - r.grad_re[...] * kernel_im[...],
        r.signal_grad,
        back,
    )
    back.own()
    up_b.product(r.turned_one, None)
    down_d.last()
    pair_c.second()
    down_b.second()
    after.wait_recv()
    for name in ("shift_taps", "mode_coef", "mode_rate", "value_next"):
        wait[name].wait()
    back.wait_recv()

    skip = r.skip_gain[...][None]
    signal_grad = r.signal_grad_home[0:ROWS, :].astype(F32) + skip * r.response_grad[...]
    r.grad_ext[0:ROWS, :] = signal_grad * r.value_a[...]
    r.mixed_grad_a[2] = (signal_grad * r.shifted[...]).astype(BF)
    signal_grad = r.signal_grad_home[ROWS:192, :].astype(F32) + skip * r.response_next[...].astype(F32)
    r.grad_ext[ROWS:192, :] = signal_grad * r.value_next[...].astype(F32)
    shift_back(r.grad_ext, r.key_ext, r.shift_taps, r.total, r.taps)
    r.mixed_grad_a[1] = r.total[...].astype(BF)
    pair_c.free_shared()
    pair_columns(r.mixed_grad_a, r.grad_b_low, r.pairs)
    pair_a.share_pairs(r.pairs)
    wait["mixer_in"].wait()
    wait["tokens"].wait()
    grad = mm_nt(r.mixed_grad_a[0], r.in_weight[:, 0:WIDE])
    for index in range(1, 3):
        grad = grad + mm_nt(r.mixed_grad_a[index], r.in_weight[:, WIDE * index : WIDE * index + WIDE])
    normal, inverse_a = pieces(r.tokens[0].astype(F32))
    grad, gain_one = pieces_back(grad, normal, inverse_a, r.mixer_norm_gain[...][None])
    r.token_grad[0] = r.grad_b[...] + grad

    gains = jnp.concatenate([gain_one, skip_part, gain_two, gain_three, gain_four, jnp.zeros((3, WIDE), F32)], axis=0)
    for block in range(4):
        r.small[block // 2, block % 2, 0:16, :] = r.taps[16 * block : 16 * block + 16, :]
        r.small[block // 2, block % 2, 16:24, :] = gains
    swap = net.send(r.small.at[:, flip(net.c)], r.small_c, net.sibling)
    re = r.grad_re[...] * signal_re[...] - r.grad_im[...] * signal_im[...]
    im = r.grad_re[...] * signal_im[...] + r.grad_im[...] * signal_re[...]
    inverse(r, re, im, r.value_grad)
    block = lanes_of(jnp.clip(net.s - 1, 0, OWNERS - 1))
    r.coef[...] = r.mode_coef[:, block]
    r.rate[...] = r.mode_rate[:, block]
    wait["normed_a_all"].wait()
    turn(r.pair_one, r.turned_one)
    wait["gated_all"].wait()
    turn(r.pair_two, r.turned_two)
    up_b.second()
    swap.wait_recv()
    r.small[:, net.c] += r.small_c[...]
    swap = net.send(r.small.at[flip(net.y), net.c], r.small_swap.at[0], net.by_y)
    pair_c.last()
    down_b.last()
    pair_a.product(r.turned_one, r.turned_two)
    modes_back(r.coef, r.rate, r.value_grad, r.mode_part.at[0, 0:64], r.mode_part.at[0, 64:128])
    mode = net.send(r.mode_part.at[0], r.mode_swap.at[0], net.sibling)
    swap.wait_recv()
    r.small_sum[0] = r.small[net.y, net.c] + r.small_swap[0]
    swap = net.send(r.small_sum.at[0], r.small_swap.at[1], net.by_x)
    up_b.last()
    mode.wait_recv()
    r.mode_part[1] = r.mode_part[0] + r.mode_swap[0]
    mode = net.send(r.mode_part.at[1], r.mode_swap.at[1], net.by_y)
    pair_a.second()
    mode.wait_recv()
    r.mode_part[2] = r.mode_part[1] + r.mode_swap[1]
    back = net.spread(lambda rank: r.mode_part.at[2], lambda block: r.mode_home.at[:, lanes_of(block)], False)
    back.start()
    back.own()
    swap.wait_recv()
    r.small_sum[1] = r.small_sum[0] + r.small_swap[1]
    swap = net.send(r.small_sum.at[1], r.small_swap.at[2], net.by_low)
    pair_a.last()
    swap.wait_recv()
    r.small_sum[2] = r.small_sum[1] + r.small_swap[2]
    swap = net.send(r.small_sum.at[2], r.small_swap.at[3], net.by_high)
    down_d.end(near)
    pair_c.end(near)
    down_b.end(near)
    turn_back = lax.rem(WIDE - 96 * net.s, WIDE)
    back.wait_recv()
    r.mode_out[...] = pltpu.roll(r.mode_home[...], turn_back, 1)[:, 0:128]
    swap.wait_recv()
    r.small_out[...] = pltpu.roll(r.small_sum[2] + r.small_swap[3], turn_back, 1)[:, 0:128]
    up_b.end(near)
    pair_a.end(near)
    net.finish()
    near.finish()


def kernel_z(*refs):
    block_in, token_in, mode, small = refs[:4]
    sums = refs[4:16]
    (
        block_out,
        token_grad,
        gain_one,
        mixer_in,
        taps,
        coef,
        rate,
        skip,
        mixer_out,
        gain_two,
        up_first,
        down_first,
        gain_three,
        project_in,
        project_out,
        gain_four,
        up_second,
        down_second,
    ) = refs[16:]
    block_out[...] = block_in[...]
    token_grad[...] = token_in[...]
    taps[...] = small[0:16, 0:96]
    for at, out in enumerate((gain_one, skip, gain_two, gain_three, gain_four)):
        out[...] = small[16 + at, 0:96]
    coef[...] = mode[0:64, 0:96]
    rate[...] = mode[64:128, 0:96]

    def block(index, first, count):
        rows = slice(first, first + count)
        return sums[2 * index][rows, :].astype(F32) + sums[2 * index + 1][rows, :].astype(F32)

    for index, up, down in ((0, up_second, down_second), (3, up_first, down_first)):
        for tile in range(6):
            up[:, 128 * tile : 128 * tile + 128] = block(index, 96 * tile, 96)
        for tile in range(3):
            down[:, 128 * tile : 128 * tile + 128] = block(index + 1, 192 * tile, 192)
    for index, wide, narrow in ((2, project_in, project_out), (5, mixer_in, mixer_out)):
        for tile in range(4):
            wide[:, 128 * tile : 128 * tile + 128] = block(index, 96 * tile, 96)
        mixed = block(index, 384, 96)
        wide[:, 512:576] = mixed[:, 0:64]
        narrow[:, 0:64] = mixed[:, 64:128]
        narrow[:, 64:192] = block(index, 480, 96)


class Refs:
    pass


def call(body, identity, inputs, hbm, smem, outs, hbm_outs, scratch, semaphores):
    names = list(inputs) + [name + "_hbm" for name in hbm] + list(smem) + list(outs) + list(hbm_outs) + list(scratch)
    names += ["ends", "send_sem", "recv_sem", "local_sem"]

    def run(*refs):
        r = Refs()
        for name, ref in zip(names, refs):
            setattr(r, name, ref)
        body(r)

    vmem = pl.BlockSpec(memory_space=pltpu.VMEM)
    results = pl.pallas_call(
        run,
        out_shape=[jax.ShapeDtypeStruct(shape, kind) for shape, kind in (*outs.values(), *hbm_outs.values())],
        in_specs=[vmem] * len(inputs)
        + [pl.BlockSpec(memory_space=pl.ANY)] * len(hbm)
        + [pl.BlockSpec(memory_space=pltpu.SMEM)] * len(smem),
        out_specs=[vmem] * len(outs) + [pl.BlockSpec(memory_space=pl.ANY)] * len(hbm_outs),
        scratch_shapes=[pltpu.VMEM(shape, kind) for shape, kind in scratch.values()]
        + [pltpu.SMEM((3,), jnp.int32)]
        + [pltpu.SemaphoreType.DMA((semaphores[0],)), pltpu.SemaphoreType.DMA((semaphores[0],))]
        + [pltpu.SemaphoreType.DMA((semaphores[1],))],
        compiler_params=pltpu.CompilerParams(
            collective_id=identity, has_side_effects=True, vmem_limit_bytes=VMEM_BYTES
        ),
    )(*inputs.values(), *hbm.values(), *smem.values())
    return dict(zip((*outs, *hbm_outs), results))


VMEM_BYTES = 66_900_000


def odd_tables():
    odd = 2 * np.arange(SPAN, dtype=np.int64) + 1
    angle = (np.outer(odd, odd) % (8 * SPAN)) * (math.pi / (4 * SPAN))
    phase = (odd * (math.pi / (4 * SPAN)))[:, None] * np.ones((1, BLOCK))
    tables = {
        "cos_table": jnp.asarray(np.cos(angle).astype(ml_dtypes.bfloat16)),
        "sin_table": jnp.asarray(np.sin(angle).astype(ml_dtypes.bfloat16)),
    }
    return tables, jnp.asarray(np.cos(phase), F32), jnp.asarray(np.sin(phase), F32)


def shards_fast(
    tokens,
    doc_lengths,
    mixer_norm_gain,
    mixer_in,
    shift_taps,
    mode_coef,
    mode_rate,
    skip_gain,
    mixer_out,
    gain_second,
    up_first,
    down_first,
    attention_norm_gain,
    project_in,
    project_out,
    gain_fourth,
    up_second,
    down_second,
    cotangent,
):
    tables, phase_cos, phase_sin = odd_tables()
    home, thrice, tall = (ROWS, WIDE), (3, ROWS, WIDE), (ROWS, 4 * WIDE)
    span = (SPAN, BLOCK)
    kept = dict(
        value_next=((64, WIDE), BF),
        query_a=(home, F32),
        value_a=(home, F32),
        key_ext=((192, WIDE), F32),
        shifted=(home, F32),
        response=(home, F32),
        stream_b=(home, F32),
        bend_b=(tall, BF),
        qkv=((3, *span), BF),
        lse=(span, F32),
        attended_full=(span, F32),
        kernel_re=(span, F32),
        kernel_im=(span, F32),
        signal_re=(span, F32),
        signal_im=(span, F32),
    )
    lefts = dict(normed_a=(home, BF), gated=(home, BF), normed_b=(home, BF), active_b=(tall, BF), normed_c=(home, BF))
    modes_scratch = dict(
        coef=((64, BLOCK), F32),
        rate=((64, BLOCK), F32),
        shift_taps=((64, WIDE), F32),
        mode_coef=((64, WIDE), F32),
        mode_rate=((64, WIDE), F32),
    )
    packs = dict(pack_re=((SPAN, 256), BF), pack_im=((SPAN, 256), BF))
    table_scratch = dict(cos_table=((SPAN, SPAN), BF), sin_table=((SPAN, SPAN), BF))
    a = call(
        kernel_a,
        0,
        dict(
            tokens=tokens,
            mixer_norm_gain=mixer_norm_gain,
            skip_gain=skip_gain,
            gain_second=gain_second,
            attention_norm_gain=attention_norm_gain,
        ),
        dict(
            mixer_in=mixer_in,
            shift_taps=shift_taps,
            mode_coef=mode_coef,
            mode_rate=mode_rate,
            **tables,
            phase_cos=phase_cos,
            phase_sin=phase_sin,
            mixer_out=mixer_out,
            up_first=up_first,
            down_first=down_first,
            project_in=project_in,
        ),
        dict(doc_lengths=doc_lengths),
        dict(stream_c=(home, F32), attended=(home, BF)),
        dict(
            **{name + "_kept": made for name, made in kept.items()},
            **{name + "_all": ((4 * shape[0], shape[1]), kind) for name, (shape, kind) in lefts.items()},
        ),
        dict(
            **kept,
            **lefts,
            **modes_scratch,
            **packs,
            rim_in=((64, WIDE), BF),
            **table_scratch,
            phase_cos=(span, F32),
            phase_sin=(span, F32),
            value_low=((64, WIDE), BF),
            product_low=(home, BF),
            signal=(span, BF),
            mode_rows=(span, F32),
            conv=(span, BF),
            conv_home=(home, BF),
            mixed_c=(thrice, BF),
            attended_low=(span, BF),
            mixer_in=((WIDE, 3 * WIDE), BF),
            mixer_out=((WIDE, WIDE), BF),
            up_first=((WIDE, 4 * WIDE), BF),
            down_first=((4 * WIDE, WIDE), BF),
            project_in=((WIDE, 3 * WIDE), BF),
        ),
        (48, 40),
    )
    kinds = dict(up_d=UP, down_d=DOWN, pair_c=PAIR, up_b=UP, down_b=DOWN, pair_a=PAIR)
    sum_outs, sums = {}, {}
    for name, kind in kinds.items():
        sum_outs[name + "_own"] = ((LENGTH, 128), BF)
        sum_outs[name + "_third"] = ((LENGTH, 128), BF)
        sums.update(sum_scratch(name, kind))
    b = call(
        kernel_b,
        1,
        dict(
            mixer_norm_gain=mixer_norm_gain,
            skip_gain=skip_gain,
            gain_second=gain_second,
            attention_norm_gain=attention_norm_gain,
            gain_fourth=gain_fourth,
        ),
        dict(
            project_out=project_out,
            attended=a["attended"],
            stream_c=a["stream_c"],
            cotangent=cotangent,
            tokens=tokens,
            up_second=up_second,
            down_second=down_second,
            **{name: a[name + "_kept"] for name in kept},
            **{name + "_all": a[name + "_all"] for name in lefts},
            **tables,
            shift_taps=shift_taps,
            mode_coef=mode_coef,
            mode_rate=mode_rate,
            project_in=project_in,
            up_first=up_first,
            down_first=down_first,
            mixer_out=mixer_out,
            mixer_in=mixer_in,
        ),
        dict(doc_lengths=doc_lengths),
        dict(
            block_out=((1, *home), BF),
            token_grad=((1, *home), F32),
            mode_out=((128, 128), F32),
            small_out=((24, 128), F32),
        ),
        sum_outs,
        dict(
            **{name: made for name, made in kept.items() if not name.startswith(("kernel", "signal"))},
            **modes_scratch,
            **packs,
            **table_scratch,
            **sums,
            attended=(home, BF),
            stream_c=(home, F32),
            cotangent=((1, *home), BF),
            tokens=((1, *home), BF),
            up=((WIDE, 4 * WIDE), BF),
            down=((4 * WIDE, WIDE), BF),
            in_weight=((WIDE, 3 * WIDE), BF),
            out_weight=((WIDE, WIDE), BF),
            layer_left=((512, WIDE), BF),
            layer_second=((512, 4 * WIDE), BF),
            pair_one=((512, WIDE), BF),
            pair_two=((512, WIDE), BF),
            turned_one=((WIDE, 512), BF),
            turned_two=((WIDE, 512), BF),
            turned=((WIDE, ROWS), BF),
            slopes=(thrice, BF),
            pairs=((4, *home), BF),
            total=(home, F32),
            grad_d=(home, F32),
            grad_d_low=(home, BF),
            att_grad_home=(home, BF),
            att_grad=(span, BF),
            query_grad=(span, F32),
            key_grad=(span, F32),
            value_grad=(span, F32),
            qkv_grad=((3, *span), BF),
            mixed_grad_c=(thrice, BF),
            grad_c_low=(home, BF),
            grad_b=(home, F32),
            grad_b_low=(home, BF),
            mixed_grad_a=(thrice, BF),
            response_grad=(home, F32),
            response_grad_low=(home, BF),
            conv_grad=(span, BF),
            grad_re=(span, F32),
            grad_im=(span, F32),
            signal_grad=((SPAN + 64, BLOCK), BF),
            signal_grad_home=((192, WIDE), BF),
            response_next=((64, WIDE), BF),
            grad_ext=((192, WIDE), F32),
            taps=((64, WIDE), F32),
            small=((2, 2, 24, WIDE), F32),
            small_c=((2, 24, WIDE), F32),
            small_swap=((4, 24, WIDE), F32),
            small_sum=((3, 24, WIDE), F32),
            mode_part=((3, 128, 128), F32),
            mode_swap=((2, 128, 128), F32),
            mode_home=((128, WIDE), F32),
        ),
        (160, 64),
    )
    vmem = pl.BlockSpec(memory_space=pltpu.VMEM)
    given = [b[name] for name in ("block_out", "token_grad", "mode_out", "small_out")]
    for name in kinds:
        given += [b[name + "_own"], b[name + "_third"]]
    gain = ((96,), F32)
    wide, narrow, up, down, mode = ((96, 576), F32), ((96, 192), F32), ((96, 768), F32), ((192, 384), F32), ((64, 96), F32)
    shapes = (
        ((1, *home), BF),
        ((1, *home), F32),
        gain,
        wide,
        ((16, 96), F32),
        mode,
        mode,
        gain,
        narrow,
        gain,
        up,
        down,
        gain,
        wide,
        narrow,
        gain,
        up,
        down,
    )
    results = pl.pallas_call(
        kernel_z,
        out_shape=[jax.ShapeDtypeStruct(shape, kind) for shape, kind in shapes],
        in_specs=[vmem] * len(given),
        out_specs=[vmem] * len(shapes),
    )(*given)
    return tuple(result.T if result.shape == (192, 384) else result for result in results)


def solution(mesh):
    in_specs = (
        P("batch", "seq", None),
        P("batch", None),
        P(),
        P(),
        P(),
        P(),
        P(),
        P(),
        P(),
        P(),
        P(),
        P(),
        P(),
        P(),
        P(),
        P(),
        P(),
        P(),
        P("batch", "seq", None),
    )
    out_specs = (
        P("batch", "seq", None),
        P("batch", "seq", None),
        P("seq"),
        P("seq", "batch"),
        P("batch", "seq"),
        P(None, "seq"),
        P(None, "seq"),
        P("seq"),
        P("seq", "batch"),
        P("seq"),
        P("seq", "batch"),
        P("seq", "batch"),
        P("seq"),
        P("seq", "batch"),
        P("seq", "batch"),
        P("seq"),
        P("seq", "batch"),
        P("seq", "batch"),
    )
    fast = mesh.shape["seq"] == RANKS and mesh.shape["batch"] == 4
    return jax.shard_map(shards_fast if fast else shards, mesh=mesh, in_specs=in_specs, out_specs=out_specs, check_vma=False)
```

```python
import math

import jax
import jax.numpy as jnp
import ml_dtypes
import numpy as np
from jax import lax
from jax.experimental import pallas as pl
from jax.experimental.pallas import tpu as pltpu
from jax.sharding import PartitionSpec as P

HEADS = 12


HIGH = lax.Precision.HIGHEST
NEGATIVE = -1e30


def shifted_2(value, axis, steps):
    count = lax.axis_size(axis)
    leading, last = (max(0, -steps), min(count, count - steps))
    return lax.ppermute(value, axis, [(source, source + steps) for source in range(leading, last)])


def shortened(x):

    def short(part):
        return part.astype(jnp.bfloat16) if part.dtype == jnp.float32 else part

    return jax.tree.map(short, x)


def mult(form, left, right):
    return jnp.einsum(form, left, right, precision=HIGH, preferred_element_type=jnp.float32)


def norm_pieces(value):
    row_mean = jnp.mean(value, axis=-1, keepdims=True)
    cent = value - row_mean
    inverse_deviation = lax.rsqrt(jnp.mean(cent * cent, axis=-1, keepdims=True) + 1e-05)
    return (cent * inverse_deviation, inverse_deviation)


def norm_backward(incoming_gradient, centered_normalized, inverse_deviation, gain_vector):
    gain_share = jnp.sum(incoming_gradient * centered_normalized, axis=0)
    scaled_rows = incoming_gradient * gain_vector
    inner_product = jnp.mean(scaled_rows, axis=-1, keepdims=True)
    cross_term = jnp.mean(scaled_rows * centered_normalized, axis=-1, keepdims=True)
    return (
        inverse_deviation * (scaled_rows - inner_product - centered_normalized * cross_term),
        gain_share,
    )


def segment_of(where, ends):
    return jnp.sum((where[:, None] >= ends[None, :]).astype(jnp.int32), axis=1)


def allowed(query_pos, key_pos, ends):
    same = segment_of(query_pos, ends)[:, None] == segment_of(key_pos, ends)[None, :]
    return (key_pos[None, :] <= query_pos[:, None]) & same


def kernel_rows(coef, rate, times):

    def step(total, pair):
        scale, decay = pair
        return (total + scale[:, None] * jnp.exp(-decay[:, None] * times[None, :]), None)

    start = jnp.zeros((coef.shape[1], times.shape[0]), jnp.float32)
    return lax.scan(step, start, (coef, rate))[0]


def kernel_grads(coef, rate, times, incoming_gradient):

    def step(carry, pair):
        scale, decay = pair
        fall = incoming_gradient * jnp.exp(-decay[:, None] * times[None, :])
        return (carry, (jnp.sum(fall, axis=1), -scale * jnp.sum(fall * times[None, :], axis=1)))

    return lax.scan(step, jnp.zeros((), jnp.float32), (coef, rate))[1]


def angle_pair(left, right, period):
    turns = left[:, None] * right[None, :] % period
    angle = turns.astype(jnp.float32) * (2.0 * math.pi / period)
    return (jnp.cos(angle), jnp.sin(angle))


def dft_tables(blocks, rows):
    wide = 2 * blocks
    block_ids = jnp.arange(blocks, dtype=jnp.int32)
    wide_ids = jnp.arange(wide, dtype=jnp.int32)
    row_ids = jnp.arange(rows, dtype=jnp.int32)
    return (
        angle_pair(block_ids, wide_ids, wide),
        angle_pair(wide_ids, row_ids, wide * rows),
        angle_pair(row_ids, row_ids, rows),
    )


def forward_spectrum(signal, tables, blocks, rows):
    (cos_one, sin_one), (cos_two, sin_two), (cos_three, sin_three) = tables
    folded = signal.reshape(signal.shape[0], blocks, rows)
    first_re = mult("cpr,pf->cfr", folded, cos_one)
    first_im = -mult("cpr,pf->cfr", folded, sin_one)
    turned_re = first_re * cos_two + first_im * sin_two
    turned_im = first_im * cos_two - first_re * sin_two
    spec_re = mult("cfr,rk->cfk", turned_re, cos_three) + mult("cfr,rk->cfk", turned_im, sin_three)
    spec_im = mult("cfr,rk->cfk", turned_im, cos_three) - mult("cfr,rk->cfk", turned_re, sin_three)
    return (spec_re, spec_im)


def inverse_signal(spec_re, spec_im, tables, blocks, rows):
    (cos_one, sin_one), (cos_two, sin_two), (cos_three, sin_three) = tables
    inner_re = mult("cfk,rk->cfr", spec_re, cos_three) - mult("cfk,rk->cfr", spec_im, sin_three)
    inner_im = mult("cfk,rk->cfr", spec_im, cos_three) + mult("cfk,rk->cfr", spec_re, sin_three)
    turned_re = inner_re * cos_two - inner_im * sin_two
    turned_im = inner_im * cos_two + inner_re * sin_two
    result_value = mult("cfr,pf->cpr", turned_re, cos_one) - mult("cfr,pf->cpr", turned_im, sin_one)
    return result_value.reshape(spec_re.shape[0], blocks * rows) / (2.0 * blocks * rows)


def attend_block(state, query, query_pos, key_block, value_block, key_pos, ends, scale):
    top, mass, accum = state
    scores = (
        jnp.einsum("qhd,khd->hqk", query, key_block, preferred_element_type=jnp.float32) * scale
    )
    mask = allowed(query_pos, key_pos, ends)[None]
    newtop = jnp.maximum(top, jnp.max(jnp.where(mask, scores, NEGATIVE), axis=-1))
    weights = jnp.where(mask, jnp.exp(scores - newtop[:, :, None]), 0.0)
    factor = jnp.exp(top - newtop)
    mass = mass * factor + jnp.sum(weights, axis=-1)
    accum = accum * factor[:, :, None] + jnp.einsum(
        "hqk,khd->hqd", weights, value_block.astype(jnp.float32), preferred_element_type=jnp.float32
    )
    return (newtop, mass, accum)


def score_grads(
    query, grads, lse_rows, delta_rows, query_pos, key_block, value_block, key_pos, ends, scale
):
    scores = (
        jnp.einsum("qhd,khd->hqk", query, key_block, preferred_element_type=jnp.float32) * scale
    )
    mask = allowed(query_pos, key_pos, ends)[None]
    probs = jnp.where(mask, jnp.exp(scores - lse_rows[:, :, None]), 0.0)
    dots = jnp.einsum("qhd,khd->hqk", grads, value_block, preferred_element_type=jnp.float32)
    return (probs, (probs * (dots - delta_rows[:, :, None])).astype(jnp.bfloat16))


def query_back(
    query, grads, lse_rows, delta_rows, query_pos, key_block, value_block, key_pos, ends, scale
):
    score_grad = score_grads(
        query, grads, lse_rows, delta_rows, query_pos, key_block, value_block, key_pos, ends, scale
    )[1]
    return (
        jnp.einsum("hqk,khd->qhd", score_grad, key_block, preferred_element_type=jnp.float32)
        * scale
    )


def key_back(
    query, grads, lse_rows, delta_rows, query_pos, key_block, value_block, key_pos, ends, scale
):
    probs, score_grad = score_grads(
        query, grads, lse_rows, delta_rows, query_pos, key_block, value_block, key_pos, ends, scale
    )
    key_part = (
        jnp.einsum("hqk,qhd->khd", score_grad, query, preferred_element_type=jnp.float32) * scale
    )
    value_part = jnp.einsum(
        "hqk,qhd->khd", probs, grads.astype(jnp.float32), preferred_element_type=jnp.float32
    )
    return (key_part, value_part)


def scan_keys(carry, keys, values, update):
    count = keys.shape[0]
    width = keys.shape[1]
    head_size = width // HEADS
    step = math.gcd(count, 1024)
    firsts = step * jnp.arange(count // step, dtype=jnp.int32)

    def inner_product(state, item):
        key_block, value_block, first = item
        key_pos = first + jnp.arange(step, dtype=jnp.int32)
        return (update(state, key_block, value_block, key_pos), None)

    items = (
        keys.reshape(count // step, step, HEADS, head_size),
        values.reshape(count // step, step, HEADS, head_size),
        firsts,
    )
    return lax.scan(inner_product, carry, items)[0]


def feed_forward(residual_stream, gain_vector, w_up, w_down):
    centered_normalized, inverse_deviation = norm_pieces(residual_stream)
    normed_rows = (centered_normalized * gain_vector).astype(jnp.bfloat16)
    raised_rows = jnp.dot(normed_rows, w_up, preferred_element_type=jnp.float32)
    active_tokens = jax.nn.gelu(raised_rows).astype(jnp.bfloat16)
    result_value = residual_stream + jnp.dot(
        active_tokens, w_down, preferred_element_type=jnp.float32
    )
    return (
        result_value,
        (centered_normalized, inverse_deviation, normed_rows, raised_rows, active_tokens),
    )


def feed_back(incoming_gradient, saved_residuals, gain_vector, w_up, w_down):
    centered_normalized, inverse_deviation, normed_rows, raised_rows, active_tokens = (
        saved_residuals
    )
    grad_low = incoming_gradient.astype(jnp.bfloat16)
    down_part = jnp.einsum("tf,td->fd", active_tokens, grad_low, preferred_element_type=jnp.float32)
    active_grad = jnp.einsum("td,fd->tf", grad_low, w_down, preferred_element_type=jnp.float32)
    slope = jax.vjp(jax.nn.gelu, raised_rows)[1](active_grad)[0].astype(jnp.bfloat16)
    up_part = jnp.einsum("td,tf->df", normed_rows, slope, preferred_element_type=jnp.float32)
    normed_gradient = jnp.einsum("tf,df->td", slope, w_up, preferred_element_type=jnp.float32)
    input_gradient, gain_share = norm_backward(
        normed_gradient, centered_normalized, inverse_deviation, gain_vector
    )
    return (incoming_gradient + input_gradient, gain_share, up_part, down_part)


def shards(
    tokens,
    doc_lengths,
    mixer_norm_gain,
    mixer_in,
    shift_taps,
    mode_coef,
    mode_rate,
    skip_gain,
    mixer_out,
    gain_second,
    up_first,
    down_first,
    attention_norm_gain,
    project_in,
    project_out,
    gain_fourth,
    up_second,
    down_second,
    cotangent,
):
    rows = tokens.shape[1]
    width = tokens.shape[2]
    blocks = lax.axis_size("seq")
    rank = lax.axis_index("seq")
    total = rows * blocks
    head_size = width // HEADS
    scale = head_size ** (-0.5)
    lags = shift_taps.shape[0]
    channels = width // blocks
    ends = jnp.cumsum(doc_lengths[0])
    here = rank * rows + jnp.arange(rows, dtype=jnp.int32)
    residual_stream = tokens[0].astype(jnp.float32)
    mixer_centered_normalized, mixer_inverse_deviation = norm_pieces(residual_stream)
    mixer_normed_rows = (mixer_centered_normalized * mixer_norm_gain).astype(jnp.bfloat16)
    mixed_a = jnp.dot(mixer_normed_rows, mixer_in, preferred_element_type=jnp.float32)
    query_a = mixed_a[:, :width]
    key_a = mixed_a[:, width : 2 * width]
    value_a = mixed_a[:, 2 * width :]
    rim = shifted_2(key_a[rows - (lags - 1) :].astype(jnp.bfloat16), "seq", 1).astype(jnp.float32)
    key_ext = jnp.concatenate([rim, key_a], axis=0)
    shifted = jnp.zeros_like(key_a)
    for lag in range(lags):
        shifted = shifted + shift_taps[lag] * key_ext[lags - 1 - lag : lags - 1 - lag + rows]
    product_kv = shifted * value_a
    channel_in = lax.all_to_all(
        product_kv.T.reshape(blocks, channels, rows).astype(jnp.bfloat16),
        "seq",
        split_axis=0,
        concat_axis=2,
        tiled=True,
    ).astype(jnp.float32)[0]
    times = jnp.arange(total, dtype=jnp.int32).astype(jnp.float32)
    coef_here = lax.dynamic_slice_in_dim(mode_coef, rank * channels, channels, 1)
    rate_here = lax.dynamic_slice_in_dim(mode_rate, rank * channels, channels, 1)
    kernel_here = kernel_rows(coef_here, rate_here, times)
    tables = dft_tables(blocks, rows)
    sig_re, sig_im = forward_spectrum(channel_in, tables, blocks, rows)
    ker_re, ker_im = forward_spectrum(kernel_here, tables, blocks, rows)
    conv_chan = inverse_signal(
        sig_re * ker_re - sig_im * ker_im, sig_re * ker_im + sig_im * ker_re, tables, blocks, rows
    )
    conv_home = lax.all_to_all(
        conv_chan.reshape(1, channels, total).astype(jnp.bfloat16),
        "seq",
        split_axis=2,
        concat_axis=0,
        tiled=True,
    ).astype(jnp.float32)
    response = conv_home.reshape(width, rows).T + skip_gain * product_kv
    gated = (query_a * response).astype(jnp.bfloat16)
    stream_b = residual_stream + jnp.dot(gated, mixer_out, preferred_element_type=jnp.float32)
    attention_residual_stream, saved_b = feed_forward(stream_b, gain_second, up_first, down_first)
    attention_centered_normalized, attention_inverse_deviation = norm_pieces(
        attention_residual_stream
    )
    attention_normed_rows = (attention_centered_normalized * attention_norm_gain).astype(
        jnp.bfloat16
    )
    mixed_c = jnp.dot(attention_normed_rows, project_in, preferred_element_type=jnp.float32).astype(
        jnp.bfloat16
    )
    query_flat = mixed_c[:, :width]
    key_flat = mixed_c[:, width : 2 * width]
    value_flat = mixed_c[:, 2 * width :]
    query_c = query_flat.reshape(rows, HEADS, head_size)
    key_heads = key_flat.reshape(rows, HEADS, head_size)
    value_heads = value_flat.reshape(rows, HEADS, head_size)

    def forward_update(state, key_block, value_block, key_pos):
        return attend_block(state, query_c, here, key_block, value_block, key_pos, ends, scale)

    begin = (
        jnp.full((HEADS, rows), NEGATIVE, jnp.float32),
        jnp.zeros((HEADS, rows), jnp.float32),
        jnp.zeros((HEADS, rows, head_size), jnp.float32),
    )
    piece = (
        lax.all_gather(key_flat, "seq", axis=0, tiled=True),
        lax.all_gather(value_flat, "seq", axis=0, tiled=True),
    )
    top, mass, accum = scan_keys(begin, piece[0], piece[1], forward_update)
    lse = top + jnp.log(mass)
    att_full = accum / mass[:, :, None]
    attended = att_full.transpose(1, 0, 2).reshape(rows, width).astype(jnp.bfloat16)
    stream_d = attention_residual_stream + jnp.dot(
        attended, project_out, preferred_element_type=jnp.float32
    )
    result_value, saved_d = feed_forward(stream_d, gain_fourth, up_second, down_second)
    block_out = result_value.astype(jnp.bfloat16)[None]
    incoming_gradient = cotangent[0].astype(jnp.float32)
    incoming_gradient, gain_four_part, up_two_part, down_two_part = feed_back(
        incoming_gradient, saved_d, gain_fourth, up_second, down_second
    )
    grad_low = incoming_gradient.astype(jnp.bfloat16)
    out_part_c = jnp.einsum("td,te->de", attended, grad_low, preferred_element_type=jnp.float32)
    att_grad = jnp.einsum(
        "te,de->td", grad_low, project_out, preferred_element_type=jnp.float32
    ).astype(jnp.bfloat16)
    grad_heads = att_grad.reshape(rows, HEADS, head_size)
    delta = jnp.sum(grad_heads.astype(jnp.float32).transpose(1, 0, 2) * att_full, axis=-1)
    zero_heads = jnp.zeros((rows, HEADS, head_size), jnp.float32)

    def query_update(summed, key_block, value_block, key_pos):
        return summed + query_back(
            query_c, grad_heads, lse, delta, here, key_block, value_block, key_pos, ends, scale
        )

    piece = (
        lax.all_gather(key_flat, "seq", axis=0, tiled=True),
        lax.all_gather(value_flat, "seq", axis=0, tiled=True),
    )
    query_grad = scan_keys(zero_heads, piece[0], piece[1], query_update)
    lse_all, delta_all = (
        lax.all_gather(lse, "seq", axis=1, tiled=True),
        lax.all_gather(delta, "seq", axis=1, tiled=True),
    )
    queries = lax.all_gather(query_flat, "seq", axis=0, tiled=True)
    grads = lax.all_gather(att_grad, "seq", axis=0, tiled=True)
    count = queries.shape[0]
    step = math.gcd(count, 1024)
    firsts = step * jnp.arange(count // step, dtype=jnp.int32)

    def inner_product(summed, item):
        query_block, grad_block, first = item
        query_pos = first + jnp.arange(step, dtype=jnp.int32)
        lse_rows = lax.dynamic_slice_in_dim(lse_all, first, step, 1)
        delta_rows = lax.dynamic_slice_in_dim(delta_all, first, step, 1)
        parts = key_back(
            query_block,
            grad_block,
            lse_rows,
            delta_rows,
            query_pos,
            key_heads,
            value_heads,
            here,
            ends,
            scale,
        )
        return ((summed[0] + parts[0], summed[1] + parts[1]), None)

    items = (
        queries.reshape(count // step, step, HEADS, head_size),
        grads.reshape(count // step, step, HEADS, head_size),
        firsts,
    )
    key_grad, value_grad = lax.scan(inner_product, (zero_heads, zero_heads), items)[0]
    key_grad = key_grad.reshape(rows, width)
    value_grad = value_grad.reshape(rows, width)
    mixed_grad_c = jnp.concatenate(
        [query_grad.reshape(rows, width), key_grad, value_grad], axis=1
    ).astype(jnp.bfloat16)
    in_part_c = jnp.einsum(
        "td,te->de", attention_normed_rows, mixed_grad_c, preferred_element_type=jnp.float32
    )
    attention_normed_gradient = jnp.einsum(
        "te,de->td", mixed_grad_c, project_in, preferred_element_type=jnp.float32
    )
    attention_norm_gradient, attention_gain_share = norm_backward(
        attention_normed_gradient,
        attention_centered_normalized,
        attention_inverse_deviation,
        attention_norm_gain,
    )
    incoming_gradient = incoming_gradient + attention_norm_gradient
    incoming_gradient, gain_two_part, up_one_part, down_one_part = feed_back(
        incoming_gradient, saved_b, gain_second, up_first, down_first
    )
    grad_low = incoming_gradient.astype(jnp.bfloat16)
    out_part_a = jnp.einsum("td,te->de", gated, grad_low, preferred_element_type=jnp.float32)
    gated_grad = jnp.einsum("te,de->td", grad_low, mixer_out, preferred_element_type=jnp.float32)
    query_grad_a = gated_grad * response
    response_grad = gated_grad * query_a
    skip_part = jnp.sum(response_grad * product_kv, axis=0)
    chan_grad = lax.all_to_all(
        response_grad.T.reshape(blocks, channels, rows).astype(jnp.bfloat16),
        "seq",
        split_axis=0,
        concat_axis=2,
        tiled=True,
    ).astype(jnp.float32)[0]
    grad_re, grad_im = forward_spectrum(chan_grad, tables, blocks, rows)
    signal_grad = inverse_signal(
        ker_re * grad_re + ker_im * grad_im,
        ker_re * grad_im - ker_im * grad_re,
        tables,
        blocks,
        rows,
    )
    kernel_grad = inverse_signal(
        sig_re * grad_re + sig_im * grad_im,
        sig_re * grad_im - sig_im * grad_re,
        tables,
        blocks,
        rows,
    )
    coef_part, rate_part = kernel_grads(coef_here, rate_here, times, kernel_grad)
    returned = lax.all_to_all(
        signal_grad.reshape(1, channels, total).astype(jnp.bfloat16),
        "seq",
        split_axis=2,
        concat_axis=0,
        tiled=True,
    ).astype(jnp.float32)
    kv_grad = returned.reshape(width, rows).T + skip_gain * response_grad
    shifted_grad = kv_grad * value_a
    value_grad_a = kv_grad * shifted
    later = shifted_2(shortened(shifted_grad[: lags - 1]), "seq", -1)
    grad_ext = jnp.concatenate([shifted_grad, later], axis=0)
    key_grad_a = jnp.zeros_like(key_a)
    tap_rows = []
    for lag in range(lags):
        key_grad_a = key_grad_a + shift_taps[lag] * grad_ext[lag : lag + rows]
        tap_rows.append(
            jnp.sum(shifted_grad * key_ext[lags - 1 - lag : lags - 1 - lag + rows], axis=0)
        )
    taps_part = jnp.stack(tap_rows)
    mixed_grad_a = jnp.concatenate([query_grad_a, key_grad_a, value_grad_a], axis=1).astype(
        jnp.bfloat16
    )
    in_part_a = jnp.einsum(
        "td,te->de", mixer_normed_rows, mixed_grad_a, preferred_element_type=jnp.float32
    )
    mixer_normed_gradient = jnp.einsum(
        "te,de->td", mixed_grad_a, mixer_in, preferred_element_type=jnp.float32
    )
    mixer_norm_gradient, mixer_gain_share = norm_backward(
        mixer_normed_gradient, mixer_centered_normalized, mixer_inverse_deviation, mixer_norm_gain
    )
    token_grad = (incoming_gradient + mixer_norm_gradient)[None]
    parts = (
        lax.psum_scatter(mixer_gain_share, "seq", scatter_dimension=0, tiled=True),
        lax.psum_scatter(in_part_a, "seq", scatter_dimension=0, tiled=True),
        lax.psum_scatter(taps_part, "seq", scatter_dimension=1, tiled=True),
        lax.psum_scatter(skip_part, "seq", scatter_dimension=0, tiled=True),
        lax.psum_scatter(out_part_a, "seq", scatter_dimension=0, tiled=True),
        lax.psum_scatter(gain_two_part, "seq", scatter_dimension=0, tiled=True),
        lax.psum_scatter(up_one_part, "seq", scatter_dimension=0, tiled=True),
        lax.psum_scatter(down_one_part, "seq", scatter_dimension=0, tiled=True),
        lax.psum_scatter(attention_gain_share, "seq", scatter_dimension=0, tiled=True),
        lax.psum_scatter(in_part_c, "seq", scatter_dimension=0, tiled=True),
        lax.psum_scatter(out_part_c, "seq", scatter_dimension=0, tiled=True),
        lax.psum_scatter(gain_four_part, "seq", scatter_dimension=0, tiled=True),
        lax.psum_scatter(up_two_part, "seq", scatter_dimension=0, tiled=True),
        lax.psum_scatter(down_two_part, "seq", scatter_dimension=0, tiled=True),
    )
    matrices = (
        lax.psum_scatter(
            parts[1].astype(jnp.bfloat16), "batch", scatter_dimension=1, tiled=True
        ).astype(jnp.float32),
        lax.psum_scatter(
            parts[2].astype(jnp.bfloat16), "batch", scatter_dimension=0, tiled=True
        ).astype(jnp.float32),
        lax.psum_scatter(
            parts[4].astype(jnp.bfloat16), "batch", scatter_dimension=1, tiled=True
        ).astype(jnp.float32),
        lax.psum_scatter(
            parts[6].astype(jnp.bfloat16), "batch", scatter_dimension=1, tiled=True
        ).astype(jnp.float32),
        lax.psum_scatter(
            parts[7].astype(jnp.bfloat16), "batch", scatter_dimension=1, tiled=True
        ).astype(jnp.float32),
        lax.psum_scatter(
            parts[9].astype(jnp.bfloat16), "batch", scatter_dimension=1, tiled=True
        ).astype(jnp.float32),
        lax.psum_scatter(
            parts[10].astype(jnp.bfloat16), "batch", scatter_dimension=1, tiled=True
        ).astype(jnp.float32),
        lax.psum_scatter(
            parts[12].astype(jnp.bfloat16), "batch", scatter_dimension=1, tiled=True
        ).astype(jnp.float32),
        lax.psum_scatter(
            parts[13].astype(jnp.bfloat16), "batch", scatter_dimension=1, tiled=True
        ).astype(jnp.float32),
    )
    smalls = lax.psum(
        (parts[0], coef_part, rate_part, parts[3], parts[5], parts[8], parts[11]), "batch"
    )
    return (
        block_out,
        token_grad,
        smalls[0],
        matrices[0],
        matrices[1],
        smalls[1],
        smalls[2],
        smalls[3],
        matrices[2],
        smalls[4],
        matrices[3],
        matrices[4],
        smalls[5],
        matrices[5],
        matrices[6],
        smalls[6],
        matrices[7],
        matrices[8],
    )


MESH = pl.DeviceIdType.MESH
BF = jnp.bfloat16
F32 = jnp.float32
ROWS, WIDE, RANKS = (128, 768, 8)
SPAN = ROWS * RANKS
BLOCK = 128
OWNERS = 6
NT = (((1,), (1,)), ((), ()))
TN = (((0,), (0,)), ((), ()))
ROOT = math.sqrt(2.0 / math.pi)
CUBIC = 0.044715


def flip(value):
    return 1 - value


def mm(left, right):
    return jnp.dot(left, right, preferred_element_type=F32)


def mm_nt(left, right):
    return lax.dot_general(left, right, NT, preferred_element_type=F32)


def mm_tn(left, right):
    return lax.dot_general(left, right, TN, preferred_element_type=F32)


def is_owner(rank):
    return jnp.logical_and(rank >= 1, rank <= OWNERS)


def rows_of(rank):
    return pl.ds(pl.multiple_of(ROWS * rank, ROWS), ROWS)


def lanes_of(block):
    return pl.ds(pl.multiple_of(BLOCK * block, BLOCK), BLOCK)


PARTNERS = ((1, 1, 1), (1, 1, 0), (1, 0, 1), (1, 0, 0), (0, 1, 1), (0, 1, 0), (0, 0, 1))


class Spread:
    def __init__(self, net, source, target, outward, need=None):
        self.net, self.source, self.target, self.outward, self.need = net, source, target, outward, need
        self.base = net.take(RANKS - 1)

    def copy(self, step, source, target, rank):
        at = self.base + step - 1
        return pltpu.make_async_remote_copy(
            src_ref=source,
            dst_ref=target,
            send_sem=self.net.send_sem.at[at],
            recv_sem=self.net.recv_sem.at[at],
            device_id=(rank, self.net.b),
            device_id_type=MESH,
        )

    def each_send(self, act, chosen=None):
        me = self.net.s
        for step in range(1, RANKS):
            rank = self.net.partner(step)
            go = is_owner(rank) if self.outward else is_owner(me)
            if self.need is not None:
                go = jnp.logical_and(go, self.need(me - 1, rank))
            if chosen is not None:
                go = jnp.logical_and(go, chosen(rank))

            @pl.when(go)
            def _(step=step, rank=rank):
                if self.outward:
                    act(self.copy(step, self.source(rank - 1), self.target(me), rank))
                else:
                    act(self.copy(step, self.source(rank), self.target(me - 1), rank))

    def start(self, chosen=None):
        self.each_send(lambda copy: copy.start(), chosen)

    def own(self):
        me = self.net.s

        @pl.when(is_owner(me))
        def _():
            if self.outward:
                self.target(me)[...] = self.source(me - 1)[...]
            else:
                self.target(me - 1)[...] = self.source(me)[...]

    def wait_recv(self, steps=range(1, RANKS)):
        me = self.net.s
        for step in steps:
            rank = self.net.partner(step)
            go = is_owner(me) if self.outward else is_owner(rank)
            if self.need is not None:
                go = jnp.logical_and(go, self.need(rank - 1, me))

            @pl.when(go)
            def _(step=step, rank=rank):
                landed = self.target(rank if self.outward else rank - 1)
                self.copy(step, landed, landed, rank).wait_recv()

    def wait_send(self):
        self.each_send(lambda copy: copy.wait_send())


class Net:
    def __init__(self, send_sem, recv_sem):
        self.send_sem, self.recv_sem = send_sem, recv_sem
        self.s = lax.axis_index("seq")
        self.b = lax.axis_index("batch")
        self.y, self.c = self.b // 2, lax.rem(self.b, 2)
        z, self.x = self.s // 2, lax.rem(self.s, 2)
        self.high, self.low = z // 2, lax.rem(z, 2)
        self.sibling = (self.s, 2 * self.y + flip(self.c))
        self.by_y = (self.s, 2 * flip(self.y) + self.c)
        self.by_both = (self.s, 2 * flip(self.y) + flip(self.c))
        self.by_x = (2 * z + flip(self.x), self.b)
        self.by_low = (2 * (2 * self.high + flip(self.low)) + self.x, self.b)
        self.by_high = (2 * (2 * flip(self.high) + self.low) + self.x, self.b)
        self.used = 0
        self.waiting = []

    def partner(self, step):
        far, near, side = PARTNERS[step - 1]
        high = flip(self.high) if far else self.high
        low = flip(self.low) if near else self.low
        return 4 * high + 2 * low + (flip(self.x) if side else self.x)

    def take(self, count):
        at = self.used
        self.used += count
        return at

    def spread(self, source, target, outward, need=None):
        made = Spread(self, source, target, outward, need)
        self.waiting.append(made)
        return made

    def send(self, source, target, other):
        at = self.take(1)
        copy = pltpu.make_async_remote_copy(
            src_ref=source,
            dst_ref=target,
            send_sem=self.send_sem.at[at],
            recv_sem=self.recv_sem.at[at],
            device_id=other,
            device_id_type=MESH,
        )
        copy.start()
        self.waiting.append(copy)
        return copy

    def hello(self):
        barrier = pltpu.get_barrier_semaphore()
        for step in range(1, RANKS):
            pl.semaphore_signal(
                barrier, inc=1, device_id=(lax.rem(self.s + step, RANKS), self.b), device_id_type=MESH
            )
        for other in (self.sibling, self.by_y, self.by_both):
            pl.semaphore_signal(barrier, inc=1, device_id=other, device_id_type=MESH)

    def ready(self):
        pl.semaphore_wait(pltpu.get_barrier_semaphore(), RANKS + 2)

    def turn_of(self, step, y, c):
        return (2 * y + flip(c), 2 * flip(y) + c, 2 * flip(y) + flip(c), 2 * y + c)[step]

    def order(self):
        owners = (self.sibling, self.by_y, self.by_both, None)
        return [(self.turn_of(step, self.y, self.c), owners[step]) for step in range(4)]

    def drop(self, copy):
        self.waiting = [made for made in self.waiting if made is not copy]

    def finish(self):
        for made in self.waiting:
            made.wait_send()


class Beside:
    def __init__(self, net, source, target, steps):
        self.net, self.steps = net, steps
        self.at = net.take(1)
        other = jnp.clip(net.s + steps, 0, RANKS - 1)
        self.copy = pltpu.make_async_remote_copy(
            src_ref=source,
            dst_ref=target,
            send_sem=net.send_sem.at[self.at],
            recv_sem=net.recv_sem.at[self.at],
            device_id=(other, net.b),
            device_id_type=MESH,
        )
        last = RANKS - 1 if steps > 0 else 0
        first = 0 if steps > 0 else RANKS - 1
        self.sends = net.s != last
        self.takes = net.s != first
        net.waiting.append(self)

    def start(self):
        @pl.when(self.sends)
        def _():
            self.copy.start()

    def wait_recv(self):
        @pl.when(self.takes)
        def _():
            self.copy.wait_recv()

    def wait_send(self):
        @pl.when(self.sends)
        def _():
            self.copy.wait_send()


def pieces(value):
    cent = value - jnp.mean(value, axis=-1, keepdims=True)
    inverse = lax.rsqrt(jnp.mean(cent * cent, axis=-1, keepdims=True) + 1e-05)
    return cent * inverse, inverse


def pieces_back(incoming, normal, inverse, gain):
    share = jnp.sum(incoming * normal, axis=0, keepdims=True)
    scaled = incoming * gain
    first = jnp.mean(scaled, axis=-1, keepdims=True)
    second = jnp.mean(scaled * normal, axis=-1, keepdims=True)
    return inverse * (scaled - first - normal * second), share


def gelu_parts(u):
    square = u * u
    bend = jnp.tanh(ROOT * u * (1.0 + CUBIC * square))
    half = 0.5 * (1.0 + bend)
    value = u * half
    slope = half + 0.5 * u * (1.0 - bend * bend) * (ROOT * (1.0 + 3.0 * CUBIC * square))
    return value, slope


def split(value):
    high = value.astype(BF)
    return high, (value - high.astype(F32)).astype(BF)


def transform(r, net, go, signal, re_out, im_out):
    for index, steps in enumerate(((7,), (5, 6), (3, 4), (1, 2))):
        go.wait_recv(steps)
        high = flip(net.high) if index >= 2 else net.high
        low = flip(net.low) if index % 2 else net.low
        some = pl.ds(pl.multiple_of(512 * high + 256 * low, 256), 256)
        re, im = mm(r.cos_table[:, some], signal[some, :]), mm(r.sin_table[:, some], signal[some, :])
        if index == 0:
            re_out[...] = re
            im_out[...] = -im
        else:
            re_out[...] += re
            im_out[...] -= im


def transform_two(r, signal, re_out, im_out):
    high, low = split(signal)
    r.pack_re[:, 0:128] = high
    r.pack_re[:, 128:256] = low

    @pl.loop(0, 4)
    def _(at):
        rows = pl.ds(pl.multiple_of(256 * at, 256), 256)
        re, im = mm(r.cos_table[rows, :], r.pack_re[...]), mm(r.sin_table[rows, :], r.pack_re[...])
        re_out[rows, :] = re[:, 0:128] + re[:, 128:256]
        im_out[rows, :] = -(im[:, 0:128] + im[:, 128:256])


def inverse(r, re, im, out, back=None):
    re_high, re_low = split(re)
    im_high, im_low = split(im)
    r.pack_re[:, 0:128] = re_high
    r.pack_re[:, 128:256] = re_low
    r.pack_im[:, 0:128] = im_high
    r.pack_im[:, 128:256] = im_low
    for at in (3, 2, 1, 0):
        rows = slice(256 * at, 256 * at + 256)
        both = mm(r.cos_table[rows, :], r.pack_re[...]) - mm(r.sin_table[rows, :], r.pack_im[...])
        out[rows, :] = ((both[:, 0:128] + both[:, 128:256]) * (1.0 / SPAN)).astype(out.dtype)
        if back is not None:
            back.start(lambda rank, at=at: rank // 2 == at)


def modes(coef_ref, rate_ref, out_ref):
    blocks, width = out_ref.shape[0] // 8, out_ref.shape[1]
    row = lax.broadcasted_iota(jnp.int32, (8, width), 0).astype(F32)
    out_ref[...] = jnp.zeros_like(out_ref)

    @pl.loop(0, 8)
    def _(group):
        some = pl.ds(pl.multiple_of(8 * group, 8), 8)
        rate, coef = rate_ref[some, :], coef_ref[some, :]
        falls = [coef[n : n + 1] * jnp.exp(-rate[n : n + 1] * row) for n in range(8)]
        steps = [jnp.exp(-rate[n : n + 1] * jnp.maximum(row, 8.0)) for n in range(8)]

        def step(at, falls):
            rows = pl.ds(pl.multiple_of(8 * at, 8), 8)
            out_ref[rows, :] += sum(falls[1:], falls[0])
            return tuple(fall * factor for fall, factor in zip(falls, steps))

        lax.fori_loop(0, blocks, step, tuple(falls), unroll=4)


def modes_back(coef_ref, rate_ref, grad_ref, coef_out, rate_out):
    blocks, width = grad_ref.shape[0] // 8, grad_ref.shape[1]
    row = lax.broadcasted_iota(jnp.int32, (8, width), 0).astype(F32)

    @pl.loop(0, 8)
    def _(group):
        some = pl.ds(pl.multiple_of(8 * group, 8), 8)
        rate, coef = rate_ref[some, :], coef_ref[some, :]
        steps = [jnp.exp(-rate[n : n + 1] * jnp.maximum(row, 8.0)) for n in range(8)]
        zero = jnp.minimum(row, 0.0)

        def step(at, carry):
            totals, slopes = carry
            here = grad_ref[pl.ds(pl.multiple_of(8 * (blocks - 1 - at), 8), 8), :]
            slopes = tuple(slope * factor + total for slope, factor, total in zip(slopes, steps, totals))
            totals = tuple(total * factor + here for total, factor in zip(totals, steps))
            return totals, slopes

        totals, slopes = lax.fori_loop(0, blocks, step, ((zero,) * 8, (zero,) * 8), unroll=2)
        coef_rows, rate_rows = [], []
        for n in range(8):
            fall = jnp.exp(-rate[n : n + 1] * row)
            coef_rows.append(jnp.sum(fall * totals[n], axis=0, keepdims=True))
            late = jnp.sum(fall * (8.0 * steps[n] * slopes[n] + row * totals[n]), axis=0, keepdims=True)
            rate_rows.append(-coef[n : n + 1] * late)
        coef_out[some, :] = jnp.concatenate(coef_rows, axis=0)
        rate_out[some, :] = jnp.concatenate(rate_rows, axis=0)


def shift_forward(keys, taps, value, shifted):
    @pl.loop(0, OWNERS)
    def _(block):
        lanes = lanes_of(block)
        near = keys[:, lanes]
        total = jnp.zeros((ROWS, BLOCK), F32)
        for rest in range(8):
            turned = pltpu.roll(near, rest, 0) if rest else near
            for part in range(8):
                total = total + taps[8 * part + rest : 8 * part + rest + 1, lanes] * turned[64 - 8 * part : 192 - 8 * part]
        shifted[:, lanes] = total


def shift_back(grads, keys, taps, key_grad, taps_grad):
    @pl.loop(0, OWNERS)
    def _(block):
        lanes = lanes_of(block)
        ahead, near = grads[:, lanes], keys[:, lanes]
        here = ahead[0:ROWS]
        total = jnp.zeros((ROWS, BLOCK), F32)
        rows = {}
        for rest in range(8):
            later = pltpu.roll(ahead, 192 - rest, 0) if rest else ahead
            turned = pltpu.roll(near, rest, 0) if rest else near
            for part in range(8):
                lag = 8 * part + rest
                total = total + taps[lag : lag + 1, lanes] * later[8 * part : 8 * part + ROWS]
                taps_grad[lag : lag + 1, lanes] = jnp.sum(here * turned[64 - 8 * part : 192 - 8 * part], axis=0, keepdims=True)
        key_grad[:, lanes] = total


def holds_columns(block, rank):
    third = (block + 3) // 3 - 1
    first = block + third
    return jnp.logical_or(rank == first, rank == first + 1)


def head_lanes(shape, head):
    return lax.broadcasted_iota(jnp.int32, shape, 1) // 64 == head


def document_start(ends, first, count):
    at = first + lax.broadcasted_iota(jnp.int32, (count, 1), 0)
    begin = jnp.zeros((count, 1), jnp.int32)
    for index in range(3):
        begin = jnp.where(at >= ends[index], ends[index], begin)
    return at, begin


def allowed_pairs(ends, part):
    query_at, begin = document_start(ends, 256 * part, 256)
    key_at = lax.broadcasted_iota(jnp.int32, (256, 256 * (part + 1)), 1)
    return jnp.logical_and(key_at <= query_at, key_at >= begin)


def attention_forward(r, part):
    rows, keys = slice(256 * part, 256 * part + 256), slice(0, 256 * part + 256)
    mask = allowed_pairs(r.ends, part)

    @pl.loop(0, 2)
    def _(head):
        lanes = head_lanes((256, BLOCK), head)
        query = jnp.where(lanes, r.qkv[0, rows, :].astype(F32) * 0.125, 0.0).astype(BF)
        scores = jnp.where(mask, mm_nt(query, r.qkv[1, keys, :]), NEGATIVE)
        top = jnp.max(scores, axis=1, keepdims=True)
        weights = jnp.exp(scores - top)
        mass = jnp.sum(weights, axis=1, keepdims=True)
        mixed = mm(weights.astype(BF), r.qkv[2, keys, :]) / mass
        r.attended_full[rows, :] = jnp.where(lanes, mixed, r.attended_full[rows, :])
        r.lse[rows, :] = jnp.where(lanes, top + jnp.log(mass), r.lse[rows, :])

    r.attended_low[rows, :] = r.attended_full[rows, :].astype(BF)


def attention_back(r, part):
    rows, keys = slice(256 * part, 256 * part + 256), slice(0, 256 * part + 256)
    mask = allowed_pairs(r.ends, part)

    @pl.loop(0, 2)
    def _(head):
        lanes = head_lanes((256, BLOCK), head)
        query = jnp.where(lanes, r.qkv[0, rows, :].astype(F32) * 0.125, 0.0).astype(BF)
        whole = r.att_grad[rows, :].astype(F32)
        grads = jnp.where(lanes, whole, 0.0)
        delta = jnp.sum(grads * r.attended_full[rows, :], axis=1, keepdims=True)
        lse = jnp.sum(jnp.where(lanes, r.lse[rows, :], 0.0), axis=1, keepdims=True) * (1.0 / 64.0)
        grads = grads.astype(BF)
        scores = mm_nt(query, r.qkv[1, keys, :])
        probs = jnp.where(mask, jnp.exp(scores - lse), 0.0)
        score_grad = (probs * (mm_nt(grads, r.qkv[2, keys, :]) - delta)).astype(BF)
        query_grad = mm(score_grad, r.qkv[1, keys, :]) * 0.125
        r.query_grad[rows, :] = jnp.where(lanes, query_grad, r.query_grad[rows, :])
        r.key_grad[keys, :] += mm_tn(score_grad, query)
        r.value_grad[keys, :] += mm_tn(probs.astype(BF), grads)

    r.qkv_grad[0, rows, :] = r.query_grad[rows, :].astype(BF)
    r.qkv_grad[1, rows, :] = r.key_grad[rows, :].astype(BF)
    r.qkv_grad[2, rows, :] = r.value_grad[rows, :].astype(BF)


class Gather:
    def __init__(self, net, source, target):
        self.net, self.target = net, target
        here = target(net.y, net.c)
        self.first = net.send(source, here, net.sibling)
        self.across = net.send(source, here, net.by_y)

    def forward(self):
        self.across.wait_recv()
        landed = self.target(flip(self.net.y), self.net.c)
        self.second = self.net.send(landed, landed, self.net.sibling)

    def wait(self):
        self.first.wait_recv()
        self.second.wait_recv()

    def free(self):
        for copy in (self.first, self.across, self.second):
            copy.wait_send()
            self.net.drop(copy)


class Locals:
    def __init__(self, sems):
        self.sems, self.used, self.waiting = sems, 0, []

    def start(self, source, target):
        copy = pltpu.make_async_copy(source, target, self.sems.at[self.used])
        self.used += 1
        copy.start()
        return copy

    def put(self, source, target):
        self.waiting.append(self.start(source, target))

    def finish(self):
        for copy in self.waiting:
            copy.wait()


UP, DOWN, PAIR = (0, 1, 2)
LENGTH = 576
FIRST = dict(up_d=352, down_d=352, pair_c=352, down_b=352, up_b=352, pair_a=352)


class Sum:
    def __init__(self, r, net, name, kind):
        self.net, self.kind, self.half = net, kind, FIRST[name]
        for part in ("grads", "near_a", "near_b", "next_a", "next_b", "own", "third"):
            setattr(self, part, getattr(r, name + "_" + part))
        if kind == DOWN:
            self.across = getattr(r, name + "_across")
        else:
            self.right = getattr(r, name + "_right")
        self.shared = []

    def give(self, kept, step, columns, other):
        own = self.right.at[rows_of(self.net.b), :]
        if other is None:
            own[...] = columns
        else:
            kept[step] = columns
            self.shared.append(self.net.send(kept.at[step], own, other))

    def share_pairs(self, pairs):
        own = self.right.at[rows_of(self.net.b), :]
        for index, other in self.net.order():
            if other is None:
                own[...] = pairs[index]
            else:
                self.shared.append(self.net.send(pairs.at[index], own, other))

    def free(self, copies):
        for copy in copies:
            copy.wait_send()
            self.net.drop(copy)

    def free_shared(self):
        self.free(self.shared)

    def share_rows(self, turned):
        net = self.net
        own = pl.ds(pl.multiple_of(192 * net.b, 64), 192)
        self.across[:, lanes_of(net.b)] = turned[own, :]
        for index, other in self.net.order()[:3]:
            rows = pl.ds(pl.multiple_of(192 * index, 64), 192)
            self.shared.append(net.send(turned.at[rows, :], self.across.at[:, lanes_of(net.b)], other))

    def wait_shared(self):
        for copy in self.shared:
            copy.wait_recv()

    def place(self, product, tile):
        for block in range(8):
            at = pl.ds(pl.multiple_of(96 * tile, 16), 96)
            self.grads[block % 2, (block // 2) % 2, block // 4, at, :] = product[96 * block : 96 * block + 96].astype(BF)

    def product(self, left, second):
        self.wait_shared()
        if self.kind == DOWN:

            @pl.loop(0, 8)
            def _(block):
                lanes = pl.ds(pl.multiple_of(384 * block, 384), 384)
                product = mm(self.across[...], second[:, lanes])
                for tile in range(3):
                    self.grads[
                        lax.rem(block, 2), lax.rem(block // 2, 2), block // 4, 192 * tile : 192 * tile + 192, :
                    ] = product[:, 128 * tile : 128 * tile + 128].astype(BF)

        else:

            @pl.loop(0, 3 if self.kind == UP else 2)
            def _(chunk):
                lanes = pl.ds(pl.multiple_of(256 * chunk, 256), 256)
                product = mm(left[...], self.right[:, lanes])
                self.place(product[:, 0:128], 2 * chunk)
                self.place(product[:, 128:256], 2 * chunk + 1)

        if self.kind == PAIR:
            right = self.right[:, 512:768]
            first = lax.broadcasted_iota(jnp.int32, right.shape, 1) < 64
            zero = jnp.zeros_like(right)
            product = mm(left[...], jnp.where(first, right, zero)) + mm(second[...], jnp.where(first, zero, right))
            self.place(product[:, 0:128], 4)
            self.place(product[:, 128:256], 5)

        net, half = self.net, self.half
        self.moving = [
            net.send(self.grads.at[flip(net.x), :, :, 0:half, :], self.near_a, net.by_x),
            net.send(self.grads.at[:, flip(net.low), :, half:, :], self.near_b, net.by_low),
        ]

    def arrive(self):
        for copy in self.moving:
            copy.wait_recv()

    def second(self):
        net, half, grads = self.net, self.half, self.grads
        self.arrive()

        @pl.loop(0, 4)
        def _(step):
            one, two = step // 2, lax.rem(step, 2)
            grads[net.x, one, two, 0:half, :] += self.near_a[one, two]
            grads[one, net.low, two, half:, :] += self.near_b[one, two]

        self.moving = [
            net.send(grads.at[net.x, flip(net.low), :, 0:half, :], self.next_a, net.by_low),
            net.send(grads.at[flip(net.x), net.low, :, half:, :], self.next_b, net.by_x),
        ]

    def last(self):
        net, half, grads = self.net, self.half, self.grads
        self.arrive()

        @pl.loop(0, 2)
        def _(step):
            grads[net.x, net.low, step, 0:half, :] += self.next_a[step]
            grads[net.x, net.low, step, half:, :] += self.next_b[step]

        self.moving = [net.send(grads.at[net.x, net.low, flip(net.high)], self.third, net.by_high)]

    def end(self, near):
        net = self.net
        near.put(self.grads.at[net.x, net.low, net.high], self.own)
        self.arrive()


def sum_scratch(name, kind):
    first = FIRST[name]
    made = {
        name + "_grads": ((2, 2, 2, LENGTH, 128), BF),
        name + "_near_a": ((2, 2, first, 128), BF),
        name + "_near_b": ((2, 2, LENGTH - first, 128), BF),
        name + "_next_a": ((2, first, 128), BF),
        name + "_next_b": ((2, LENGTH - first, 128), BF),
    }
    if kind == DOWN:
        made[name + "_across"] = ((192, 512), BF)
    else:
        made[name + "_right"] = ((512, WIDE), BF)
    return made


def pair_columns(wide, narrow, out):
    first = lax.broadcasted_iota(jnp.int32, (ROWS, BLOCK), 1) < 64

    def tile(at):
        at = at % (3 * WIDE)
        return wide[at // WIDE, :, at % WIDE : at % WIDE + BLOCK].astype(F32)

    def turned(at):
        return jnp.where(first, pltpu.roll(tile(at - BLOCK), 64, 1), pltpu.roll(tile(at), 64, 1))

    def thin(at):
        return narrow[:, at : at + BLOCK].astype(F32)

    def thin_turned(at):
        upper = pltpu.roll(thin(at), 64, 1)
        return jnp.where(first, pltpu.roll(thin(at - BLOCK), 64, 1), upper) if at else upper

    for block in range(4):
        start = 576 * block
        if block % 2 == 0:
            for part in range(4):
                out[block, :, BLOCK * part : BLOCK * part + BLOCK] = tile(start + BLOCK * part).astype(BF)
            lower, upper, rest = tile(start + 512), thin_turned(192 * block), thin_turned(192 * block + BLOCK)
        else:
            for part in range(4):
                out[block, :, BLOCK * part : BLOCK * part + BLOCK] = turned(start + 64 + BLOCK * part).astype(BF)
            lower, upper, rest = turned(start + 576), thin(192 * block - 64), thin(192 * block + 64)
        out[block, :, 512:640] = jnp.where(first, lower, upper).astype(BF)
        out[block, :, 640:768] = rest.astype(BF)


def turn(blocks, out):
    for block in range(4):
        out[:, BLOCK * block : BLOCK * block + BLOCK] = blocks[BLOCK * block : BLOCK * block + BLOCK, :].T


TABLES = ("cos_table", "sin_table")
KEPT = (
    "value_next",
    "qkv",
    "lse",
    "attended_full",
    "bend_b",
    "stream_b",
    "response",
    "query_a",
    "shifted",
    "value_a",
    "key_ext",
    "kernel_re",
    "kernel_im",
    "signal_re",
    "signal_im",
)
LEFTS = ("normed_a", "gated", "normed_b", "active_b", "normed_c")


def kernel_a(r):
    net = Net(r.send_sem, r.recv_sem)
    near = Locals(r.local_sem)
    net.hello()
    wait = {}

    def fetch(*names):
        for name in names:
            wait[name] = near.start(getattr(r, name + "_hbm"), getattr(r, name))

    thirds = []
    for index in (2, 0, 1):
        lanes = slice(WIDE * index, WIDE * index + WIDE)
        thirds.append(near.start(r.mixer_in_hbm.at[:, lanes], r.mixer_in.at[:, lanes]))
    r.ends[0] = r.doc_lengths[0, 0]
    r.ends[1] = r.ends[0] + r.doc_lengths[0, 1]
    r.ends[2] = r.ends[1] + r.doc_lengths[0, 2]

    def keep(*names):
        for name in names:
            near.put(getattr(r, name), getattr(r, name + "_kept"))

    gathers = []

    def gather(name, lanes=slice(None)):
        all_of = getattr(r, name + "_all")
        mine = getattr(r, name).at[:, lanes]
        near.put(mine, all_of.at[rows_of(net.b), lanes])
        gathers.append(Gather(net, mine, lambda y, c: all_of.at[rows_of(2 * y + c), lanes]))

    me = net.s
    gain_a = r.mixer_norm_gain[...][None]
    net.ready()
    rim = Beside(net, r.tokens.at[0, 64:128, :], r.rim_in, 1)
    rim.start()

    @pl.when(me == 0)
    def _():
        r.rim_in[...] = jnp.zeros_like(r.rim_in)

    normal, _ = pieces(r.tokens[0].astype(F32))
    r.normed_a[...] = (normal * gain_a).astype(BF)
    gather("normed_a")
    thirds[0].wait()
    r.value_a[...] = mm(r.normed_a[...], r.mixer_in[:, 2 * WIDE :])
    r.value_low[...] = r.value_a[0:64, :].astype(BF)
    later = Beside(net, r.value_low, r.value_next, -1)
    later.start()

    @pl.when(me == RANKS - 1)
    def _():
        r.value_next[...] = jnp.zeros_like(r.value_next)

    thirds[1].wait()
    r.query_a[...] = mm(r.normed_a[...], r.mixer_in[:, 0:WIDE])
    keep("query_a", "value_a")
    thirds[2].wait()
    fetch("shift_taps", "mode_coef", "mode_rate", *TABLES, "phase_cos", "phase_sin", "mixer_out")
    fetch("up_first", "down_first", "project_in")
    r.key_ext[64:192, :] = mm(r.normed_a[...], r.mixer_in[:, WIDE : 2 * WIDE])
    rim.wait_recv()
    normal, _ = pieces(r.rim_in[...].astype(F32))
    r.key_ext[0:64, :] = mm((normal * gain_a).astype(BF), r.mixer_in[:, WIDE : 2 * WIDE])
    for name in ("shift_taps", "mode_coef", "mode_rate"):
        wait[name].wait()
    shift_forward(r.key_ext, r.shift_taps, None, r.shifted)
    r.product_low[...] = (r.shifted[...] * r.value_a[...]).astype(BF)
    go = net.spread(lambda block: r.product_low.at[:, lanes_of(block)], lambda rank: r.signal.at[rows_of(rank), :], True)
    go.start()
    go.own()
    keep("key_ext", "shifted")
    block = lanes_of(jnp.clip(me - 1, 0, OWNERS - 1))
    r.coef[...] = r.mode_coef[:, block]
    r.rate[...] = r.mode_rate[:, block]
    modes(r.coef, r.rate, r.mode_rows)
    for name in TABLES + ("phase_cos", "phase_sin"):
        wait[name].wait()
    transform_two(r, r.mode_rows[...], r.kernel_re, r.kernel_im)
    turned = r.kernel_re[...] * r.phase_cos[...] - r.kernel_im[...] * r.phase_sin[...]
    r.kernel_im[...] = r.kernel_im[...] * r.phase_cos[...] + r.kernel_re[...] * r.phase_sin[...]
    r.kernel_re[...] = turned
    keep("kernel_re", "kernel_im")
    transform(r, net, go, r.signal, r.signal_re, r.signal_im)
    back = net.spread(lambda rank: r.conv.at[rows_of(rank), :], lambda block: r.conv_home.at[:, lanes_of(block)], False)
    inverse(
        r,
        r.signal_re[...] * r.kernel_re[...] - r.signal_im[...] * r.kernel_im[...],
        r.signal_re[...] * r.kernel_im[...] + r.signal_im[...] * r.kernel_re[...],
        r.conv,
        back,
    )
    back.own()
    for name in ("mixer_out", "up_first", "down_first", "project_in"):
        wait[name].wait()
    back.wait_recv()
    r.response[...] = r.conv_home[...].astype(F32) + r.skip_gain[...][None] * (r.shifted[...] * r.value_a[...])
    r.gated[...] = (r.query_a[...] * r.response[...]).astype(BF)
    gather("gated")
    stream_b = r.tokens[0].astype(F32) + mm(r.gated[...], r.mixer_out[...])
    r.stream_b[...] = stream_b
    normal, _ = pieces(stream_b)
    r.normed_b[...] = (normal * r.gain_second[...][None]).astype(BF)
    gather("normed_b")
    r.stream_c[...] = stream_b
    for chunk in range(4):
        lanes = slice(WIDE * chunk, WIDE * chunk + WIDE)
        active, bend = gelu_parts(mm(r.normed_b[...], r.up_first[:, lanes]))
        r.bend_b[:, lanes] = bend.astype(BF)
        active = active.astype(BF)
        r.active_b[:, lanes] = active
        gather("active_b", lanes)
        r.stream_c[...] += mm(active, r.down_first[lanes, :])
    normal, _ = pieces(r.stream_c[...])
    r.normed_c[...] = (normal * r.attention_norm_gain[...][None]).astype(BF)
    gather("normed_c")
    for index in range(3):
        r.mixed_c[index] = mm(r.normed_c[...], r.project_in[:, WIDE * index : WIDE * index + WIDE]).astype(BF)
    go = net.spread(lambda block: r.mixed_c.at[:, :, lanes_of(block)], lambda rank: r.qkv.at[:, rows_of(rank), :], True)
    go.start()
    go.own()
    keep("response", "stream_b", "bend_b")
    for made in gathers[:3]:
        made.forward()
    turned = r.signal_re[...] * r.phase_cos[...] - r.signal_im[...] * r.phase_sin[...]
    r.signal_im[...] = -(r.signal_im[...] * r.phase_cos[...] + r.signal_re[...] * r.phase_sin[...])
    r.signal_re[...] = turned
    keep("signal_re", "signal_im")
    later.wait_recv()
    keep("value_next")
    go.wait_recv()
    keep("qkv")
    back = net.spread(lambda rank: r.attended_low.at[rows_of(rank), :], lambda block: r.attended.at[:, lanes_of(block)], False)
    for part in (3, 2, 1, 0):
        attention_forward(r, part)
        back.start(lambda rank, part=part: rank // 2 == part)
    back.own()
    keep("lse", "attended_full")
    for made in gathers[3:]:
        made.forward()
    back.wait_recv()
    for made in gathers:
        made.wait()
    net.finish()
    near.finish()


def kernel_b(r):
    net = Net(r.send_sem, r.recv_sem)
    near = Locals(r.local_sem)
    net.hello()
    wait = {}

    def fetch(name, into=None):
        wait[name] = near.start(getattr(r, name + "_hbm"), getattr(r, into or name))

    for name, into in (("project_out", "out_weight"), ("attended", "attended"), ("stream_c", "stream_c"), ("cotangent", "cotangent")):
        fetch(name, into)
    chunks = []
    for step, (index, other) in enumerate(net.order()):
        lanes = pl.ds(pl.multiple_of(WIDE * index, WIDE), WIDE)
        chunks.append(
            (
                near.start(r.up_second_hbm.at[:, lanes], r.up.at[:, lanes]),
                near.start(r.down_second_hbm.at[lanes, :], r.down.at[lanes, :]),
            )
        )
    r.ends[0] = r.doc_lengths[0, 0]
    r.ends[1] = r.ends[0] + r.doc_lengths[0, 1]
    r.ends[2] = r.ends[1] + r.doc_lengths[0, 2]
    up_d, down_d, pair_c = Sum(r, net, "up_d", UP), Sum(r, net, "down_d", DOWN), Sum(r, net, "pair_c", PAIR)
    up_b, down_b, pair_a = Sum(r, net, "up_b", UP), Sum(r, net, "down_b", DOWN), Sum(r, net, "pair_a", PAIR)
    own_rows = rows_of(net.b)

    gain_d = r.gain_fourth[...][None]
    for name in ("project_out", "attended", "stream_c", "cotangent"):
        wait[name].wait()
    stream_d = r.stream_c[...] + mm(r.attended[...], r.out_weight[...])
    normal, inverse_d = pieces(stream_d)
    normed_d = (normal * gain_d).astype(BF)
    r.layer_left[own_rows, :] = normed_d
    r.total[...] = stream_d
    r.turned[...] = r.cotangent[0].T
    r.pair_two[own_rows, :] = r.attended[...]
    net.ready()
    gather_d = Gather(net, r.layer_left.at[own_rows, :], lambda y, c: r.layer_left.at[rows_of(2 * y + c), :])
    down_d.share_rows(r.turned)
    spots = []
    for step, (index, other) in enumerate(net.order()):
        lanes = pl.ds(pl.multiple_of(WIDE * index, WIDE), WIDE)
        for copy in chunks[step]:
            copy.wait()
        if step == 3:
            for name in KEPT[:11]:
                fetch(name)
            fetch("project_in", "in_weight")
            fetch("normed_c_all", "pair_one")
            fetch("tokens")
            for name in ("shift_taps", "mode_coef", "mode_rate") + TABLES:
                fetch(name)
        raised = mm(r.layer_left[own_rows, :], r.up[:, lanes])
        active, slope = gelu_parts(raised)
        active = active.astype(BF)
        r.layer_second[own_rows, lanes] = active

        def spot(y, c, step=step):
            at = pl.ds(pl.multiple_of(WIDE * net.turn_of(step, y, c), WIDE), WIDE)
            return r.layer_second.at[rows_of(2 * y + c), at]

        spots.append(spot)
        slope = (slope * mm_nt(r.cotangent[0], r.down[lanes, :])).astype(BF)
        up_d.give(r.slopes, step, slope, other)
        back = mm_nt(slope, r.up[:, lanes])
        if step == 0:
            r.grad_d[...] = back
        else:
            r.grad_d[...] += back
    gathers = [Gather(net, spot(net.y, net.c), spot) for spot in spots]
    grad, gain_four = pieces_back(r.grad_d[...], normal, inverse_d, gain_d)
    grad = r.cotangent[0].astype(F32) + grad
    r.grad_d[...] = grad
    r.grad_d_low[...] = grad.astype(BF)
    r.att_grad_home[...] = mm_nt(r.grad_d_low[...], r.out_weight[...]).astype(BF)
    go = net.spread(lambda block: r.att_grad_home.at[:, lanes_of(block)], lambda rank: r.att_grad.at[rows_of(rank), :], True)
    go.start()
    go.own()
    gather_att = Gather(net, r.pair_two.at[own_rows, :], lambda y, c: r.pair_two.at[rows_of(2 * y + c), :])
    fetch("up_first", "up")
    fetch("mixer_out", "out_weight")

    r.key_grad[...] = jnp.zeros_like(r.key_grad)
    r.value_grad[...] = jnp.zeros_like(r.value_grad)
    gather_d.forward()
    for name in ("qkv", "lse", "attended_full"):
        wait[name].wait()
    gather_d.wait()
    turn(r.layer_left, r.turned_one)
    gather_d.free()
    fetch("normed_b_all", "layer_left")
    up_d.product(r.turned_one, None)
    go.wait_recv()
    back = net.spread(
        lambda rank: r.qkv_grad.at[:, rows_of(rank), :], lambda block: r.mixed_grad_c.at[:, :, lanes_of(block)], False
    )
    for part in (3, 2, 1, 0):
        attention_back(r, part)
        back.start(lambda rank, part=part: rank // 2 == part)
    back.own()
    for name, into in (
        ("kernel_re", "lse"),
        ("kernel_im", "attended_full"),
        ("signal_re", "query_grad"),
        ("signal_im", "key_grad"),
    ):
        fetch(name, into)
    up_d.second()
    r.block_out[0] = (r.total[...] + mm(r.layer_second[own_rows, :], r.down[...])).astype(BF)
    fetch("down_first", "down")
    for made in gathers:
        made.forward()
    for made in gathers:
        made.wait()
    down_d.product(None, r.layer_second)
    for made in gathers:
        made.free()
    fetch("active_b_all", "layer_second")
    up_d.last()

    normal, inverse_c = pieces(r.stream_c[...])
    wait["project_in"].wait()
    back.wait_recv()
    grad = mm_nt(r.mixed_grad_c[0], r.in_weight[:, 0:WIDE])
    for index in range(1, 3):
        grad = grad + mm_nt(r.mixed_grad_c[index], r.in_weight[:, WIDE * index : WIDE * index + WIDE])
    fetch("mixer_in", "in_weight")
    pair_columns(r.mixed_grad_c, r.grad_d_low, r.pairs)
    pair_c.share_pairs(r.pairs)
    grad, gain_three = pieces_back(grad, normal, inverse_c, r.attention_norm_gain[...][None])
    grad = grad + r.grad_d[...]
    r.total[...] = grad
    r.grad_c_low[...] = grad.astype(BF)
    down_d.free_shared()
    r.turned[...] = r.grad_c_low[...].T
    down_b.share_rows(r.turned)
    up_d.free_shared()
    wait["up_first"].wait()
    wait["down_first"].wait()
    wait["bend_b"].wait()
    for step, (index, other) in enumerate(net.order()):
        lanes = pl.ds(pl.multiple_of(WIDE * index, WIDE), WIDE)
        slope = (r.bend_b[:, lanes].astype(F32) * mm_nt(r.grad_c_low[...], r.down[lanes, :])).astype(BF)
        up_b.give(r.slopes, step, slope, other)
        part = mm_nt(slope, r.up[:, lanes])
        if step == 0:
            r.grad_b[...] = part
        else:
            r.grad_b[...] += part
    for name in ("stream_b", "response", "query_a", "shifted", "value_a", "key_ext", "mixer_out"):
        wait[name].wait()
    normal, inverse_b = pieces(r.stream_b[...])
    grad, gain_two = pieces_back(r.grad_b[...], normal, inverse_b, r.gain_second[...][None])
    grad = grad + r.total[...]
    r.grad_b[...] = grad
    r.grad_b_low[...] = grad.astype(BF)
    gated_grad = mm_nt(r.grad_b_low[...], r.out_weight[...])
    r.mixed_grad_a[0] = (gated_grad * r.response[...]).astype(BF)
    response_grad = gated_grad * r.query_a[...]
    r.response_grad[...] = response_grad
    r.response_grad_low[...] = response_grad.astype(BF)
    go = net.spread(
        lambda block: r.response_grad_low.at[:, lanes_of(block)], lambda rank: r.conv_grad.at[rows_of(rank), :], True
    )
    go.start()
    go.own()
    after = Beside(net, r.response_grad_low.at[0:64, :], r.response_next, -1)
    after.start()

    @pl.when(net.s == RANKS - 1)
    def _():
        r.response_next[...] = jnp.zeros_like(r.response_next)

    skip_part = jnp.sum(response_grad * (r.shifted[...] * r.value_a[...]), axis=0, keepdims=True)
    down_d.second()
    gather_att.forward()
    wait["normed_c_all"].wait()
    turn(r.pair_one, r.turned_one)
    gather_att.wait()
    turn(r.pair_two, r.turned_two)
    gather_att.free()
    fetch("normed_a_all", "pair_one")
    fetch("gated_all", "pair_two")
    pair_c.product(r.turned_one, r.turned_two)
    wait["active_b_all"].wait()
    down_b.product(None, r.layer_second)
    wait["normed_b_all"].wait()
    turn(r.layer_left, r.turned_one)
    up_d.end(near)

    for name in TABLES + ("kernel_re", "kernel_im", "signal_re", "signal_im"):
        wait[name].wait()
    kernel_re, kernel_im, signal_re, signal_im = r.lse, r.attended_full, r.query_grad, r.key_grad
    r.signal_grad[SPAN:, :] = jnp.zeros((64, BLOCK), BF)
    transform(r, net, go, r.conv_grad, r.grad_re, r.grad_im)
    back = net.spread(
        lambda rank: r.signal_grad.at[pl.ds(pl.multiple_of(ROWS * rank, ROWS), 192), :],
        lambda block: r.signal_grad_home.at[:, lanes_of(block)],
        False,
    )
    inverse(
        r,
        r.grad_re[...] * kernel_re[...] + r.grad_im[...] * kernel_im[...],
        r.grad_im[...] * kernel_re[...] - r.grad_re[...] * kernel_im[...],
        r.signal_grad,
        back,
    )
    back.own()
    up_b.product(r.turned_one, None)
    down_d.last()
    pair_c.second()
    down_b.second()
    after.wait_recv()
    for name in ("shift_taps", "mode_coef", "mode_rate", "value_next"):
        wait[name].wait()
    back.wait_recv()

    skip = r.skip_gain[...][None]
    signal_grad = r.signal_grad_home[0:ROWS, :].astype(F32) + skip * r.response_grad[...]
    r.grad_ext[0:ROWS, :] = signal_grad * r.value_a[...]
    r.mixed_grad_a[2] = (signal_grad * r.shifted[...]).astype(BF)
    signal_grad = r.signal_grad_home[ROWS:192, :].astype(F32) + skip * r.response_next[...].astype(F32)
    r.grad_ext[ROWS:192, :] = signal_grad * r.value_next[...].astype(F32)
    shift_back(r.grad_ext, r.key_ext, r.shift_taps, r.total, r.taps)
    r.mixed_grad_a[1] = r.total[...].astype(BF)
    pair_c.free_shared()
    pair_columns(r.mixed_grad_a, r.grad_b_low, r.pairs)
    pair_a.share_pairs(r.pairs)
    wait["mixer_in"].wait()
    wait["tokens"].wait()
    grad = mm_nt(r.mixed_grad_a[0], r.in_weight[:, 0:WIDE])
    for index in range(1, 3):
        grad = grad + mm_nt(r.mixed_grad_a[index], r.in_weight[:, WIDE * index : WIDE * index + WIDE])
    normal, inverse_a = pieces(r.tokens[0].astype(F32))
    grad, gain_one = pieces_back(grad, normal, inverse_a, r.mixer_norm_gain[...][None])
    r.token_grad[0] = r.grad_b[...] + grad

    gains = jnp.concatenate([gain_one, skip_part, gain_two, gain_three, gain_four, jnp.zeros((3, WIDE), F32)], axis=0)
    for block in range(4):
        r.small[block // 2, block % 2, 0:16, :] = r.taps[16 * block : 16 * block + 16, :]
        r.small[block // 2, block % 2, 16:24, :] = gains
    swap = net.send(r.small.at[:, flip(net.c)], r.small_c, net.sibling)
    re = r.grad_re[...] * signal_re[...] - r.grad_im[...] * signal_im[...]
    im = r.grad_re[...] * signal_im[...] + r.grad_im[...] * signal_re[...]
    inverse(r, re, im, r.value_grad)
    block = lanes_of(jnp.clip(net.s - 1, 0, OWNERS - 1))
    r.coef[...] = r.mode_coef[:, block]
    r.rate[...] = r.mode_rate[:, block]
    wait["normed_a_all"].wait()
    turn(r.pair_one, r.turned_one)
    wait["gated_all"].wait()
    turn(r.pair_two, r.turned_two)
    up_b.second()
    swap.wait_recv()
    r.small[:, net.c] += r.small_c[...]
    swap = net.send(r.small.at[flip(net.y), net.c], r.small_swap.at[0], net.by_y)
    pair_c.last()
    down_b.last()
    pair_a.product(r.turned_one, r.turned_two)
    modes_back(r.coef, r.rate, r.value_grad, r.mode_part.at[0, 0:64], r.mode_part.at[0, 64:128])
    mode = net.send(r.mode_part.at[0], r.mode_swap.at[0], net.sibling)
    swap.wait_recv()
    r.small_sum[0] = r.small[net.y, net.c] + r.small_swap[0]
    swap = net.send(r.small_sum.at[0], r.small_swap.at[1], net.by_x)
    up_b.last()
    mode.wait_recv()
    r.mode_part[1] = r.mode_part[0] + r.mode_swap[0]
    mode = net.send(r.mode_part.at[1], r.mode_swap.at[1], net.by_y)
    pair_a.second()
    mode.wait_recv()
    r.mode_part[2] = r.mode_part[1] + r.mode_swap[1]
    back = net.spread(
        lambda rank: r.mode_part.at[2], lambda block: r.mode_home.at[:, lanes_of(block)], False, holds_columns
    )
    back.start()
    back.own()
    swap.wait_recv()
    r.small_sum[1] = r.small_sum[0] + r.small_swap[1]
    swap = net.send(r.small_sum.at[1], r.small_swap.at[2], net.by_low)
    pair_a.last()
    swap.wait_recv()
    r.small_sum[2] = r.small_sum[1] + r.small_swap[2]
    swap = net.send(r.small_sum.at[2], r.small_swap.at[3], net.by_high)
    down_d.end(near)
    pair_c.end(near)
    down_b.end(near)
    turn_back = lax.rem(WIDE - 96 * net.s, WIDE)
    back.wait_recv()
    r.mode_out[...] = pltpu.roll(r.mode_home[...], turn_back, 1)[:, 0:128]
    swap.wait_recv()
    r.small_out[...] = pltpu.roll(r.small_sum[2] + r.small_swap[3], turn_back, 1)[:, 0:128]
    up_b.end(near)
    pair_a.end(near)
    net.finish()
    near.finish()


def kernel_z(*refs):
    block_in, token_in, mode, small = refs[:4]
    sums = refs[4:16]
    (
        block_out,
        token_grad,
        gain_one,
        mixer_in,
        taps,
        coef,
        rate,
        skip,
        mixer_out,
        gain_two,
        up_first,
        down_first,
        gain_three,
        project_in,
        project_out,
        gain_four,
        up_second,
        down_second,
    ) = refs[16:]
    block_out[...] = block_in[...]
    token_grad[...] = token_in[...]
    taps[...] = small[0:16, 0:96]
    for at, out in enumerate((gain_one, skip, gain_two, gain_three, gain_four)):
        out[...] = small[16 + at, 0:96]
    coef[...] = mode[0:64, 0:96]
    rate[...] = mode[64:128, 0:96]

    def block(index, first, count):
        rows = slice(first, first + count)
        return sums[2 * index][rows, :].astype(F32) + sums[2 * index + 1][rows, :].astype(F32)

    for index, up, down in ((0, up_second, down_second), (3, up_first, down_first)):
        for tile in range(6):
            up[:, 128 * tile : 128 * tile + 128] = block(index, 96 * tile, 96)
        for tile in range(3):
            down[:, 128 * tile : 128 * tile + 128] = block(index + 1, 192 * tile, 192)
    for index, wide, narrow in ((2, project_in, project_out), (5, mixer_in, mixer_out)):
        for tile in range(4):
            wide[:, 128 * tile : 128 * tile + 128] = block(index, 96 * tile, 96)
        mixed = block(index, 384, 96)
        wide[:, 512:576] = mixed[:, 0:64]
        narrow[:, 0:64] = mixed[:, 64:128]
        narrow[:, 64:192] = block(index, 480, 96)


class Refs:
    pass


def call(body, identity, inputs, hbm, smem, outs, hbm_outs, scratch, semaphores):
    names = list(inputs) + [name + "_hbm" for name in hbm] + list(smem) + list(outs) + list(hbm_outs) + list(scratch)
    names += ["ends", "send_sem", "recv_sem", "local_sem"]

    def run(*refs):
        r = Refs()
        for name, ref in zip(names, refs):
            setattr(r, name, ref)
        body(r)

    vmem = pl.BlockSpec(memory_space=pltpu.VMEM)
    results = pl.pallas_call(
        run,
        out_shape=[jax.ShapeDtypeStruct(shape, kind) for shape, kind in (*outs.values(), *hbm_outs.values())],
        in_specs=[vmem] * len(inputs)
        + [pl.BlockSpec(memory_space=pl.ANY)] * len(hbm)
        + [pl.BlockSpec(memory_space=pltpu.SMEM)] * len(smem),
        out_specs=[vmem] * len(outs) + [pl.BlockSpec(memory_space=pl.ANY)] * len(hbm_outs),
        scratch_shapes=[pltpu.VMEM(shape, kind) for shape, kind in scratch.values()]
        + [pltpu.SMEM((3,), jnp.int32)]
        + [pltpu.SemaphoreType.DMA((semaphores[0],)), pltpu.SemaphoreType.DMA((semaphores[0],))]
        + [pltpu.SemaphoreType.DMA((semaphores[1],))],
        compiler_params=pltpu.CompilerParams(
            collective_id=identity, has_side_effects=True, vmem_limit_bytes=VMEM_BYTES
        ),
    )(*inputs.values(), *hbm.values(), *smem.values())
    return dict(zip((*outs, *hbm_outs), results))


VMEM_BYTES = 66_900_000


def odd_tables():
    odd = 2 * np.arange(SPAN, dtype=np.int64) + 1
    angle = (np.outer(odd, odd) % (8 * SPAN)) * (math.pi / (4 * SPAN))
    phase = (odd * (math.pi / (4 * SPAN)))[:, None] * np.ones((1, BLOCK))
    tables = {
        "cos_table": jnp.asarray(np.cos(angle).astype(ml_dtypes.bfloat16)),
        "sin_table": jnp.asarray(np.sin(angle).astype(ml_dtypes.bfloat16)),
    }
    return tables, jnp.asarray(np.cos(phase), F32), jnp.asarray(np.sin(phase), F32)


def shards_fast(
    tokens,
    doc_lengths,
    mixer_norm_gain,
    mixer_in,
    shift_taps,
    mode_coef,
    mode_rate,
    skip_gain,
    mixer_out,
    gain_second,
    up_first,
    down_first,
    attention_norm_gain,
    project_in,
    project_out,
    gain_fourth,
    up_second,
    down_second,
    cotangent,
):
    tables, phase_cos, phase_sin = odd_tables()
    home, thrice, tall = (ROWS, WIDE), (3, ROWS, WIDE), (ROWS, 4 * WIDE)
    span = (SPAN, BLOCK)
    kept = dict(
        value_next=((64, WIDE), BF),
        query_a=(home, F32),
        value_a=(home, F32),
        key_ext=((192, WIDE), F32),
        shifted=(home, F32),
        response=(home, F32),
        stream_b=(home, F32),
        bend_b=(tall, BF),
        qkv=((3, *span), BF),
        lse=(span, F32),
        attended_full=(span, F32),
        kernel_re=(span, F32),
        kernel_im=(span, F32),
        signal_re=(span, F32),
        signal_im=(span, F32),
    )
    lefts = dict(normed_a=(home, BF), gated=(home, BF), normed_b=(home, BF), active_b=(tall, BF), normed_c=(home, BF))
    modes_scratch = dict(
        coef=((64, BLOCK), F32),
        rate=((64, BLOCK), F32),
        shift_taps=((64, WIDE), F32),
        mode_coef=((64, WIDE), F32),
        mode_rate=((64, WIDE), F32),
    )
    packs = dict(pack_re=((SPAN, 256), BF), pack_im=((SPAN, 256), BF))
    table_scratch = dict(cos_table=((SPAN, SPAN), BF), sin_table=((SPAN, SPAN), BF))
    a = call(
        kernel_a,
        0,
        dict(
            tokens=tokens,
            mixer_norm_gain=mixer_norm_gain,
            skip_gain=skip_gain,
            gain_second=gain_second,
            attention_norm_gain=attention_norm_gain,
        ),
        dict(
            mixer_in=mixer_in,
            shift_taps=shift_taps,
            mode_coef=mode_coef,
            mode_rate=mode_rate,
            **tables,
            phase_cos=phase_cos,
            phase_sin=phase_sin,
            mixer_out=mixer_out,
            up_first=up_first,
            down_first=down_first,
            project_in=project_in,
        ),
        dict(doc_lengths=doc_lengths),
        dict(stream_c=(home, F32), attended=(home, BF)),
        dict(
            **{name + "_kept": made for name, made in kept.items()},
            **{name + "_all": ((4 * shape[0], shape[1]), kind) for name, (shape, kind) in lefts.items()},
        ),
        dict(
            **kept,
            **lefts,
            **modes_scratch,
            **packs,
            rim_in=((64, WIDE), BF),
            **table_scratch,
            phase_cos=(span, F32),
            phase_sin=(span, F32),
            value_low=((64, WIDE), BF),
            product_low=(home, BF),
            signal=(span, BF),
            mode_rows=(span, F32),
            conv=(span, BF),
            conv_home=(home, BF),
            mixed_c=(thrice, BF),
            attended_low=(span, BF),
            mixer_in=((WIDE, 3 * WIDE), BF),
            mixer_out=((WIDE, WIDE), BF),
            up_first=((WIDE, 4 * WIDE), BF),
            down_first=((4 * WIDE, WIDE), BF),
            project_in=((WIDE, 3 * WIDE), BF),
        ),
        (64, 48),
    )
    kinds = dict(up_d=UP, down_d=DOWN, pair_c=PAIR, up_b=UP, down_b=DOWN, pair_a=PAIR)
    sum_outs, sums = {}, {}
    for name, kind in kinds.items():
        sum_outs[name + "_own"] = ((LENGTH, 128), BF)
        sum_outs[name + "_third"] = ((LENGTH, 128), BF)
        sums.update(sum_scratch(name, kind))
    b = call(
        kernel_b,
        1,
        dict(
            mixer_norm_gain=mixer_norm_gain,
            skip_gain=skip_gain,
            gain_second=gain_second,
            attention_norm_gain=attention_norm_gain,
            gain_fourth=gain_fourth,
        ),
        dict(
            project_out=project_out,
            attended=a["attended"],
            stream_c=a["stream_c"],
            cotangent=cotangent,
            tokens=tokens,
            up_second=up_second,
            down_second=down_second,
            **{name: a[name + "_kept"] for name in kept},
            **{name + "_all": a[name + "_all"] for name in lefts},
            **tables,
            shift_taps=shift_taps,
            mode_coef=mode_coef,
            mode_rate=mode_rate,
            project_in=project_in,
            up_first=up_first,
            down_first=down_first,
            mixer_out=mixer_out,
            mixer_in=mixer_in,
        ),
        dict(doc_lengths=doc_lengths),
        dict(
            block_out=((1, *home), BF),
            token_grad=((1, *home), F32),
            mode_out=((128, 128), F32),
            small_out=((24, 128), F32),
        ),
        sum_outs,
        dict(
            **{name: made for name, made in kept.items() if not name.startswith(("kernel", "signal"))},
            **modes_scratch,
            **packs,
            **table_scratch,
            **sums,
            attended=(home, BF),
            stream_c=(home, F32),
            cotangent=((1, *home), BF),
            tokens=((1, *home), BF),
            up=((WIDE, 4 * WIDE), BF),
            down=((4 * WIDE, WIDE), BF),
            in_weight=((WIDE, 3 * WIDE), BF),
            out_weight=((WIDE, WIDE), BF),
            layer_left=((512, WIDE), BF),
            layer_second=((512, 4 * WIDE), BF),
            pair_one=((512, WIDE), BF),
            pair_two=((512, WIDE), BF),
            turned_one=((WIDE, 512), BF),
            turned_two=((WIDE, 512), BF),
            turned=((WIDE, ROWS), BF),
            slopes=(thrice, BF),
            pairs=((4, *home), BF),
            total=(home, F32),
            grad_d=(home, F32),
            grad_d_low=(home, BF),
            att_grad_home=(home, BF),
            att_grad=(span, BF),
            query_grad=(span, F32),
            key_grad=(span, F32),
            value_grad=(span, F32),
            qkv_grad=((3, *span), BF),
            mixed_grad_c=(thrice, BF),
            grad_c_low=(home, BF),
            grad_b=(home, F32),
            grad_b_low=(home, BF),
            mixed_grad_a=(thrice, BF),
            response_grad=(home, F32),
            response_grad_low=(home, BF),
            conv_grad=(span, BF),
            grad_re=(span, F32),
            grad_im=(span, F32),
            signal_grad=((SPAN + 64, BLOCK), BF),
            signal_grad_home=((192, WIDE), BF),
            response_next=((64, WIDE), BF),
            grad_ext=((192, WIDE), F32),
            taps=((64, WIDE), F32),
            small=((2, 2, 24, WIDE), F32),
            small_c=((2, 24, WIDE), F32),
            small_swap=((4, 24, WIDE), F32),
            small_sum=((3, 24, WIDE), F32),
            mode_part=((3, 128, 128), F32),
            mode_swap=((2, 128, 128), F32),
            mode_home=((128, WIDE), F32),
        ),
        (160, 64),
    )
    vmem = pl.BlockSpec(memory_space=pltpu.VMEM)
    given = [b[name] for name in ("block_out", "token_grad", "mode_out", "small_out")]
    for name in kinds:
        given += [b[name + "_own"], b[name + "_third"]]
    gain = ((96,), F32)
    wide, narrow, up, down, mode = ((96, 576), F32), ((96, 192), F32), ((96, 768), F32), ((192, 384), F32), ((64, 96), F32)
    shapes = (
        ((1, *home), BF),
        ((1, *home), F32),
        gain,
        wide,
        ((16, 96), F32),
        mode,
        mode,
        gain,
        narrow,
        gain,
        up,
        down,
        gain,
        wide,
        narrow,
        gain,
        up,
        down,
    )
    results = pl.pallas_call(
        kernel_z,
        out_shape=[jax.ShapeDtypeStruct(shape, kind) for shape, kind in shapes],
        in_specs=[vmem] * len(given),
        out_specs=[vmem] * len(shapes),
    )(*given)
    return tuple(result.T if result.shape == (192, 384) else result for result in results)


def solution(mesh):
    in_specs = (
        P("batch", "seq", None),
        P("batch", None),
        P(),
        P(),
        P(),
        P(),
        P(),
        P(),
        P(),
        P(),
        P(),
        P(),
        P(),
        P(),
        P(),
        P(),
        P(),
        P(),
        P("batch", "seq", None),
    )
    out_specs = (
        P("batch", "seq", None),
        P("batch", "seq", None),
        P("seq"),
        P("seq", "batch"),
        P("batch", "seq"),
        P(None, "seq"),
        P(None, "seq"),
        P("seq"),
        P("seq", "batch"),
        P("seq"),
        P("seq", "batch"),
        P("seq", "batch"),
        P("seq"),
        P("seq", "batch"),
        P("seq", "batch"),
        P("seq"),
        P("seq", "batch"),
        P("seq", "batch"),
    )
    fast = mesh.shape["seq"] == RANKS and mesh.shape["batch"] == 4
    return jax.shard_map(shards_fast if fast else shards, mesh=mesh, in_specs=in_specs, out_specs=out_specs, check_vma=False)
```

```python
import math

import jax
import jax.numpy as jnp
import ml_dtypes
import numpy as np
from jax import lax
from jax.experimental import pallas as pl
from jax.experimental.pallas import tpu as pltpu
from jax.sharding import PartitionSpec as P

HEADS = 12


HIGH = lax.Precision.HIGHEST
NEGATIVE = -1e30


def shifted_2(value, axis, steps):
    count = lax.axis_size(axis)
    leading, last = (max(0, -steps), min(count, count - steps))
    return lax.ppermute(value, axis, [(source, source + steps) for source in range(leading, last)])


def shortened(x):

    def short(part):
        return part.astype(jnp.bfloat16) if part.dtype == jnp.float32 else part

    return jax.tree.map(short, x)


def mult(form, left, right):
    return jnp.einsum(form, left, right, precision=HIGH, preferred_element_type=jnp.float32)


def norm_pieces(value):
    row_mean = jnp.mean(value, axis=-1, keepdims=True)
    cent = value - row_mean
    inverse_deviation = lax.rsqrt(jnp.mean(cent * cent, axis=-1, keepdims=True) + 1e-05)
    return (cent * inverse_deviation, inverse_deviation)


def norm_backward(incoming_gradient, centered_normalized, inverse_deviation, gain_vector):
    gain_share = jnp.sum(incoming_gradient * centered_normalized, axis=0)
    scaled_rows = incoming_gradient * gain_vector
    inner_product = jnp.mean(scaled_rows, axis=-1, keepdims=True)
    cross_term = jnp.mean(scaled_rows * centered_normalized, axis=-1, keepdims=True)
    return (
        inverse_deviation * (scaled_rows - inner_product - centered_normalized * cross_term),
        gain_share,
    )


def segment_of(where, ends):
    return jnp.sum((where[:, None] >= ends[None, :]).astype(jnp.int32), axis=1)


def allowed(query_pos, key_pos, ends):
    same = segment_of(query_pos, ends)[:, None] == segment_of(key_pos, ends)[None, :]
    return (key_pos[None, :] <= query_pos[:, None]) & same


def kernel_rows(coef, rate, times):

    def step(total, pair):
        scale, decay = pair
        return (total + scale[:, None] * jnp.exp(-decay[:, None] * times[None, :]), None)

    start = jnp.zeros((coef.shape[1], times.shape[0]), jnp.float32)
    return lax.scan(step, start, (coef, rate))[0]


def kernel_grads(coef, rate, times, incoming_gradient):

    def step(carry, pair):
        scale, decay = pair
        fall = incoming_gradient * jnp.exp(-decay[:, None] * times[None, :])
        return (carry, (jnp.sum(fall, axis=1), -scale * jnp.sum(fall * times[None, :], axis=1)))

    return lax.scan(step, jnp.zeros((), jnp.float32), (coef, rate))[1]


def angle_pair(left, right, period):
    turns = left[:, None] * right[None, :] % period
    angle = turns.astype(jnp.float32) * (2.0 * math.pi / period)
    return (jnp.cos(angle), jnp.sin(angle))


def dft_tables(blocks, rows):
    wide = 2 * blocks
    block_ids = jnp.arange(blocks, dtype=jnp.int32)
    wide_ids = jnp.arange(wide, dtype=jnp.int32)
    row_ids = jnp.arange(rows, dtype=jnp.int32)
    return (
        angle_pair(block_ids, wide_ids, wide),
        angle_pair(wide_ids, row_ids, wide * rows),
        angle_pair(row_ids, row_ids, rows),
    )


def forward_spectrum(signal, tables, blocks, rows):
    (cos_one, sin_one), (cos_two, sin_two), (cos_three, sin_three) = tables
    folded = signal.reshape(signal.shape[0], blocks, rows)
    first_re = mult("cpr,pf->cfr", folded, cos_one)
    first_im = -mult("cpr,pf->cfr", folded, sin_one)
    turned_re = first_re * cos_two + first_im * sin_two
    turned_im = first_im * cos_two - first_re * sin_two
    spec_re = mult("cfr,rk->cfk", turned_re, cos_three) + mult("cfr,rk->cfk", turned_im, sin_three)
    spec_im = mult("cfr,rk->cfk", turned_im, cos_three) - mult("cfr,rk->cfk", turned_re, sin_three)
    return (spec_re, spec_im)


def inverse_signal(spec_re, spec_im, tables, blocks, rows):
    (cos_one, sin_one), (cos_two, sin_two), (cos_three, sin_three) = tables
    inner_re = mult("cfk,rk->cfr", spec_re, cos_three) - mult("cfk,rk->cfr", spec_im, sin_three)
    inner_im = mult("cfk,rk->cfr", spec_im, cos_three) + mult("cfk,rk->cfr", spec_re, sin_three)
    turned_re = inner_re * cos_two - inner_im * sin_two
    turned_im = inner_im * cos_two + inner_re * sin_two
    result_value = mult("cfr,pf->cpr", turned_re, cos_one) - mult("cfr,pf->cpr", turned_im, sin_one)
    return result_value.reshape(spec_re.shape[0], blocks * rows) / (2.0 * blocks * rows)


def attend_block(state, query, query_pos, key_block, value_block, key_pos, ends, scale):
    top, mass, accum = state
    scores = (
        jnp.einsum("qhd,khd->hqk", query, key_block, preferred_element_type=jnp.float32) * scale
    )
    mask = allowed(query_pos, key_pos, ends)[None]
    newtop = jnp.maximum(top, jnp.max(jnp.where(mask, scores, NEGATIVE), axis=-1))
    weights = jnp.where(mask, jnp.exp(scores - newtop[:, :, None]), 0.0)
    factor = jnp.exp(top - newtop)
    mass = mass * factor + jnp.sum(weights, axis=-1)
    accum = accum * factor[:, :, None] + jnp.einsum(
        "hqk,khd->hqd", weights, value_block.astype(jnp.float32), preferred_element_type=jnp.float32
    )
    return (newtop, mass, accum)


def score_grads(
    query, grads, lse_rows, delta_rows, query_pos, key_block, value_block, key_pos, ends, scale
):
    scores = (
        jnp.einsum("qhd,khd->hqk", query, key_block, preferred_element_type=jnp.float32) * scale
    )
    mask = allowed(query_pos, key_pos, ends)[None]
    probs = jnp.where(mask, jnp.exp(scores - lse_rows[:, :, None]), 0.0)
    dots = jnp.einsum("qhd,khd->hqk", grads, value_block, preferred_element_type=jnp.float32)
    return (probs, (probs * (dots - delta_rows[:, :, None])).astype(jnp.bfloat16))


def query_back(
    query, grads, lse_rows, delta_rows, query_pos, key_block, value_block, key_pos, ends, scale
):
    score_grad = score_grads(
        query, grads, lse_rows, delta_rows, query_pos, key_block, value_block, key_pos, ends, scale
    )[1]
    return (
        jnp.einsum("hqk,khd->qhd", score_grad, key_block, preferred_element_type=jnp.float32)
        * scale
    )


def key_back(
    query, grads, lse_rows, delta_rows, query_pos, key_block, value_block, key_pos, ends, scale
):
    probs, score_grad = score_grads(
        query, grads, lse_rows, delta_rows, query_pos, key_block, value_block, key_pos, ends, scale
    )
    key_part = (
        jnp.einsum("hqk,qhd->khd", score_grad, query, preferred_element_type=jnp.float32) * scale
    )
    value_part = jnp.einsum(
        "hqk,qhd->khd", probs, grads.astype(jnp.float32), preferred_element_type=jnp.float32
    )
    return (key_part, value_part)


def scan_keys(carry, keys, values, update):
    count = keys.shape[0]
    width = keys.shape[1]
    head_size = width // HEADS
    step = math.gcd(count, 1024)
    firsts = step * jnp.arange(count // step, dtype=jnp.int32)

    def inner_product(state, item):
        key_block, value_block, first = item
        key_pos = first + jnp.arange(step, dtype=jnp.int32)
        return (update(state, key_block, value_block, key_pos), None)

    items = (
        keys.reshape(count // step, step, HEADS, head_size),
        values.reshape(count // step, step, HEADS, head_size),
        firsts,
    )
    return lax.scan(inner_product, carry, items)[0]


def feed_forward(residual_stream, gain_vector, w_up, w_down):
    centered_normalized, inverse_deviation = norm_pieces(residual_stream)
    normed_rows = (centered_normalized * gain_vector).astype(jnp.bfloat16)
    raised_rows = jnp.dot(normed_rows, w_up, preferred_element_type=jnp.float32)
    active_tokens = jax.nn.gelu(raised_rows).astype(jnp.bfloat16)
    result_value = residual_stream + jnp.dot(
        active_tokens, w_down, preferred_element_type=jnp.float32
    )
    return (
        result_value,
        (centered_normalized, inverse_deviation, normed_rows, raised_rows, active_tokens),
    )


def feed_back(incoming_gradient, saved_residuals, gain_vector, w_up, w_down):
    centered_normalized, inverse_deviation, normed_rows, raised_rows, active_tokens = (
        saved_residuals
    )
    grad_low = incoming_gradient.astype(jnp.bfloat16)
    down_part = jnp.einsum("tf,td->fd", active_tokens, grad_low, preferred_element_type=jnp.float32)
    active_grad = jnp.einsum("td,fd->tf", grad_low, w_down, preferred_element_type=jnp.float32)
    slope = jax.vjp(jax.nn.gelu, raised_rows)[1](active_grad)[0].astype(jnp.bfloat16)
    up_part = jnp.einsum("td,tf->df", normed_rows, slope, preferred_element_type=jnp.float32)
    normed_gradient = jnp.einsum("tf,df->td", slope, w_up, preferred_element_type=jnp.float32)
    input_gradient, gain_share = norm_backward(
        normed_gradient, centered_normalized, inverse_deviation, gain_vector
    )
    return (incoming_gradient + input_gradient, gain_share, up_part, down_part)


def shards(
    tokens,
    doc_lengths,
    mixer_norm_gain,
    mixer_in,
    shift_taps,
    mode_coef,
    mode_rate,
    skip_gain,
    mixer_out,
    gain_second,
    up_first,
    down_first,
    attention_norm_gain,
    project_in,
    project_out,
    gain_fourth,
    up_second,
    down_second,
    cotangent,
):
    rows = tokens.shape[1]
    width = tokens.shape[2]
    blocks = lax.axis_size("seq")
    rank = lax.axis_index("seq")
    total = rows * blocks
    head_size = width // HEADS
    scale = head_size ** (-0.5)
    lags = shift_taps.shape[0]
    channels = width // blocks
    ends = jnp.cumsum(doc_lengths[0])
    here = rank * rows + jnp.arange(rows, dtype=jnp.int32)
    residual_stream = tokens[0].astype(jnp.float32)
    mixer_centered_normalized, mixer_inverse_deviation = norm_pieces(residual_stream)
    mixer_normed_rows = (mixer_centered_normalized * mixer_norm_gain).astype(jnp.bfloat16)
    mixed_a = jnp.dot(mixer_normed_rows, mixer_in, preferred_element_type=jnp.float32)
    query_a = mixed_a[:, :width]
    key_a = mixed_a[:, width : 2 * width]
    value_a = mixed_a[:, 2 * width :]
    rim = shifted_2(key_a[rows - (lags - 1) :].astype(jnp.bfloat16), "seq", 1).astype(jnp.float32)
    key_ext = jnp.concatenate([rim, key_a], axis=0)
    shifted = jnp.zeros_like(key_a)
    for lag in range(lags):
        shifted = shifted + shift_taps[lag] * key_ext[lags - 1 - lag : lags - 1 - lag + rows]
    product_kv = shifted * value_a
    channel_in = lax.all_to_all(
        product_kv.T.reshape(blocks, channels, rows).astype(jnp.bfloat16),
        "seq",
        split_axis=0,
        concat_axis=2,
        tiled=True,
    ).astype(jnp.float32)[0]
    times = jnp.arange(total, dtype=jnp.int32).astype(jnp.float32)
    coef_here = lax.dynamic_slice_in_dim(mode_coef, rank * channels, channels, 1)
    rate_here = lax.dynamic_slice_in_dim(mode_rate, rank * channels, channels, 1)
    kernel_here = kernel_rows(coef_here, rate_here, times)
    tables = dft_tables(blocks, rows)
    sig_re, sig_im = forward_spectrum(channel_in, tables, blocks, rows)
    ker_re, ker_im = forward_spectrum(kernel_here, tables, blocks, rows)
    conv_chan = inverse_signal(
        sig_re * ker_re - sig_im * ker_im, sig_re * ker_im + sig_im * ker_re, tables, blocks, rows
    )
    conv_home = lax.all_to_all(
        conv_chan.reshape(1, channels, total).astype(jnp.bfloat16),
        "seq",
        split_axis=2,
        concat_axis=0,
        tiled=True,
    ).astype(jnp.float32)
    response = conv_home.reshape(width, rows).T + skip_gain * product_kv
    gated = (query_a * response).astype(jnp.bfloat16)
    stream_b = residual_stream + jnp.dot(gated, mixer_out, preferred_element_type=jnp.float32)
    attention_residual_stream, saved_b = feed_forward(stream_b, gain_second, up_first, down_first)
    attention_centered_normalized, attention_inverse_deviation = norm_pieces(
        attention_residual_stream
    )
    attention_normed_rows = (attention_centered_normalized * attention_norm_gain).astype(
        jnp.bfloat16
    )
    mixed_c = jnp.dot(attention_normed_rows, project_in, preferred_element_type=jnp.float32).astype(
        jnp.bfloat16
    )
    query_flat = mixed_c[:, :width]
    key_flat = mixed_c[:, width : 2 * width]
    value_flat = mixed_c[:, 2 * width :]
    query_c = query_flat.reshape(rows, HEADS, head_size)
    key_heads = key_flat.reshape(rows, HEADS, head_size)
    value_heads = value_flat.reshape(rows, HEADS, head_size)

    def forward_update(state, key_block, value_block, key_pos):
        return attend_block(state, query_c, here, key_block, value_block, key_pos, ends, scale)

    begin = (
        jnp.full((HEADS, rows), NEGATIVE, jnp.float32),
        jnp.zeros((HEADS, rows), jnp.float32),
        jnp.zeros((HEADS, rows, head_size), jnp.float32),
    )
    piece = (
        lax.all_gather(key_flat, "seq", axis=0, tiled=True),
        lax.all_gather(value_flat, "seq", axis=0, tiled=True),
    )
    top, mass, accum = scan_keys(begin, piece[0], piece[1], forward_update)
    lse = top + jnp.log(mass)
    att_full = accum / mass[:, :, None]
    attended = att_full.transpose(1, 0, 2).reshape(rows, width).astype(jnp.bfloat16)
    stream_d = attention_residual_stream + jnp.dot(
        attended, project_out, preferred_element_type=jnp.float32
    )
    result_value, saved_d = feed_forward(stream_d, gain_fourth, up_second, down_second)
    block_out = result_value.astype(jnp.bfloat16)[None]
    incoming_gradient = cotangent[0].astype(jnp.float32)
    incoming_gradient, gain_four_part, up_two_part, down_two_part = feed_back(
        incoming_gradient, saved_d, gain_fourth, up_second, down_second
    )
    grad_low = incoming_gradient.astype(jnp.bfloat16)
    out_part_c = jnp.einsum("td,te->de", attended, grad_low, preferred_element_type=jnp.float32)
    att_grad = jnp.einsum(
        "te,de->td", grad_low, project_out, preferred_element_type=jnp.float32
    ).astype(jnp.bfloat16)
    grad_heads = att_grad.reshape(rows, HEADS, head_size)
    delta = jnp.sum(grad_heads.astype(jnp.float32).transpose(1, 0, 2) * att_full, axis=-1)
    zero_heads = jnp.zeros((rows, HEADS, head_size), jnp.float32)

    def query_update(summed, key_block, value_block, key_pos):
        return summed + query_back(
            query_c, grad_heads, lse, delta, here, key_block, value_block, key_pos, ends, scale
        )

    piece = (
        lax.all_gather(key_flat, "seq", axis=0, tiled=True),
        lax.all_gather(value_flat, "seq", axis=0, tiled=True),
    )
    query_grad = scan_keys(zero_heads, piece[0], piece[1], query_update)
    lse_all, delta_all = (
        lax.all_gather(lse, "seq", axis=1, tiled=True),
        lax.all_gather(delta, "seq", axis=1, tiled=True),
    )
    queries = lax.all_gather(query_flat, "seq", axis=0, tiled=True)
    grads = lax.all_gather(att_grad, "seq", axis=0, tiled=True)
    count = queries.shape[0]
    step = math.gcd(count, 1024)
    firsts = step * jnp.arange(count // step, dtype=jnp.int32)

    def inner_product(summed, item):
        query_block, grad_block, first = item
        query_pos = first + jnp.arange(step, dtype=jnp.int32)
        lse_rows = lax.dynamic_slice_in_dim(lse_all, first, step, 1)
        delta_rows = lax.dynamic_slice_in_dim(delta_all, first, step, 1)
        parts = key_back(
            query_block,
            grad_block,
            lse_rows,
            delta_rows,
            query_pos,
            key_heads,
            value_heads,
            here,
            ends,
            scale,
        )
        return ((summed[0] + parts[0], summed[1] + parts[1]), None)

    items = (
        queries.reshape(count // step, step, HEADS, head_size),
        grads.reshape(count // step, step, HEADS, head_size),
        firsts,
    )
    key_grad, value_grad = lax.scan(inner_product, (zero_heads, zero_heads), items)[0]
    key_grad = key_grad.reshape(rows, width)
    value_grad = value_grad.reshape(rows, width)
    mixed_grad_c = jnp.concatenate(
        [query_grad.reshape(rows, width), key_grad, value_grad], axis=1
    ).astype(jnp.bfloat16)
    in_part_c = jnp.einsum(
        "td,te->de", attention_normed_rows, mixed_grad_c, preferred_element_type=jnp.float32
    )
    attention_normed_gradient = jnp.einsum(
        "te,de->td", mixed_grad_c, project_in, preferred_element_type=jnp.float32
    )
    attention_norm_gradient, attention_gain_share = norm_backward(
        attention_normed_gradient,
        attention_centered_normalized,
        attention_inverse_deviation,
        attention_norm_gain,
    )
    incoming_gradient = incoming_gradient + attention_norm_gradient
    incoming_gradient, gain_two_part, up_one_part, down_one_part = feed_back(
        incoming_gradient, saved_b, gain_second, up_first, down_first
    )
    grad_low = incoming_gradient.astype(jnp.bfloat16)
    out_part_a = jnp.einsum("td,te->de", gated, grad_low, preferred_element_type=jnp.float32)
    gated_grad = jnp.einsum("te,de->td", grad_low, mixer_out, preferred_element_type=jnp.float32)
    query_grad_a = gated_grad * response
    response_grad = gated_grad * query_a
    skip_part = jnp.sum(response_grad * product_kv, axis=0)
    chan_grad = lax.all_to_all(
        response_grad.T.reshape(blocks, channels, rows).astype(jnp.bfloat16),
        "seq",
        split_axis=0,
        concat_axis=2,
        tiled=True,
    ).astype(jnp.float32)[0]
    grad_re, grad_im = forward_spectrum(chan_grad, tables, blocks, rows)
    signal_grad = inverse_signal(
        ker_re * grad_re + ker_im * grad_im,
        ker_re * grad_im - ker_im * grad_re,
        tables,
        blocks,
        rows,
    )
    kernel_grad = inverse_signal(
        sig_re * grad_re + sig_im * grad_im,
        sig_re * grad_im - sig_im * grad_re,
        tables,
        blocks,
        rows,
    )
    coef_part, rate_part = kernel_grads(coef_here, rate_here, times, kernel_grad)
    returned = lax.all_to_all(
        signal_grad.reshape(1, channels, total).astype(jnp.bfloat16),
        "seq",
        split_axis=2,
        concat_axis=0,
        tiled=True,
    ).astype(jnp.float32)
    kv_grad = returned.reshape(width, rows).T + skip_gain * response_grad
    shifted_grad = kv_grad * value_a
    value_grad_a = kv_grad * shifted
    later = shifted_2(shortened(shifted_grad[: lags - 1]), "seq", -1)
    grad_ext = jnp.concatenate([shifted_grad, later], axis=0)
    key_grad_a = jnp.zeros_like(key_a)
    tap_rows = []
    for lag in range(lags):
        key_grad_a = key_grad_a + shift_taps[lag] * grad_ext[lag : lag + rows]
        tap_rows.append(
            jnp.sum(shifted_grad * key_ext[lags - 1 - lag : lags - 1 - lag + rows], axis=0)
        )
    taps_part = jnp.stack(tap_rows)
    mixed_grad_a = jnp.concatenate([query_grad_a, key_grad_a, value_grad_a], axis=1).astype(
        jnp.bfloat16
    )
    in_part_a = jnp.einsum(
        "td,te->de", mixer_normed_rows, mixed_grad_a, preferred_element_type=jnp.float32
    )
    mixer_normed_gradient = jnp.einsum(
        "te,de->td", mixed_grad_a, mixer_in, preferred_element_type=jnp.float32
    )
    mixer_norm_gradient, mixer_gain_share = norm_backward(
        mixer_normed_gradient, mixer_centered_normalized, mixer_inverse_deviation, mixer_norm_gain
    )
    token_grad = (incoming_gradient + mixer_norm_gradient)[None]
    parts = (
        lax.psum_scatter(mixer_gain_share, "seq", scatter_dimension=0, tiled=True),
        lax.psum_scatter(in_part_a, "seq", scatter_dimension=0, tiled=True),
        lax.psum_scatter(taps_part, "seq", scatter_dimension=1, tiled=True),
        lax.psum_scatter(skip_part, "seq", scatter_dimension=0, tiled=True),
        lax.psum_scatter(out_part_a, "seq", scatter_dimension=0, tiled=True),
        lax.psum_scatter(gain_two_part, "seq", scatter_dimension=0, tiled=True),
        lax.psum_scatter(up_one_part, "seq", scatter_dimension=0, tiled=True),
        lax.psum_scatter(down_one_part, "seq", scatter_dimension=0, tiled=True),
        lax.psum_scatter(attention_gain_share, "seq", scatter_dimension=0, tiled=True),
        lax.psum_scatter(in_part_c, "seq", scatter_dimension=0, tiled=True),
        lax.psum_scatter(out_part_c, "seq", scatter_dimension=0, tiled=True),
        lax.psum_scatter(gain_four_part, "seq", scatter_dimension=0, tiled=True),
        lax.psum_scatter(up_two_part, "seq", scatter_dimension=0, tiled=True),
        lax.psum_scatter(down_two_part, "seq", scatter_dimension=0, tiled=True),
    )
    matrices = (
        lax.psum_scatter(
            parts[1].astype(jnp.bfloat16), "batch", scatter_dimension=1, tiled=True
        ).astype(jnp.float32),
        lax.psum_scatter(
            parts[2].astype(jnp.bfloat16), "batch", scatter_dimension=0, tiled=True
        ).astype(jnp.float32),
        lax.psum_scatter(
            parts[4].astype(jnp.bfloat16), "batch", scatter_dimension=1, tiled=True
        ).astype(jnp.float32),
        lax.psum_scatter(
            parts[6].astype(jnp.bfloat16), "batch", scatter_dimension=1, tiled=True
        ).astype(jnp.float32),
        lax.psum_scatter(
            parts[7].astype(jnp.bfloat16), "batch", scatter_dimension=1, tiled=True
        ).astype(jnp.float32),
        lax.psum_scatter(
            parts[9].astype(jnp.bfloat16), "batch", scatter_dimension=1, tiled=True
        ).astype(jnp.float32),
        lax.psum_scatter(
            parts[10].astype(jnp.bfloat16), "batch", scatter_dimension=1, tiled=True
        ).astype(jnp.float32),
        lax.psum_scatter(
            parts[12].astype(jnp.bfloat16), "batch", scatter_dimension=1, tiled=True
        ).astype(jnp.float32),
        lax.psum_scatter(
            parts[13].astype(jnp.bfloat16), "batch", scatter_dimension=1, tiled=True
        ).astype(jnp.float32),
    )
    smalls = lax.psum(
        (parts[0], coef_part, rate_part, parts[3], parts[5], parts[8], parts[11]), "batch"
    )
    return (
        block_out,
        token_grad,
        smalls[0],
        matrices[0],
        matrices[1],
        smalls[1],
        smalls[2],
        smalls[3],
        matrices[2],
        smalls[4],
        matrices[3],
        matrices[4],
        smalls[5],
        matrices[5],
        matrices[6],
        smalls[6],
        matrices[7],
        matrices[8],
    )


MESH = pl.DeviceIdType.MESH
BF = jnp.bfloat16
F32 = jnp.float32
ROWS, WIDE, RANKS = (128, 768, 8)
SPAN = ROWS * RANKS
BLOCK = 128
OWNERS = 6
NT = (((1,), (1,)), ((), ()))
TN = (((0,), (0,)), ((), ()))
ROOT = math.sqrt(2.0 / math.pi)
CUBIC = 0.044715


def flip(value):
    return 1 - value


def mm(left, right):
    return jnp.dot(left, right, preferred_element_type=F32)


def mm_nt(left, right):
    return lax.dot_general(left, right, NT, preferred_element_type=F32)


def mm_tn(left, right):
    return lax.dot_general(left, right, TN, preferred_element_type=F32)


def is_owner(rank):
    return jnp.logical_and(rank >= 1, rank <= OWNERS)


def rows_of(rank):
    return pl.ds(pl.multiple_of(ROWS * rank, ROWS), ROWS)


def lanes_of(block):
    return pl.ds(pl.multiple_of(BLOCK * block, BLOCK), BLOCK)


PARTNERS = ((1, 1, 1), (1, 1, 0), (1, 0, 1), (1, 0, 0), (0, 1, 1), (0, 1, 0), (0, 0, 1))


class Spread:
    def __init__(self, net, source, target, outward, need=None):
        self.net, self.source, self.target, self.outward, self.need = net, source, target, outward, need
        self.base = net.take(RANKS - 1)

    def copy(self, step, source, target, rank):
        at = self.base + step - 1
        return pltpu.make_async_remote_copy(
            src_ref=source,
            dst_ref=target,
            send_sem=self.net.send_sem.at[at],
            recv_sem=self.net.recv_sem.at[at],
            device_id=(rank, self.net.b),
            device_id_type=MESH,
        )

    def each_send(self, act, chosen=None):
        me = self.net.s
        for step in range(1, RANKS):
            rank = self.net.partner(step)
            go = is_owner(rank) if self.outward else is_owner(me)
            if self.need is not None:
                go = jnp.logical_and(go, self.need(me - 1, rank))
            if chosen is not None:
                go = jnp.logical_and(go, chosen(rank))

            @pl.when(go)
            def _(step=step, rank=rank):
                if self.outward:
                    act(self.copy(step, self.source(rank - 1), self.target(me), rank))
                else:
                    act(self.copy(step, self.source(rank), self.target(me - 1), rank))

    def start(self, chosen=None):
        self.each_send(lambda copy: copy.start(), chosen)

    def own(self):
        me = self.net.s

        @pl.when(is_owner(me))
        def _():
            if self.outward:
                self.target(me)[...] = self.source(me - 1)[...]
            else:
                self.target(me - 1)[...] = self.source(me)[...]

    def wait_recv(self, steps=range(1, RANKS)):
        me = self.net.s
        for step in steps:
            rank = self.net.partner(step)
            go = is_owner(me) if self.outward else is_owner(rank)
            if self.need is not None:
                go = jnp.logical_and(go, self.need(rank - 1, me))

            @pl.when(go)
            def _(step=step, rank=rank):
                landed = self.target(rank if self.outward else rank - 1)
                self.copy(step, landed, landed, rank).wait_recv()

    def wait_send(self):
        self.each_send(lambda copy: copy.wait_send())


class Net:
    def __init__(self, send_sem, recv_sem):
        self.send_sem, self.recv_sem = send_sem, recv_sem
        self.s = lax.axis_index("seq")
        self.b = lax.axis_index("batch")
        self.y, self.c = self.b // 2, lax.rem(self.b, 2)
        z, self.x = self.s // 2, lax.rem(self.s, 2)
        self.high, self.low = z // 2, lax.rem(z, 2)
        self.sibling = (self.s, 2 * self.y + flip(self.c))
        self.by_y = (self.s, 2 * flip(self.y) + self.c)
        self.by_both = (self.s, 2 * flip(self.y) + flip(self.c))
        self.by_x = (2 * z + flip(self.x), self.b)
        self.by_low = (2 * (2 * self.high + flip(self.low)) + self.x, self.b)
        self.by_high = (2 * (2 * flip(self.high) + self.low) + self.x, self.b)
        self.used = 0
        self.waiting = []

    def partner(self, step):
        far, near, side = PARTNERS[step - 1]
        high = flip(self.high) if far else self.high
        low = flip(self.low) if near else self.low
        return 4 * high + 2 * low + (flip(self.x) if side else self.x)

    def take(self, count):
        at = self.used
        self.used += count
        return at

    def spread(self, source, target, outward, need=None):
        made = Spread(self, source, target, outward, need)
        self.waiting.append(made)
        return made

    def send(self, source, target, other):
        at = self.take(1)
        copy = pltpu.make_async_remote_copy(
            src_ref=source,
            dst_ref=target,
            send_sem=self.send_sem.at[at],
            recv_sem=self.recv_sem.at[at],
            device_id=other,
            device_id_type=MESH,
        )
        copy.start()
        self.waiting.append(copy)
        return copy

    def hello(self):
        barrier = pltpu.get_barrier_semaphore()
        for step in range(1, RANKS):
            pl.semaphore_signal(
                barrier, inc=1, device_id=(lax.rem(self.s + step, RANKS), self.b), device_id_type=MESH
            )
        for other in (self.sibling, self.by_y, self.by_both):
            pl.semaphore_signal(barrier, inc=1, device_id=other, device_id_type=MESH)

    def ready(self):
        pl.semaphore_wait(pltpu.get_barrier_semaphore(), RANKS + 2)

    def turn_of(self, step, y, c):
        return (2 * y + flip(c), 2 * flip(y) + c, 2 * flip(y) + flip(c), 2 * y + c)[step]

    def order(self):
        owners = (self.sibling, self.by_y, self.by_both, None)
        return [(self.turn_of(step, self.y, self.c), owners[step]) for step in range(4)]

    def drop(self, copy):
        self.waiting = [made for made in self.waiting if made is not copy]

    def finish(self):
        for made in self.waiting:
            made.wait_send()


class Beside:
    def __init__(self, net, source, target, steps):
        self.net, self.steps = net, steps
        self.at = net.take(1)
        other = jnp.clip(net.s + steps, 0, RANKS - 1)
        self.copy = pltpu.make_async_remote_copy(
            src_ref=source,
            dst_ref=target,
            send_sem=net.send_sem.at[self.at],
            recv_sem=net.recv_sem.at[self.at],
            device_id=(other, net.b),
            device_id_type=MESH,
        )
        last = RANKS - 1 if steps > 0 else 0
        first = 0 if steps > 0 else RANKS - 1
        self.sends = net.s != last
        self.takes = net.s != first
        net.waiting.append(self)

    def start(self):
        @pl.when(self.sends)
        def _():
            self.copy.start()

    def wait_recv(self):
        @pl.when(self.takes)
        def _():
            self.copy.wait_recv()

    def wait_send(self):
        @pl.when(self.sends)
        def _():
            self.copy.wait_send()


def pieces(value):
    cent = value - jnp.mean(value, axis=-1, keepdims=True)
    inverse = lax.rsqrt(jnp.mean(cent * cent, axis=-1, keepdims=True) + 1e-05)
    return cent * inverse, inverse


def pieces_back(incoming, normal, inverse, gain):
    share = jnp.sum(incoming * normal, axis=0, keepdims=True)
    scaled = incoming * gain
    first = jnp.mean(scaled, axis=-1, keepdims=True)
    second = jnp.mean(scaled * normal, axis=-1, keepdims=True)
    return inverse * (scaled - first - normal * second), share


def gelu_parts(u):
    square = u * u
    bend = jnp.tanh(ROOT * u * (1.0 + CUBIC * square))
    half = 0.5 * (1.0 + bend)
    value = u * half
    slope = half + 0.5 * u * (1.0 - bend * bend) * (ROOT * (1.0 + 3.0 * CUBIC * square))
    return value, slope


def split(value):
    high = value.astype(BF)
    return high, (value - high.astype(F32)).astype(BF)


def transform(r, net, go, signal, re_out, im_out):
    for index, steps in enumerate(((7,), (5, 6), (3, 4), (1, 2))):
        go.wait_recv(steps)
        high = flip(net.high) if index >= 2 else net.high
        low = flip(net.low) if index % 2 else net.low
        some = pl.ds(pl.multiple_of(512 * high + 256 * low, 256), 256)
        re, im = mm(r.cos_table[:, some], signal[some, :]), mm(r.sin_table[:, some], signal[some, :])
        if index == 0:
            re_out[...] = re
            im_out[...] = -im
        else:
            re_out[...] += re
            im_out[...] -= im


def transform_two(r, signal, re_out, im_out):
    high, low = split(signal)
    r.pack_re[:, 0:128] = high
    r.pack_re[:, 128:256] = low

    @pl.loop(0, 4)
    def _(at):
        rows = pl.ds(pl.multiple_of(256 * at, 256), 256)
        re, im = mm(r.cos_table[rows, :], r.pack_re[...]), mm(r.sin_table[rows, :], r.pack_re[...])
        re_out[rows, :] = re[:, 0:128] + re[:, 128:256]
        im_out[rows, :] = -(im[:, 0:128] + im[:, 128:256])


def inverse(r, re, im, out, back=None):
    re_high, re_low = split(re)
    im_high, im_low = split(im)
    r.pack_re[:, 0:128] = re_high
    r.pack_re[:, 128:256] = re_low
    r.pack_im[:, 0:128] = im_high
    r.pack_im[:, 128:256] = im_low
    for at in (3, 2, 1, 0):
        rows = slice(256 * at, 256 * at + 256)
        both = mm(r.cos_table[rows, :], r.pack_re[...]) - mm(r.sin_table[rows, :], r.pack_im[...])
        out[rows, :] = ((both[:, 0:128] + both[:, 128:256]) * (1.0 / SPAN)).astype(out.dtype)
        if back is not None:
            back.start(lambda rank, at=at: rank // 2 == at)


def modes(coef_ref, rate_ref, out_ref):
    blocks, width = out_ref.shape[0] // 8, out_ref.shape[1]
    row = lax.broadcasted_iota(jnp.int32, (8, width), 0).astype(F32)
    out_ref[...] = jnp.zeros_like(out_ref)

    @pl.loop(0, 8)
    def _(group):
        some = pl.ds(pl.multiple_of(8 * group, 8), 8)
        rate, coef = rate_ref[some, :], coef_ref[some, :]
        falls = [coef[n : n + 1] * jnp.exp(-rate[n : n + 1] * row) for n in range(8)]
        steps = [jnp.exp(-rate[n : n + 1] * jnp.maximum(row, 8.0)) for n in range(8)]

        def step(at, falls):
            rows = pl.ds(pl.multiple_of(8 * at, 8), 8)
            out_ref[rows, :] += sum(falls[1:], falls[0])
            return tuple(fall * factor for fall, factor in zip(falls, steps))

        lax.fori_loop(0, blocks, step, tuple(falls), unroll=4)


def modes_back(coef_ref, rate_ref, grad_ref, coef_out, rate_out):
    blocks, width = grad_ref.shape[0] // 8, grad_ref.shape[1]
    row = lax.broadcasted_iota(jnp.int32, (8, width), 0).astype(F32)

    @pl.loop(0, 8)
    def _(group):
        some = pl.ds(pl.multiple_of(8 * group, 8), 8)
        rate, coef = rate_ref[some, :], coef_ref[some, :]
        steps = [jnp.exp(-rate[n : n + 1] * jnp.maximum(row, 8.0)) for n in range(8)]
        zero = jnp.minimum(row, 0.0)

        def step(at, carry):
            totals, slopes = carry
            here = grad_ref[pl.ds(pl.multiple_of(8 * (blocks - 1 - at), 8), 8), :]
            slopes = tuple(slope * factor + total for slope, factor, total in zip(slopes, steps, totals))
            totals = tuple(total * factor + here for total, factor in zip(totals, steps))
            return totals, slopes

        totals, slopes = lax.fori_loop(0, blocks, step, ((zero,) * 8, (zero,) * 8), unroll=2)
        coef_rows, rate_rows = [], []
        for n in range(8):
            fall = jnp.exp(-rate[n : n + 1] * row)
            coef_rows.append(jnp.sum(fall * totals[n], axis=0, keepdims=True))
            late = jnp.sum(fall * (8.0 * steps[n] * slopes[n] + row * totals[n]), axis=0, keepdims=True)
            rate_rows.append(-coef[n : n + 1] * late)
        coef_out[some, :] = jnp.concatenate(coef_rows, axis=0)
        rate_out[some, :] = jnp.concatenate(rate_rows, axis=0)


def shift_forward(keys, taps, value, shifted):
    @pl.loop(0, OWNERS)
    def _(block):
        lanes = lanes_of(block)
        near = keys[:, lanes]
        total = jnp.zeros((ROWS, BLOCK), F32)
        for rest in range(8):
            turned = pltpu.roll(near, rest, 0) if rest else near
            for part in range(8):
                total = total + taps[8 * part + rest : 8 * part + rest + 1, lanes] * turned[64 - 8 * part : 192 - 8 * part]
        shifted[:, lanes] = total


def shift_back(grads, keys, taps, key_grad, taps_grad):
    @pl.loop(0, OWNERS)
    def _(block):
        lanes = lanes_of(block)
        ahead, near = grads[:, lanes], keys[:, lanes]
        here = ahead[0:ROWS]
        total = jnp.zeros((ROWS, BLOCK), F32)
        rows = {}
        for rest in range(8):
            later = pltpu.roll(ahead, 192 - rest, 0) if rest else ahead
            turned = pltpu.roll(near, rest, 0) if rest else near
            for part in range(8):
                lag = 8 * part + rest
                total = total + taps[lag : lag + 1, lanes] * later[8 * part : 8 * part + ROWS]
                taps_grad[lag : lag + 1, lanes] = jnp.sum(here * turned[64 - 8 * part : 192 - 8 * part], axis=0, keepdims=True)
        key_grad[:, lanes] = total


def holds_columns(block, rank):
    third = (block + 3) // 3 - 1
    first = block + third
    return jnp.logical_or(rank == first, rank == first + 1)


def head_lanes(shape, head):
    return lax.broadcasted_iota(jnp.int32, shape, 1) // 64 == head


def document_start(ends, first, count):
    at = first + lax.broadcasted_iota(jnp.int32, (count, 1), 0)
    begin = jnp.zeros((count, 1), jnp.int32)
    for index in range(3):
        begin = jnp.where(at >= ends[index], ends[index], begin)
    return at, begin


def allowed_pairs(ends, part):
    query_at, begin = document_start(ends, 256 * part, 256)
    key_at = lax.broadcasted_iota(jnp.int32, (256, 256 * (part + 1)), 1)
    return jnp.logical_and(key_at <= query_at, key_at >= begin)


def attention_forward(r, part):
    rows, keys = slice(256 * part, 256 * part + 256), slice(0, 256 * part + 256)
    mask = allowed_pairs(r.ends, part)

    @pl.loop(0, 2)
    def _(head):
        lanes = head_lanes((256, BLOCK), head)
        query = jnp.where(lanes, r.qkv[0, rows, :].astype(F32) * 0.125, 0.0).astype(BF)
        scores = jnp.where(mask, mm_nt(query, r.qkv[1, keys, :]), NEGATIVE)
        top = jnp.max(scores, axis=1, keepdims=True)
        weights = jnp.exp(scores - top)
        mass = jnp.sum(weights, axis=1, keepdims=True)
        mixed = mm(weights.astype(BF), r.qkv[2, keys, :]) / mass
        r.attended_full[rows, :] = jnp.where(lanes, mixed, r.attended_full[rows, :])
        r.lse[rows, :] = jnp.where(lanes, top + jnp.log(mass), r.lse[rows, :])

    r.attended_low[rows, :] = r.attended_full[rows, :].astype(BF)


def attention_back(r, part):
    rows, keys = slice(256 * part, 256 * part + 256), slice(0, 256 * part + 256)
    mask = allowed_pairs(r.ends, part)

    @pl.loop(0, 2)
    def _(head):
        lanes = head_lanes((256, BLOCK), head)
        query = jnp.where(lanes, r.qkv[0, rows, :].astype(F32) * 0.125, 0.0).astype(BF)
        whole = r.att_grad[rows, :].astype(F32)
        grads = jnp.where(lanes, whole, 0.0)
        delta = jnp.sum(grads * r.attended_full[rows, :], axis=1, keepdims=True)
        lse = jnp.sum(jnp.where(lanes, r.lse[rows, :], 0.0), axis=1, keepdims=True) * (1.0 / 64.0)
        grads = grads.astype(BF)
        scores = mm_nt(query, r.qkv[1, keys, :])
        probs = jnp.where(mask, jnp.exp(scores - lse), 0.0)
        score_grad = (probs * (mm_nt(grads, r.qkv[2, keys, :]) - delta)).astype(BF)
        query_grad = mm(score_grad, r.qkv[1, keys, :]) * 0.125
        r.query_grad[rows, :] = jnp.where(lanes, query_grad, r.query_grad[rows, :])
        r.key_grad[keys, :] += mm_tn(score_grad, query)
        r.value_grad[keys, :] += mm_tn(probs.astype(BF), grads)

    r.qkv_grad[0, rows, :] = r.query_grad[rows, :].astype(BF)
    r.qkv_grad[1, rows, :] = r.key_grad[rows, :].astype(BF)
    r.qkv_grad[2, rows, :] = r.value_grad[rows, :].astype(BF)


class Gather:
    def __init__(self, net, source, target):
        self.net, self.target = net, target
        here = target(net.y, net.c)
        self.first = net.send(source, here, net.sibling)
        self.across = net.send(source, here, net.by_y)

    def forward(self):
        self.across.wait_recv()
        landed = self.target(flip(self.net.y), self.net.c)
        self.second = self.net.send(landed, landed, self.net.sibling)

    def wait(self):
        self.first.wait_recv()
        self.second.wait_recv()

    def free(self):
        for copy in (self.first, self.across, self.second):
            copy.wait_send()
            self.net.drop(copy)


class Locals:
    def __init__(self, sems):
        self.sems, self.used, self.waiting = sems, 0, []

    def start(self, source, target):
        copy = pltpu.make_async_copy(source, target, self.sems.at[self.used])
        self.used += 1
        copy.start()
        return copy

    def put(self, source, target):
        self.waiting.append(self.start(source, target))

    def finish(self):
        for copy in self.waiting:
            copy.wait()


UP, DOWN, PAIR = (0, 1, 2)
LENGTH = 576
FIRST = dict(up_d=352, down_d=352, pair_c=352, down_b=352, up_b=352, pair_a=352)


class Sum:
    def __init__(self, r, net, name, kind):
        self.net, self.kind, self.half = net, kind, FIRST[name]
        for part in ("grads", "near_a", "near_b", "next_a", "next_b", "own", "third"):
            setattr(self, part, getattr(r, name + "_" + part))
        if kind == DOWN:
            self.across = getattr(r, name + "_across")
        else:
            self.right = getattr(r, name + "_right")
        self.shared = []

    def give(self, kept, step, columns, other):
        own = self.right.at[rows_of(self.net.b), :]
        if other is None:
            own[...] = columns
        else:
            kept[step] = columns
            self.shared.append(self.net.send(kept.at[step], own, other))

    def share_pairs(self, pairs):
        own = self.right.at[rows_of(self.net.b), :]
        for index, other in self.net.order():
            if other is None:
                own[...] = pairs[index]
            else:
                self.shared.append(self.net.send(pairs.at[index], own, other))

    def free(self, copies):
        for copy in copies:
            copy.wait_send()
            self.net.drop(copy)

    def free_shared(self):
        self.free(self.shared)

    def share_rows(self, turned):
        net = self.net
        own = pl.ds(pl.multiple_of(192 * net.b, 64), 192)
        self.across[:, lanes_of(net.b)] = turned[own, :]
        for index, other in self.net.order()[:3]:
            rows = pl.ds(pl.multiple_of(192 * index, 64), 192)
            self.shared.append(net.send(turned.at[rows, :], self.across.at[:, lanes_of(net.b)], other))

    def wait_shared(self):
        for copy in self.shared:
            copy.wait_recv()

    def place(self, product, tile):
        for block in range(8):
            at = pl.ds(pl.multiple_of(96 * tile, 16), 96)
            self.grads[block % 2, (block // 2) % 2, block // 4, at, :] = product[96 * block : 96 * block + 96].astype(BF)

    def product(self, left, second):
        self.wait_shared()
        if self.kind == DOWN:

            @pl.loop(0, 8)
            def _(block):
                lanes = pl.ds(pl.multiple_of(384 * block, 384), 384)
                product = mm(self.across[...], second[:, lanes])
                for tile in range(3):
                    self.grads[
                        lax.rem(block, 2), lax.rem(block // 2, 2), block // 4, 192 * tile : 192 * tile + 192, :
                    ] = product[:, 128 * tile : 128 * tile + 128].astype(BF)

        else:

            @pl.loop(0, 3 if self.kind == UP else 2)
            def _(chunk):
                lanes = pl.ds(pl.multiple_of(256 * chunk, 256), 256)
                product = mm(left[...], self.right[:, lanes])
                self.place(product[:, 0:128], 2 * chunk)
                self.place(product[:, 128:256], 2 * chunk + 1)

        if self.kind == PAIR:
            right = self.right[:, 512:768]
            first = lax.broadcasted_iota(jnp.int32, right.shape, 1) < 64
            zero = jnp.zeros_like(right)
            product = mm(left[...], jnp.where(first, right, zero)) + mm(second[...], jnp.where(first, zero, right))
            self.place(product[:, 0:128], 4)
            self.place(product[:, 128:256], 5)

        net, half = self.net, self.half
        self.moving = [
            net.send(self.grads.at[flip(net.x), :, :, 0:half, :], self.near_a, net.by_x),
            net.send(self.grads.at[:, flip(net.low), :, half:, :], self.near_b, net.by_low),
        ]

    def arrive(self):
        for copy in self.moving:
            copy.wait_recv()

    def second(self):
        net, half, grads = self.net, self.half, self.grads
        self.arrive()

        @pl.loop(0, 4)
        def _(step):
            one, two = step // 2, lax.rem(step, 2)
            grads[net.x, one, two, 0:half, :] += self.near_a[one, two]
            grads[one, net.low, two, half:, :] += self.near_b[one, two]

        self.moving = [
            net.send(grads.at[net.x, flip(net.low), :, 0:half, :], self.next_a, net.by_low),
            net.send(grads.at[flip(net.x), net.low, :, half:, :], self.next_b, net.by_x),
        ]

    def last(self):
        net, half, grads = self.net, self.half, self.grads
        self.arrive()

        @pl.loop(0, 2)
        def _(step):
            grads[net.x, net.low, step, 0:half, :] += self.next_a[step]
            grads[net.x, net.low, step, half:, :] += self.next_b[step]

        self.moving = [net.send(grads.at[net.x, net.low, flip(net.high)], self.third, net.by_high)]

    def end(self, near):
        net = self.net
        near.put(self.grads.at[net.x, net.low, net.high], self.own)
        self.arrive()


def sum_scratch(name, kind):
    first = FIRST[name]
    made = {
        name + "_grads": ((2, 2, 2, LENGTH, 128), BF),
        name + "_near_a": ((2, 2, first, 128), BF),
        name + "_near_b": ((2, 2, LENGTH - first, 128), BF),
        name + "_next_a": ((2, first, 128), BF),
        name + "_next_b": ((2, LENGTH - first, 128), BF),
    }
    if kind == DOWN:
        made[name + "_across"] = ((192, 512), BF)
    else:
        made[name + "_right"] = ((512, WIDE), BF)
    return made


def pair_columns(wide, narrow, out):
    first = lax.broadcasted_iota(jnp.int32, (ROWS, BLOCK), 1) < 64

    def tile(at):
        at = at % (3 * WIDE)
        return wide[at // WIDE, :, at % WIDE : at % WIDE + BLOCK].astype(F32)

    def turned(at):
        return jnp.where(first, pltpu.roll(tile(at - BLOCK), 64, 1), pltpu.roll(tile(at), 64, 1))

    def thin(at):
        return narrow[:, at : at + BLOCK].astype(F32)

    def thin_turned(at):
        upper = pltpu.roll(thin(at), 64, 1)
        return jnp.where(first, pltpu.roll(thin(at - BLOCK), 64, 1), upper) if at else upper

    for block in range(4):
        start = 576 * block
        if block % 2 == 0:
            for part in range(4):
                out[block, :, BLOCK * part : BLOCK * part + BLOCK] = tile(start + BLOCK * part).astype(BF)
            lower, upper, rest = tile(start + 512), thin_turned(192 * block), thin_turned(192 * block + BLOCK)
        else:
            for part in range(4):
                out[block, :, BLOCK * part : BLOCK * part + BLOCK] = turned(start + 64 + BLOCK * part).astype(BF)
            lower, upper, rest = turned(start + 576), thin(192 * block - 64), thin(192 * block + 64)
        out[block, :, 512:640] = jnp.where(first, lower, upper).astype(BF)
        out[block, :, 640:768] = rest.astype(BF)


def turn(blocks, out):
    for block in range(4):
        out[:, BLOCK * block : BLOCK * block + BLOCK] = blocks[BLOCK * block : BLOCK * block + BLOCK, :].T


TABLES = ("cos_table", "sin_table")
KEPT = (
    "value_next",
    "qkv",
    "lse",
    "attended_full",
    "bend_b",
    "stream_b",
    "response",
    "query_a",
    "shifted",
    "value_a",
    "key_ext",
    "kernel_re",
    "kernel_im",
    "signal_re",
    "signal_im",
)
LEFTS = ("normed_a", "gated", "normed_b", "active_b", "normed_c")


def kernel_a(r):
    net = Net(r.send_sem, r.recv_sem)
    near = Locals(r.local_sem)
    net.hello()
    wait = {}

    def fetch(*names):
        for name in names:
            wait[name] = near.start(getattr(r, name + "_hbm"), getattr(r, name))

    thirds = []
    for index in (2, 0, 1):
        lanes = slice(WIDE * index, WIDE * index + WIDE)
        thirds.append(near.start(r.mixer_in_hbm.at[:, lanes], r.mixer_in.at[:, lanes]))
    r.ends[0] = r.doc_lengths[0, 0]
    r.ends[1] = r.ends[0] + r.doc_lengths[0, 1]
    r.ends[2] = r.ends[1] + r.doc_lengths[0, 2]

    def keep(*names):
        for name in names:
            near.put(getattr(r, name), getattr(r, name + "_kept"))

    gathers = []

    def gather(name, lanes=slice(None)):
        all_of = getattr(r, name + "_all")
        mine = getattr(r, name).at[:, lanes]
        near.put(mine, all_of.at[rows_of(net.b), lanes])
        gathers.append(Gather(net, mine, lambda y, c: all_of.at[rows_of(2 * y + c), lanes]))

    me = net.s
    gain_a = r.mixer_norm_gain[...][None]
    net.ready()
    rim = Beside(net, r.tokens.at[0, 64:128, :], r.rim_in, 1)
    rim.start()

    @pl.when(me == 0)
    def _():
        r.rim_in[...] = jnp.zeros_like(r.rim_in)

    normal, _ = pieces(r.tokens[0].astype(F32))
    r.normed_a[...] = (normal * gain_a).astype(BF)
    gather("normed_a")
    thirds[0].wait()
    r.value_a[...] = mm(r.normed_a[...], r.mixer_in[:, 2 * WIDE :])
    r.value_low[...] = r.value_a[0:64, :].astype(BF)
    later = Beside(net, r.value_low, r.value_next, -1)
    later.start()

    @pl.when(me == RANKS - 1)
    def _():
        r.value_next[...] = jnp.zeros_like(r.value_next)

    thirds[1].wait()
    r.query_a[...] = mm(r.normed_a[...], r.mixer_in[:, 0:WIDE])
    keep("query_a", "value_a")
    thirds[2].wait()
    fetch("shift_taps", "mode_coef", "mode_rate", *TABLES, "phase_cos", "phase_sin", "mixer_out")
    fetch("up_first", "down_first", "project_in")
    r.key_ext[64:192, :] = mm(r.normed_a[...], r.mixer_in[:, WIDE : 2 * WIDE])
    rim.wait_recv()
    normal, _ = pieces(r.rim_in[...].astype(F32))
    r.key_ext[0:64, :] = mm((normal * gain_a).astype(BF), r.mixer_in[:, WIDE : 2 * WIDE])
    for name in ("shift_taps", "mode_coef", "mode_rate"):
        wait[name].wait()
    shift_forward(r.key_ext, r.shift_taps, None, r.shifted)
    r.product_low[...] = (r.shifted[...] * r.value_a[...]).astype(BF)
    go = net.spread(lambda block: r.product_low.at[:, lanes_of(block)], lambda rank: r.signal.at[rows_of(rank), :], True)
    go.start()
    go.own()
    keep("key_ext", "shifted")
    block = lanes_of(jnp.clip(me - 1, 0, OWNERS - 1))
    r.coef[...] = r.mode_coef[:, block]
    r.rate[...] = r.mode_rate[:, block]
    modes(r.coef, r.rate, r.mode_rows)
    for name in TABLES + ("phase_cos", "phase_sin"):
        wait[name].wait()
    transform_two(r, r.mode_rows[...], r.kernel_re, r.kernel_im)
    turned = r.kernel_re[...] * r.phase_cos[...] - r.kernel_im[...] * r.phase_sin[...]
    r.kernel_im[...] = r.kernel_im[...] * r.phase_cos[...] + r.kernel_re[...] * r.phase_sin[...]
    r.kernel_re[...] = turned
    keep("kernel_re", "kernel_im")
    transform(r, net, go, r.signal, r.signal_re, r.signal_im)
    back = net.spread(lambda rank: r.conv.at[rows_of(rank), :], lambda block: r.conv_home.at[:, lanes_of(block)], False)
    inverse(
        r,
        r.signal_re[...] * r.kernel_re[...] - r.signal_im[...] * r.kernel_im[...],
        r.signal_re[...] * r.kernel_im[...] + r.signal_im[...] * r.kernel_re[...],
        r.conv,
        back,
    )
    back.own()
    for name in ("mixer_out", "up_first", "down_first", "project_in"):
        wait[name].wait()
    back.wait_recv()
    r.response[...] = r.conv_home[...].astype(F32) + r.skip_gain[...][None] * (r.shifted[...] * r.value_a[...])
    r.gated[...] = (r.query_a[...] * r.response[...]).astype(BF)
    gather("gated")
    stream_b = r.tokens[0].astype(F32) + mm(r.gated[...], r.mixer_out[...])
    r.stream_b[...] = stream_b
    normal, _ = pieces(stream_b)
    r.normed_b[...] = (normal * r.gain_second[...][None]).astype(BF)
    gather("normed_b")
    r.stream_c[...] = stream_b
    for chunk in range(4):
        lanes = slice(WIDE * chunk, WIDE * chunk + WIDE)
        active, bend = gelu_parts(mm(r.normed_b[...], r.up_first[:, lanes]))
        r.bend_b[:, lanes] = bend.astype(BF)
        active = active.astype(BF)
        r.active_b[:, lanes] = active
        gather("active_b", lanes)
        r.stream_c[...] += mm(active, r.down_first[lanes, :])
    normal, _ = pieces(r.stream_c[...])
    r.normed_c[...] = (normal * r.attention_norm_gain[...][None]).astype(BF)
    gather("normed_c")
    for index in range(3):
        r.mixed_c[index] = mm(r.normed_c[...], r.project_in[:, WIDE * index : WIDE * index + WIDE]).astype(BF)
    go = net.spread(lambda block: r.mixed_c.at[:, :, lanes_of(block)], lambda rank: r.qkv.at[:, rows_of(rank), :], True)
    go.start()
    go.own()
    keep("response", "stream_b", "bend_b")
    for made in gathers[:3]:
        made.forward()
    turned = r.signal_re[...] * r.phase_cos[...] - r.signal_im[...] * r.phase_sin[...]
    r.signal_im[...] = -(r.signal_im[...] * r.phase_cos[...] + r.signal_re[...] * r.phase_sin[...])
    r.signal_re[...] = turned
    keep("signal_re", "signal_im")
    later.wait_recv()
    keep("value_next")
    go.wait_recv()
    keep("qkv")
    back = net.spread(lambda rank: r.attended_low.at[rows_of(rank), :], lambda block: r.attended.at[:, lanes_of(block)], False)
    for part in (3, 2, 1, 0):
        attention_forward(r, part)
        back.start(lambda rank, part=part: rank // 2 == part)
    back.own()
    keep("lse", "attended_full")
    for made in gathers[3:]:
        made.forward()
    back.wait_recv()
    for made in gathers:
        made.wait()
    net.finish()
    near.finish()


def kernel_b(r):
    net = Net(r.send_sem, r.recv_sem)
    near = Locals(r.local_sem)
    net.hello()
    wait = {}

    def fetch(name, into=None):
        wait[name] = near.start(getattr(r, name + "_hbm"), getattr(r, into or name))

    for name, into in (("project_out", "out_weight"), ("attended", "attended"), ("stream_c", "stream_c"), ("cotangent", "cotangent")):
        fetch(name, into)
    chunks = []
    for step, (index, other) in enumerate(net.order()):
        lanes = pl.ds(pl.multiple_of(WIDE * index, WIDE), WIDE)
        chunks.append(
            (
                near.start(r.up_second_hbm.at[:, lanes], r.up.at[:, lanes]),
                near.start(r.down_second_hbm.at[lanes, :], r.down.at[lanes, :]),
            )
        )
    r.ends[0] = r.doc_lengths[0, 0]
    r.ends[1] = r.ends[0] + r.doc_lengths[0, 1]
    r.ends[2] = r.ends[1] + r.doc_lengths[0, 2]
    up_d, down_d, pair_c = Sum(r, net, "up_d", UP), Sum(r, net, "down_d", DOWN), Sum(r, net, "pair_c", PAIR)
    up_b, down_b, pair_a = Sum(r, net, "up_b", UP), Sum(r, net, "down_b", DOWN), Sum(r, net, "pair_a", PAIR)
    own_rows = rows_of(net.b)

    gain_d = r.gain_fourth[...][None]
    for name in ("project_out", "attended", "stream_c", "cotangent"):
        wait[name].wait()
    stream_d = r.stream_c[...] + mm(r.attended[...], r.out_weight[...])
    normal, inverse_d = pieces(stream_d)
    normed_d = (normal * gain_d).astype(BF)
    r.layer_left[own_rows, :] = normed_d
    r.total[...] = stream_d
    r.turned[...] = r.cotangent[0].T
    r.pair_two[own_rows, :] = r.attended[...]
    net.ready()
    gather_d = Gather(net, r.layer_left.at[own_rows, :], lambda y, c: r.layer_left.at[rows_of(2 * y + c), :])
    down_d.share_rows(r.turned)
    spots = []
    for step, (index, other) in enumerate(net.order()):
        lanes = pl.ds(pl.multiple_of(WIDE * index, WIDE), WIDE)
        for copy in chunks[step]:
            copy.wait()
        if step == 3:
            for name in KEPT[:11]:
                fetch(name)
            fetch("project_in", "in_weight")
            fetch("normed_c_all", "pair_one")
            fetch("tokens")
            for name in ("shift_taps", "mode_coef", "mode_rate") + TABLES:
                fetch(name)
        raised = mm(r.layer_left[own_rows, :], r.up[:, lanes])
        active, slope = gelu_parts(raised)
        active = active.astype(BF)
        r.layer_second[own_rows, lanes] = active

        def spot(y, c, step=step):
            at = pl.ds(pl.multiple_of(WIDE * net.turn_of(step, y, c), WIDE), WIDE)
            return r.layer_second.at[rows_of(2 * y + c), at]

        spots.append(spot)
        slope = (slope * mm_nt(r.cotangent[0], r.down[lanes, :])).astype(BF)
        up_d.give(r.slopes, step, slope, other)
        back = mm_nt(slope, r.up[:, lanes])
        if step == 0:
            r.grad_d[...] = back
        else:
            r.grad_d[...] += back
    gathers = [Gather(net, spot(net.y, net.c), spot) for spot in spots]
    grad, gain_four = pieces_back(r.grad_d[...], normal, inverse_d, gain_d)
    grad = r.cotangent[0].astype(F32) + grad
    r.grad_d[...] = grad
    r.grad_d_low[...] = grad.astype(BF)
    r.att_grad_home[...] = mm_nt(r.grad_d_low[...], r.out_weight[...]).astype(BF)
    go = net.spread(lambda block: r.att_grad_home.at[:, lanes_of(block)], lambda rank: r.att_grad.at[rows_of(rank), :], True)
    go.start()
    go.own()
    gather_att = Gather(net, r.pair_two.at[own_rows, :], lambda y, c: r.pair_two.at[rows_of(2 * y + c), :])
    fetch("up_first", "up")
    fetch("mixer_out", "out_weight")

    r.key_grad[...] = jnp.zeros_like(r.key_grad)
    r.value_grad[...] = jnp.zeros_like(r.value_grad)
    gather_d.forward()
    for name in ("qkv", "lse", "attended_full"):
        wait[name].wait()
    gather_d.wait()
    turn(r.layer_left, r.turned_one)
    gather_d.free()
    fetch("normed_b_all", "layer_left")
    up_d.product(r.turned_one, None)
    go.wait_recv()
    back = net.spread(
        lambda rank: r.qkv_grad.at[:, rows_of(rank), :], lambda block: r.mixed_grad_c.at[:, :, lanes_of(block)], False
    )
    for part in (3, 2, 1, 0):
        attention_back(r, part)
        back.start(lambda rank, part=part: rank // 2 == part)
    back.own()
    for name, into in (
        ("kernel_re", "lse"),
        ("kernel_im", "attended_full"),
        ("signal_re", "query_grad"),
        ("signal_im", "key_grad"),
    ):
        fetch(name, into)
    up_d.second()
    r.block_out[0] = (r.total[...] + mm(r.layer_second[own_rows, :], r.down[...])).astype(BF)
    fetch("down_first", "down")
    for made in gathers:
        made.forward()
    for made in gathers:
        made.wait()
    down_d.product(None, r.layer_second)
    for made in gathers:
        made.free()
    fetch("active_b_all", "layer_second")
    up_d.last()

    normal, inverse_c = pieces(r.stream_c[...])
    wait["project_in"].wait()
    back.wait_recv()
    grad = mm_nt(r.mixed_grad_c[0], r.in_weight[:, 0:WIDE])
    for index in range(1, 3):
        grad = grad + mm_nt(r.mixed_grad_c[index], r.in_weight[:, WIDE * index : WIDE * index + WIDE])
    fetch("mixer_in", "in_weight")
    pair_columns(r.mixed_grad_c, r.grad_d_low, r.pairs)
    pair_c.share_pairs(r.pairs)
    grad, gain_three = pieces_back(grad, normal, inverse_c, r.attention_norm_gain[...][None])
    grad = grad + r.grad_d[...]
    r.total[...] = grad
    r.grad_c_low[...] = grad.astype(BF)
    down_d.free_shared()
    r.turned[...] = r.grad_c_low[...].T
    down_b.share_rows(r.turned)
    up_d.free_shared()
    wait["up_first"].wait()
    wait["down_first"].wait()
    wait["bend_b"].wait()
    for step, (index, other) in enumerate(net.order()):
        lanes = pl.ds(pl.multiple_of(WIDE * index, WIDE), WIDE)
        slope = (r.bend_b[:, lanes].astype(F32) * mm_nt(r.grad_c_low[...], r.down[lanes, :])).astype(BF)
        up_b.give(r.slopes, step, slope, other)
        part = mm_nt(slope, r.up[:, lanes])
        if step == 0:
            r.grad_b[...] = part
        else:
            r.grad_b[...] += part
    for name in ("stream_b", "response", "query_a", "shifted", "value_a", "key_ext", "mixer_out"):
        wait[name].wait()
    normal, inverse_b = pieces(r.stream_b[...])
    grad, gain_two = pieces_back(r.grad_b[...], normal, inverse_b, r.gain_second[...][None])
    grad = grad + r.total[...]
    r.grad_b[...] = grad
    r.grad_b_low[...] = grad.astype(BF)
    gated_grad = mm_nt(r.grad_b_low[...], r.out_weight[...])
    r.mixed_grad_a[0] = (gated_grad * r.response[...]).astype(BF)
    response_grad = gated_grad * r.query_a[...]
    r.response_grad[...] = response_grad
    r.response_grad_low[...] = response_grad.astype(BF)
    go = net.spread(
        lambda block: r.response_grad_low.at[:, lanes_of(block)], lambda rank: r.conv_grad.at[rows_of(rank), :], True
    )
    go.start()
    go.own()
    after = Beside(net, r.response_grad_low.at[0:64, :], r.response_next, -1)
    after.start()

    @pl.when(net.s == RANKS - 1)
    def _():
        r.response_next[...] = jnp.zeros_like(r.response_next)

    skip_part = jnp.sum(response_grad * (r.shifted[...] * r.value_a[...]), axis=0, keepdims=True)
    down_d.second()
    gather_att.forward()
    wait["normed_c_all"].wait()
    turn(r.pair_one, r.turned_one)
    gather_att.wait()
    turn(r.pair_two, r.turned_two)
    gather_att.free()
    fetch("normed_a_all", "pair_one")
    fetch("gated_all", "pair_two")
    pair_c.product(r.turned_one, r.turned_two)
    wait["active_b_all"].wait()
    down_b.product(None, r.layer_second)
    wait["normed_b_all"].wait()
    turn(r.layer_left, r.turned_one)
    up_d.end(near)

    for name in TABLES + ("kernel_re", "kernel_im", "signal_re", "signal_im"):
        wait[name].wait()
    kernel_re, kernel_im, signal_re, signal_im = r.lse, r.attended_full, r.query_grad, r.key_grad
    r.signal_grad[SPAN:, :] = jnp.zeros((64, BLOCK), BF)
    transform(r, net, go, r.conv_grad, r.grad_re, r.grad_im)
    back = net.spread(
        lambda rank: r.signal_grad.at[pl.ds(pl.multiple_of(ROWS * rank, ROWS), 192), :],
        lambda block: r.signal_grad_home.at[:, lanes_of(block)],
        False,
    )
    inverse(
        r,
        r.grad_re[...] * kernel_re[...] + r.grad_im[...] * kernel_im[...],
        r.grad_im[...] * kernel_re[...] - r.grad_re[...] * kernel_im[...],
        r.signal_grad,
        back,
    )
    back.own()
    up_b.product(r.turned_one, None)
    down_d.last()
    pair_c.second()
    down_b.second()
    after.wait_recv()
    for name in ("shift_taps", "mode_coef", "mode_rate", "value_next"):
        wait[name].wait()
    back.wait_recv()

    skip = r.skip_gain[...][None]
    signal_grad = r.signal_grad_home[0:ROWS, :].astype(F32) + skip * r.response_grad[...]
    r.grad_ext[0:ROWS, :] = signal_grad * r.value_a[...]
    r.mixed_grad_a[2] = (signal_grad * r.shifted[...]).astype(BF)
    signal_grad = r.signal_grad_home[ROWS:192, :].astype(F32) + skip * r.response_next[...].astype(F32)
    r.grad_ext[ROWS:192, :] = signal_grad * r.value_next[...].astype(F32)
    shift_back(r.grad_ext, r.key_ext, r.shift_taps, r.total, r.taps)
    r.mixed_grad_a[1] = r.total[...].astype(BF)
    pair_c.free_shared()
    pair_columns(r.mixed_grad_a, r.grad_b_low, r.pairs)
    pair_a.share_pairs(r.pairs)
    wait["mixer_in"].wait()
    wait["tokens"].wait()
    grad = mm_nt(r.mixed_grad_a[0], r.in_weight[:, 0:WIDE])
    for index in range(1, 3):
        grad = grad + mm_nt(r.mixed_grad_a[index], r.in_weight[:, WIDE * index : WIDE * index + WIDE])
    normal, inverse_a = pieces(r.tokens[0].astype(F32))
    grad, gain_one = pieces_back(grad, normal, inverse_a, r.mixer_norm_gain[...][None])
    r.token_grad[0] = r.grad_b[...] + grad

    gains = jnp.concatenate([gain_one, skip_part, gain_two, gain_three, gain_four, jnp.zeros((3, WIDE), F32)], axis=0)
    for block in range(4):
        r.small[block // 2, block % 2, 0:16, :] = r.taps[16 * block : 16 * block + 16, :]
        r.small[block // 2, block % 2, 16:24, :] = gains
    swap = net.send(r.small.at[:, flip(net.c)], r.small_c, net.sibling)
    re = r.grad_re[...] * signal_re[...] - r.grad_im[...] * signal_im[...]
    im = r.grad_re[...] * signal_im[...] + r.grad_im[...] * signal_re[...]
    inverse(r, re, im, r.value_grad)
    block = lanes_of(jnp.clip(net.s - 1, 0, OWNERS - 1))
    r.coef[...] = r.mode_coef[:, block]
    r.rate[...] = r.mode_rate[:, block]
    wait["normed_a_all"].wait()
    turn(r.pair_one, r.turned_one)
    wait["gated_all"].wait()
    turn(r.pair_two, r.turned_two)
    up_b.second()
    swap.wait_recv()
    r.small[:, net.c] += r.small_c[...]
    swap = net.send(r.small.at[flip(net.y), net.c], r.small_y, net.by_y)
    pair_c.last()
    down_b.last()
    pair_a.product(r.turned_one, r.turned_two)
    modes_back(r.coef, r.rate, r.value_grad, r.mode_part.at[0, 0:64], r.mode_part.at[0, 64:128])
    mode = net.send(r.mode_part.at[0], r.mode_swap.at[0], net.sibling)
    swap.wait_recv()
    r.small_sum[...] = r.small[net.y, net.c] + r.small_y[...]
    here = pl.ds(pl.multiple_of(384 * net.high, BLOCK), 384)
    there = pl.ds(pl.multiple_of(384 * flip(net.high), BLOCK), 384)
    swap = net.send(r.small_sum.at[:, there], r.half_swap.at[0], net.by_high)
    up_b.last()
    mode.wait_recv()
    r.mode_part[1] = r.mode_part[0] + r.mode_swap[0]
    mode = net.send(r.mode_part.at[1], r.mode_swap.at[1], net.by_y)
    pair_a.second()
    mode.wait_recv()
    r.mode_part[2] = r.mode_part[1] + r.mode_swap[1]
    back = net.spread(
        lambda rank: r.mode_part.at[2], lambda block: r.mode_home.at[:, lanes_of(block)], False, holds_columns
    )
    back.start()
    back.own()
    swap.wait_recv()
    r.half_sum[0] = r.small_sum[:, here] + r.half_swap[0]
    swap = net.send(r.half_sum.at[0], r.half_swap.at[1], net.by_low)
    pair_a.last()
    swap.wait_recv()
    r.half_sum[1] = r.half_sum[0] + r.half_swap[1]
    swap = net.send(r.half_sum.at[1], r.half_swap.at[2], net.by_x)
    down_d.end(near)
    pair_c.end(near)
    down_b.end(near)
    turn_back = lax.rem(WIDE - 96 * net.s, WIDE)
    back.wait_recv()
    r.mode_out[...] = pltpu.roll(r.mode_home[...], turn_back, 1)[:, 0:128]
    swap.wait_recv()
    half_back = lax.rem(4 * 96 - 96 * lax.rem(net.s, 4), 384)
    r.small_out[...] = pltpu.roll(r.half_sum[1] + r.half_swap[2], half_back, 1)[:, 0:128]
    up_b.end(near)
    pair_a.end(near)
    net.finish()
    near.finish()


def kernel_z(*refs):
    block_in, token_in, mode, small = refs[:4]
    sums = refs[4:16]
    (
        block_out,
        token_grad,
        gain_one,
        mixer_in,
        taps,
        coef,
        rate,
        skip,
        mixer_out,
        gain_two,
        up_first,
        down_first,
        gain_three,
        project_in,
        project_out,
        gain_four,
        up_second,
        down_second,
    ) = refs[16:]
    block_out[...] = block_in[...]
    token_grad[...] = token_in[...]
    taps[...] = small[0:16, 0:96]
    for at, out in enumerate((gain_one, skip, gain_two, gain_three, gain_four)):
        out[...] = small[16 + at, 0:96]
    coef[...] = mode[0:64, 0:96]
    rate[...] = mode[64:128, 0:96]

    def block(index, first, count):
        rows = slice(first, first + count)
        return sums[2 * index][rows, :].astype(F32) + sums[2 * index + 1][rows, :].astype(F32)

    for index, up, down in ((0, up_second, down_second), (3, up_first, down_first)):
        for tile in range(6):
            up[:, 128 * tile : 128 * tile + 128] = block(index, 96 * tile, 96)
        for tile in range(3):
            down[:, 128 * tile : 128 * tile + 128] = block(index + 1, 192 * tile, 192)
    for index, wide, narrow in ((2, project_in, project_out), (5, mixer_in, mixer_out)):
        for tile in range(4):
            wide[:, 128 * tile : 128 * tile + 128] = block(index, 96 * tile, 96)
        mixed = block(index, 384, 96)
        wide[:, 512:576] = mixed[:, 0:64]
        narrow[:, 0:64] = mixed[:, 64:128]
        narrow[:, 64:192] = block(index, 480, 96)


class Refs:
    pass


def call(body, identity, inputs, hbm, smem, outs, hbm_outs, scratch, semaphores):
    names = list(inputs) + [name + "_hbm" for name in hbm] + list(smem) + list(outs) + list(hbm_outs) + list(scratch)
    names += ["ends", "send_sem", "recv_sem", "local_sem"]

    def run(*refs):
        r = Refs()
        for name, ref in zip(names, refs):
            setattr(r, name, ref)
        body(r)

    vmem = pl.BlockSpec(memory_space=pltpu.VMEM)
    results = pl.pallas_call(
        run,
        out_shape=[jax.ShapeDtypeStruct(shape, kind) for shape, kind in (*outs.values(), *hbm_outs.values())],
        in_specs=[vmem] * len(inputs)
        + [pl.BlockSpec(memory_space=pl.ANY)] * len(hbm)
        + [pl.BlockSpec(memory_space=pltpu.SMEM)] * len(smem),
        out_specs=[vmem] * len(outs) + [pl.BlockSpec(memory_space=pl.ANY)] * len(hbm_outs),
        scratch_shapes=[pltpu.VMEM(shape, kind) for shape, kind in scratch.values()]
        + [pltpu.SMEM((3,), jnp.int32)]
        + [pltpu.SemaphoreType.DMA((semaphores[0],)), pltpu.SemaphoreType.DMA((semaphores[0],))]
        + [pltpu.SemaphoreType.DMA((semaphores[1],))],
        compiler_params=pltpu.CompilerParams(
            collective_id=identity, has_side_effects=True, vmem_limit_bytes=VMEM_BYTES
        ),
    )(*inputs.values(), *hbm.values(), *smem.values())
    return dict(zip((*outs, *hbm_outs), results))


VMEM_BYTES = 66_900_000


def odd_tables():
    odd = 2 * np.arange(SPAN, dtype=np.int64) + 1
    angle = (np.outer(odd, odd) % (8 * SPAN)) * (math.pi / (4 * SPAN))
    phase = (odd * (math.pi / (4 * SPAN)))[:, None] * np.ones((1, BLOCK))
    tables = {
        "cos_table": jnp.asarray(np.cos(angle).astype(ml_dtypes.bfloat16)),
        "sin_table": jnp.asarray(np.sin(angle).astype(ml_dtypes.bfloat16)),
    }
    return tables, jnp.asarray(np.cos(phase), F32), jnp.asarray(np.sin(phase), F32)


def shards_fast(
    tokens,
    doc_lengths,
    mixer_norm_gain,
    mixer_in,
    shift_taps,
    mode_coef,
    mode_rate,
    skip_gain,
    mixer_out,
    gain_second,
    up_first,
    down_first,
    attention_norm_gain,
    project_in,
    project_out,
    gain_fourth,
    up_second,
    down_second,
    cotangent,
):
    tables, phase_cos, phase_sin = odd_tables()
    home, thrice, tall = (ROWS, WIDE), (3, ROWS, WIDE), (ROWS, 4 * WIDE)
    span = (SPAN, BLOCK)
    kept = dict(
        value_next=((64, WIDE), BF),
        query_a=(home, F32),
        value_a=(home, F32),
        key_ext=((192, WIDE), F32),
        shifted=(home, F32),
        response=(home, F32),
        stream_b=(home, F32),
        bend_b=(tall, BF),
        qkv=((3, *span), BF),
        lse=(span, F32),
        attended_full=(span, F32),
        kernel_re=(span, F32),
        kernel_im=(span, F32),
        signal_re=(span, F32),
        signal_im=(span, F32),
    )
    lefts = dict(normed_a=(home, BF), gated=(home, BF), normed_b=(home, BF), active_b=(tall, BF), normed_c=(home, BF))
    modes_scratch = dict(
        coef=((64, BLOCK), F32),
        rate=((64, BLOCK), F32),
        shift_taps=((64, WIDE), F32),
        mode_coef=((64, WIDE), F32),
        mode_rate=((64, WIDE), F32),
    )
    packs = dict(pack_re=((SPAN, 256), BF), pack_im=((SPAN, 256), BF))
    table_scratch = dict(cos_table=((SPAN, SPAN), BF), sin_table=((SPAN, SPAN), BF))
    a = call(
        kernel_a,
        0,
        dict(
            tokens=tokens,
            mixer_norm_gain=mixer_norm_gain,
            skip_gain=skip_gain,
            gain_second=gain_second,
            attention_norm_gain=attention_norm_gain,
        ),
        dict(
            mixer_in=mixer_in,
            shift_taps=shift_taps,
            mode_coef=mode_coef,
            mode_rate=mode_rate,
            **tables,
            phase_cos=phase_cos,
            phase_sin=phase_sin,
            mixer_out=mixer_out,
            up_first=up_first,
            down_first=down_first,
            project_in=project_in,
        ),
        dict(doc_lengths=doc_lengths),
        dict(stream_c=(home, F32), attended=(home, BF)),
        dict(
            **{name + "_kept": made for name, made in kept.items()},
            **{name + "_all": ((4 * shape[0], shape[1]), kind) for name, (shape, kind) in lefts.items()},
        ),
        dict(
            **kept,
            **lefts,
            **modes_scratch,
            **packs,
            rim_in=((64, WIDE), BF),
            **table_scratch,
            phase_cos=(span, F32),
            phase_sin=(span, F32),
            value_low=((64, WIDE), BF),
            product_low=(home, BF),
            signal=(span, BF),
            mode_rows=(span, F32),
            conv=(span, BF),
            conv_home=(home, BF),
            mixed_c=(thrice, BF),
            attended_low=(span, BF),
            mixer_in=((WIDE, 3 * WIDE), BF),
            mixer_out=((WIDE, WIDE), BF),
            up_first=((WIDE, 4 * WIDE), BF),
            down_first=((4 * WIDE, WIDE), BF),
            project_in=((WIDE, 3 * WIDE), BF),
        ),
        (64, 48),
    )
    kinds = dict(up_d=UP, down_d=DOWN, pair_c=PAIR, up_b=UP, down_b=DOWN, pair_a=PAIR)
    sum_outs, sums = {}, {}
    for name, kind in kinds.items():
        sum_outs[name + "_own"] = ((LENGTH, 128), BF)
        sum_outs[name + "_third"] = ((LENGTH, 128), BF)
        sums.update(sum_scratch(name, kind))
    b = call(
        kernel_b,
        1,
        dict(
            mixer_norm_gain=mixer_norm_gain,
            skip_gain=skip_gain,
            gain_second=gain_second,
            attention_norm_gain=attention_norm_gain,
            gain_fourth=gain_fourth,
        ),
        dict(
            project_out=project_out,
            attended=a["attended"],
            stream_c=a["stream_c"],
            cotangent=cotangent,
            tokens=tokens,
            up_second=up_second,
            down_second=down_second,
            **{name: a[name + "_kept"] for name in kept},
            **{name + "_all": a[name + "_all"] for name in lefts},
            **tables,
            shift_taps=shift_taps,
            mode_coef=mode_coef,
            mode_rate=mode_rate,
            project_in=project_in,
            up_first=up_first,
            down_first=down_first,
            mixer_out=mixer_out,
            mixer_in=mixer_in,
        ),
        dict(doc_lengths=doc_lengths),
        dict(
            block_out=((1, *home), BF),
            token_grad=((1, *home), F32),
            mode_out=((128, 128), F32),
            small_out=((24, 128), F32),
        ),
        sum_outs,
        dict(
            **{name: made for name, made in kept.items() if not name.startswith(("kernel", "signal"))},
            **modes_scratch,
            **packs,
            **table_scratch,
            **sums,
            attended=(home, BF),
            stream_c=(home, F32),
            cotangent=((1, *home), BF),
            tokens=((1, *home), BF),
            up=((WIDE, 4 * WIDE), BF),
            down=((4 * WIDE, WIDE), BF),
            in_weight=((WIDE, 3 * WIDE), BF),
            out_weight=((WIDE, WIDE), BF),
            layer_left=((512, WIDE), BF),
            layer_second=((512, 4 * WIDE), BF),
            pair_one=((512, WIDE), BF),
            pair_two=((512, WIDE), BF),
            turned_one=((WIDE, 512), BF),
            turned_two=((WIDE, 512), BF),
            turned=((WIDE, ROWS), BF),
            slopes=(thrice, BF),
            pairs=((4, *home), BF),
            total=(home, F32),
            grad_d=(home, F32),
            grad_d_low=(home, BF),
            att_grad_home=(home, BF),
            att_grad=(span, BF),
            query_grad=(span, F32),
            key_grad=(span, F32),
            value_grad=(span, F32),
            qkv_grad=((3, *span), BF),
            mixed_grad_c=(thrice, BF),
            grad_c_low=(home, BF),
            grad_b=(home, F32),
            grad_b_low=(home, BF),
            mixed_grad_a=(thrice, BF),
            response_grad=(home, F32),
            response_grad_low=(home, BF),
            conv_grad=(span, BF),
            grad_re=(span, F32),
            grad_im=(span, F32),
            signal_grad=((SPAN + 64, BLOCK), BF),
            signal_grad_home=((192, WIDE), BF),
            response_next=((64, WIDE), BF),
            grad_ext=((192, WIDE), F32),
            taps=((64, WIDE), F32),
            small=((2, 2, 24, WIDE), F32),
            small_c=((2, 24, WIDE), F32),
            small_y=((24, WIDE), F32),
            small_sum=((24, WIDE), F32),
            half_swap=((3, 24, 384), F32),
            half_sum=((2, 24, 384), F32),
            mode_part=((3, 128, 128), F32),
            mode_swap=((2, 128, 128), F32),
            mode_home=((128, WIDE), F32),
        ),
        (160, 64),
    )
    vmem = pl.BlockSpec(memory_space=pltpu.VMEM)
    given = [b[name] for name in ("block_out", "token_grad", "mode_out", "small_out")]
    for name in kinds:
        given += [b[name + "_own"], b[name + "_third"]]
    gain = ((96,), F32)
    wide, narrow, up, down, mode = ((96, 576), F32), ((96, 192), F32), ((96, 768), F32), ((192, 384), F32), ((64, 96), F32)
    shapes = (
        ((1, *home), BF),
        ((1, *home), F32),
        gain,
        wide,
        ((16, 96), F32),
        mode,
        mode,
        gain,
        narrow,
        gain,
        up,
        down,
        gain,
        wide,
        narrow,
        gain,
        up,
        down,
    )
    results = pl.pallas_call(
        kernel_z,
        out_shape=[jax.ShapeDtypeStruct(shape, kind) for shape, kind in shapes],
        in_specs=[vmem] * len(given),
        out_specs=[vmem] * len(shapes),
    )(*given)
    return tuple(result.T if result.shape == (192, 384) else result for result in results)


def solution(mesh):
    in_specs = (
        P("batch", "seq", None),
        P("batch", None),
        P(),
        P(),
        P(),
        P(),
        P(),
        P(),
        P(),
        P(),
        P(),
        P(),
        P(),
        P(),
        P(),
        P(),
        P(),
        P(),
        P("batch", "seq", None),
    )
    out_specs = (
        P("batch", "seq", None),
        P("batch", "seq", None),
        P("seq"),
        P("seq", "batch"),
        P("batch", "seq"),
        P(None, "seq"),
        P(None, "seq"),
        P("seq"),
        P("seq", "batch"),
        P("seq"),
        P("seq", "batch"),
        P("seq", "batch"),
        P("seq"),
        P("seq", "batch"),
        P("seq", "batch"),
        P("seq"),
        P("seq", "batch"),
        P("seq", "batch"),
    )
    fast = mesh.shape["seq"] == RANKS and mesh.shape["batch"] == 4
    return jax.shard_map(shards_fast if fast else shards, mesh=mesh, in_specs=in_specs, out_specs=out_specs, check_vma=False)
```

```python
import math

import jax
import jax.numpy as jnp
import ml_dtypes
import numpy as np
from jax import lax
from jax.experimental import pallas as pl
from jax.experimental.pallas import tpu as pltpu
from jax.sharding import PartitionSpec as P

HEADS = 12


HIGH = lax.Precision.HIGHEST
NEGATIVE = -1e30


def shifted_2(value, axis, steps):
    count = lax.axis_size(axis)
    leading, last = (max(0, -steps), min(count, count - steps))
    return lax.ppermute(value, axis, [(source, source + steps) for source in range(leading, last)])


def shortened(x):

    def short(part):
        return part.astype(jnp.bfloat16) if part.dtype == jnp.float32 else part

    return jax.tree.map(short, x)


def mult(form, left, right):
    return jnp.einsum(form, left, right, precision=HIGH, preferred_element_type=jnp.float32)


def norm_pieces(value):
    row_mean = jnp.mean(value, axis=-1, keepdims=True)
    cent = value - row_mean
    inverse_deviation = lax.rsqrt(jnp.mean(cent * cent, axis=-1, keepdims=True) + 1e-05)
    return (cent * inverse_deviation, inverse_deviation)


def norm_backward(incoming_gradient, centered_normalized, inverse_deviation, gain_vector):
    gain_share = jnp.sum(incoming_gradient * centered_normalized, axis=0)
    scaled_rows = incoming_gradient * gain_vector
    inner_product = jnp.mean(scaled_rows, axis=-1, keepdims=True)
    cross_term = jnp.mean(scaled_rows * centered_normalized, axis=-1, keepdims=True)
    return (
        inverse_deviation * (scaled_rows - inner_product - centered_normalized * cross_term),
        gain_share,
    )


def segment_of(where, ends):
    return jnp.sum((where[:, None] >= ends[None, :]).astype(jnp.int32), axis=1)


def allowed(query_pos, key_pos, ends):
    same = segment_of(query_pos, ends)[:, None] == segment_of(key_pos, ends)[None, :]
    return (key_pos[None, :] <= query_pos[:, None]) & same


def kernel_rows(coef, rate, times):

    def step(total, pair):
        scale, decay = pair
        return (total + scale[:, None] * jnp.exp(-decay[:, None] * times[None, :]), None)

    start = jnp.zeros((coef.shape[1], times.shape[0]), jnp.float32)
    return lax.scan(step, start, (coef, rate))[0]


def kernel_grads(coef, rate, times, incoming_gradient):

    def step(carry, pair):
        scale, decay = pair
        fall = incoming_gradient * jnp.exp(-decay[:, None] * times[None, :])
        return (carry, (jnp.sum(fall, axis=1), -scale * jnp.sum(fall * times[None, :], axis=1)))

    return lax.scan(step, jnp.zeros((), jnp.float32), (coef, rate))[1]


def angle_pair(left, right, period):
    turns = left[:, None] * right[None, :] % period
    angle = turns.astype(jnp.float32) * (2.0 * math.pi / period)
    return (jnp.cos(angle), jnp.sin(angle))


def dft_tables(blocks, rows):
    wide = 2 * blocks
    block_ids = jnp.arange(blocks, dtype=jnp.int32)
    wide_ids = jnp.arange(wide, dtype=jnp.int32)
    row_ids = jnp.arange(rows, dtype=jnp.int32)
    return (
        angle_pair(block_ids, wide_ids, wide),
        angle_pair(wide_ids, row_ids, wide * rows),
        angle_pair(row_ids, row_ids, rows),
    )


def forward_spectrum(signal, tables, blocks, rows):
    (cos_one, sin_one), (cos_two, sin_two), (cos_three, sin_three) = tables
    folded = signal.reshape(signal.shape[0], blocks, rows)
    first_re = mult("cpr,pf->cfr", folded, cos_one)
    first_im = -mult("cpr,pf->cfr", folded, sin_one)
    turned_re = first_re * cos_two + first_im * sin_two
    turned_im = first_im * cos_two - first_re * sin_two
    spec_re = mult("cfr,rk->cfk", turned_re, cos_three) + mult("cfr,rk->cfk", turned_im, sin_three)
    spec_im = mult("cfr,rk->cfk", turned_im, cos_three) - mult("cfr,rk->cfk", turned_re, sin_three)
    return (spec_re, spec_im)


def inverse_signal(spec_re, spec_im, tables, blocks, rows):
    (cos_one, sin_one), (cos_two, sin_two), (cos_three, sin_three) = tables
    inner_re = mult("cfk,rk->cfr", spec_re, cos_three) - mult("cfk,rk->cfr", spec_im, sin_three)
    inner_im = mult("cfk,rk->cfr", spec_im, cos_three) + mult("cfk,rk->cfr", spec_re, sin_three)
    turned_re = inner_re * cos_two - inner_im * sin_two
    turned_im = inner_im * cos_two + inner_re * sin_two
    result_value = mult("cfr,pf->cpr", turned_re, cos_one) - mult("cfr,pf->cpr", turned_im, sin_one)
    return result_value.reshape(spec_re.shape[0], blocks * rows) / (2.0 * blocks * rows)


def attend_block(state, query, query_pos, key_block, value_block, key_pos, ends, scale):
    top, mass, accum = state
    scores = (
        jnp.einsum("qhd,khd->hqk", query, key_block, preferred_element_type=jnp.float32) * scale
    )
    mask = allowed(query_pos, key_pos, ends)[None]
    newtop = jnp.maximum(top, jnp.max(jnp.where(mask, scores, NEGATIVE), axis=-1))
    weights = jnp.where(mask, jnp.exp(scores - newtop[:, :, None]), 0.0)
    factor = jnp.exp(top - newtop)
    mass = mass * factor + jnp.sum(weights, axis=-1)
    accum = accum * factor[:, :, None] + jnp.einsum(
        "hqk,khd->hqd", weights, value_block.astype(jnp.float32), preferred_element_type=jnp.float32
    )
    return (newtop, mass, accum)


def score_grads(
    query, grads, lse_rows, delta_rows, query_pos, key_block, value_block, key_pos, ends, scale
):
    scores = (
        jnp.einsum("qhd,khd->hqk", query, key_block, preferred_element_type=jnp.float32) * scale
    )
    mask = allowed(query_pos, key_pos, ends)[None]
    probs = jnp.where(mask, jnp.exp(scores - lse_rows[:, :, None]), 0.0)
    dots = jnp.einsum("qhd,khd->hqk", grads, value_block, preferred_element_type=jnp.float32)
    return (probs, (probs * (dots - delta_rows[:, :, None])).astype(jnp.bfloat16))


def query_back(
    query, grads, lse_rows, delta_rows, query_pos, key_block, value_block, key_pos, ends, scale
):
    score_grad = score_grads(
        query, grads, lse_rows, delta_rows, query_pos, key_block, value_block, key_pos, ends, scale
    )[1]
    return (
        jnp.einsum("hqk,khd->qhd", score_grad, key_block, preferred_element_type=jnp.float32)
        * scale
    )


def key_back(
    query, grads, lse_rows, delta_rows, query_pos, key_block, value_block, key_pos, ends, scale
):
    probs, score_grad = score_grads(
        query, grads, lse_rows, delta_rows, query_pos, key_block, value_block, key_pos, ends, scale
    )
    key_part = (
        jnp.einsum("hqk,qhd->khd", score_grad, query, preferred_element_type=jnp.float32) * scale
    )
    value_part = jnp.einsum(
        "hqk,qhd->khd", probs, grads.astype(jnp.float32), preferred_element_type=jnp.float32
    )
    return (key_part, value_part)


def scan_keys(carry, keys, values, update):
    count = keys.shape[0]
    width = keys.shape[1]
    head_size = width // HEADS
    step = math.gcd(count, 1024)
    firsts = step * jnp.arange(count // step, dtype=jnp.int32)

    def inner_product(state, item):
        key_block, value_block, first = item
        key_pos = first + jnp.arange(step, dtype=jnp.int32)
        return (update(state, key_block, value_block, key_pos), None)

    items = (
        keys.reshape(count // step, step, HEADS, head_size),
        values.reshape(count // step, step, HEADS, head_size),
        firsts,
    )
    return lax.scan(inner_product, carry, items)[0]


def feed_forward(residual_stream, gain_vector, w_up, w_down):
    centered_normalized, inverse_deviation = norm_pieces(residual_stream)
    normed_rows = (centered_normalized * gain_vector).astype(jnp.bfloat16)
    raised_rows = jnp.dot(normed_rows, w_up, preferred_element_type=jnp.float32)
    active_tokens = jax.nn.gelu(raised_rows).astype(jnp.bfloat16)
    result_value = residual_stream + jnp.dot(
        active_tokens, w_down, preferred_element_type=jnp.float32
    )
    return (
        result_value,
        (centered_normalized, inverse_deviation, normed_rows, raised_rows, active_tokens),
    )


def feed_back(incoming_gradient, saved_residuals, gain_vector, w_up, w_down):
    centered_normalized, inverse_deviation, normed_rows, raised_rows, active_tokens = (
        saved_residuals
    )
    grad_low = incoming_gradient.astype(jnp.bfloat16)
    down_part = jnp.einsum("tf,td->fd", active_tokens, grad_low, preferred_element_type=jnp.float32)
    active_grad = jnp.einsum("td,fd->tf", grad_low, w_down, preferred_element_type=jnp.float32)
    slope = jax.vjp(jax.nn.gelu, raised_rows)[1](active_grad)[0].astype(jnp.bfloat16)
    up_part = jnp.einsum("td,tf->df", normed_rows, slope, preferred_element_type=jnp.float32)
    normed_gradient = jnp.einsum("tf,df->td", slope, w_up, preferred_element_type=jnp.float32)
    input_gradient, gain_share = norm_backward(
        normed_gradient, centered_normalized, inverse_deviation, gain_vector
    )
    return (incoming_gradient + input_gradient, gain_share, up_part, down_part)


def shards(
    tokens,
    doc_lengths,
    mixer_norm_gain,
    mixer_in,
    shift_taps,
    mode_coef,
    mode_rate,
    skip_gain,
    mixer_out,
    gain_second,
    up_first,
    down_first,
    attention_norm_gain,
    project_in,
    project_out,
    gain_fourth,
    up_second,
    down_second,
    cotangent,
):
    rows = tokens.shape[1]
    width = tokens.shape[2]
    blocks = lax.axis_size("seq")
    rank = lax.axis_index("seq")
    total = rows * blocks
    head_size = width // HEADS
    scale = head_size ** (-0.5)
    lags = shift_taps.shape[0]
    channels = width // blocks
    ends = jnp.cumsum(doc_lengths[0])
    here = rank * rows + jnp.arange(rows, dtype=jnp.int32)
    residual_stream = tokens[0].astype(jnp.float32)
    mixer_centered_normalized, mixer_inverse_deviation = norm_pieces(residual_stream)
    mixer_normed_rows = (mixer_centered_normalized * mixer_norm_gain).astype(jnp.bfloat16)
    mixed_a = jnp.dot(mixer_normed_rows, mixer_in, preferred_element_type=jnp.float32)
    query_a = mixed_a[:, :width]
    key_a = mixed_a[:, width : 2 * width]
    value_a = mixed_a[:, 2 * width :]
    rim = shifted_2(key_a[rows - (lags - 1) :].astype(jnp.bfloat16), "seq", 1).astype(jnp.float32)
    key_ext = jnp.concatenate([rim, key_a], axis=0)
    shifted = jnp.zeros_like(key_a)
    for lag in range(lags):
        shifted = shifted + shift_taps[lag] * key_ext[lags - 1 - lag : lags - 1 - lag + rows]
    product_kv = shifted * value_a
    channel_in = lax.all_to_all(
        product_kv.T.reshape(blocks, channels, rows).astype(jnp.bfloat16),
        "seq",
        split_axis=0,
        concat_axis=2,
        tiled=True,
    ).astype(jnp.float32)[0]
    times = jnp.arange(total, dtype=jnp.int32).astype(jnp.float32)
    coef_here = lax.dynamic_slice_in_dim(mode_coef, rank * channels, channels, 1)
    rate_here = lax.dynamic_slice_in_dim(mode_rate, rank * channels, channels, 1)
    kernel_here = kernel_rows(coef_here, rate_here, times)
    tables = dft_tables(blocks, rows)
    sig_re, sig_im = forward_spectrum(channel_in, tables, blocks, rows)
    ker_re, ker_im = forward_spectrum(kernel_here, tables, blocks, rows)
    conv_chan = inverse_signal(
        sig_re * ker_re - sig_im * ker_im, sig_re * ker_im + sig_im * ker_re, tables, blocks, rows
    )
    conv_home = lax.all_to_all(
        conv_chan.reshape(1, channels, total).astype(jnp.bfloat16),
        "seq",
        split_axis=2,
        concat_axis=0,
        tiled=True,
    ).astype(jnp.float32)
    response = conv_home.reshape(width, rows).T + skip_gain * product_kv
    gated = (query_a * response).astype(jnp.bfloat16)
    stream_b = residual_stream + jnp.dot(gated, mixer_out, preferred_element_type=jnp.float32)
    attention_residual_stream, saved_b = feed_forward(stream_b, gain_second, up_first, down_first)
    attention_centered_normalized, attention_inverse_deviation = norm_pieces(
        attention_residual_stream
    )
    attention_normed_rows = (attention_centered_normalized * attention_norm_gain).astype(
        jnp.bfloat16
    )
    mixed_c = jnp.dot(attention_normed_rows, project_in, preferred_element_type=jnp.float32).astype(
        jnp.bfloat16
    )
    query_flat = mixed_c[:, :width]
    key_flat = mixed_c[:, width : 2 * width]
    value_flat = mixed_c[:, 2 * width :]
    query_c = query_flat.reshape(rows, HEADS, head_size)
    key_heads = key_flat.reshape(rows, HEADS, head_size)
    value_heads = value_flat.reshape(rows, HEADS, head_size)

    def forward_update(state, key_block, value_block, key_pos):
        return attend_block(state, query_c, here, key_block, value_block, key_pos, ends, scale)

    begin = (
        jnp.full((HEADS, rows), NEGATIVE, jnp.float32),
        jnp.zeros((HEADS, rows), jnp.float32),
        jnp.zeros((HEADS, rows, head_size), jnp.float32),
    )
    piece = (
        lax.all_gather(key_flat, "seq", axis=0, tiled=True),
        lax.all_gather(value_flat, "seq", axis=0, tiled=True),
    )
    top, mass, accum = scan_keys(begin, piece[0], piece[1], forward_update)
    lse = top + jnp.log(mass)
    att_full = accum / mass[:, :, None]
    attended = att_full.transpose(1, 0, 2).reshape(rows, width).astype(jnp.bfloat16)
    stream_d = attention_residual_stream + jnp.dot(
        attended, project_out, preferred_element_type=jnp.float32
    )
    result_value, saved_d = feed_forward(stream_d, gain_fourth, up_second, down_second)
    block_out = result_value.astype(jnp.bfloat16)[None]
    incoming_gradient = cotangent[0].astype(jnp.float32)
    incoming_gradient, gain_four_part, up_two_part, down_two_part = feed_back(
        incoming_gradient, saved_d, gain_fourth, up_second, down_second
    )
    grad_low = incoming_gradient.astype(jnp.bfloat16)
    out_part_c = jnp.einsum("td,te->de", attended, grad_low, preferred_element_type=jnp.float32)
    att_grad = jnp.einsum(
        "te,de->td", grad_low, project_out, preferred_element_type=jnp.float32
    ).astype(jnp.bfloat16)
    grad_heads = att_grad.reshape(rows, HEADS, head_size)
    delta = jnp.sum(grad_heads.astype(jnp.float32).transpose(1, 0, 2) * att_full, axis=-1)
    zero_heads = jnp.zeros((rows, HEADS, head_size), jnp.float32)

    def query_update(summed, key_block, value_block, key_pos):
        return summed + query_back(
            query_c, grad_heads, lse, delta, here, key_block, value_block, key_pos, ends, scale
        )

    piece = (
        lax.all_gather(key_flat, "seq", axis=0, tiled=True),
        lax.all_gather(value_flat, "seq", axis=0, tiled=True),
    )
    query_grad = scan_keys(zero_heads, piece[0], piece[1], query_update)
    lse_all, delta_all = (
        lax.all_gather(lse, "seq", axis=1, tiled=True),
        lax.all_gather(delta, "seq", axis=1, tiled=True),
    )
    queries = lax.all_gather(query_flat, "seq", axis=0, tiled=True)
    grads = lax.all_gather(att_grad, "seq", axis=0, tiled=True)
    count = queries.shape[0]
    step = math.gcd(count, 1024)
    firsts = step * jnp.arange(count // step, dtype=jnp.int32)

    def inner_product(summed, item):
        query_block, grad_block, first = item
        query_pos = first + jnp.arange(step, dtype=jnp.int32)
        lse_rows = lax.dynamic_slice_in_dim(lse_all, first, step, 1)
        delta_rows = lax.dynamic_slice_in_dim(delta_all, first, step, 1)
        parts = key_back(
            query_block,
            grad_block,
            lse_rows,
            delta_rows,
            query_pos,
            key_heads,
            value_heads,
            here,
            ends,
            scale,
        )
        return ((summed[0] + parts[0], summed[1] + parts[1]), None)

    items = (
        queries.reshape(count // step, step, HEADS, head_size),
        grads.reshape(count // step, step, HEADS, head_size),
        firsts,
    )
    key_grad, value_grad = lax.scan(inner_product, (zero_heads, zero_heads), items)[0]
    key_grad = key_grad.reshape(rows, width)
    value_grad = value_grad.reshape(rows, width)
    mixed_grad_c = jnp.concatenate(
        [query_grad.reshape(rows, width), key_grad, value_grad], axis=1
    ).astype(jnp.bfloat16)
    in_part_c = jnp.einsum(
        "td,te->de", attention_normed_rows, mixed_grad_c, preferred_element_type=jnp.float32
    )
    attention_normed_gradient = jnp.einsum(
        "te,de->td", mixed_grad_c, project_in, preferred_element_type=jnp.float32
    )
    attention_norm_gradient, attention_gain_share = norm_backward(
        attention_normed_gradient,
        attention_centered_normalized,
        attention_inverse_deviation,
        attention_norm_gain,
    )
    incoming_gradient = incoming_gradient + attention_norm_gradient
    incoming_gradient, gain_two_part, up_one_part, down_one_part = feed_back(
        incoming_gradient, saved_b, gain_second, up_first, down_first
    )
    grad_low = incoming_gradient.astype(jnp.bfloat16)
    out_part_a = jnp.einsum("td,te->de", gated, grad_low, preferred_element_type=jnp.float32)
    gated_grad = jnp.einsum("te,de->td", grad_low, mixer_out, preferred_element_type=jnp.float32)
    query_grad_a = gated_grad * response
    response_grad = gated_grad * query_a
    skip_part = jnp.sum(response_grad * product_kv, axis=0)
    chan_grad = lax.all_to_all(
        response_grad.T.reshape(blocks, channels, rows).astype(jnp.bfloat16),
        "seq",
        split_axis=0,
        concat_axis=2,
        tiled=True,
    ).astype(jnp.float32)[0]
    grad_re, grad_im = forward_spectrum(chan_grad, tables, blocks, rows)
    signal_grad = inverse_signal(
        ker_re * grad_re + ker_im * grad_im,
        ker_re * grad_im - ker_im * grad_re,
        tables,
        blocks,
        rows,
    )
    kernel_grad = inverse_signal(
        sig_re * grad_re + sig_im * grad_im,
        sig_re * grad_im - sig_im * grad_re,
        tables,
        blocks,
        rows,
    )
    coef_part, rate_part = kernel_grads(coef_here, rate_here, times, kernel_grad)
    returned = lax.all_to_all(
        signal_grad.reshape(1, channels, total).astype(jnp.bfloat16),
        "seq",
        split_axis=2,
        concat_axis=0,
        tiled=True,
    ).astype(jnp.float32)
    kv_grad = returned.reshape(width, rows).T + skip_gain * response_grad
    shifted_grad = kv_grad * value_a
    value_grad_a = kv_grad * shifted
    later = shifted_2(shortened(shifted_grad[: lags - 1]), "seq", -1)
    grad_ext = jnp.concatenate([shifted_grad, later], axis=0)
    key_grad_a = jnp.zeros_like(key_a)
    tap_rows = []
    for lag in range(lags):
        key_grad_a = key_grad_a + shift_taps[lag] * grad_ext[lag : lag + rows]
        tap_rows.append(
            jnp.sum(shifted_grad * key_ext[lags - 1 - lag : lags - 1 - lag + rows], axis=0)
        )
    taps_part = jnp.stack(tap_rows)
    mixed_grad_a = jnp.concatenate([query_grad_a, key_grad_a, value_grad_a], axis=1).astype(
        jnp.bfloat16
    )
    in_part_a = jnp.einsum(
        "td,te->de", mixer_normed_rows, mixed_grad_a, preferred_element_type=jnp.float32
    )
    mixer_normed_gradient = jnp.einsum(
        "te,de->td", mixed_grad_a, mixer_in, preferred_element_type=jnp.float32
    )
    mixer_norm_gradient, mixer_gain_share = norm_backward(
        mixer_normed_gradient, mixer_centered_normalized, mixer_inverse_deviation, mixer_norm_gain
    )
    token_grad = (incoming_gradient + mixer_norm_gradient)[None]
    parts = (
        lax.psum_scatter(mixer_gain_share, "seq", scatter_dimension=0, tiled=True),
        lax.psum_scatter(in_part_a, "seq", scatter_dimension=0, tiled=True),
        lax.psum_scatter(taps_part, "seq", scatter_dimension=1, tiled=True),
        lax.psum_scatter(skip_part, "seq", scatter_dimension=0, tiled=True),
        lax.psum_scatter(out_part_a, "seq", scatter_dimension=0, tiled=True),
        lax.psum_scatter(gain_two_part, "seq", scatter_dimension=0, tiled=True),
        lax.psum_scatter(up_one_part, "seq", scatter_dimension=0, tiled=True),
        lax.psum_scatter(down_one_part, "seq", scatter_dimension=0, tiled=True),
        lax.psum_scatter(attention_gain_share, "seq", scatter_dimension=0, tiled=True),
        lax.psum_scatter(in_part_c, "seq", scatter_dimension=0, tiled=True),
        lax.psum_scatter(out_part_c, "seq", scatter_dimension=0, tiled=True),
        lax.psum_scatter(gain_four_part, "seq", scatter_dimension=0, tiled=True),
        lax.psum_scatter(up_two_part, "seq", scatter_dimension=0, tiled=True),
        lax.psum_scatter(down_two_part, "seq", scatter_dimension=0, tiled=True),
    )
    matrices = (
        lax.psum_scatter(
            parts[1].astype(jnp.bfloat16), "batch", scatter_dimension=1, tiled=True
        ).astype(jnp.float32),
        lax.psum_scatter(
            parts[2].astype(jnp.bfloat16), "batch", scatter_dimension=0, tiled=True
        ).astype(jnp.float32),
        lax.psum_scatter(
            parts[4].astype(jnp.bfloat16), "batch", scatter_dimension=1, tiled=True
        ).astype(jnp.float32),
        lax.psum_scatter(
            parts[6].astype(jnp.bfloat16), "batch", scatter_dimension=1, tiled=True
        ).astype(jnp.float32),
        lax.psum_scatter(
            parts[7].astype(jnp.bfloat16), "batch", scatter_dimension=1, tiled=True
        ).astype(jnp.float32),
        lax.psum_scatter(
            parts[9].astype(jnp.bfloat16), "batch", scatter_dimension=1, tiled=True
        ).astype(jnp.float32),
        lax.psum_scatter(
            parts[10].astype(jnp.bfloat16), "batch", scatter_dimension=1, tiled=True
        ).astype(jnp.float32),
        lax.psum_scatter(
            parts[12].astype(jnp.bfloat16), "batch", scatter_dimension=1, tiled=True
        ).astype(jnp.float32),
        lax.psum_scatter(
            parts[13].astype(jnp.bfloat16), "batch", scatter_dimension=1, tiled=True
        ).astype(jnp.float32),
    )
    smalls = lax.psum(
        (parts[0], coef_part, rate_part, parts[3], parts[5], parts[8], parts[11]), "batch"
    )
    return (
        block_out,
        token_grad,
        smalls[0],
        matrices[0],
        matrices[1],
        smalls[1],
        smalls[2],
        smalls[3],
        matrices[2],
        smalls[4],
        matrices[3],
        matrices[4],
        smalls[5],
        matrices[5],
        matrices[6],
        smalls[6],
        matrices[7],
        matrices[8],
    )


MESH = pl.DeviceIdType.MESH
BF = jnp.bfloat16
F32 = jnp.float32
ROWS, WIDE, RANKS = (128, 768, 8)
SPAN = ROWS * RANKS
BLOCK = 128
OWNERS = 6
NT = (((1,), (1,)), ((), ()))
TN = (((0,), (0,)), ((), ()))
ROOT = math.sqrt(2.0 / math.pi)
CUBIC = 0.044715


def flip(value):
    return 1 - value


def mm(left, right):
    return jnp.dot(left, right, preferred_element_type=F32)


def mm_nt(left, right):
    return lax.dot_general(left, right, NT, preferred_element_type=F32)


def mm_tn(left, right):
    return lax.dot_general(left, right, TN, preferred_element_type=F32)


def is_owner(rank):
    return jnp.logical_and(rank >= 1, rank <= OWNERS)


def rows_of(rank):
    return pl.ds(pl.multiple_of(ROWS * rank, ROWS), ROWS)


def lanes_of(block):
    return pl.ds(pl.multiple_of(BLOCK * block, BLOCK), BLOCK)


PARTNERS = ((1, 1, 1), (1, 1, 0), (1, 0, 1), (1, 0, 0), (0, 1, 1), (0, 1, 0), (0, 0, 1))


class Spread:
    def __init__(self, net, source, target, outward, need=None):
        self.net, self.source, self.target, self.outward, self.need = net, source, target, outward, need
        self.base = net.take(RANKS - 1)

    def copy(self, step, source, target, rank):
        at = self.base + step - 1
        return pltpu.make_async_remote_copy(
            src_ref=source,
            dst_ref=target,
            send_sem=self.net.send_sem.at[at],
            recv_sem=self.net.recv_sem.at[at],
            device_id=(rank, self.net.b),
            device_id_type=MESH,
        )

    def each_send(self, act, chosen=None):
        me = self.net.s
        for step in range(1, RANKS):
            rank = self.net.partner(step)
            go = is_owner(rank) if self.outward else is_owner(me)
            if self.need is not None:
                go = jnp.logical_and(go, self.need(me - 1, rank))
            if chosen is not None:
                go = jnp.logical_and(go, chosen(rank))

            @pl.when(go)
            def _(step=step, rank=rank):
                if self.outward:
                    act(self.copy(step, self.source(rank - 1), self.target(me), rank))
                else:
                    act(self.copy(step, self.source(rank), self.target(me - 1), rank))

    def start(self, chosen=None):
        self.each_send(lambda copy: copy.start(), chosen)

    def own(self):
        me = self.net.s

        @pl.when(is_owner(me))
        def _():
            if self.outward:
                self.target(me)[...] = self.source(me - 1)[...]
            else:
                self.target(me - 1)[...] = self.source(me)[...]

    def wait_recv(self, steps=range(1, RANKS)):
        me = self.net.s
        for step in steps:
            rank = self.net.partner(step)
            go = is_owner(me) if self.outward else is_owner(rank)
            if self.need is not None:
                go = jnp.logical_and(go, self.need(rank - 1, me))

            @pl.when(go)
            def _(step=step, rank=rank):
                landed = self.target(rank if self.outward else rank - 1)
                self.copy(step, landed, landed, rank).wait_recv()

    def wait_send(self):
        self.each_send(lambda copy: copy.wait_send())


class Net:
    def __init__(self, send_sem, recv_sem):
        self.send_sem, self.recv_sem = send_sem, recv_sem
        self.s = lax.axis_index("seq")
        self.b = lax.axis_index("batch")
        self.y, self.c = self.b // 2, lax.rem(self.b, 2)
        z, self.x = self.s // 2, lax.rem(self.s, 2)
        self.high, self.low = z // 2, lax.rem(z, 2)
        self.sibling = (self.s, 2 * self.y + flip(self.c))
        self.by_y = (self.s, 2 * flip(self.y) + self.c)
        self.by_both = (self.s, 2 * flip(self.y) + flip(self.c))
        self.by_x = (2 * z + flip(self.x), self.b)
        self.by_low = (2 * (2 * self.high + flip(self.low)) + self.x, self.b)
        self.by_high = (2 * (2 * flip(self.high) + self.low) + self.x, self.b)
        self.used = 0
        self.waiting = []

    def partner(self, step):
        far, near, side = PARTNERS[step - 1]
        high = flip(self.high) if far else self.high
        low = flip(self.low) if near else self.low
        return 4 * high + 2 * low + (flip(self.x) if side else self.x)

    def take(self, count):
        at = self.used
        self.used += count
        return at

    def spread(self, source, target, outward, need=None):
        made = Spread(self, source, target, outward, need)
        self.waiting.append(made)
        return made

    def send(self, source, target, other):
        at = self.take(1)
        copy = pltpu.make_async_remote_copy(
            src_ref=source,
            dst_ref=target,
            send_sem=self.send_sem.at[at],
            recv_sem=self.recv_sem.at[at],
            device_id=other,
            device_id_type=MESH,
        )
        copy.start()
        self.waiting.append(copy)
        return copy

    def hello(self):
        barrier = pltpu.get_barrier_semaphore()
        for step in range(1, RANKS):
            pl.semaphore_signal(
                barrier, inc=1, device_id=(lax.rem(self.s + step, RANKS), self.b), device_id_type=MESH
            )
        for other in (self.sibling, self.by_y, self.by_both):
            pl.semaphore_signal(barrier, inc=1, device_id=other, device_id_type=MESH)

    def ready(self):
        pl.semaphore_wait(pltpu.get_barrier_semaphore(), RANKS + 2)

    def turn_of(self, step, y, c):
        return (2 * y + flip(c), 2 * flip(y) + c, 2 * flip(y) + flip(c), 2 * y + c)[step]

    def order(self):
        owners = (self.sibling, self.by_y, self.by_both, None)
        return [(self.turn_of(step, self.y, self.c), owners[step]) for step in range(4)]

    def drop(self, copy):
        self.waiting = [made for made in self.waiting if made is not copy]

    def finish(self):
        for made in self.waiting:
            made.wait_send()


class Beside:
    def __init__(self, net, source, target, steps):
        self.net, self.steps = net, steps
        self.at = net.take(1)
        other = jnp.clip(net.s + steps, 0, RANKS - 1)
        self.copy = pltpu.make_async_remote_copy(
            src_ref=source,
            dst_ref=target,
            send_sem=net.send_sem.at[self.at],
            recv_sem=net.recv_sem.at[self.at],
            device_id=(other, net.b),
            device_id_type=MESH,
        )
        last = RANKS - 1 if steps > 0 else 0
        first = 0 if steps > 0 else RANKS - 1
        self.sends = net.s != last
        self.takes = net.s != first
        net.waiting.append(self)

    def start(self):
        @pl.when(self.sends)
        def _():
            self.copy.start()

    def wait_recv(self):
        @pl.when(self.takes)
        def _():
            self.copy.wait_recv()

    def wait_send(self):
        @pl.when(self.sends)
        def _():
            self.copy.wait_send()


def pieces(value):
    cent = value - jnp.mean(value, axis=-1, keepdims=True)
    inverse = lax.rsqrt(jnp.mean(cent * cent, axis=-1, keepdims=True) + 1e-05)
    return cent * inverse, inverse


def pieces_back(incoming, normal, inverse, gain):
    share = jnp.sum(incoming * normal, axis=0, keepdims=True)
    scaled = incoming * gain
    first = jnp.mean(scaled, axis=-1, keepdims=True)
    second = jnp.mean(scaled * normal, axis=-1, keepdims=True)
    return inverse * (scaled - first - normal * second), share


def gelu_parts(u):
    square = u * u
    bend = jnp.tanh(ROOT * u * (1.0 + CUBIC * square))
    half = 0.5 * (1.0 + bend)
    value = u * half
    slope = half + 0.5 * u * (1.0 - bend * bend) * (ROOT * (1.0 + 3.0 * CUBIC * square))
    return value, slope


def split(value):
    high = value.astype(BF)
    return high, (value - high.astype(F32)).astype(BF)


def transform(r, net, go, signal, re_out, im_out):
    for index, steps in enumerate(((7,), (5, 6), (3, 4), (1, 2))):
        go.wait_recv(steps)
        high = flip(net.high) if index >= 2 else net.high
        low = flip(net.low) if index % 2 else net.low
        some = pl.ds(pl.multiple_of(512 * high + 256 * low, 256), 256)
        re, im = mm(r.cos_table[:, some], signal[some, :]), mm(r.sin_table[:, some], signal[some, :])
        if index == 0:
            re_out[...] = re
            im_out[...] = -im
        else:
            re_out[...] += re
            im_out[...] -= im


def transform_two(r, signal, re_out, im_out):
    high, low = split(signal)
    r.pack_re[:, 0:128] = high
    r.pack_re[:, 128:256] = low

    @pl.loop(0, 4)
    def _(at):
        rows = pl.ds(pl.multiple_of(256 * at, 256), 256)
        re, im = mm(r.cos_table[rows, :], r.pack_re[...]), mm(r.sin_table[rows, :], r.pack_re[...])
        re_out[rows, :] = re[:, 0:128] + re[:, 128:256]
        im_out[rows, :] = -(im[:, 0:128] + im[:, 128:256])


def inverse(r, re, im, out, back=None):
    re_high, re_low = split(re)
    im_high, im_low = split(im)
    r.pack_re[:, 0:128] = re_high
    r.pack_re[:, 128:256] = re_low
    r.pack_im[:, 0:128] = im_high
    r.pack_im[:, 128:256] = im_low
    for at in (3, 2, 1, 0):
        rows = slice(256 * at, 256 * at + 256)
        both = mm(r.cos_table[rows, :], r.pack_re[...]) - mm(r.sin_table[rows, :], r.pack_im[...])
        out[rows, :] = ((both[:, 0:128] + both[:, 128:256]) * (1.0 / SPAN)).astype(out.dtype)
        if back is not None:
            back.start(lambda rank, at=at: rank // 2 == at)


def modes(coef_ref, rate_ref, out_ref):
    blocks, width = out_ref.shape[0] // 8, out_ref.shape[1]
    row = lax.broadcasted_iota(jnp.int32, (8, width), 0).astype(F32)
    out_ref[...] = jnp.zeros_like(out_ref)

    @pl.loop(0, 8)
    def _(group):
        some = pl.ds(pl.multiple_of(8 * group, 8), 8)
        rate, coef = rate_ref[some, :], coef_ref[some, :]
        falls = [coef[n : n + 1] * jnp.exp(-rate[n : n + 1] * row) for n in range(8)]
        steps = [jnp.exp(-rate[n : n + 1] * jnp.maximum(row, 8.0)) for n in range(8)]

        def step(at, falls):
            rows = pl.ds(pl.multiple_of(8 * at, 8), 8)
            out_ref[rows, :] += sum(falls[1:], falls[0])
            return tuple(fall * factor for fall, factor in zip(falls, steps))

        lax.fori_loop(0, blocks, step, tuple(falls), unroll=4)


def modes_back(coef_ref, rate_ref, grad_ref, coef_out, rate_out):
    blocks, width = grad_ref.shape[0] // 8, grad_ref.shape[1]
    row = lax.broadcasted_iota(jnp.int32, (8, width), 0).astype(F32)

    @pl.loop(0, 8)
    def _(group):
        some = pl.ds(pl.multiple_of(8 * group, 8), 8)
        rate, coef = rate_ref[some, :], coef_ref[some, :]
        steps = [jnp.exp(-rate[n : n + 1] * jnp.maximum(row, 8.0)) for n in range(8)]
        zero = jnp.minimum(row, 0.0)

        def step(at, carry):
            totals, slopes = carry
            here = grad_ref[pl.ds(pl.multiple_of(8 * (blocks - 1 - at), 8), 8), :]
            slopes = tuple(slope * factor + total for slope, factor, total in zip(slopes, steps, totals))
            totals = tuple(total * factor + here for total, factor in zip(totals, steps))
            return totals, slopes

        totals, slopes = lax.fori_loop(0, blocks, step, ((zero,) * 8, (zero,) * 8), unroll=2)
        coef_rows, rate_rows = [], []
        for n in range(8):
            fall = jnp.exp(-rate[n : n + 1] * row)
            coef_rows.append(jnp.sum(fall * totals[n], axis=0, keepdims=True))
            late = jnp.sum(fall * (8.0 * steps[n] * slopes[n] + row * totals[n]), axis=0, keepdims=True)
            rate_rows.append(-coef[n : n + 1] * late)
        coef_out[some, :] = jnp.concatenate(coef_rows, axis=0)
        rate_out[some, :] = jnp.concatenate(rate_rows, axis=0)


def shift_forward(keys, taps, value, shifted):
    @pl.loop(0, OWNERS)
    def _(block):
        lanes = lanes_of(block)
        near = keys[:, lanes]
        total = jnp.zeros((ROWS, BLOCK), F32)
        for rest in range(8):
            turned = pltpu.roll(near, rest, 0) if rest else near
            for part in range(8):
                total = total + taps[8 * part + rest : 8 * part + rest + 1, lanes] * turned[64 - 8 * part : 192 - 8 * part]
        shifted[:, lanes] = total


def shift_back(grads, keys, taps, key_grad, taps_grad):
    @pl.loop(0, OWNERS)
    def _(block):
        lanes = lanes_of(block)
        ahead, near = grads[:, lanes], keys[:, lanes]
        here = ahead[0:ROWS]
        total = jnp.zeros((ROWS, BLOCK), F32)
        rows = {}
        for rest in range(8):
            later = pltpu.roll(ahead, 192 - rest, 0) if rest else ahead
            turned = pltpu.roll(near, rest, 0) if rest else near
            for part in range(8):
                lag = 8 * part + rest
                total = total + taps[lag : lag + 1, lanes] * later[8 * part : 8 * part + ROWS]
                taps_grad[lag : lag + 1, lanes] = jnp.sum(here * turned[64 - 8 * part : 192 - 8 * part], axis=0, keepdims=True)
        key_grad[:, lanes] = total


def holds_columns(block, rank):
    third = (block + 3) // 3 - 1
    first = block + third
    return jnp.logical_or(rank == first, rank == first + 1)


def head_lanes(shape, head):
    return lax.broadcasted_iota(jnp.int32, shape, 1) // 64 == head


def document_start(ends, first, count):
    at = first + lax.broadcasted_iota(jnp.int32, (count, 1), 0)
    begin = jnp.zeros((count, 1), jnp.int32)
    for index in range(3):
        begin = jnp.where(at >= ends[index], ends[index], begin)
    return at, begin


def allowed_pairs(ends, part):
    query_at, begin = document_start(ends, 256 * part, 256)
    key_at = lax.broadcasted_iota(jnp.int32, (256, 256 * (part + 1)), 1)
    return jnp.logical_and(key_at <= query_at, key_at >= begin)


def attention_forward(r, part):
    rows, keys = slice(256 * part, 256 * part + 256), slice(0, 256 * part + 256)
    mask = allowed_pairs(r.ends, part)

    @pl.loop(0, 2)
    def _(head):
        lanes = head_lanes((256, BLOCK), head)
        query = jnp.where(lanes, r.qkv[0, rows, :].astype(F32) * 0.125, 0.0).astype(BF)
        scores = jnp.where(mask, mm_nt(query, r.qkv[1, keys, :]), NEGATIVE)
        top = jnp.max(scores, axis=1, keepdims=True)
        weights = jnp.exp(scores - top)
        mass = jnp.sum(weights, axis=1, keepdims=True)
        mixed = mm(weights.astype(BF), r.qkv[2, keys, :]) / mass
        r.attended_full[rows, :] = jnp.where(lanes, mixed, r.attended_full[rows, :])
        r.lse[rows, :] = jnp.where(lanes, top + jnp.log(mass), r.lse[rows, :])

    r.attended_low[rows, :] = r.attended_full[rows, :].astype(BF)


def attention_back(r, part):
    rows, keys = slice(256 * part, 256 * part + 256), slice(0, 256 * part + 256)
    mask = allowed_pairs(r.ends, part)

    @pl.loop(0, 2)
    def _(head):
        lanes = head_lanes((256, BLOCK), head)
        query = jnp.where(lanes, r.qkv[0, rows, :].astype(F32) * 0.125, 0.0).astype(BF)
        whole = r.att_grad[rows, :].astype(F32)
        grads = jnp.where(lanes, whole, 0.0)
        delta = jnp.sum(grads * r.attended_full[rows, :], axis=1, keepdims=True)
        lse = jnp.sum(jnp.where(lanes, r.lse[rows, :], 0.0), axis=1, keepdims=True) * (1.0 / 64.0)
        grads = grads.astype(BF)
        scores = mm_nt(query, r.qkv[1, keys, :])
        probs = jnp.where(mask, jnp.exp(scores - lse), 0.0)
        score_grad = (probs * (mm_nt(grads, r.qkv[2, keys, :]) - delta)).astype(BF)
        query_grad = mm(score_grad, r.qkv[1, keys, :]) * 0.125
        r.query_grad[rows, :] = jnp.where(lanes, query_grad, r.query_grad[rows, :])
        r.key_grad[keys, :] += mm_tn(score_grad, query)
        r.value_grad[keys, :] += mm_tn(probs.astype(BF), grads)

    r.qkv_grad[0, rows, :] = r.query_grad[rows, :].astype(BF)
    r.qkv_grad[1, rows, :] = r.key_grad[rows, :].astype(BF)
    r.qkv_grad[2, rows, :] = r.value_grad[rows, :].astype(BF)


class Gather:
    def __init__(self, net, source, target):
        self.net, self.target = net, target
        here = target(net.y, net.c)
        self.first = net.send(source, here, net.sibling)
        self.across = net.send(source, here, net.by_y)

    def forward(self):
        self.across.wait_recv()
        landed = self.target(flip(self.net.y), self.net.c)
        self.second = self.net.send(landed, landed, self.net.sibling)

    def wait(self):
        self.first.wait_recv()
        self.second.wait_recv()

    def free(self):
        for copy in (self.first, self.across, self.second):
            copy.wait_send()
            self.net.drop(copy)


class Locals:
    def __init__(self, sems):
        self.sems, self.used, self.waiting = sems, 0, []

    def start(self, source, target):
        copy = pltpu.make_async_copy(source, target, self.sems.at[self.used])
        self.used += 1
        copy.start()
        return copy

    def put(self, source, target):
        self.waiting.append(self.start(source, target))

    def finish(self):
        for copy in self.waiting:
            copy.wait()


UP, DOWN, PAIR = (0, 1, 2)
LENGTH = 576
FIRST = dict(up_d=352, down_d=352, pair_c=352, down_b=352, up_b=352, pair_a=352)


class Sum:
    def __init__(self, r, net, name, kind):
        self.net, self.kind, self.half = net, kind, FIRST[name]
        for part in ("grads", "near_a", "near_b", "next_a", "next_b", "own", "third"):
            setattr(self, part, getattr(r, name + "_" + part))
        if kind == DOWN:
            self.across = getattr(r, name + "_across")
        else:
            self.right = getattr(r, name + "_right")
        self.shared = []

    def give(self, kept, step, columns, other):
        own = self.right.at[rows_of(self.net.b), :]
        if other is None:
            own[...] = columns
        else:
            kept[step] = columns
            self.shared.append(self.net.send(kept.at[step], own, other))

    def share_pairs(self, pairs):
        own = self.right.at[rows_of(self.net.b), :]
        for index, other in self.net.order():
            if other is None:
                own[...] = pairs[index]
            else:
                self.shared.append(self.net.send(pairs.at[index], own, other))

    def free(self, copies):
        for copy in copies:
            copy.wait_send()
            self.net.drop(copy)

    def free_shared(self):
        self.free(self.shared)

    def share_rows(self, turned):
        net = self.net
        own = pl.ds(pl.multiple_of(192 * net.b, 64), 192)
        self.across[:, lanes_of(net.b)] = turned[own, :]
        for index, other in self.net.order()[:3]:
            rows = pl.ds(pl.multiple_of(192 * index, 64), 192)
            self.shared.append(net.send(turned.at[rows, :], self.across.at[:, lanes_of(net.b)], other))

    def wait_shared(self):
        for copy in self.shared:
            copy.wait_recv()

    def place(self, product, tile):
        for block in range(8):
            at = pl.ds(pl.multiple_of(96 * tile, 16), 96)
            self.grads[block % 2, (block // 2) % 2, block // 4, at, :] = product[96 * block : 96 * block + 96].astype(BF)

    def product(self, left, second):
        self.wait_shared()
        if self.kind == DOWN:

            @pl.loop(0, 8)
            def _(block):
                lanes = pl.ds(pl.multiple_of(384 * block, 384), 384)
                product = mm(self.across[...], second[:, lanes])
                for tile in range(3):
                    self.grads[
                        lax.rem(block, 2), lax.rem(block // 2, 2), block // 4, 192 * tile : 192 * tile + 192, :
                    ] = product[:, 128 * tile : 128 * tile + 128].astype(BF)

        else:

            @pl.loop(0, 3 if self.kind == UP else 2)
            def _(chunk):
                lanes = pl.ds(pl.multiple_of(256 * chunk, 256), 256)
                product = mm(left[...], self.right[:, lanes])
                self.place(product[:, 0:128], 2 * chunk)
                self.place(product[:, 128:256], 2 * chunk + 1)

        if self.kind == PAIR:
            right = self.right[:, 512:768]
            first = lax.broadcasted_iota(jnp.int32, right.shape, 1) < 64
            zero = jnp.zeros_like(right)
            product = mm(left[...], jnp.where(first, right, zero)) + mm(second[...], jnp.where(first, zero, right))
            self.place(product[:, 0:128], 4)
            self.place(product[:, 128:256], 5)

        net, half = self.net, self.half
        self.moving = [
            net.send(self.grads.at[flip(net.x), :, :, 0:half, :], self.near_a, net.by_x),
            net.send(self.grads.at[:, flip(net.low), :, half:, :], self.near_b, net.by_low),
        ]

    def arrive(self):
        for copy in self.moving:
            copy.wait_recv()

    def second(self):
        net, half, grads = self.net, self.half, self.grads
        self.arrive()

        @pl.loop(0, 4)
        def _(step):
            one, two = step // 2, lax.rem(step, 2)
            grads[net.x, one, two, 0:half, :] += self.near_a[one, two]
            grads[one, net.low, two, half:, :] += self.near_b[one, two]

        self.moving = [
            net.send(grads.at[net.x, flip(net.low), :, 0:half, :], self.next_a, net.by_low),
            net.send(grads.at[flip(net.x), net.low, :, half:, :], self.next_b, net.by_x),
        ]

    def last(self):
        net, half, grads = self.net, self.half, self.grads
        self.arrive()

        @pl.loop(0, 2)
        def _(step):
            grads[net.x, net.low, step, 0:half, :] += self.next_a[step]
            grads[net.x, net.low, step, half:, :] += self.next_b[step]

        self.moving = [net.send(grads.at[net.x, net.low, flip(net.high)], self.third, net.by_high)]

    def end(self, near):
        net = self.net
        near.put(self.grads.at[net.x, net.low, net.high], self.own)
        self.arrive()


def sum_scratch(name, kind):
    first = FIRST[name]
    made = {
        name + "_grads": ((2, 2, 2, LENGTH, 128), BF),
        name + "_near_a": ((2, 2, first, 128), BF),
        name + "_near_b": ((2, 2, LENGTH - first, 128), BF),
        name + "_next_a": ((2, first, 128), BF),
        name + "_next_b": ((2, LENGTH - first, 128), BF),
    }
    if kind == DOWN:
        made[name + "_across"] = ((192, 512), BF)
    else:
        made[name + "_right"] = ((512, WIDE), BF)
    return made


def pair_columns(wide, narrow, out):
    first = lax.broadcasted_iota(jnp.int32, (ROWS, BLOCK), 1) < 64

    def tile(at):
        at = at % (3 * WIDE)
        return wide[at // WIDE, :, at % WIDE : at % WIDE + BLOCK].astype(F32)

    def turned(at):
        return jnp.where(first, pltpu.roll(tile(at - BLOCK), 64, 1), pltpu.roll(tile(at), 64, 1))

    def thin(at):
        return narrow[:, at : at + BLOCK].astype(F32)

    def thin_turned(at):
        upper = pltpu.roll(thin(at), 64, 1)
        return jnp.where(first, pltpu.roll(thin(at - BLOCK), 64, 1), upper) if at else upper

    for block in range(4):
        start = 576 * block
        if block % 2 == 0:
            for part in range(4):
                out[block, :, BLOCK * part : BLOCK * part + BLOCK] = tile(start + BLOCK * part).astype(BF)
            lower, upper, rest = tile(start + 512), thin_turned(192 * block), thin_turned(192 * block + BLOCK)
        else:
            for part in range(4):
                out[block, :, BLOCK * part : BLOCK * part + BLOCK] = turned(start + 64 + BLOCK * part).astype(BF)
            lower, upper, rest = turned(start + 576), thin(192 * block - 64), thin(192 * block + 64)
        out[block, :, 512:640] = jnp.where(first, lower, upper).astype(BF)
        out[block, :, 640:768] = rest.astype(BF)


def turn(blocks, out):
    for block in range(4):
        out[:, BLOCK * block : BLOCK * block + BLOCK] = blocks[BLOCK * block : BLOCK * block + BLOCK, :].T


TABLES = ("cos_table", "sin_table")
KEPT = (
    "value_next",
    "qkv",
    "lse",
    "attended_full",
    "bend_b",
    "stream_b",
    "response",
    "query_a",
    "shifted",
    "value_a",
    "key_ext",
    "kernel_re",
    "kernel_im",
    "signal_re",
    "signal_im",
)
LEFTS = ("normed_a", "gated", "normed_b", "active_b", "normed_c")


def kernel_a(r):
    net = Net(r.send_sem, r.recv_sem)
    near = Locals(r.local_sem)
    net.hello()
    wait = {}

    def fetch(*names):
        for name in names:
            wait[name] = near.start(getattr(r, name + "_hbm"), getattr(r, name))

    thirds = []
    for index in (2, 0, 1):
        lanes = slice(WIDE * index, WIDE * index + WIDE)
        thirds.append(near.start(r.mixer_in_hbm.at[:, lanes], r.mixer_in.at[:, lanes]))
    r.ends[0] = r.doc_lengths[0, 0]
    r.ends[1] = r.ends[0] + r.doc_lengths[0, 1]
    r.ends[2] = r.ends[1] + r.doc_lengths[0, 2]

    def keep(*names):
        for name in names:
            near.put(getattr(r, name), getattr(r, name + "_kept"))

    gathers = []

    def gather(name, lanes=slice(None)):
        all_of = getattr(r, name + "_all")
        mine = getattr(r, name).at[:, lanes]
        near.put(mine, all_of.at[rows_of(net.b), lanes])
        gathers.append(Gather(net, mine, lambda y, c: all_of.at[rows_of(2 * y + c), lanes]))

    me = net.s
    gain_a = r.mixer_norm_gain[...][None]
    net.ready()
    rim = Beside(net, r.tokens.at[0, 64:128, :], r.rim_in, 1)
    rim.start()

    @pl.when(me == 0)
    def _():
        r.rim_in[...] = jnp.zeros_like(r.rim_in)

    normal, _ = pieces(r.tokens[0].astype(F32))
    r.normed_a[...] = (normal * gain_a).astype(BF)
    gather("normed_a")
    for part in range(8):
        rows = slice(BLOCK * part, BLOCK * part + BLOCK)
        r.phase_cos[rows, :] = jnp.broadcast_to(r.phases[part : part + 1, :], (BLOCK, BLOCK)).T
        r.phase_sin[rows, :] = jnp.broadcast_to(r.phases[8 + part : 9 + part, :], (BLOCK, BLOCK)).T
    thirds[0].wait()
    r.value_a[...] = mm(r.normed_a[...], r.mixer_in[:, 2 * WIDE :])
    r.value_low[...] = r.value_a[0:64, :].astype(BF)
    later = Beside(net, r.value_low, r.value_next, -1)
    later.start()

    @pl.when(me == RANKS - 1)
    def _():
        r.value_next[...] = jnp.zeros_like(r.value_next)

    thirds[1].wait()
    r.query_a[...] = mm(r.normed_a[...], r.mixer_in[:, 0:WIDE])
    keep("query_a", "value_a")
    thirds[2].wait()
    fetch("shift_taps", "mode_coef", "mode_rate", *TABLES, "mixer_out")
    fetch("up_first", "down_first", "project_in")
    r.key_ext[64:192, :] = mm(r.normed_a[...], r.mixer_in[:, WIDE : 2 * WIDE])
    rim.wait_recv()
    normal, _ = pieces(r.rim_in[...].astype(F32))
    r.key_ext[0:64, :] = mm((normal * gain_a).astype(BF), r.mixer_in[:, WIDE : 2 * WIDE])
    for name in ("shift_taps", "mode_coef", "mode_rate"):
        wait[name].wait()
    shift_forward(r.key_ext, r.shift_taps, None, r.shifted)
    r.product_low[...] = (r.shifted[...] * r.value_a[...]).astype(BF)
    go = net.spread(lambda block: r.product_low.at[:, lanes_of(block)], lambda rank: r.signal.at[rows_of(rank), :], True)
    go.start()
    go.own()
    keep("key_ext", "shifted")
    block = lanes_of(jnp.clip(me - 1, 0, OWNERS - 1))
    r.coef[...] = r.mode_coef[:, block]
    r.rate[...] = r.mode_rate[:, block]
    modes(r.coef, r.rate, r.mode_rows)
    for name in TABLES:
        wait[name].wait()
    transform_two(r, r.mode_rows[...], r.kernel_re, r.kernel_im)
    turned = r.kernel_re[...] * r.phase_cos[...] - r.kernel_im[...] * r.phase_sin[...]
    r.kernel_im[...] = r.kernel_im[...] * r.phase_cos[...] + r.kernel_re[...] * r.phase_sin[...]
    r.kernel_re[...] = turned
    keep("kernel_re", "kernel_im")
    transform(r, net, go, r.signal, r.signal_re, r.signal_im)
    back = net.spread(lambda rank: r.conv.at[rows_of(rank), :], lambda block: r.conv_home.at[:, lanes_of(block)], False)
    inverse(
        r,
        r.signal_re[...] * r.kernel_re[...] - r.signal_im[...] * r.kernel_im[...],
        r.signal_re[...] * r.kernel_im[...] + r.signal_im[...] * r.kernel_re[...],
        r.conv,
        back,
    )
    back.own()
    for name in ("mixer_out", "up_first", "down_first", "project_in"):
        wait[name].wait()
    back.wait_recv()
    r.response[...] = r.conv_home[...].astype(F32) + r.skip_gain[...][None] * (r.shifted[...] * r.value_a[...])
    r.gated[...] = (r.query_a[...] * r.response[...]).astype(BF)
    gather("gated")
    stream_b = r.tokens[0].astype(F32) + mm(r.gated[...], r.mixer_out[...])
    r.stream_b[...] = stream_b
    normal, _ = pieces(stream_b)
    r.normed_b[...] = (normal * r.gain_second[...][None]).astype(BF)
    gather("normed_b")
    r.stream_c[...] = stream_b
    for chunk in range(4):
        lanes = slice(WIDE * chunk, WIDE * chunk + WIDE)
        active, bend = gelu_parts(mm(r.normed_b[...], r.up_first[:, lanes]))
        r.bend_b[:, lanes] = bend.astype(BF)
        active = active.astype(BF)
        r.active_b[:, lanes] = active
        gather("active_b", lanes)
        r.stream_c[...] += mm(active, r.down_first[lanes, :])
    normal, _ = pieces(r.stream_c[...])
    r.normed_c[...] = (normal * r.attention_norm_gain[...][None]).astype(BF)
    gather("normed_c")
    for index in range(3):
        r.mixed_c[index] = mm(r.normed_c[...], r.project_in[:, WIDE * index : WIDE * index + WIDE]).astype(BF)
    go = net.spread(lambda block: r.mixed_c.at[:, :, lanes_of(block)], lambda rank: r.qkv.at[:, rows_of(rank), :], True)
    go.start()
    go.own()
    keep("response", "stream_b", "bend_b")
    for made in gathers[:3]:
        made.forward()
    turned = r.signal_re[...] * r.phase_cos[...] - r.signal_im[...] * r.phase_sin[...]
    r.signal_im[...] = -(r.signal_im[...] * r.phase_cos[...] + r.signal_re[...] * r.phase_sin[...])
    r.signal_re[...] = turned
    keep("signal_re", "signal_im")
    later.wait_recv()
    keep("value_next")
    go.wait_recv()
    keep("qkv")
    back = net.spread(lambda rank: r.attended_low.at[rows_of(rank), :], lambda block: r.attended.at[:, lanes_of(block)], False)
    for part in (3, 2, 1, 0):
        attention_forward(r, part)
        back.start(lambda rank, part=part: rank // 2 == part)
    back.own()
    keep("lse", "attended_full")
    for made in gathers[3:]:
        made.forward()
    back.wait_recv()
    for made in gathers:
        made.wait()
    net.finish()
    near.finish()


def kernel_b(r):
    net = Net(r.send_sem, r.recv_sem)
    near = Locals(r.local_sem)
    net.hello()
    wait = {}

    def fetch(name, into=None):
        wait[name] = near.start(getattr(r, name + "_hbm"), getattr(r, into or name))

    for name, into in (("project_out", "out_weight"), ("attended", "attended"), ("stream_c", "stream_c"), ("cotangent", "cotangent")):
        fetch(name, into)
    chunks = []
    for step, (index, other) in enumerate(net.order()):
        lanes = pl.ds(pl.multiple_of(WIDE * index, WIDE), WIDE)
        chunks.append(
            (
                near.start(r.up_second_hbm.at[:, lanes], r.up.at[:, lanes]),
                near.start(r.down_second_hbm.at[lanes, :], r.down.at[lanes, :]),
            )
        )
    r.ends[0] = r.doc_lengths[0, 0]
    r.ends[1] = r.ends[0] + r.doc_lengths[0, 1]
    r.ends[2] = r.ends[1] + r.doc_lengths[0, 2]
    up_d, down_d, pair_c = Sum(r, net, "up_d", UP), Sum(r, net, "down_d", DOWN), Sum(r, net, "pair_c", PAIR)
    up_b, down_b, pair_a = Sum(r, net, "up_b", UP), Sum(r, net, "down_b", DOWN), Sum(r, net, "pair_a", PAIR)
    own_rows = rows_of(net.b)

    gain_d = r.gain_fourth[...][None]
    for name in ("project_out", "attended", "stream_c", "cotangent"):
        wait[name].wait()
    stream_d = r.stream_c[...] + mm(r.attended[...], r.out_weight[...])
    normal, inverse_d = pieces(stream_d)
    normed_d = (normal * gain_d).astype(BF)
    r.layer_left[own_rows, :] = normed_d
    r.total[...] = stream_d
    r.turned[...] = r.cotangent[0].T
    r.pair_two[own_rows, :] = r.attended[...]
    net.ready()
    gather_d = Gather(net, r.layer_left.at[own_rows, :], lambda y, c: r.layer_left.at[rows_of(2 * y + c), :])
    down_d.share_rows(r.turned)
    spots = []
    for step, (index, other) in enumerate(net.order()):
        lanes = pl.ds(pl.multiple_of(WIDE * index, WIDE), WIDE)
        for copy in chunks[step]:
            copy.wait()
        if step == 3:
            for name in KEPT[:11]:
                fetch(name)
            fetch("project_in", "in_weight")
            fetch("normed_c_all", "pair_one")
            fetch("tokens")
            for name in ("shift_taps", "mode_coef", "mode_rate") + TABLES:
                fetch(name)
        raised = mm(r.layer_left[own_rows, :], r.up[:, lanes])
        active, slope = gelu_parts(raised)
        active = active.astype(BF)
        r.layer_second[own_rows, lanes] = active

        def spot(y, c, step=step):
            at = pl.ds(pl.multiple_of(WIDE * net.turn_of(step, y, c), WIDE), WIDE)
            return r.layer_second.at[rows_of(2 * y + c), at]

        spots.append(spot)
        slope = (slope * mm_nt(r.cotangent[0], r.down[lanes, :])).astype(BF)
        up_d.give(r.slopes, step, slope, other)
        back = mm_nt(slope, r.up[:, lanes])
        if step == 0:
            r.grad_d[...] = back
        else:
            r.grad_d[...] += back
    gathers = [Gather(net, spot(net.y, net.c), spot) for spot in spots]
    grad, gain_four = pieces_back(r.grad_d[...], normal, inverse_d, gain_d)
    grad = r.cotangent[0].astype(F32) + grad
    r.grad_d[...] = grad
    r.grad_d_low[...] = grad.astype(BF)
    r.att_grad_home[...] = mm_nt(r.grad_d_low[...], r.out_weight[...]).astype(BF)
    go = net.spread(lambda block: r.att_grad_home.at[:, lanes_of(block)], lambda rank: r.att_grad.at[rows_of(rank), :], True)
    go.start()
    go.own()
    gather_att = Gather(net, r.pair_two.at[own_rows, :], lambda y, c: r.pair_two.at[rows_of(2 * y + c), :])
    fetch("up_first", "up")
    fetch("mixer_out", "out_weight")

    r.key_grad[...] = jnp.zeros_like(r.key_grad)
    r.value_grad[...] = jnp.zeros_like(r.value_grad)
    gather_d.forward()
    for name in ("qkv", "lse", "attended_full"):
        wait[name].wait()
    gather_d.wait()
    turn(r.layer_left, r.turned_one)
    gather_d.free()
    fetch("normed_b_all", "layer_left")
    up_d.product(r.turned_one, None)
    go.wait_recv()
    back = net.spread(
        lambda rank: r.qkv_grad.at[:, rows_of(rank), :], lambda block: r.mixed_grad_c.at[:, :, lanes_of(block)], False
    )
    for part in (3, 2, 1, 0):
        attention_back(r, part)
        back.start(lambda rank, part=part: rank // 2 == part)
    back.own()
    for name, into in (
        ("kernel_re", "lse"),
        ("kernel_im", "attended_full"),
        ("signal_re", "query_grad"),
        ("signal_im", "key_grad"),
    ):
        fetch(name, into)
    up_d.second()
    r.block_out[0] = (r.total[...] + mm(r.layer_second[own_rows, :], r.down[...])).astype(BF)
    fetch("down_first", "down")
    for made in gathers:
        made.forward()
    for made in gathers:
        made.wait()
    down_d.product(None, r.layer_second)
    for made in gathers:
        made.free()
    fetch("active_b_all", "layer_second")
    up_d.last()

    normal, inverse_c = pieces(r.stream_c[...])
    wait["project_in"].wait()
    back.wait_recv()
    grad = mm_nt(r.mixed_grad_c[0], r.in_weight[:, 0:WIDE])
    for index in range(1, 3):
        grad = grad + mm_nt(r.mixed_grad_c[index], r.in_weight[:, WIDE * index : WIDE * index + WIDE])
    fetch("mixer_in", "in_weight")
    pair_columns(r.mixed_grad_c, r.grad_d_low, r.pairs)
    pair_c.share_pairs(r.pairs)
    grad, gain_three = pieces_back(grad, normal, inverse_c, r.attention_norm_gain[...][None])
    grad = grad + r.grad_d[...]
    r.total[...] = grad
    r.grad_c_low[...] = grad.astype(BF)
    down_d.free_shared()
    r.turned[...] = r.grad_c_low[...].T
    down_b.share_rows(r.turned)
    up_d.free_shared()
    wait["up_first"].wait()
    wait["down_first"].wait()
    wait["bend_b"].wait()
    for step, (index, other) in enumerate(net.order()):
        lanes = pl.ds(pl.multiple_of(WIDE * index, WIDE), WIDE)
        slope = (r.bend_b[:, lanes].astype(F32) * mm_nt(r.grad_c_low[...], r.down[lanes, :])).astype(BF)
        up_b.give(r.slopes, step, slope, other)
        part = mm_nt(slope, r.up[:, lanes])
        if step == 0:
            r.grad_b[...] = part
        else:
            r.grad_b[...] += part
    for name in ("stream_b", "response", "query_a", "shifted", "value_a", "key_ext", "mixer_out"):
        wait[name].wait()
    normal, inverse_b = pieces(r.stream_b[...])
    grad, gain_two = pieces_back(r.grad_b[...], normal, inverse_b, r.gain_second[...][None])
    grad = grad + r.total[...]
    r.grad_b[...] = grad
    r.grad_b_low[...] = grad.astype(BF)
    gated_grad = mm_nt(r.grad_b_low[...], r.out_weight[...])
    r.mixed_grad_a[0] = (gated_grad * r.response[...]).astype(BF)
    response_grad = gated_grad * r.query_a[...]
    r.response_grad[...] = response_grad
    r.response_grad_low[...] = response_grad.astype(BF)
    go = net.spread(
        lambda block: r.response_grad_low.at[:, lanes_of(block)], lambda rank: r.conv_grad.at[rows_of(rank), :], True
    )
    go.start()
    go.own()
    after = Beside(net, r.response_grad_low.at[0:64, :], r.response_next, -1)
    after.start()

    @pl.when(net.s == RANKS - 1)
    def _():
        r.response_next[...] = jnp.zeros_like(r.response_next)

    skip_part = jnp.sum(response_grad * (r.shifted[...] * r.value_a[...]), axis=0, keepdims=True)
    down_d.second()
    gather_att.forward()
    wait["normed_c_all"].wait()
    turn(r.pair_one, r.turned_one)
    gather_att.wait()
    turn(r.pair_two, r.turned_two)
    gather_att.free()
    fetch("normed_a_all", "pair_one")
    fetch("gated_all", "pair_two")
    pair_c.product(r.turned_one, r.turned_two)
    wait["active_b_all"].wait()
    down_b.product(None, r.layer_second)
    wait["normed_b_all"].wait()
    turn(r.layer_left, r.turned_one)
    up_d.end(near)

    for name in TABLES + ("kernel_re", "kernel_im", "signal_re", "signal_im"):
        wait[name].wait()
    kernel_re, kernel_im, signal_re, signal_im = r.lse, r.attended_full, r.query_grad, r.key_grad
    r.signal_grad[SPAN:, :] = jnp.zeros((64, BLOCK), BF)
    transform(r, net, go, r.conv_grad, r.grad_re, r.grad_im)
    back = net.spread(
        lambda rank: r.signal_grad.at[pl.ds(pl.multiple_of(ROWS * rank, ROWS), 192), :],
        lambda block: r.signal_grad_home.at[:, lanes_of(block)],
        False,
    )
    inverse(
        r,
        r.grad_re[...] * kernel_re[...] + r.grad_im[...] * kernel_im[...],
        r.grad_im[...] * kernel_re[...] - r.grad_re[...] * kernel_im[...],
        r.signal_grad,
        back,
    )
    back.own()
    up_b.product(r.turned_one, None)
    down_d.last()
    pair_c.second()
    down_b.second()
    after.wait_recv()
    for name in ("shift_taps", "mode_coef", "mode_rate", "value_next"):
        wait[name].wait()
    back.wait_recv()

    skip = r.skip_gain[...][None]
    signal_grad = r.signal_grad_home[0:ROWS, :].astype(F32) + skip * r.response_grad[...]
    r.grad_ext[0:ROWS, :] = signal_grad * r.value_a[...]
    r.mixed_grad_a[2] = (signal_grad * r.shifted[...]).astype(BF)
    signal_grad = r.signal_grad_home[ROWS:192, :].astype(F32) + skip * r.response_next[...].astype(F32)
    r.grad_ext[ROWS:192, :] = signal_grad * r.value_next[...].astype(F32)
    shift_back(r.grad_ext, r.key_ext, r.shift_taps, r.total, r.taps)
    r.mixed_grad_a[1] = r.total[...].astype(BF)
    pair_c.free_shared()
    pair_columns(r.mixed_grad_a, r.grad_b_low, r.pairs)
    pair_a.share_pairs(r.pairs)
    wait["mixer_in"].wait()
    wait["tokens"].wait()
    grad = mm_nt(r.mixed_grad_a[0], r.in_weight[:, 0:WIDE])
    for index in range(1, 3):
        grad = grad + mm_nt(r.mixed_grad_a[index], r.in_weight[:, WIDE * index : WIDE * index + WIDE])
    normal, inverse_a = pieces(r.tokens[0].astype(F32))
    grad, gain_one = pieces_back(grad, normal, inverse_a, r.mixer_norm_gain[...][None])
    r.token_grad[0] = r.grad_b[...] + grad

    gains = jnp.concatenate([gain_one, skip_part, gain_two, gain_three, gain_four, jnp.zeros((3, WIDE), F32)], axis=0)
    for block in range(4):
        r.small[block // 2, block % 2, 0:16, :] = r.taps[16 * block : 16 * block + 16, :]
        r.small[block // 2, block % 2, 16:24, :] = gains
    swap = net.send(r.small.at[:, flip(net.c)], r.small_c, net.sibling)
    re = r.grad_re[...] * signal_re[...] - r.grad_im[...] * signal_im[...]
    im = r.grad_re[...] * signal_im[...] + r.grad_im[...] * signal_re[...]
    inverse(r, re, im, r.value_grad)
    block = lanes_of(jnp.clip(net.s - 1, 0, OWNERS - 1))
    r.coef[...] = r.mode_coef[:, block]
    r.rate[...] = r.mode_rate[:, block]
    wait["normed_a_all"].wait()
    turn(r.pair_one, r.turned_one)
    wait["gated_all"].wait()
    turn(r.pair_two, r.turned_two)
    up_b.second()
    swap.wait_recv()
    r.small[:, net.c] += r.small_c[...]
    swap = net.send(r.small.at[flip(net.y), net.c], r.small_y, net.by_y)
    pair_c.last()
    down_b.last()
    pair_a.product(r.turned_one, r.turned_two)
    modes_back(r.coef, r.rate, r.value_grad, r.mode_part.at[0, 0:64], r.mode_part.at[0, 64:128])
    mode = net.send(r.mode_part.at[0], r.mode_swap.at[0], net.sibling)
    swap.wait_recv()
    r.small_sum[...] = r.small[net.y, net.c] + r.small_y[...]
    here = pl.ds(pl.multiple_of(384 * net.high, BLOCK), 384)
    there = pl.ds(pl.multiple_of(384 * flip(net.high), BLOCK), 384)
    swap = net.send(r.small_sum.at[:, there], r.half_swap.at[0], net.by_high)
    up_b.last()
    mode.wait_recv()
    r.mode_part[1] = r.mode_part[0] + r.mode_swap[0]
    mode = net.send(r.mode_part.at[1], r.mode_swap.at[1], net.by_y)
    pair_a.second()
    mode.wait_recv()
    r.mode_part[2] = r.mode_part[1] + r.mode_swap[1]
    back = net.spread(
        lambda rank: r.mode_part.at[2], lambda block: r.mode_home.at[:, lanes_of(block)], False, holds_columns
    )
    back.start()
    back.own()
    swap.wait_recv()
    r.half_sum[0] = r.small_sum[:, here] + r.half_swap[0]
    swap = net.send(r.half_sum.at[0], r.half_swap.at[1], net.by_low)
    pair_a.last()
    swap.wait_recv()
    r.half_sum[1] = r.half_sum[0] + r.half_swap[1]
    swap = net.send(r.half_sum.at[1], r.half_swap.at[2], net.by_x)
    down_d.end(near)
    pair_c.end(near)
    down_b.end(near)
    turn_back = lax.rem(WIDE - 96 * net.s, WIDE)
    back.wait_recv()
    r.mode_out[...] = pltpu.roll(r.mode_home[...], turn_back, 1)[:, 0:128]
    swap.wait_recv()
    half_back = lax.rem(4 * 96 - 96 * lax.rem(net.s, 4), 384)
    r.small_out[...] = pltpu.roll(r.half_sum[1] + r.half_swap[2], half_back, 1)[:, 0:128]
    up_b.end(near)
    pair_a.end(near)
    net.finish()
    near.finish()


def kernel_z(*refs):
    block_in, token_in, mode, small = refs[:4]
    sums = refs[4:16]
    (
        block_out,
        token_grad,
        gain_one,
        mixer_in,
        taps,
        coef,
        rate,
        skip,
        mixer_out,
        gain_two,
        up_first,
        down_first,
        gain_three,
        project_in,
        project_out,
        gain_four,
        up_second,
        down_second,
    ) = refs[16:]
    block_out[...] = block_in[...]
    token_grad[...] = token_in[...]
    taps[...] = small[0:16, 0:96]
    for at, out in enumerate((gain_one, skip, gain_two, gain_three, gain_four)):
        out[...] = small[16 + at, 0:96]
    coef[...] = mode[0:64, 0:96]
    rate[...] = mode[64:128, 0:96]

    def block(index, first, count):
        rows = slice(first, first + count)
        return sums[2 * index][rows, :].astype(F32) + sums[2 * index + 1][rows, :].astype(F32)

    for index, up, down in ((0, up_second, down_second), (3, up_first, down_first)):
        for tile in range(6):
            up[:, 128 * tile : 128 * tile + 128] = block(index, 96 * tile, 96)
        for tile in range(3):
            down[:, 128 * tile : 128 * tile + 128] = block(index + 1, 192 * tile, 192)
    for index, wide, narrow in ((2, project_in, project_out), (5, mixer_in, mixer_out)):
        for tile in range(4):
            wide[:, 128 * tile : 128 * tile + 128] = block(index, 96 * tile, 96)
        mixed = block(index, 384, 96)
        wide[:, 512:576] = mixed[:, 0:64]
        narrow[:, 0:64] = mixed[:, 64:128]
        narrow[:, 64:192] = block(index, 480, 96)


class Refs:
    pass


def call(body, identity, inputs, hbm, smem, outs, hbm_outs, scratch, semaphores):
    names = list(inputs) + [name + "_hbm" for name in hbm] + list(smem) + list(outs) + list(hbm_outs) + list(scratch)
    names += ["ends", "send_sem", "recv_sem", "local_sem"]

    def run(*refs):
        r = Refs()
        for name, ref in zip(names, refs):
            setattr(r, name, ref)
        body(r)

    vmem = pl.BlockSpec(memory_space=pltpu.VMEM)
    results = pl.pallas_call(
        run,
        out_shape=[jax.ShapeDtypeStruct(shape, kind) for shape, kind in (*outs.values(), *hbm_outs.values())],
        in_specs=[vmem] * len(inputs)
        + [pl.BlockSpec(memory_space=pl.ANY)] * len(hbm)
        + [pl.BlockSpec(memory_space=pltpu.SMEM)] * len(smem),
        out_specs=[vmem] * len(outs) + [pl.BlockSpec(memory_space=pl.ANY)] * len(hbm_outs),
        scratch_shapes=[pltpu.VMEM(shape, kind) for shape, kind in scratch.values()]
        + [pltpu.SMEM((3,), jnp.int32)]
        + [pltpu.SemaphoreType.DMA((semaphores[0],)), pltpu.SemaphoreType.DMA((semaphores[0],))]
        + [pltpu.SemaphoreType.DMA((semaphores[1],))],
        compiler_params=pltpu.CompilerParams(
            collective_id=identity, has_side_effects=True, vmem_limit_bytes=VMEM_BYTES
        ),
    )(*inputs.values(), *hbm.values(), *smem.values())
    return dict(zip((*outs, *hbm_outs), results))


VMEM_BYTES = 66_900_000


def odd_tables():
    odd = 2 * np.arange(SPAN, dtype=np.int64) + 1
    angle = (np.outer(odd, odd) % (8 * SPAN)) * (math.pi / (4 * SPAN))
    phase = (odd * (math.pi / (4 * SPAN))).reshape(8, BLOCK)
    tables = {
        "cos_table": jnp.asarray(np.cos(angle).astype(ml_dtypes.bfloat16)),
        "sin_table": jnp.asarray(np.sin(angle).astype(ml_dtypes.bfloat16)),
    }
    return tables, jnp.asarray(np.concatenate([np.cos(phase), np.sin(phase)]), F32)


def shards_fast(
    tokens,
    doc_lengths,
    mixer_norm_gain,
    mixer_in,
    shift_taps,
    mode_coef,
    mode_rate,
    skip_gain,
    mixer_out,
    gain_second,
    up_first,
    down_first,
    attention_norm_gain,
    project_in,
    project_out,
    gain_fourth,
    up_second,
    down_second,
    cotangent,
):
    tables, phases = odd_tables()
    home, thrice, tall = (ROWS, WIDE), (3, ROWS, WIDE), (ROWS, 4 * WIDE)
    span = (SPAN, BLOCK)
    kept = dict(
        value_next=((64, WIDE), BF),
        query_a=(home, F32),
        value_a=(home, F32),
        key_ext=((192, WIDE), F32),
        shifted=(home, F32),
        response=(home, F32),
        stream_b=(home, F32),
        bend_b=(tall, BF),
        qkv=((3, *span), BF),
        lse=(span, F32),
        attended_full=(span, F32),
        kernel_re=(span, F32),
        kernel_im=(span, F32),
        signal_re=(span, F32),
        signal_im=(span, F32),
    )
    lefts = dict(normed_a=(home, BF), gated=(home, BF), normed_b=(home, BF), active_b=(tall, BF), normed_c=(home, BF))
    modes_scratch = dict(
        coef=((64, BLOCK), F32),
        rate=((64, BLOCK), F32),
        shift_taps=((64, WIDE), F32),
        mode_coef=((64, WIDE), F32),
        mode_rate=((64, WIDE), F32),
    )
    packs = dict(pack_re=((SPAN, 256), BF), pack_im=((SPAN, 256), BF))
    table_scratch = dict(cos_table=((SPAN, SPAN), BF), sin_table=((SPAN, SPAN), BF))
    a = call(
        kernel_a,
        0,
        dict(
            tokens=tokens,
            mixer_norm_gain=mixer_norm_gain,
            skip_gain=skip_gain,
            gain_second=gain_second,
            attention_norm_gain=attention_norm_gain,
            phases=phases,
        ),
        dict(
            mixer_in=mixer_in,
            shift_taps=shift_taps,
            mode_coef=mode_coef,
            mode_rate=mode_rate,
            **tables,
            mixer_out=mixer_out,
            up_first=up_first,
            down_first=down_first,
            project_in=project_in,
        ),
        dict(doc_lengths=doc_lengths),
        dict(stream_c=(home, F32), attended=(home, BF)),
        dict(
            **{name + "_kept": made for name, made in kept.items()},
            **{name + "_all": ((4 * shape[0], shape[1]), kind) for name, (shape, kind) in lefts.items()},
        ),
        dict(
            **kept,
            **lefts,
            **modes_scratch,
            **packs,
            rim_in=((64, WIDE), BF),
            **table_scratch,
            phase_cos=(span, F32),
            phase_sin=(span, F32),
            value_low=((64, WIDE), BF),
            product_low=(home, BF),
            signal=(span, BF),
            mode_rows=(span, F32),
            conv=(span, BF),
            conv_home=(home, BF),
            mixed_c=(thrice, BF),
            attended_low=(span, BF),
            mixer_in=((WIDE, 3 * WIDE), BF),
            mixer_out=((WIDE, WIDE), BF),
            up_first=((WIDE, 4 * WIDE), BF),
            down_first=((4 * WIDE, WIDE), BF),
            project_in=((WIDE, 3 * WIDE), BF),
        ),
        (64, 48),
    )
    kinds = dict(up_d=UP, down_d=DOWN, pair_c=PAIR, up_b=UP, down_b=DOWN, pair_a=PAIR)
    sum_outs, sums = {}, {}
    for name, kind in kinds.items():
        sum_outs[name + "_own"] = ((LENGTH, 128), BF)
        sum_outs[name + "_third"] = ((LENGTH, 128), BF)
        sums.update(sum_scratch(name, kind))
    b = call(
        kernel_b,
        1,
        dict(
            mixer_norm_gain=mixer_norm_gain,
            skip_gain=skip_gain,
            gain_second=gain_second,
            attention_norm_gain=attention_norm_gain,
            gain_fourth=gain_fourth,
        ),
        dict(
            project_out=project_out,
            attended=a["attended"],
            stream_c=a["stream_c"],
            cotangent=cotangent,
            tokens=tokens,
            up_second=up_second,
            down_second=down_second,
            **{name: a[name + "_kept"] for name in kept},
            **{name + "_all": a[name + "_all"] for name in lefts},
            **tables,
            shift_taps=shift_taps,
            mode_coef=mode_coef,
            mode_rate=mode_rate,
            project_in=project_in,
            up_first=up_first,
            down_first=down_first,
            mixer_out=mixer_out,
            mixer_in=mixer_in,
        ),
        dict(doc_lengths=doc_lengths),
        dict(
            block_out=((1, *home), BF),
            token_grad=((1, *home), F32),
            mode_out=((128, 128), F32),
            small_out=((24, 128), F32),
        ),
        sum_outs,
        dict(
            **{name: made for name, made in kept.items() if not name.startswith(("kernel", "signal"))},
            **modes_scratch,
            **packs,
            **table_scratch,
            **sums,
            attended=(home, BF),
            stream_c=(home, F32),
            cotangent=((1, *home), BF),
            tokens=((1, *home), BF),
            up=((WIDE, 4 * WIDE), BF),
            down=((4 * WIDE, WIDE), BF),
            in_weight=((WIDE, 3 * WIDE), BF),
            out_weight=((WIDE, WIDE), BF),
            layer_left=((512, WIDE), BF),
            layer_second=((512, 4 * WIDE), BF),
            pair_one=((512, WIDE), BF),
            pair_two=((512, WIDE), BF),
            turned_one=((WIDE, 512), BF),
            turned_two=((WIDE, 512), BF),
            turned=((WIDE, ROWS), BF),
            slopes=(thrice, BF),
            pairs=((4, *home), BF),
            total=(home, F32),
            grad_d=(home, F32),
            grad_d_low=(home, BF),
            att_grad_home=(home, BF),
            att_grad=(span, BF),
            query_grad=(span, F32),
            key_grad=(span, F32),
            value_grad=(span, F32),
            qkv_grad=((3, *span), BF),
            mixed_grad_c=(thrice, BF),
            grad_c_low=(home, BF),
            grad_b=(home, F32),
            grad_b_low=(home, BF),
            mixed_grad_a=(thrice, BF),
            response_grad=(home, F32),
            response_grad_low=(home, BF),
            conv_grad=(span, BF),
            grad_re=(span, F32),
            grad_im=(span, F32),
            signal_grad=((SPAN + 64, BLOCK), BF),
            signal_grad_home=((192, WIDE), BF),
            response_next=((64, WIDE), BF),
            grad_ext=((192, WIDE), F32),
            taps=((64, WIDE), F32),
            small=((2, 2, 24, WIDE), F32),
            small_c=((2, 24, WIDE), F32),
            small_y=((24, WIDE), F32),
            small_sum=((24, WIDE), F32),
            half_swap=((3, 24, 384), F32),
            half_sum=((2, 24, 384), F32),
            mode_part=((3, 128, 128), F32),
            mode_swap=((2, 128, 128), F32),
            mode_home=((128, WIDE), F32),
        ),
        (160, 64),
    )
    vmem = pl.BlockSpec(memory_space=pltpu.VMEM)
    given = [b[name] for name in ("block_out", "token_grad", "mode_out", "small_out")]
    for name in kinds:
        given += [b[name + "_own"], b[name + "_third"]]
    gain = ((96,), F32)
    wide, narrow, up, down, mode = ((96, 576), F32), ((96, 192), F32), ((96, 768), F32), ((192, 384), F32), ((64, 96), F32)
    shapes = (
        ((1, *home), BF),
        ((1, *home), F32),
        gain,
        wide,
        ((16, 96), F32),
        mode,
        mode,
        gain,
        narrow,
        gain,
        up,
        down,
        gain,
        wide,
        narrow,
        gain,
        up,
        down,
    )
    results = pl.pallas_call(
        kernel_z,
        out_shape=[jax.ShapeDtypeStruct(shape, kind) for shape, kind in shapes],
        in_specs=[vmem] * len(given),
        out_specs=[vmem] * len(shapes),
    )(*given)
    return tuple(result.T if result.shape == (192, 384) else result for result in results)


def solution(mesh):
    in_specs = (
        P("batch", "seq", None),
        P("batch", None),
        P(),
        P(),
        P(),
        P(),
        P(),
        P(),
        P(),
        P(),
        P(),
        P(),
        P(),
        P(),
        P(),
        P(),
        P(),
        P(),
        P("batch", "seq", None),
    )
    out_specs = (
        P("batch", "seq", None),
        P("batch", "seq", None),
        P("seq"),
        P("seq", "batch"),
        P("batch", "seq"),
        P(None, "seq"),
        P(None, "seq"),
        P("seq"),
        P("seq", "batch"),
        P("seq"),
        P("seq", "batch"),
        P("seq", "batch"),
        P("seq"),
        P("seq", "batch"),
        P("seq", "batch"),
        P("seq"),
        P("seq", "batch"),
        P("seq", "batch"),
    )
    fast = mesh.shape["seq"] == RANKS and mesh.shape["batch"] == 4
    return jax.shard_map(shards_fast if fast else shards, mesh=mesh, in_specs=in_specs, out_specs=out_specs, check_vma=False)
```
